32 devices in a mesh: blk: 16 (over z, y, core), rep: 2 (over x).
Axes of the slice: x: 2, y: 2, z: 4, core: 2. Of those that a mesh axis runs over, the one named last changes fastest.
Arguments:
- hidden_in: bfloat16 [2, 2048, 1536], P('rep', 'blk'), may hold values from -12 to 12
- lengths: int32 [32], P('rep'), may hold values from 1 to 128, 2048 in all
- routes: int32 [2, 2048, 8], P('rep', 'blk'), may hold values from 0 to 31, all different within a row; in each aligned block of 128 rows (0 to 127, 128 to 255, ..., all dimensions but the last counted through in order) at most 36 rows name the same one
- route_weights: float32 [2, 2048, 8], P('rep', 'blk'), may hold values from 0.03 to 0.3
- norm_gain: float32 [1536], replicated, may hold values from 0.1 to 1.9
- master: float32 [3, 1536, 16, 1024], P(None, 'blk', None, 'rep'), may hold values from -1 to 1
- unembed: bfloat16 [32768, 1536], P('blk'), may hold values from -0.5 to 0.5
- final_gain: float32 [1536], replicated, may hold values from 0.5 to 1.5
- target_ids: int32 [32], P('rep'), may hold values from 0 to 32767
Outputs:
- hidden_out: bfloat16 [2, 2048, 1536], P('rep', 'blk')
- server_blocks: bfloat16 [3, 1536, 16384], P(None, None, 'blk')
- request_stats: float32 [3, 32], P(None, 'rep')
The draws below stay inside these ranges and needn't reach their ends.
Inputs may be any that keep to these rules, and one draw needn't show every extreme that they name: `routes`: in the 128 slots of one device no expert is named by more than 36 slots, and in some device one expert is named by exactly 36. The lengths of all 32 prompts sum to 2048 and the longest is exactly 128.
All inputs are finite; a program needn't handle non-finite values. No bound on the sum of `lengths` on one device may be relied on, other than what follows from the above.
Results may differ from the reference program's by a relative error of at most 0.0022.
Values may be sent and summed in bfloat16 or wider, within the bound.
No kernel may reach another device: no remote copies, remote signals or barrier semaphores. Data moves between devices by JAX's collectives and lax.ppermute only.
A program may use at most 128 MiB of HBM per device.

```python
import math
import jax
import jax.numpy as jnp
import numpy as np
from jax import lax

D = 1536
FF = 512
EXPERTS = 32
TOP = 8
VOCAB = 32768
LEN = 128
ROWS = 128
CAP = 36
UNITS_DEV = 1024
UNIT_BLOCKS = 16
TOKENS_REP = 2048
PROMPTS_REP = 16
REPLICAS = 2
PROMPTS = 32
TOKENS = 4096
N_BLK = 16


def draw_hidden_in(key, part):
    values = jnp.clip(jax.random.normal(key, (REPLICAS, TOKENS_REP, D), jnp.float32), -4.0, 4.0)
    position = (jnp.arange(TOKENS_REP) % LEN).astype(jnp.float32)
    rising = 1.0 + 2.0 * position / LEN
    return (values * rising[None, :, None]).astype(jnp.bfloat16)


def draw_master(key, part):
    shape_all = (3, D, UNIT_BLOCKS, UNITS_DEV)
    values = jnp.clip(jax.random.normal(key, shape_all, jnp.float32), -4.0, 4.0)
    fan_in = jnp.array([D, D, FF], jnp.float32)
    return (values * (fan_in ** (-0.5))[:, None, None, None]).astype(jnp.float32)


def with_ends(values, rng, smallest, largest):
    index_at = [jax.random.randint(jax.random.fold_in(rng, axis), (), 0, length) for axis, length in enumerate(values.shape)]
    main_axis = values.shape.index(max(values.shape))
    neighbour = index_at[:main_axis] + [(index_at[main_axis] + 1) % values.shape[main_axis]] + index_at[main_axis + 1:]
    return values.at[tuple(index_at)].set(smallest).at[tuple(neighbour)].set(largest)


def levels(own_key, shape, shards, low, top_value):
    factor_of, own = 1.0, jax.random.fold_in(own_key, 6)
    for dim, parts in shards:
        heights = jnp.exp(jax.random.uniform(jax.random.fold_in(own, dim), (parts,), jnp.float32, low / len(shards), top_value / len(shards)))
        factor_of = factor_of * jnp.repeat(heights, shape[dim] // parts).reshape([-1 if axis == dim else 1 for axis in range(len(shape))])
    return factor_of


def cumulative_ranks(number_of, lean):
    weights = [(1 << 20) // math.isqrt(grade ** lean) + 1 for grade in range(1, number_of + 1)]
    deviation = 1 + sum(weights) // (1 << 30)
    return np.cumsum(np.array([max(1, weight // deviation) for weight in weights]))


def skewed_ids(stream_key, dims, number_of, lean):
    grid = cumulative_ranks(number_of, lean)
    lot = jax.random.randint(jax.random.fold_in(stream_key, 1), dims, 0, int(grid[number_of - 1]))
    standing = jnp.searchsorted(jnp.asarray(grid, jnp.int32), lot, side="right")
    return jax.random.permutation(jax.random.fold_in(stream_key, 2), number_of)[standing].astype(jnp.int32)


def profile(amount, total, limit, lean):
    portions = [(1 << 20) // math.isqrt(standing ** lean) + 1 for standing in range(2, amount + 1)]
    spare, given = total - limit - (amount - 1), [1] * (amount - 1)
    while spare > 0:
        free = [i for i in range(amount - 1) if given[i] < limit]
        mass, budget = sum([portions[i] for i in free]), spare
        for i in free:
            addition = min(limit - given[i], max(1, budget * portions[i] // mass), spare)
            given[i] = given[i] + addition
            spare = spare - addition
    return np.array([limit] + given)


def ragged(stream_key, amount, total, bound, slope):
    if amount == 2:
        one = jax.random.randint(stream_key, (), max(1, total - bound), min(bound, total - 1) + 1)
        return jnp.stack([one, total - one])
    sizes = jnp.asarray(profile(amount, total, bound, slope), jnp.int32)
    pairs = (amount - 1) // 2
    giver, sink = sizes[1:1 + 2 * pairs:2], sizes[2:2 + 2 * pairs:2]
    slack = jnp.minimum(giver - 1, bound - sink)
    shifted = jax.random.randint(jax.random.fold_in(stream_key, 1), (pairs,), 0, 1 << 20) % (slack + 1)
    sizes = sizes.at[1:1 + 2 * pairs:2].set(giver - shifted).at[2:2 + 2 * pairs:2].set(sink + shifted)
    return sizes[jax.random.permutation(jax.random.fold_in(stream_key, 2), amount)]


def assign_block(key, own, number, rows, number_of, top, bound, skew):
    order = jax.random.permutation(key, number_of)
    packed, common = load_shares(number_of, rows * top, bound, skew, True), load_shares(number_of, rows * top, bound, skew, False)
    places = jnp.arange(number_of)

    def named(sizes, offset_by):
        used = int((sizes > 0).sum())
        fixed = max(1, used // 4)
        passed = fixed + (places - fixed + offset_by * (used - fixed)) % max(1, number_of - fixed)
        return jnp.zeros((number_of,), jnp.int32).at[order[jnp.where(places < fixed, places, passed)]].set(jnp.asarray(sizes, jnp.int32))

    sizes = jnp.where(number % 4 == 0, named(packed, number // 4), named(common, number - number // 4 - 1))
    mixed = jax.random.permutation(jax.random.fold_in(own, 3), number_of)
    giver, taker = mixed[0:number_of // 2 * 2:2], mixed[1:number_of // 2 * 2:2]
    slack = jnp.minimum(sizes[giver] - 1, bound - sizes[taker]) // 2
    slack = jnp.where((giver == order[0]) | (taker == order[0]) | (sizes[taker] == 0), 0, jnp.maximum(slack, 0))
    passed = jax.random.randint(jax.random.fold_in(own, 4), (number_of // 2,), 0, 1 << 20) % (slack + 1)
    sizes = sizes.at[giver].add(-passed).at[taker].add(passed)
    members = jnp.searchsorted(jnp.cumsum(sizes), jnp.arange(rows * top), side="right").astype(jnp.int32)
    grid = members.reshape(top, rows).T
    grid = grid[jax.random.permutation(jax.random.fold_in(own, 1), rows)]
    offset_by = jax.random.randint(jax.random.fold_in(own, 2), (rows, 1), 0, top)
    return jnp.take_along_axis(grid, (jnp.arange(top)[None, :] + offset_by) % top, axis=1)


def load_shares(number_of, total, limit, skew, full):
    loads = [(1 << 20) // math.isqrt(grade ** skew) + 1 for grade in range(1, number_of + 1)]
    largest = limit if full else min(limit, max(-(-total // number_of), total * loads[0] // sum(loads)))
    least = 1 if total - largest >= number_of - 1 else 0
    given, surplus = [largest] + [least] * (number_of - 1), total - largest - least * (number_of - 1)
    while surplus > 0:
        free = [i for i in range(1, number_of) if given[i] < largest] or [i for i in range(1, number_of) if given[i] < limit]
        pool, remaining = sum([loads[i] for i in free]), surplus
        for i in free:
            more = min(limit - given[i], max(1, remaining * loads[i] // pool), surplus)
            given[i] = given[i] + more
            surplus = surplus - more
    return np.array(given)


def centred(key, dims, spread, limit, shards=(), kind=jnp.bfloat16):
    factor_of = levels(key, dims, shards, -0.22, 0.18) if shards else 1.0
    drawn = jax.random.normal(key, dims, jnp.float32) * spread * factor_of
    return jnp.minimum(jnp.maximum(drawn, -limit), limit).astype(kind)


def setup_inputs(seed: int = 0) -> dict:
    arg_keys = jax.random.split(jax.random.key(seed), 10)
    hidden_in = draw_hidden_in(jax.random.fold_in(arg_keys[9], 71), 0)
    lengths = ragged(arg_keys[1], PROMPTS, PROMPTS * LEN // 2, LEN, 2).astype(jnp.int32)
    routes_keys = jax.random.split(jax.random.fold_in(arg_keys[2], 1), REPLICAS * TOKENS_REP // ROWS)
    routes_turns = jax.random.permutation(jax.random.fold_in(arg_keys[2], 3), REPLICAS * TOKENS_REP // ROWS)
    routes = jax.vmap(lambda own, number: assign_block(jax.random.fold_in(arg_keys[2], 2), own, number, ROWS, EXPERTS, TOP, CAP, 2))(routes_keys, routes_turns).reshape((REPLICAS, TOKENS_REP, TOP))
    route_weights = jnp.clip(jnp.exp(math.log(0.3) - 2.3025852 * jax.random.uniform(arg_keys[3], (REPLICAS, TOKENS_REP, TOP), jnp.float32) ** levels(arg_keys[3], (REPLICAS, TOKENS_REP, TOP), ((0, 2), (1, 16)), -0.2, 0.2)), 0.03, 0.3)
    norm_gain = jnp.clip(1.0 + 0.18 * jax.random.normal(arg_keys[4], (D,), jnp.float32), 0.1, 1.9)
    master = draw_master(jax.random.fold_in(arg_keys[9], 71), 0)
    unembed = centred(arg_keys[6], (VOCAB, D), 0.08, 0.5, ((0, 16),))
    final_gain = jnp.clip(1.0 + 0.1 * jax.random.normal(arg_keys[7], (D,), jnp.float32), 0.5, 1.5)
    target_ids = with_ends(skewed_ids(arg_keys[8], (PROMPTS,), VOCAB, 2), jax.random.fold_in(arg_keys[8], 3), 0, VOCAB - 1).astype(jnp.int32)
    return dict(hidden_in=hidden_in, lengths=lengths, routes=routes, route_weights=route_weights, norm_gain=norm_gain, master=master, unembed=unembed, final_gain=final_gain, target_ids=target_ids)


def reference(hidden_in, lengths, routes, route_weights, norm_gain, master, unembed, final_gain, target_ids):
    unit_count = EXPERTS * FF // N_BLK
    group_width = min(unit_count, FF)
    server = master.astype(jnp.bfloat16).reshape(3, D, EXPERTS * FF)
    tokens_all = hidden_in.reshape(TOKENS, D)
    token_index = jnp.arange(TOKENS, dtype=jnp.int32)
    slot_index = token_index % TOKENS_REP
    prompt_of = token_index // TOKENS_REP * PROMPTS_REP + slot_index // LEN
    position = slot_index % LEN
    row_len = lengths[prompt_of]
    is_valid = position < row_len
    resid_f = tokens_all.astype(jnp.float32)
    normed = (resid_f * lax.rsqrt(lax.optimization_barrier(jnp.mean(resid_f * resid_f, axis=-1, keepdims=True)) + 1e-05) * norm_gain).astype(jnp.bfloat16)
    choices_all = routes.reshape(TOKENS, TOP)
    weight_all = route_weights.reshape(TOKENS, TOP) * is_valid[:, None].astype(jnp.float32)
    most_rows = TOKENS // ROWS * CAP

    def per_expert(expert, total):
        expert = jnp.asarray(expert).astype(jnp.int32)
        match = choices_all == expert
        weight_row = lax.optimization_barrier(jnp.sum(jnp.where(match, weight_all, 0.0), axis=1))
        chosen = jnp.any(match, axis=1)
        picked = jnp.nonzero(chosen, size=most_rows, fill_value=0)[0].astype(jnp.int32)
        live = jnp.arange(most_rows) < jnp.sum(chosen)
        weight_pick = jnp.where(live, weight_row[picked], 0.0)
        rows_in = normed[picked]
        start_col = (expert * FF).astype(jnp.int32)
        gate_cols = lax.dynamic_slice_in_dim(server[0], start_col, FF, 1)
        up_cols = lax.dynamic_slice_in_dim(server[1], start_col, FF, 1)
        down_cols = lax.dynamic_slice_in_dim(server[2], start_col, FF, 1)
        gate_out = jnp.dot(rows_in, gate_cols, preferred_element_type=jnp.float32)
        up_out = jnp.dot(rows_in, up_cols, preferred_element_type=jnp.float32)
        hidden = (jax.nn.silu(gate_out) * up_out).astype(jnp.bfloat16)
        expert_out = jnp.zeros((most_rows, D), jnp.float32)
        for start in range(0, FF, group_width):
            piece_out = jnp.dot(hidden[:, start:start + group_width], down_cols[:, start:start + group_width].T, preferred_element_type=jnp.float32).astype(jnp.bfloat16)
            piece_out = lax.optimization_barrier(piece_out)
            expert_out = expert_out + piece_out.astype(jnp.float32)
        expert_round = lax.optimization_barrier(expert_out.astype(jnp.bfloat16))
        return total.at[picked].add(expert_round.astype(jnp.float32) * weight_pick[:, None])
    moe = lax.fori_loop(0, EXPERTS, per_expert, jnp.zeros((TOKENS, D), jnp.float32))
    out_rows = (resid_f + moe).astype(jnp.bfloat16)
    hidden_out = out_rows.reshape(REPLICAS, TOKENS_REP, D)
    out_f = out_rows.astype(jnp.float32)
    row_squares = lax.optimization_barrier(jnp.sum(out_f * out_f, axis=-1)) * is_valid.astype(jnp.float32)
    square_sums = jax.ops.segment_sum(row_squares, prompt_of, num_segments=PROMPTS)
    norms = jnp.sqrt(square_sums / (lengths.astype(jnp.float32) * D) + 1e-06)
    prompt_ids = jnp.arange(PROMPTS, dtype=jnp.int32)
    last_index = prompt_ids // PROMPTS_REP * TOKENS_REP + prompt_ids % PROMPTS_REP * LEN + lengths.astype(jnp.int32) - 1
    last_rows = out_f[last_index]
    final = (last_rows * lax.rsqrt(lax.optimization_barrier(jnp.mean(last_rows * last_rows, axis=-1, keepdims=True)) + 1e-05) * final_gain).astype(jnp.bfloat16)
    logits = jnp.dot(final, unembed.T, preferred_element_type=jnp.float32)
    top_logit = lax.optimization_barrier(jnp.max(logits, axis=1))
    target_logit = jnp.take_along_axis(logits, target_ids.astype(jnp.int32)[:, None], axis=1)[:, 0]
    request_stats = jnp.stack([norms, top_logit, target_logit])
    return (hidden_out, server, request_stats)
```

```python
import functools

import jax
import jax.numpy as jnp
from jax import lax
from jax.experimental import pallas as pl
from jax.experimental.pallas import tpu as pltpu
from jax.sharding import PartitionSpec as P

FF = 512
EXPERTS = 32
LEN = 128
CAP = 36
LANES = 128
VMEM = 56 * 1024 * 1024


def merged(x, axis, combine):
    everything = jax.tree.map(lambda part: lax.all_gather(part, axis), x)
    initial = jax.tree.map(lambda part: part[0], everything)

    def turn(k, so_far):
        return combine(so_far, jax.tree.map(lambda part: part[k], everything))

    return lax.fori_loop(1, lax.axis_size(axis), turn, initial)


def combine_stats(first, second):
    return (first[0] + second[0], jnp.maximum(first[1], second[1]))


def general(
    hidden_in, lengths, routes, route_weights, norm_gain, master, unembed, final_gain, target_ids
):
    rows_here = hidden_in.shape[1]
    width = hidden_in.shape[2]
    top_count = routes.shape[2]
    blk_count = lax.axis_size("blk")
    rep_count = lax.axis_size("rep")
    blk_index = lax.axis_index("blk")
    unit_count = master.shape[3] * rep_count
    split_ways = max(1, FF // unit_count)
    local_exp = max(1, unit_count // FF)
    group_width = min(unit_count, FF)
    capacity = CAP
    blocks = master.astype(jnp.bfloat16)
    arrived_blocks = lax.all_to_all(blocks, "blk", split_axis=2, concat_axis=1, tiled=True)
    server = lax.all_gather(arrived_blocks, "rep", axis=3, tiled=True)[:, :, 0, :]
    gate_w = server[0].reshape(width, local_exp, group_width)
    up_w = server[1].reshape(width, local_exp, group_width)
    down_w = server[2].reshape(width, local_exp, group_width)
    prompts_here = lengths.shape[0]
    slot_index = blk_index * rows_here + jnp.arange(rows_here, dtype=jnp.int32)
    prompt_of = slot_index // LEN
    position = slot_index % LEN
    prompt_match = prompt_of[:, None] == jnp.arange(prompts_here, dtype=jnp.int32)[None, :]
    row_len = jnp.sum(jnp.where(prompt_match, lengths[None, :], 0), axis=1)
    is_valid = position < row_len
    resid_f = hidden_in[0].astype(jnp.float32)
    normed = (
        resid_f * lax.rsqrt(jnp.mean(resid_f * resid_f, axis=-1, keepdims=True) + 1e-05) * norm_gain
    ).astype(jnp.bfloat16)
    expert_ids = routes[0].reshape(-1)
    pair_live = jnp.repeat(is_valid, top_count)
    pair_row = jnp.repeat(jnp.arange(rows_here, dtype=jnp.int32), top_count)
    expert_hits = (
        (expert_ids[:, None] == jnp.arange(EXPERTS, dtype=jnp.int32)[None, :]) & pair_live[:, None]
    ).astype(jnp.int32)
    slot_rank = jnp.sum((jnp.cumsum(expert_hits, axis=0) - 1) * expert_hits, axis=1)
    slot_id = jnp.where(pair_live, expert_ids * capacity + slot_rank, EXPERTS * capacity)
    source_row = jnp.zeros((EXPERTS * capacity + 1,), jnp.int32).at[slot_id].set(pair_row)[:-1]
    filled = jnp.zeros((EXPERTS * capacity + 1,), jnp.bfloat16).at[slot_id].set(1.0)[:-1]
    outgoing = (normed[source_row] * filled[:, None]).reshape(EXPERTS, capacity, width)
    sending = jnp.repeat(outgoing, split_ways, axis=0).reshape(
        blk_count, local_exp, capacity, width
    )
    arrived = lax.all_to_all(sending, "blk", split_axis=0, concat_axis=0, tiled=True)
    sources = arrived.shape[0]
    slot_count = arrived.shape[2]
    stride = sources
    while stride % 2 == 0 and stride * local_exp * slot_count > 1024:
        stride = stride // 2
    grouped = arrived.reshape(sources // stride, stride, local_exp, slot_count, width)

    def one_block(portion):
        gate_out = jnp.einsum("slnd,dlf->slnf", portion, gate_w, preferred_element_type=jnp.float32)
        up_out = jnp.einsum("slnd,dlf->slnf", portion, up_w, preferred_element_type=jnp.float32)
        hidden = (jax.nn.silu(gate_out) * up_out).astype(jnp.bfloat16)
        return jnp.einsum(
            "slnf,dlf->slnd", hidden, down_w, preferred_element_type=jnp.float32
        ).astype(jnp.bfloat16)

    returned = lax.all_to_all(
        lax.map(one_block, grouped).reshape(sources, local_exp, slot_count, width),
        "blk",
        split_axis=0,
        concat_axis=0,
        tiled=True,
    )
    summed_f = jnp.sum(
        returned.reshape(EXPERTS, split_ways, capacity, width).astype(jnp.float32), axis=1
    )
    expert_out = lax.optimization_barrier(summed_f.astype(jnp.bfloat16)).reshape(
        EXPERTS * capacity, width
    )
    gather_index = jnp.where(pair_live, expert_ids * capacity + slot_rank, 0)
    pair_weight = route_weights[0].reshape(-1) * pair_live.astype(jnp.float32)
    moe = jnp.sum(
        (expert_out[gather_index].astype(jnp.float32) * pair_weight[:, None]).reshape(
            rows_here, top_count, width
        ),
        axis=1,
    )
    out_rows = (resid_f + moe).astype(jnp.bfloat16)
    out_f = out_rows.astype(jnp.float32)
    row_squares = jnp.sum(out_f * out_f, axis=-1) * is_valid.astype(jnp.float32)
    square_local = jnp.sum(jnp.where(prompt_match, row_squares[:, None], 0.0), axis=0)
    is_last = is_valid & (position == row_len - 1)
    picker = (prompt_match & is_last[:, None]).astype(jnp.bfloat16)
    last_local = lax.dot_general(
        picker, out_rows, (((0,), (0,)), ((), ())), preferred_element_type=jnp.float32
    )
    last_rows, square_total = lax.psum((last_local, square_local), "blk")
    norms = jnp.sqrt(square_total / (lengths.astype(jnp.float32) * width) + 1e-06)
    final = (
        last_rows
        * lax.rsqrt(jnp.mean(last_rows * last_rows, axis=-1, keepdims=True) + 1e-05)
        * final_gain
    ).astype(jnp.bfloat16)
    logits = lax.dot_general(
        final, unembed, (((1,), (1,)), ((), ())), preferred_element_type=jnp.float32
    )
    vocab_base = blk_index * unembed.shape[0]
    target_hit = (
        target_ids[:, None] == vocab_base + jnp.arange(unembed.shape[0], dtype=jnp.int32)[None, :]
    )
    target_part = jnp.sum(jnp.where(target_hit, logits, 0.0), axis=1)
    top_part = jnp.max(logits, axis=1)
    target_logit, top_logit = merged((target_part, top_part), "blk", combine_stats)
    request_stats = jnp.stack([norms, top_logit, target_logit])
    return (out_rows[None], server, request_stats)


def iota(shape, dim):
    return lax.broadcasted_iota(jnp.int32, shape, dim)


def prep_kernel(info, hidden_ref, routes_ref, weights_ref, gain_ref, rows_ref, pieces_ref):
    rows, width = hidden_ref.shape
    length = info[3]
    x = hidden_ref[...].astype(jnp.float32)
    scale = lax.rsqrt(jnp.mean(x * x, axis=-1, keepdims=True) + 1e-05)
    rows_ref[:, :width] = (x * scale * gain_ref[...]).astype(jnp.bfloat16)
    lane = iota((rows, LANES), 1)
    row = iota((rows, LANES), 0)
    hit = jnp.zeros((rows, LANES), jnp.float32)
    weight = jnp.zeros((rows, LANES), jnp.float32)
    for k in range(routes_ref.shape[1]):
        named = routes_ref[:, k : k + 1] == lane
        hit = hit + jnp.where(named, 1.0, 0.0)
        weight = weight + jnp.where(named, weights_ref[:, k : k + 1], 0.0)
    live = row < length
    hit = jnp.where(live, hit, 0.0)
    weight = jnp.where(live, weight, 0.0)
    before = jnp.where(iota((rows, rows), 1) < iota((rows, rows), 0), 1.0, 0.0)
    rank = jnp.dot(
        before.astype(jnp.bfloat16), hit.astype(jnp.bfloat16), preferred_element_type=jnp.float32
    )
    rows_ref[:, width:] = jnp.where(hit > 0.0, rank, -1.0).astype(jnp.bfloat16)
    for k in range(3):
        piece = weight.astype(jnp.bfloat16)
        pieces_ref[k * rows : (k + 1) * rows, :] = piece
        weight = weight - piece.astype(jnp.float32)


def hidden_kernel(groups, info, x_ref, g_own, u_own, g_oth, u_oth, out_ref, picked):
    step = pl.program_id(0)
    rows = x_ref.shape[0]
    width = g_own.shape[0]
    sources = rows // LEN
    slots = sources * CAP
    ranks = x_ref[:, width:].astype(jnp.float32)
    lane = iota((rows, LANES), 1)
    source = (iota((rows, 1), 0) // LEN).astype(jnp.float32)
    slot_lane = iota((rows, slots), 1).astype(jnp.float32)
    for i in range(2):
        rank = jnp.sum(jnp.where(lane == info[i], ranks, 0.0), axis=1, keepdims=True)
        slot = jnp.where(rank >= 0.0, source * CAP + rank, -1.0)
        one_hot = jnp.where(slot == slot_lane, 1.0, 0.0).astype(jnp.bfloat16)
        chosen = lax.dot_general(
            one_hot, x_ref[:, :width], (((0,), (0,)), ((), ())), preferred_element_type=jnp.float32
        )
        picked[i, pl.ds(pl.multiple_of(step * slots, slots), slots), :] = chosen.astype(jnp.bfloat16)

    @pl.when(step == groups - 1)
    def _():
        column = iota((2 * slots, slots), 1)
        owner = jnp.zeros_like(column)
        for s in range(1, sources):
            owner = owner + jnp.where(column >= s * CAP, 1, 0)
        for i, (g, u) in enumerate(((g_own, u_own), (g_oth, u_oth))):
            gate = jnp.dot(picked[i], g[...], preferred_element_type=jnp.float32)
            up = jnp.dot(picked[i], u[...], preferred_element_type=jnp.float32)
            hidden = (gate / (1.0 + jnp.exp(-gate)) * up).astype(jnp.bfloat16)
            place = jnp.where(
                iota((2 * slots, slots), 0) == column + (owner + i) * CAP, 1.0, 0.0
            ).astype(jnp.bfloat16)
            for k in range(groups):
                placed = jnp.dot(
                    place, hidden[k * slots : (k + 1) * slots], preferred_element_type=jnp.float32
                )
                out_ref[k * 2 * slots : (k + 1) * 2 * slots, i * FF : (i + 1) * FF] = placed.astype(
                    jnp.bfloat16
                )


def down_kernel(hidden_ref, d_own, d_oth, out_ref):
    dims = (((1,), (1,)), ((), ()))
    total = lax.dot_general(
        hidden_ref[:, :FF], d_own[...], dims, preferred_element_type=jnp.float32
    ) + lax.dot_general(hidden_ref[:, FF:], d_oth[...], dims, preferred_element_type=jnp.float32)
    out_ref[...] = total.astype(jnp.bfloat16)


def combine_kernel(
    info, rank_ref, pieces_ref, back_ref, resid_ref, out_ref, last_ref, square_ref, mix, squares
):
    step = pl.program_id(0)
    rows = resid_ref.shape[0]
    slots = back_ref.shape[0]
    length = info[3]

    @pl.when(step == 0)
    def _():
        expert = iota((LANES, slots), 0)
        lane = iota((LANES, slots), 1)
        odd = expert & 1
        start = (expert - odd + jnp.where(odd == info[2], 0, 1)) * CAP
        inside = (lane >= start) & (lane < start + CAP)
        spread = jnp.where(inside, 1.0, 0.0).astype(jnp.bfloat16)
        within = jnp.sum(jnp.where(inside, lane - start, 0), axis=0, keepdims=True).astype(jnp.float32)
        rank = jnp.dot(rank_ref[...], spread, preferred_element_type=jnp.float32)
        match = rank == within
        for k in range(3):
            part = jnp.dot(
                pieces_ref[k * rows : (k + 1) * rows, :], spread, preferred_element_type=jnp.float32
            )
            mix[k * rows : (k + 1) * rows, :] = jnp.where(match, part, 0.0).astype(jnp.bfloat16)
        squares[...] = jnp.zeros_like(squares)

    parts = jnp.dot(mix[...], back_ref[...], preferred_element_type=jnp.float32)
    moe = parts[2 * rows :] + parts[rows : 2 * rows] + parts[:rows]
    out = (resid_ref[...].astype(jnp.float32) + moe).astype(jnp.bfloat16)
    out_ref[...] = out
    out_f = out.astype(jnp.float32)
    row = iota(out_f.shape, 0)
    last_ref[...] = jnp.sum(jnp.where(row == length - 1, out_f, 0.0), axis=0, keepdims=True)
    squares[...] += jnp.sum(jnp.where(row < length, out_f * out_f, 0.0), axis=0, keepdims=True)

    @pl.when(step == pl.num_programs(0) - 1)
    def _():
        square_ref[...] = jnp.broadcast_to(
            jnp.sum(squares[...], axis=1, keepdims=True), square_ref.shape
        )


def place_kernel(info, *refs):
    out_ref, sems = refs[-2], refs[-1]
    copies = []
    for k in range(3):
        for i in range(2):
            half = refs[2 * k + i]
            column = info[2] if i == 0 else 1 - info[2]
            target = out_ref.at[k, :, pl.ds(pl.multiple_of(column * FF, FF), FF)]
            copies.append(pltpu.make_async_copy(half, target, sems.at[2 * k + i]))
    for copy in copies:
        copy.start()
    for copy in copies:
        copy.wait()


def params():
    return pltpu.CompilerParams(vmem_limit_bytes=VMEM, dimension_semantics=("arbitrary",))


def whole(shape):
    return pl.BlockSpec(shape, lambda *_: tuple(0 for _ in shape))


def paired(
    hidden_in, lengths, routes, route_weights, norm_gain, master, unembed, final_gain, target_ids
):
    rows = hidden_in.shape[1]
    width = hidden_in.shape[2]
    blk_count = lax.axis_size("blk")
    blk = lax.axis_index("blk")
    rep = lax.axis_index("rep")
    back_rows = 2 * CAP
    slots = blk_count * back_rows
    resid = hidden_in[0]
    info = jnp.stack([2 * blk + rep, 2 * blk + 1 - rep, rep, lengths[blk]]).astype(jnp.int32)

    def moved(k):
        turned = jnp.transpose(master[k], (1, 0, 2)).astype(jnp.bfloat16)
        own = lax.all_to_all(turned, "blk", split_axis=0, concat_axis=0, tiled=True)
        own = own.reshape(width, FF)
        return own, lax.ppermute(own, "rep", [(0, 1), (1, 0)])

    g_own, g_oth = moved(0)
    u_own, u_oth = moved(1)
    d_own, d_oth = moved(2)

    row_ext, pieces = pl.pallas_call(
        prep_kernel,
        grid_spec=pltpu.PrefetchScalarGridSpec(
            num_scalar_prefetch=1,
            grid=(1,),
            in_specs=[
                whole((rows, width)),
                whole((rows, routes.shape[2])),
                whole((rows, routes.shape[2])),
                whole((1, width)),
            ],
            out_specs=[whole((rows, width + LANES)), whole((3 * rows, LANES))],
        ),
        out_shape=[
            jax.ShapeDtypeStruct((rows, width + LANES), jnp.bfloat16),
            jax.ShapeDtypeStruct((3 * rows, LANES), jnp.bfloat16),
        ],
        compiler_params=params(),
        name="prep",
    )(info, resid, routes[0], route_weights[0], norm_gain[None])
    tokens = lax.all_gather(row_ext, "blk", axis=0, tiled=True)

    groups = 4 if blk_count % 4 == 0 else 1
    group_rows = blk_count // groups * rows
    hidden = pl.pallas_call(
        functools.partial(hidden_kernel, groups),
        grid_spec=pltpu.PrefetchScalarGridSpec(
            num_scalar_prefetch=1,
            grid=(groups,),
            in_specs=[pl.BlockSpec((group_rows, width + LANES), lambda i, *_: (i, 0))]
            + [whole((width, FF))] * 4,
            out_specs=whole((slots, 2 * FF)),
            scratch_shapes=[pltpu.VMEM((2, slots // 2, width), jnp.bfloat16)],
        ),
        out_shape=jax.ShapeDtypeStruct((slots, 2 * FF), jnp.bfloat16),
        compiler_params=params(),
        name="gate_up",
    )(info, tokens, g_own, u_own, g_oth, u_oth)

    step = 512
    outputs = pl.pallas_call(
        down_kernel,
        grid=(width // step,),
        in_specs=[
            whole((slots, 2 * FF)),
            pl.BlockSpec((step, FF), lambda i: (i, 0)),
            pl.BlockSpec((step, FF), lambda i: (i, 0)),
        ],
        out_specs=pl.BlockSpec((slots, step), lambda i: (0, i)),
        out_shape=jax.ShapeDtypeStruct((slots, width), jnp.bfloat16),
        compiler_params=params(),
        name="down",
    )(hidden, d_own, d_oth)
    back = lax.all_to_all(
        outputs.reshape(blk_count, back_rows, width), "blk", split_axis=0, concat_axis=0, tiled=True
    ).reshape(slots, width)

    server = pl.pallas_call(
        place_kernel,
        grid_spec=pltpu.PrefetchScalarGridSpec(
            num_scalar_prefetch=1,
            grid=(1,),
            in_specs=[pl.BlockSpec(memory_space=pl.ANY)] * 6,
            out_specs=pl.BlockSpec(memory_space=pl.ANY),
            scratch_shapes=[pltpu.SemaphoreType.DMA((6,))],
        ),
        out_shape=jax.ShapeDtypeStruct((3, width, 2 * FF), jnp.bfloat16),
        compiler_params=params(),
        name="place",
    )(info, g_own, g_oth, u_own, u_oth, d_own, d_oth)

    out_rows, last, square = pl.pallas_call(
        combine_kernel,
        grid_spec=pltpu.PrefetchScalarGridSpec(
            num_scalar_prefetch=1,
            grid=(width // step,),
            in_specs=[
                pl.BlockSpec((rows, LANES), lambda i, *_: (0, width // LANES)),
                whole((3 * rows, LANES)),
                pl.BlockSpec((slots, step), lambda i, *_: (0, i)),
                pl.BlockSpec((rows, step), lambda i, *_: (0, i)),
            ],
            out_specs=[
                pl.BlockSpec((rows, step), lambda i, *_: (0, i)),
                pl.BlockSpec((1, step), lambda i, *_: (0, i)),
                whole((1, LANES)),
            ],
            scratch_shapes=[
                pltpu.VMEM((3 * rows, slots), jnp.bfloat16),
                pltpu.VMEM((1, step), jnp.float32),
            ],
        ),
        out_shape=[
            jax.ShapeDtypeStruct((rows, width), jnp.bfloat16),
            jax.ShapeDtypeStruct((1, width), jnp.float32),
            jax.ShapeDtypeStruct((1, LANES), jnp.float32),
        ],
        compiler_params=params(),
        name="combine",
    )(info, row_ext, pieces, back, resid)

    def everywhere(x):
        copies = jnp.broadcast_to(x[None], (blk_count,) + x.shape)
        return lax.all_to_all(copies, "blk", split_axis=0, concat_axis=0, tiled=True)

    gathered = everywhere(jnp.concatenate([last, square], axis=1))[:, 0]
    last_rows, square_total = gathered[:, :width], gathered[:, width]
    norms = jnp.sqrt(square_total / (lengths.astype(jnp.float32) * width) + 1e-06)
    final = (
        last_rows
        * lax.rsqrt(jnp.mean(last_rows * last_rows, axis=-1, keepdims=True) + 1e-05)
        * final_gain
    ).astype(jnp.bfloat16)
    logits = lax.dot_general(
        final, unembed, (((1,), (1,)), ((), ())), preferred_element_type=jnp.float32
    )
    vocab_base = blk * unembed.shape[0]
    target_hit = (
        target_ids[:, None] == vocab_base + jnp.arange(unembed.shape[0], dtype=jnp.int32)[None, :]
    )
    target_part = jnp.sum(jnp.where(target_hit, logits, 0.0), axis=1)
    top_part = jnp.max(logits, axis=1)
    parts = everywhere(jnp.stack([top_part, target_part]))
    request_stats = jnp.stack([norms, jnp.max(parts[:, 0], axis=0), jnp.sum(parts[:, 1], axis=0)])
    return (out_rows[None], server, request_stats)


def local(hidden_in, lengths, routes, route_weights, norm_gain, master, *rest):
    blk_count = lax.axis_size("blk")
    fits = (
        lax.axis_size("rep") == 2
        and master.shape[3] == FF
        and EXPERTS == 2 * blk_count
        and hidden_in.shape[1] == LEN
        and lengths.shape[0] == blk_count
    )
    form = paired if fits else general
    return form(hidden_in, lengths, routes, route_weights, norm_gain, master, *rest)


def solution(mesh):
    return jax.shard_map(
        local,
        mesh=mesh,
        in_specs=(
            P("rep", "blk", None),
            P("rep"),
            P("rep", "blk", None),
            P("rep", "blk", None),
            P(),
            P(None, "blk", None, "rep"),
            P("blk", None),
            P(),
            P("rep"),
        ),
        out_specs=(P("rep", "blk", None), P(None, None, "blk"), P(None, "rep")),
        check_vma=False,
    )
```

```python
import functools

import jax
import jax.numpy as jnp
from jax import lax
from jax.experimental import pallas as pl
from jax.experimental.pallas import tpu as pltpu
from jax.sharding import PartitionSpec as P

FF = 512
EXPERTS = 32
LEN = 128
CAP = 36
LANES = 128
VMEM = 56 * 1024 * 1024


def merged(x, axis, combine):
    everything = jax.tree.map(lambda part: lax.all_gather(part, axis), x)
    initial = jax.tree.map(lambda part: part[0], everything)

    def turn(k, so_far):
        return combine(so_far, jax.tree.map(lambda part: part[k], everything))

    return lax.fori_loop(1, lax.axis_size(axis), turn, initial)


def combine_stats(first, second):
    return (first[0] + second[0], jnp.maximum(first[1], second[1]))


def general(
    hidden_in, lengths, routes, route_weights, norm_gain, master, unembed, final_gain, target_ids
):
    rows_here = hidden_in.shape[1]
    width = hidden_in.shape[2]
    top_count = routes.shape[2]
    blk_count = lax.axis_size("blk")
    rep_count = lax.axis_size("rep")
    blk_index = lax.axis_index("blk")
    unit_count = master.shape[3] * rep_count
    split_ways = max(1, FF // unit_count)
    local_exp = max(1, unit_count // FF)
    group_width = min(unit_count, FF)
    capacity = CAP
    blocks = master.astype(jnp.bfloat16)
    arrived_blocks = lax.all_to_all(blocks, "blk", split_axis=2, concat_axis=1, tiled=True)
    server = lax.all_gather(arrived_blocks, "rep", axis=3, tiled=True)[:, :, 0, :]
    gate_w = server[0].reshape(width, local_exp, group_width)
    up_w = server[1].reshape(width, local_exp, group_width)
    down_w = server[2].reshape(width, local_exp, group_width)
    prompts_here = lengths.shape[0]
    slot_index = blk_index * rows_here + jnp.arange(rows_here, dtype=jnp.int32)
    prompt_of = slot_index // LEN
    position = slot_index % LEN
    prompt_match = prompt_of[:, None] == jnp.arange(prompts_here, dtype=jnp.int32)[None, :]
    row_len = jnp.sum(jnp.where(prompt_match, lengths[None, :], 0), axis=1)
    is_valid = position < row_len
    resid_f = hidden_in[0].astype(jnp.float32)
    normed = (
        resid_f * lax.rsqrt(jnp.mean(resid_f * resid_f, axis=-1, keepdims=True) + 1e-05) * norm_gain
    ).astype(jnp.bfloat16)
    expert_ids = routes[0].reshape(-1)
    pair_live = jnp.repeat(is_valid, top_count)
    pair_row = jnp.repeat(jnp.arange(rows_here, dtype=jnp.int32), top_count)
    expert_hits = (
        (expert_ids[:, None] == jnp.arange(EXPERTS, dtype=jnp.int32)[None, :]) & pair_live[:, None]
    ).astype(jnp.int32)
    slot_rank = jnp.sum((jnp.cumsum(expert_hits, axis=0) - 1) * expert_hits, axis=1)
    slot_id = jnp.where(pair_live, expert_ids * capacity + slot_rank, EXPERTS * capacity)
    source_row = jnp.zeros((EXPERTS * capacity + 1,), jnp.int32).at[slot_id].set(pair_row)[:-1]
    filled = jnp.zeros((EXPERTS * capacity + 1,), jnp.bfloat16).at[slot_id].set(1.0)[:-1]
    outgoing = (normed[source_row] * filled[:, None]).reshape(EXPERTS, capacity, width)
    sending = jnp.repeat(outgoing, split_ways, axis=0).reshape(
        blk_count, local_exp, capacity, width
    )
    arrived = lax.all_to_all(sending, "blk", split_axis=0, concat_axis=0, tiled=True)
    sources = arrived.shape[0]
    slot_count = arrived.shape[2]
    stride = sources
    while stride % 2 == 0 and stride * local_exp * slot_count > 1024:
        stride = stride // 2
    grouped = arrived.reshape(sources // stride, stride, local_exp, slot_count, width)

    def one_block(portion):
        gate_out = jnp.einsum("slnd,dlf->slnf", portion, gate_w, preferred_element_type=jnp.float32)
        up_out = jnp.einsum("slnd,dlf->slnf", portion, up_w, preferred_element_type=jnp.float32)
        hidden = (jax.nn.silu(gate_out) * up_out).astype(jnp.bfloat16)
        return jnp.einsum(
            "slnf,dlf->slnd", hidden, down_w, preferred_element_type=jnp.float32
        ).astype(jnp.bfloat16)

    returned = lax.all_to_all(
        lax.map(one_block, grouped).reshape(sources, local_exp, slot_count, width),
        "blk",
        split_axis=0,
        concat_axis=0,
        tiled=True,
    )
    summed_f = jnp.sum(
        returned.reshape(EXPERTS, split_ways, capacity, width).astype(jnp.float32), axis=1
    )
    expert_out = lax.optimization_barrier(summed_f.astype(jnp.bfloat16)).reshape(
        EXPERTS * capacity, width
    )
    gather_index = jnp.where(pair_live, expert_ids * capacity + slot_rank, 0)
    pair_weight = route_weights[0].reshape(-1) * pair_live.astype(jnp.float32)
    moe = jnp.sum(
        (expert_out[gather_index].astype(jnp.float32) * pair_weight[:, None]).reshape(
            rows_here, top_count, width
        ),
        axis=1,
    )
    out_rows = (resid_f + moe).astype(jnp.bfloat16)
    out_f = out_rows.astype(jnp.float32)
    row_squares = jnp.sum(out_f * out_f, axis=-1) * is_valid.astype(jnp.float32)
    square_local = jnp.sum(jnp.where(prompt_match, row_squares[:, None], 0.0), axis=0)
    is_last = is_valid & (position == row_len - 1)
    picker = (prompt_match & is_last[:, None]).astype(jnp.bfloat16)
    last_local = lax.dot_general(
        picker, out_rows, (((0,), (0,)), ((), ())), preferred_element_type=jnp.float32
    )
    last_rows, square_total = lax.psum((last_local, square_local), "blk")
    norms = jnp.sqrt(square_total / (lengths.astype(jnp.float32) * width) + 1e-06)
    final = (
        last_rows
        * lax.rsqrt(jnp.mean(last_rows * last_rows, axis=-1, keepdims=True) + 1e-05)
        * final_gain
    ).astype(jnp.bfloat16)
    logits = lax.dot_general(
        final, unembed, (((1,), (1,)), ((), ())), preferred_element_type=jnp.float32
    )
    vocab_base = blk_index * unembed.shape[0]
    target_hit = (
        target_ids[:, None] == vocab_base + jnp.arange(unembed.shape[0], dtype=jnp.int32)[None, :]
    )
    target_part = jnp.sum(jnp.where(target_hit, logits, 0.0), axis=1)
    top_part = jnp.max(logits, axis=1)
    target_logit, top_logit = merged((target_part, top_part), "blk", combine_stats)
    request_stats = jnp.stack([norms, top_logit, target_logit])
    return (out_rows[None], server, request_stats)


def iota(shape, dim):
    return lax.broadcasted_iota(jnp.int32, shape, dim)


def prep_kernel(info, hidden_ref, routes_ref, weights_ref, gain_ref, rows_ref, pieces_ref):
    rows, width = hidden_ref.shape
    length = info[3]
    x = hidden_ref[...].astype(jnp.float32)
    scale = lax.rsqrt(jnp.mean(x * x, axis=-1, keepdims=True) + 1e-05)
    rows_ref[:, :width] = (x * scale * gain_ref[...]).astype(jnp.bfloat16)
    lane = iota((rows, LANES), 1)
    row = iota((rows, LANES), 0)
    hit = jnp.zeros((rows, LANES), jnp.float32)
    weight = jnp.zeros((rows, LANES), jnp.float32)
    for k in range(routes_ref.shape[1]):
        named = routes_ref[:, k : k + 1] == lane
        hit = hit + jnp.where(named, 1.0, 0.0)
        weight = weight + jnp.where(named, weights_ref[:, k : k + 1], 0.0)
    live = row < length
    hit = jnp.where(live, hit, 0.0)
    weight = jnp.where(live, weight, 0.0)
    before = jnp.where(iota((rows, rows), 1) < iota((rows, rows), 0), 1.0, 0.0)
    rank = jnp.dot(
        before.astype(jnp.bfloat16), hit.astype(jnp.bfloat16), preferred_element_type=jnp.float32
    )
    rows_ref[:, width:] = jnp.where(hit > 0.0, rank, -1.0).astype(jnp.bfloat16)
    for k in range(3):
        piece = weight.astype(jnp.bfloat16)
        pieces_ref[k * rows : (k + 1) * rows, :] = piece
        weight = weight - piece.astype(jnp.float32)


def hidden_kernel(groups, info, x_ref, g_own, u_own, g_oth, u_oth, out_ref, picked):
    step = pl.program_id(0)
    rows = x_ref.shape[0]
    width = g_own.shape[0]
    sources = rows // LEN
    slots = sources * CAP
    ranks = x_ref[:, width:].astype(jnp.float32)
    lane = iota((rows, LANES), 1)
    source = (iota((rows, 1), 0) // LEN).astype(jnp.float32)
    slot_lane = iota((rows, slots), 1).astype(jnp.float32)
    for i in range(2):
        rank = jnp.sum(jnp.where(lane == info[i], ranks, 0.0), axis=1, keepdims=True)
        slot = jnp.where(rank >= 0.0, source * CAP + rank, -1.0)
        one_hot = jnp.where(slot == slot_lane, 1.0, 0.0).astype(jnp.bfloat16)
        chosen = lax.dot_general(
            one_hot, x_ref[:, :width], (((0,), (0,)), ((), ())), preferred_element_type=jnp.float32
        )
        picked[i, pl.ds(pl.multiple_of(step * slots, slots), slots), :] = chosen.astype(jnp.bfloat16)

    @pl.when(step == groups - 1)
    def _():
        column = iota((2 * slots, slots), 1)
        owner = jnp.zeros_like(column)
        for s in range(1, sources):
            owner = owner + jnp.where(column >= s * CAP, 1, 0)
        for i, (g, u) in enumerate(((g_own, u_own), (g_oth, u_oth))):
            gate = jnp.dot(picked[i], g[...], preferred_element_type=jnp.float32)
            up = jnp.dot(picked[i], u[...], preferred_element_type=jnp.float32)
            hidden = (gate / (1.0 + jnp.exp(-gate)) * up).astype(jnp.bfloat16)
            place = jnp.where(
                iota((2 * slots, slots), 0) == column + (owner + i) * CAP, 1.0, 0.0
            ).astype(jnp.bfloat16)
            for k in range(groups):
                placed = jnp.dot(
                    place, hidden[k * slots : (k + 1) * slots], preferred_element_type=jnp.float32
                )
                out_ref[k * 2 * slots : (k + 1) * 2 * slots, i * FF : (i + 1) * FF] = placed.astype(
                    jnp.bfloat16
                )


def down_kernel(hidden_ref, d_own, d_oth, out_ref):
    dims = (((1,), (1,)), ((), ()))
    total = lax.dot_general(
        hidden_ref[:, :FF], d_own[...], dims, preferred_element_type=jnp.float32
    ) + lax.dot_general(hidden_ref[:, FF:], d_oth[...], dims, preferred_element_type=jnp.float32)
    out_ref[...] = total.astype(jnp.bfloat16)


def combine_kernel(
    info, rank_ref, pieces_ref, back_ref, resid_ref, _, out_ref, last_ref, square_ref, mix, squares
):
    step = pl.program_id(0)
    rows = resid_ref.shape[0]
    slots = back_ref.shape[0]
    length = info[3]

    @pl.when(step == 0)
    def _():
        expert = iota((LANES, slots), 0)
        lane = iota((LANES, slots), 1)
        odd = expert & 1
        start = (expert - odd + jnp.where(odd == info[2], 0, 1)) * CAP
        inside = (lane >= start) & (lane < start + CAP)
        spread = jnp.where(inside, 1.0, 0.0).astype(jnp.bfloat16)
        within = jnp.sum(jnp.where(inside, lane - start, 0), axis=0, keepdims=True).astype(jnp.float32)
        rank = jnp.dot(rank_ref[...], spread, preferred_element_type=jnp.float32)
        match = rank == within
        for k in range(3):
            part = jnp.dot(
                pieces_ref[k * rows : (k + 1) * rows, :], spread, preferred_element_type=jnp.float32
            )
            mix[k * rows : (k + 1) * rows, :] = jnp.where(match, part, 0.0).astype(jnp.bfloat16)
        squares[...] = jnp.zeros_like(squares)

    parts = jnp.dot(mix[...], back_ref[...], preferred_element_type=jnp.float32)
    moe = parts[2 * rows :] + parts[rows : 2 * rows] + parts[:rows]
    out = (resid_ref[...].astype(jnp.float32) + moe).astype(jnp.bfloat16)
    out_ref[...] = out
    out_f = out.astype(jnp.float32)
    row = iota(out_f.shape, 0)
    last_ref[...] = jnp.sum(jnp.where(row == length - 1, out_f, 0.0), axis=0, keepdims=True)
    squares[...] += jnp.sum(jnp.where(row < length, out_f * out_f, 0.0), axis=0, keepdims=True)

    @pl.when(step == pl.num_programs(0) - 1)
    def _():
        square_ref[...] = jnp.broadcast_to(
            jnp.sum(squares[...], axis=1, keepdims=True), square_ref.shape
        )


def place_kernel(info, g_own, g_oth, u_own, u_oth, d_own, d_oth, _, out_ref):
    for k, (own, oth) in enumerate(((g_own, g_oth), (u_own, u_oth), (d_own, d_oth))):

        @pl.when(info[2] == 0)
        def _():
            out_ref[k, :, :FF] = own[...]
            out_ref[k, :, FF:] = oth[...]

        @pl.when(info[2] != 0)
        def _():
            out_ref[k, :, :FF] = oth[...]
            out_ref[k, :, FF:] = own[...]


def cast_kernel(blocks, x_ref, *refs):
    out_ref = refs[-1]
    rows = out_ref.shape[1]
    for b in range(blocks):
        out_ref[b] = x_ref[pl.ds(b, rows, stride=blocks), :].astype(jnp.bfloat16)


def params():
    return pltpu.CompilerParams(vmem_limit_bytes=VMEM, dimension_semantics=("arbitrary",))


def whole(shape):
    return pl.BlockSpec(shape, lambda *_: tuple(0 for _ in shape))


def paired(
    hidden_in, lengths, routes, route_weights, norm_gain, master, unembed, final_gain, target_ids
):
    rows = hidden_in.shape[1]
    width = hidden_in.shape[2]
    blk_count = lax.axis_size("blk")
    blk = lax.axis_index("blk")
    rep = lax.axis_index("rep")
    back_rows = 2 * CAP
    slots = blk_count * back_rows
    resid = hidden_in[0]
    info = jnp.stack([2 * blk + rep, 2 * blk + 1 - rep, rep, lengths[blk]]).astype(jnp.int32)

    shard_rows = master.shape[1]
    flat = master.reshape(3 * shard_rows * blk_count, FF)

    def moved(k, *after):
        turned = pl.pallas_call(
            functools.partial(cast_kernel, blk_count),
            grid=(FF // LANES,),
            in_specs=[pl.BlockSpec((shard_rows * blk_count, LANES), lambda i: (k, i))]
            + [pl.BlockSpec(memory_space=pl.ANY)] * len(after),
            out_specs=pl.BlockSpec((blk_count, shard_rows, LANES), lambda i: (0, 0, i)),
            out_shape=jax.ShapeDtypeStruct((blk_count, shard_rows, FF), jnp.bfloat16),
            compiler_params=params(),
            name="cast",
        )(flat, *after)
        own = lax.all_to_all(turned, "blk", split_axis=0, concat_axis=0, tiled=True)
        own = own.reshape(width, FF)
        return own, lax.ppermute(own, "rep", [(0, 1), (1, 0)])

    g_own, g_oth = moved(0)
    u_own, u_oth = moved(1)
    d_own, d_oth = moved(2, g_oth)

    row_ext, pieces = pl.pallas_call(
        prep_kernel,
        grid_spec=pltpu.PrefetchScalarGridSpec(
            num_scalar_prefetch=1,
            grid=(1,),
            in_specs=[
                whole((rows, width)),
                whole((rows, routes.shape[2])),
                whole((rows, routes.shape[2])),
                whole((1, width)),
            ],
            out_specs=[whole((rows, width + LANES)), whole((3 * rows, LANES))],
        ),
        out_shape=[
            jax.ShapeDtypeStruct((rows, width + LANES), jnp.bfloat16),
            jax.ShapeDtypeStruct((3 * rows, LANES), jnp.bfloat16),
        ],
        compiler_params=params(),
        name="prep",
    )(info, resid, routes[0], route_weights[0], norm_gain[None])
    tokens = lax.all_gather(row_ext, "blk", axis=0, tiled=True)

    groups = 4 if blk_count % 4 == 0 else 1
    group_rows = blk_count // groups * rows
    hidden = pl.pallas_call(
        functools.partial(hidden_kernel, groups),
        grid_spec=pltpu.PrefetchScalarGridSpec(
            num_scalar_prefetch=1,
            grid=(groups,),
            in_specs=[pl.BlockSpec((group_rows, width + LANES), lambda i, *_: (i, 0))]
            + [whole((width, FF))] * 4,
            out_specs=whole((slots, 2 * FF)),
            scratch_shapes=[pltpu.VMEM((2, slots // 2, width), jnp.bfloat16)],
        ),
        out_shape=jax.ShapeDtypeStruct((slots, 2 * FF), jnp.bfloat16),
        compiler_params=params(),
        name="gate_up",
    )(info, tokens, g_own, u_own, g_oth, u_oth)

    step = 512
    outputs = pl.pallas_call(
        down_kernel,
        grid=(width // step,),
        in_specs=[
            whole((slots, 2 * FF)),
            pl.BlockSpec((step, FF), lambda i: (i, 0)),
            pl.BlockSpec((step, FF), lambda i: (i, 0)),
        ],
        out_specs=pl.BlockSpec((slots, step), lambda i: (0, i)),
        out_shape=jax.ShapeDtypeStruct((slots, width), jnp.bfloat16),
        compiler_params=params(),
        name="down",
    )(hidden, d_own, d_oth)
    back = lax.all_to_all(
        outputs.reshape(blk_count, back_rows, width), "blk", split_axis=0, concat_axis=0, tiled=True
    ).reshape(slots, width)

    part = width // 4
    server = pl.pallas_call(
        place_kernel,
        grid_spec=pltpu.PrefetchScalarGridSpec(
            num_scalar_prefetch=1,
            grid=(width // part,),
            in_specs=[pl.BlockSpec((part, FF), lambda i, *_: (i, 0))] * 6
            + [pl.BlockSpec(memory_space=pl.ANY)],
            out_specs=pl.BlockSpec((3, part, 2 * FF), lambda i, *_: (0, i, 0)),
        ),
        out_shape=jax.ShapeDtypeStruct((3, width, 2 * FF), jnp.bfloat16),
        compiler_params=params(),
        name="place",
    )(info, g_own, g_oth, u_own, u_oth, d_own, d_oth, outputs)

    out_rows, last, square = pl.pallas_call(
        combine_kernel,
        grid_spec=pltpu.PrefetchScalarGridSpec(
            num_scalar_prefetch=1,
            grid=(width // step,),
            in_specs=[
                pl.BlockSpec((rows, LANES), lambda i, *_: (0, width // LANES)),
                whole((3 * rows, LANES)),
                pl.BlockSpec((slots, step), lambda i, *_: (0, i)),
                pl.BlockSpec((rows, step), lambda i, *_: (0, i)),
                pl.BlockSpec(memory_space=pl.ANY),
            ],
            out_specs=[
                pl.BlockSpec((rows, step), lambda i, *_: (0, i)),
                pl.BlockSpec((1, step), lambda i, *_: (0, i)),
                whole((1, LANES)),
            ],
            scratch_shapes=[
                pltpu.VMEM((3 * rows, slots), jnp.bfloat16),
                pltpu.VMEM((1, step), jnp.float32),
            ],
        ),
        out_shape=[
            jax.ShapeDtypeStruct((rows, width), jnp.bfloat16),
            jax.ShapeDtypeStruct((1, width), jnp.float32),
            jax.ShapeDtypeStruct((1, LANES), jnp.float32),
        ],
        compiler_params=params(),
        name="combine",
    )(info, row_ext, pieces, back, resid, server)

    def everywhere(x):
        copies = jnp.broadcast_to(x[None], (blk_count,) + x.shape)
        return lax.all_to_all(copies, "blk", split_axis=0, concat_axis=0, tiled=True)

    gathered = everywhere(jnp.concatenate([last, square], axis=1))[:, 0]
    last_rows, square_total = gathered[:, :width], gathered[:, width]
    norms = jnp.sqrt(square_total / (lengths.astype(jnp.float32) * width) + 1e-06)
    final = (
        last_rows
        * lax.rsqrt(jnp.mean(last_rows * last_rows, axis=-1, keepdims=True) + 1e-05)
        * final_gain
    ).astype(jnp.bfloat16)
    logits = lax.dot_general(
        final, unembed, (((1,), (1,)), ((), ())), preferred_element_type=jnp.float32
    )
    vocab_base = blk * unembed.shape[0]
    target_hit = (
        target_ids[:, None] == vocab_base + jnp.arange(unembed.shape[0], dtype=jnp.int32)[None, :]
    )
    target_part = jnp.sum(jnp.where(target_hit, logits, 0.0), axis=1)
    top_part = jnp.max(logits, axis=1)
    parts = everywhere(jnp.stack([top_part, target_part]))
    request_stats = jnp.stack([norms, jnp.max(parts[:, 0], axis=0), jnp.sum(parts[:, 1], axis=0)])
    return (out_rows[None], server, request_stats)


def local(hidden_in, lengths, routes, route_weights, norm_gain, master, *rest):
    blk_count = lax.axis_size("blk")
    fits = (
        lax.axis_size("rep") == 2
        and master.shape[3] == FF
        and EXPERTS == 2 * blk_count
        and hidden_in.shape[1] == LEN
        and lengths.shape[0] == blk_count
    )
    form = paired if fits else general
    return form(hidden_in, lengths, routes, route_weights, norm_gain, master, *rest)


def solution(mesh):
    return jax.shard_map(
        local,
        mesh=mesh,
        in_specs=(
            P("rep", "blk", None),
            P("rep"),
            P("rep", "blk", None),
            P("rep", "blk", None),
            P(),
            P(None, "blk", None, "rep"),
            P("blk", None),
            P(),
            P("rep"),
        ),
        out_specs=(P("rep", "blk", None), P(None, None, "blk"), P(None, "rep")),
        check_vma=False,
    )
```

```python
import functools

import jax
import jax.numpy as jnp
from jax import lax
from jax.experimental import pallas as pl
from jax.experimental.pallas import tpu as pltpu
from jax.sharding import PartitionSpec as P

FF = 512
EXPERTS = 32
LEN = 128
CAP = 36
ROOM = 40
PLANE = 4
LANES = 128
VMEM = 56 * 1024 * 1024


def merged(x, axis, combine):
    everything = jax.tree.map(lambda part: lax.all_gather(part, axis), x)
    initial = jax.tree.map(lambda part: part[0], everything)

    def turn(k, so_far):
        return combine(so_far, jax.tree.map(lambda part: part[k], everything))

    return lax.fori_loop(1, lax.axis_size(axis), turn, initial)


def combine_stats(first, second):
    return (first[0] + second[0], jnp.maximum(first[1], second[1]))


def general(
    hidden_in, lengths, routes, route_weights, norm_gain, master, unembed, final_gain, target_ids
):
    rows_here = hidden_in.shape[1]
    width = hidden_in.shape[2]
    top_count = routes.shape[2]
    blk_count = lax.axis_size("blk")
    rep_count = lax.axis_size("rep")
    blk_index = lax.axis_index("blk")
    unit_count = master.shape[3] * rep_count
    split_ways = max(1, FF // unit_count)
    local_exp = max(1, unit_count // FF)
    group_width = min(unit_count, FF)
    capacity = CAP
    blocks = master.astype(jnp.bfloat16)
    arrived_blocks = lax.all_to_all(blocks, "blk", split_axis=2, concat_axis=1, tiled=True)
    server = lax.all_gather(arrived_blocks, "rep", axis=3, tiled=True)[:, :, 0, :]
    gate_w = server[0].reshape(width, local_exp, group_width)
    up_w = server[1].reshape(width, local_exp, group_width)
    down_w = server[2].reshape(width, local_exp, group_width)
    prompts_here = lengths.shape[0]
    slot_index = blk_index * rows_here + jnp.arange(rows_here, dtype=jnp.int32)
    prompt_of = slot_index // LEN
    position = slot_index % LEN
    prompt_match = prompt_of[:, None] == jnp.arange(prompts_here, dtype=jnp.int32)[None, :]
    row_len = jnp.sum(jnp.where(prompt_match, lengths[None, :], 0), axis=1)
    is_valid = position < row_len
    resid_f = hidden_in[0].astype(jnp.float32)
    normed = (
        resid_f * lax.rsqrt(jnp.mean(resid_f * resid_f, axis=-1, keepdims=True) + 1e-05) * norm_gain
    ).astype(jnp.bfloat16)
    expert_ids = routes[0].reshape(-1)
    pair_live = jnp.repeat(is_valid, top_count)
    pair_row = jnp.repeat(jnp.arange(rows_here, dtype=jnp.int32), top_count)
    expert_hits = (
        (expert_ids[:, None] == jnp.arange(EXPERTS, dtype=jnp.int32)[None, :]) & pair_live[:, None]
    ).astype(jnp.int32)
    slot_rank = jnp.sum((jnp.cumsum(expert_hits, axis=0) - 1) * expert_hits, axis=1)
    slot_id = jnp.where(pair_live, expert_ids * capacity + slot_rank, EXPERTS * capacity)
    source_row = jnp.zeros((EXPERTS * capacity + 1,), jnp.int32).at[slot_id].set(pair_row)[:-1]
    filled = jnp.zeros((EXPERTS * capacity + 1,), jnp.bfloat16).at[slot_id].set(1.0)[:-1]
    outgoing = (normed[source_row] * filled[:, None]).reshape(EXPERTS, capacity, width)
    sending = jnp.repeat(outgoing, split_ways, axis=0).reshape(
        blk_count, local_exp, capacity, width
    )
    arrived = lax.all_to_all(sending, "blk", split_axis=0, concat_axis=0, tiled=True)
    sources = arrived.shape[0]
    slot_count = arrived.shape[2]
    stride = sources
    while stride % 2 == 0 and stride * local_exp * slot_count > 1024:
        stride = stride // 2
    grouped = arrived.reshape(sources // stride, stride, local_exp, slot_count, width)

    def one_block(portion):
        gate_out = jnp.einsum("slnd,dlf->slnf", portion, gate_w, preferred_element_type=jnp.float32)
        up_out = jnp.einsum("slnd,dlf->slnf", portion, up_w, preferred_element_type=jnp.float32)
        hidden = (jax.nn.silu(gate_out) * up_out).astype(jnp.bfloat16)
        return jnp.einsum(
            "slnf,dlf->slnd", hidden, down_w, preferred_element_type=jnp.float32
        ).astype(jnp.bfloat16)

    returned = lax.all_to_all(
        lax.map(one_block, grouped).reshape(sources, local_exp, slot_count, width),
        "blk",
        split_axis=0,
        concat_axis=0,
        tiled=True,
    )
    summed_f = jnp.sum(
        returned.reshape(EXPERTS, split_ways, capacity, width).astype(jnp.float32), axis=1
    )
    expert_out = lax.optimization_barrier(summed_f.astype(jnp.bfloat16)).reshape(
        EXPERTS * capacity, width
    )
    gather_index = jnp.where(pair_live, expert_ids * capacity + slot_rank, 0)
    pair_weight = route_weights[0].reshape(-1) * pair_live.astype(jnp.float32)
    moe = jnp.sum(
        (expert_out[gather_index].astype(jnp.float32) * pair_weight[:, None]).reshape(
            rows_here, top_count, width
        ),
        axis=1,
    )
    out_rows = (resid_f + moe).astype(jnp.bfloat16)
    out_f = out_rows.astype(jnp.float32)
    row_squares = jnp.sum(out_f * out_f, axis=-1) * is_valid.astype(jnp.float32)
    square_local = jnp.sum(jnp.where(prompt_match, row_squares[:, None], 0.0), axis=0)
    is_last = is_valid & (position == row_len - 1)
    picker = (prompt_match & is_last[:, None]).astype(jnp.bfloat16)
    last_local = lax.dot_general(
        picker, out_rows, (((0,), (0,)), ((), ())), preferred_element_type=jnp.float32
    )
    last_rows, square_total = lax.psum((last_local, square_local), "blk")
    norms = jnp.sqrt(square_total / (lengths.astype(jnp.float32) * width) + 1e-06)
    final = (
        last_rows
        * lax.rsqrt(jnp.mean(last_rows * last_rows, axis=-1, keepdims=True) + 1e-05)
        * final_gain
    ).astype(jnp.bfloat16)
    logits = lax.dot_general(
        final, unembed, (((1,), (1,)), ((), ())), preferred_element_type=jnp.float32
    )
    vocab_base = blk_index * unembed.shape[0]
    target_hit = (
        target_ids[:, None] == vocab_base + jnp.arange(unembed.shape[0], dtype=jnp.int32)[None, :]
    )
    target_part = jnp.sum(jnp.where(target_hit, logits, 0.0), axis=1)
    top_part = jnp.max(logits, axis=1)
    target_logit, top_logit = merged((target_part, top_part), "blk", combine_stats)
    request_stats = jnp.stack([norms, top_logit, target_logit])
    return (out_rows[None], server, request_stats)


def iota(shape, dim):
    return lax.broadcasted_iota(jnp.int32, shape, dim)


def prep_kernel(info, hidden_ref, routes_ref, weights_ref, gain_ref, _, rows_ref, pieces_ref):
    rows, width = hidden_ref.shape
    length = info[3]
    x = hidden_ref[...].astype(jnp.float32)
    scale = lax.rsqrt(jnp.mean(x * x, axis=-1, keepdims=True) + 1e-05)
    rows_ref[:, :width] = (x * scale * gain_ref[...]).astype(jnp.bfloat16)
    lane = iota((rows, LANES), 1)
    row = iota((rows, LANES), 0)
    hit = jnp.zeros((rows, LANES), jnp.float32)
    weight = jnp.zeros((rows, LANES), jnp.float32)
    for k in range(routes_ref.shape[1]):
        named = routes_ref[:, k : k + 1] == lane
        hit = hit + jnp.where(named, 1.0, 0.0)
        weight = weight + jnp.where(named, weights_ref[:, k : k + 1], 0.0)
    live = row < length
    hit = jnp.where(live, hit, 0.0)
    weight = jnp.where(live, weight, 0.0)
    before = jnp.where(iota((rows, rows), 1) < iota((rows, rows), 0), 1.0, 0.0)
    rank = jnp.dot(
        before.astype(jnp.bfloat16), hit.astype(jnp.bfloat16), preferred_element_type=jnp.float32
    )
    rows_ref[:, width:] = jnp.where(hit > 0.0, rank, -1.0).astype(jnp.bfloat16)
    for k in range(3):
        piece = weight.astype(jnp.bfloat16)
        pieces_ref[k * rows : (k + 1) * rows, :] = piece
        weight = weight - piece.astype(jnp.float32)


def gate_up_kernel(which, info, x_ref, g_ref, u_ref, out_ref, picked):
    step = pl.program_id(0)
    rows = x_ref.shape[0]
    width = g_ref.shape[0]
    sources = rows // LEN
    slots = sources * ROOM
    ranks = x_ref[:, width:].astype(jnp.float32)
    lane = iota((rows, LANES), 1)
    source = (iota((rows, 1), 0) // LEN).astype(jnp.float32)
    rank = jnp.sum(jnp.where(lane == info[which], ranks, 0.0), axis=1, keepdims=True)
    slot = jnp.where(rank >= 0.0, source * ROOM + rank, -1.0)
    slot_lane = iota((rows, slots), 1).astype(jnp.float32)
    one_hot = jnp.where(slot == slot_lane, 1.0, 0.0).astype(jnp.bfloat16)
    chosen = lax.dot_general(
        one_hot, x_ref[:, :width], (((0,), (0,)), ((), ())), preferred_element_type=jnp.float32
    )
    for s in range(sources):
        start = pl.multiple_of((s * PLANE + step) * ROOM, ROOM)
        picked[pl.ds(start, ROOM), :] = chosen[s * ROOM : (s + 1) * ROOM]

    @pl.when(step == PLANE - 1)
    def _():
        x = picked[...].astype(jnp.bfloat16)
        gate = jnp.dot(x, g_ref[...], preferred_element_type=jnp.float32)
        up = jnp.dot(x, u_ref[...], preferred_element_type=jnp.float32)
        out_ref[...] = (gate / (1.0 + jnp.exp(-gate)) * up).astype(jnp.bfloat16)


def down_kernel(hidden_ref, d_ref, out_ref):
    total = lax.dot_general(
        hidden_ref[...], d_ref[...], (((1,), (1,)), ((), ())), preferred_element_type=jnp.float32
    )
    out_ref[...] = total.astype(jnp.bfloat16)


def weigh(parity, rank_ref, pieces_ref, back_ref, mix, step):
    slots = back_ref.shape[0]
    rows = rank_ref.shape[0]

    @pl.when(step == 0)
    def _():
        expert = iota((LANES, slots), 0)
        lane = iota((LANES, slots), 1)
        start = jnp.where((expert & 1) == parity, (expert >> 1) * ROOM, slots)
        inside = (lane >= start) & (lane < start + ROOM)
        spread = jnp.where(inside, 1.0, 0.0).astype(jnp.bfloat16)
        within = jnp.sum(jnp.where(inside, lane - start, 0), axis=0, keepdims=True).astype(jnp.float32)
        rank = jnp.dot(rank_ref[...], spread, preferred_element_type=jnp.float32)
        match = rank == within
        for k in range(3):
            part = jnp.dot(
                pieces_ref[k * rows : (k + 1) * rows, :], spread, preferred_element_type=jnp.float32
            )
            mix[k * rows : (k + 1) * rows, :] = jnp.where(match, part, 0.0).astype(jnp.bfloat16)

    parts = jnp.dot(mix[...], back_ref[...], preferred_element_type=jnp.float32)
    return parts[2 * rows :] + parts[rows : 2 * rows] + parts[:rows]


def first_kernel(info, rank_ref, pieces_ref, back_ref, moe_ref, mix):
    moe_ref[...] = weigh(info[2], rank_ref, pieces_ref, back_ref, mix, pl.program_id(0))


def combine_kernel(
    info,
    rank_ref,
    pieces_ref,
    back_ref,
    moe_ref,
    resid_ref,
    _,
    out_ref,
    last_ref,
    square_ref,
    mix,
    squares,
):
    step = pl.program_id(0)
    length = info[3]
    moe = moe_ref[...] + weigh(1 - info[2], rank_ref, pieces_ref, back_ref, mix, step)

    @pl.when(step == 0)
    def _():
        squares[...] = jnp.zeros_like(squares)

    out = (resid_ref[...].astype(jnp.float32) + moe).astype(jnp.bfloat16)
    out_ref[...] = out
    out_f = out.astype(jnp.float32)
    row = iota(out_f.shape, 0)
    last_ref[...] = jnp.sum(jnp.where(row == length - 1, out_f, 0.0), axis=0, keepdims=True)
    squares[...] += jnp.sum(jnp.where(row < length, out_f * out_f, 0.0), axis=0, keepdims=True)

    @pl.when(step == pl.num_programs(0) - 1)
    def _():
        square_ref[...] = jnp.broadcast_to(
            jnp.sum(squares[...], axis=1, keepdims=True), square_ref.shape
        )


def place_kernel(info, g_own, g_oth, u_own, u_oth, d_own, d_oth, _, out_ref):
    for k, (own, oth) in enumerate(((g_own, g_oth), (u_own, u_oth), (d_own, d_oth))):

        @pl.when(info[2] == 0)
        def _():
            out_ref[k, :, :FF] = own[...]
            out_ref[k, :, FF:] = oth[...]

        @pl.when(info[2] != 0)
        def _():
            out_ref[k, :, :FF] = oth[...]
            out_ref[k, :, FF:] = own[...]


def cast_kernel(blocks, x_ref, *refs):
    out_ref = refs[-1]
    rows = out_ref.shape[1]
    for b in range(blocks):
        out_ref[b] = x_ref[pl.ds(b, rows, stride=blocks), :].astype(jnp.bfloat16)


def tie_kernel(x_ref, _, out_ref):
    pass


def params():
    return pltpu.CompilerParams(vmem_limit_bytes=VMEM, dimension_semantics=("arbitrary",))


def whole(shape):
    return pl.BlockSpec(shape, lambda *_: tuple(0 for _ in shape))


def paired(
    hidden_in, lengths, routes, route_weights, norm_gain, master, unembed, final_gain, target_ids
):
    rows = hidden_in.shape[1]
    width = hidden_in.shape[2]
    blk_count = lax.axis_size("blk")
    blk = lax.axis_index("blk")
    rep = lax.axis_index("rep")
    slots = blk_count * ROOM
    resid = hidden_in[0]
    info = jnp.stack([2 * blk + rep, 2 * blk + 1 - rep, rep, lengths[blk]]).astype(jnp.int32)

    shard_rows = master.shape[1]
    flat = master.reshape(3 * shard_rows * blk_count, FF)

    def turned(k, *after):
        return pl.pallas_call(
            functools.partial(cast_kernel, blk_count),
            grid=(FF // LANES,),
            in_specs=[pl.BlockSpec((shard_rows * blk_count, LANES), lambda i: (k, i))]
            + [pl.BlockSpec(memory_space=pl.ANY)] * len(after),
            out_specs=pl.BlockSpec((blk_count, shard_rows, LANES), lambda i: (0, 0, i)),
            out_shape=jax.ShapeDtypeStruct((blk_count, shard_rows, FF), jnp.bfloat16),
            compiler_params=params(),
            name="cast",
        )(flat, *after)

    def moved(x):
        own = lax.all_to_all(x, "blk", split_axis=0, concat_axis=0, tiled=True)
        own = own.reshape(width, FF)
        return own, lax.ppermute(own, "rep", [(0, 1), (1, 0)])

    def tied(x, after):
        return pl.pallas_call(
            tie_kernel,
            in_specs=[pl.BlockSpec(memory_space=pl.ANY)] * 2,
            out_specs=pl.BlockSpec(memory_space=pl.ANY),
            out_shape=jax.ShapeDtypeStruct(x.shape, x.dtype),
            input_output_aliases={0: 0},
            name="tie",
        )(x, after)

    g_turned = turned(0)
    g_own, g_oth = moved(g_turned)
    u_own, u_oth = moved(turned(1))
    d_own, d_oth = moved(tied(turned(2), g_oth))

    row_ext, pieces = pl.pallas_call(
        prep_kernel,
        grid_spec=pltpu.PrefetchScalarGridSpec(
            num_scalar_prefetch=1,
            grid=(1,),
            in_specs=[
                whole((rows, width)),
                whole((rows, routes.shape[2])),
                whole((rows, routes.shape[2])),
                whole((1, width)),
                pl.BlockSpec(memory_space=pl.ANY),
            ],
            out_specs=[whole((rows, width + LANES)), whole((3 * rows, LANES))],
        ),
        out_shape=[
            jax.ShapeDtypeStruct((rows, width + LANES), jnp.bfloat16),
            jax.ShapeDtypeStruct((3 * rows, LANES), jnp.bfloat16),
        ],
        compiler_params=params(),
        name="prep",
    )(info, resid, routes[0], route_weights[0], norm_gain[None], g_turned)
    count = blk_count // PLANE
    lines = [[p + PLANE * q for q in range(count)] for p in range(PLANE)]
    planes = [[p + PLANE * q for p in range(PLANE)] for q in range(count)]
    line = lax.all_gather(row_ext, "blk", axis_index_groups=lines, axis=0, tiled=True)
    tokens = lax.all_gather(line, "blk", axis_index_groups=planes, axis=0, tiled=True)

    def hidden_of(which, g, u):
        return pl.pallas_call(
            functools.partial(gate_up_kernel, which),
            grid_spec=pltpu.PrefetchScalarGridSpec(
                num_scalar_prefetch=1,
                grid=(PLANE,),
                in_specs=[pl.BlockSpec((count * rows, width + LANES), lambda i, *_: (i, 0))]
                + [whole((width, FF))] * 2,
                out_specs=whole((slots, FF)),
                scratch_shapes=[pltpu.VMEM((slots, width), jnp.float32)],
            ),
            out_shape=jax.ShapeDtypeStruct((slots, FF), jnp.bfloat16),
            compiler_params=params(),
            name="gate_up",
        )(info, tokens, g, u)

    step = 512

    def outputs_of(hidden, d):
        return pl.pallas_call(
            down_kernel,
            grid=(width // step,),
            in_specs=[whole((slots, FF)), pl.BlockSpec((step, FF), lambda i: (i, 0))],
            out_specs=pl.BlockSpec((slots, step), lambda i: (0, i)),
            out_shape=jax.ShapeDtypeStruct((slots, width), jnp.bfloat16),
            compiler_params=params(),
            name="down",
        )(hidden, d)

    def returned(x):
        x = x.reshape(blk_count, ROOM, width)
        x = lax.all_to_all(x, "blk", split_axis=0, concat_axis=0, tiled=True)
        return x.reshape(slots, width)

    own_out = outputs_of(hidden_of(0, g_own, u_own), d_own)
    own_back = returned(own_out)
    oth_out = outputs_of(hidden_of(1, g_oth, u_oth), d_oth)
    oth_back = returned(oth_out)

    part = width // 4
    server = pl.pallas_call(
        place_kernel,
        grid_spec=pltpu.PrefetchScalarGridSpec(
            num_scalar_prefetch=1,
            grid=(width // part,),
            in_specs=[pl.BlockSpec((part, FF), lambda i, *_: (i, 0))] * 6
            + [pl.BlockSpec(memory_space=pl.ANY)],
            out_specs=pl.BlockSpec((3, part, 2 * FF), lambda i, *_: (0, i, 0)),
        ),
        out_shape=jax.ShapeDtypeStruct((3, width, 2 * FF), jnp.bfloat16),
        compiler_params=params(),
        name="place",
    )(info, g_own, g_oth, u_own, u_oth, d_own, d_oth, oth_out)

    weigh_specs = [
        pl.BlockSpec((rows, LANES), lambda i, *_: (0, width // LANES)),
        whole((3 * rows, LANES)),
        pl.BlockSpec((slots, step), lambda i, *_: (0, i)),
    ]
    column = pl.BlockSpec((rows, step), lambda i, *_: (0, i))
    mix = pltpu.VMEM((3 * rows, slots), jnp.bfloat16)
    moe = pl.pallas_call(
        first_kernel,
        grid_spec=pltpu.PrefetchScalarGridSpec(
            num_scalar_prefetch=1,
            grid=(width // step,),
            in_specs=weigh_specs,
            out_specs=column,
            scratch_shapes=[mix],
        ),
        out_shape=jax.ShapeDtypeStruct((rows, width), jnp.float32),
        compiler_params=params(),
        name="first",
    )(info, row_ext, pieces, own_back)
    out_rows, last, square = pl.pallas_call(
        combine_kernel,
        grid_spec=pltpu.PrefetchScalarGridSpec(
            num_scalar_prefetch=1,
            grid=(width // step,),
            in_specs=weigh_specs + [column, column, pl.BlockSpec(memory_space=pl.ANY)],
            out_specs=[
                column,
                pl.BlockSpec((1, step), lambda i, *_: (0, i)),
                whole((1, LANES)),
            ],
            scratch_shapes=[mix, pltpu.VMEM((1, step), jnp.float32)],
        ),
        out_shape=[
            jax.ShapeDtypeStruct((rows, width), jnp.bfloat16),
            jax.ShapeDtypeStruct((1, width), jnp.float32),
            jax.ShapeDtypeStruct((1, LANES), jnp.float32),
        ],
        compiler_params=params(),
        name="combine",
    )(info, row_ext, pieces, oth_back, moe, resid, server)

    def everywhere(x):
        copies = jnp.broadcast_to(x[None], (blk_count,) + x.shape)
        return lax.all_to_all(copies, "blk", split_axis=0, concat_axis=0, tiled=True)

    gathered = everywhere(jnp.concatenate([last, square], axis=1))[:, 0]
    last_rows, square_total = gathered[:, :width], gathered[:, width]
    norms = jnp.sqrt(square_total / (lengths.astype(jnp.float32) * width) + 1e-06)
    final = (
        last_rows
        * lax.rsqrt(jnp.mean(last_rows * last_rows, axis=-1, keepdims=True) + 1e-05)
        * final_gain
    ).astype(jnp.bfloat16)
    logits = lax.dot_general(
        final, unembed, (((1,), (1,)), ((), ())), preferred_element_type=jnp.float32
    )
    vocab_base = blk * unembed.shape[0]
    target_hit = (
        target_ids[:, None] == vocab_base + jnp.arange(unembed.shape[0], dtype=jnp.int32)[None, :]
    )
    target_part = jnp.sum(jnp.where(target_hit, logits, 0.0), axis=1)
    top_part = jnp.max(logits, axis=1)
    parts = everywhere(jnp.stack([top_part, target_part]))
    request_stats = jnp.stack([norms, jnp.max(parts[:, 0], axis=0), jnp.sum(parts[:, 1], axis=0)])
    return (out_rows[None], server, request_stats)


def local(hidden_in, lengths, routes, route_weights, norm_gain, master, *rest):
    blk_count = lax.axis_size("blk")
    fits = (
        lax.axis_size("rep") == 2
        and master.shape[3] == FF
        and EXPERTS == 2 * blk_count
        and blk_count == PLANE * PLANE
        and hidden_in.shape[1] == LEN
        and lengths.shape[0] == blk_count
    )
    form = paired if fits else general
    return form(hidden_in, lengths, routes, route_weights, norm_gain, master, *rest)


def solution(mesh):
    return jax.shard_map(
        local,
        mesh=mesh,
        in_specs=(
            P("rep", "blk", None),
            P("rep"),
            P("rep", "blk", None),
            P("rep", "blk", None),
            P(),
            P(None, "blk", None, "rep"),
            P("blk", None),
            P(),
            P("rep"),
        ),
        out_specs=(P("rep", "blk", None), P(None, None, "blk"), P(None, "rep")),
        check_vma=False,
    )
```

```python
import functools

import jax
import jax.numpy as jnp
from jax import lax
from jax.experimental import pallas as pl
from jax.experimental.pallas import tpu as pltpu
from jax.sharding import PartitionSpec as P

FF = 512
EXPERTS = 32
LEN = 128
CAP = 36
FIRST = 32
SECOND = 40
PLANE = 4
LANES = 128
VMEM = 56 * 1024 * 1024


def merged(x, axis, combine):
    everything = jax.tree.map(lambda part: lax.all_gather(part, axis), x)
    initial = jax.tree.map(lambda part: part[0], everything)

    def turn(k, so_far):
        return combine(so_far, jax.tree.map(lambda part: part[k], everything))

    return lax.fori_loop(1, lax.axis_size(axis), turn, initial)


def combine_stats(first, second):
    return (first[0] + second[0], jnp.maximum(first[1], second[1]))


def general(
    hidden_in, lengths, routes, route_weights, norm_gain, master, unembed, final_gain, target_ids
):
    rows_here = hidden_in.shape[1]
    width = hidden_in.shape[2]
    top_count = routes.shape[2]
    blk_count = lax.axis_size("blk")
    rep_count = lax.axis_size("rep")
    blk_index = lax.axis_index("blk")
    unit_count = master.shape[3] * rep_count
    split_ways = max(1, FF // unit_count)
    local_exp = max(1, unit_count // FF)
    group_width = min(unit_count, FF)
    capacity = CAP
    blocks = master.astype(jnp.bfloat16)
    arrived_blocks = lax.all_to_all(blocks, "blk", split_axis=2, concat_axis=1, tiled=True)
    server = lax.all_gather(arrived_blocks, "rep", axis=3, tiled=True)[:, :, 0, :]
    gate_w = server[0].reshape(width, local_exp, group_width)
    up_w = server[1].reshape(width, local_exp, group_width)
    down_w = server[2].reshape(width, local_exp, group_width)
    prompts_here = lengths.shape[0]
    slot_index = blk_index * rows_here + jnp.arange(rows_here, dtype=jnp.int32)
    prompt_of = slot_index // LEN
    position = slot_index % LEN
    prompt_match = prompt_of[:, None] == jnp.arange(prompts_here, dtype=jnp.int32)[None, :]
    row_len = jnp.sum(jnp.where(prompt_match, lengths[None, :], 0), axis=1)
    is_valid = position < row_len
    resid_f = hidden_in[0].astype(jnp.float32)
    normed = (
        resid_f * lax.rsqrt(jnp.mean(resid_f * resid_f, axis=-1, keepdims=True) + 1e-05) * norm_gain
    ).astype(jnp.bfloat16)
    expert_ids = routes[0].reshape(-1)
    pair_live = jnp.repeat(is_valid, top_count)
    pair_row = jnp.repeat(jnp.arange(rows_here, dtype=jnp.int32), top_count)
    expert_hits = (
        (expert_ids[:, None] == jnp.arange(EXPERTS, dtype=jnp.int32)[None, :]) & pair_live[:, None]
    ).astype(jnp.int32)
    slot_rank = jnp.sum((jnp.cumsum(expert_hits, axis=0) - 1) * expert_hits, axis=1)
    slot_id = jnp.where(pair_live, expert_ids * capacity + slot_rank, EXPERTS * capacity)
    source_row = jnp.zeros((EXPERTS * capacity + 1,), jnp.int32).at[slot_id].set(pair_row)[:-1]
    filled = jnp.zeros((EXPERTS * capacity + 1,), jnp.bfloat16).at[slot_id].set(1.0)[:-1]
    outgoing = (normed[source_row] * filled[:, None]).reshape(EXPERTS, capacity, width)
    sending = jnp.repeat(outgoing, split_ways, axis=0).reshape(
        blk_count, local_exp, capacity, width
    )
    arrived = lax.all_to_all(sending, "blk", split_axis=0, concat_axis=0, tiled=True)
    sources = arrived.shape[0]
    slot_count = arrived.shape[2]
    stride = sources
    while stride % 2 == 0 and stride * local_exp * slot_count > 1024:
        stride = stride // 2
    grouped = arrived.reshape(sources // stride, stride, local_exp, slot_count, width)

    def one_block(portion):
        gate_out = jnp.einsum("slnd,dlf->slnf", portion, gate_w, preferred_element_type=jnp.float32)
        up_out = jnp.einsum("slnd,dlf->slnf", portion, up_w, preferred_element_type=jnp.float32)
        hidden = (jax.nn.silu(gate_out) * up_out).astype(jnp.bfloat16)
        return jnp.einsum(
            "slnf,dlf->slnd", hidden, down_w, preferred_element_type=jnp.float32
        ).astype(jnp.bfloat16)

    returned = lax.all_to_all(
        lax.map(one_block, grouped).reshape(sources, local_exp, slot_count, width),
        "blk",
        split_axis=0,
        concat_axis=0,
        tiled=True,
    )
    summed_f = jnp.sum(
        returned.reshape(EXPERTS, split_ways, capacity, width).astype(jnp.float32), axis=1
    )
    expert_out = lax.optimization_barrier(summed_f.astype(jnp.bfloat16)).reshape(
        EXPERTS * capacity, width
    )
    gather_index = jnp.where(pair_live, expert_ids * capacity + slot_rank, 0)
    pair_weight = route_weights[0].reshape(-1) * pair_live.astype(jnp.float32)
    moe = jnp.sum(
        (expert_out[gather_index].astype(jnp.float32) * pair_weight[:, None]).reshape(
            rows_here, top_count, width
        ),
        axis=1,
    )
    out_rows = (resid_f + moe).astype(jnp.bfloat16)
    out_f = out_rows.astype(jnp.float32)
    row_squares = jnp.sum(out_f * out_f, axis=-1) * is_valid.astype(jnp.float32)
    square_local = jnp.sum(jnp.where(prompt_match, row_squares[:, None], 0.0), axis=0)
    is_last = is_valid & (position == row_len - 1)
    picker = (prompt_match & is_last[:, None]).astype(jnp.bfloat16)
    last_local = lax.dot_general(
        picker, out_rows, (((0,), (0,)), ((), ())), preferred_element_type=jnp.float32
    )
    last_rows, square_total = lax.psum((last_local, square_local), "blk")
    norms = jnp.sqrt(square_total / (lengths.astype(jnp.float32) * width) + 1e-06)
    final = (
        last_rows
        * lax.rsqrt(jnp.mean(last_rows * last_rows, axis=-1, keepdims=True) + 1e-05)
        * final_gain
    ).astype(jnp.bfloat16)
    logits = lax.dot_general(
        final, unembed, (((1,), (1,)), ((), ())), preferred_element_type=jnp.float32
    )
    vocab_base = blk_index * unembed.shape[0]
    target_hit = (
        target_ids[:, None] == vocab_base + jnp.arange(unembed.shape[0], dtype=jnp.int32)[None, :]
    )
    target_part = jnp.sum(jnp.where(target_hit, logits, 0.0), axis=1)
    top_part = jnp.max(logits, axis=1)
    target_logit, top_logit = merged((target_part, top_part), "blk", combine_stats)
    request_stats = jnp.stack([norms, top_logit, target_logit])
    return (out_rows[None], server, request_stats)


def iota(shape, dim):
    return lax.broadcasted_iota(jnp.int32, shape, dim)


def prep_kernel(info, hidden_ref, routes_ref, weights_ref, gain_ref, _, rows_ref, pieces_ref):
    rows, width = hidden_ref.shape
    length = info[3]
    x = hidden_ref[...].astype(jnp.float32)
    scale = lax.rsqrt(jnp.mean(x * x, axis=-1, keepdims=True) + 1e-05)
    rows_ref[:, :width] = (x * scale * gain_ref[...]).astype(jnp.bfloat16)
    lane = iota((rows, LANES), 1)
    row = iota((rows, LANES), 0)
    hit = jnp.zeros((rows, LANES), jnp.float32)
    weight = jnp.zeros((rows, LANES), jnp.float32)
    named_by = jnp.transpose(routes_ref[...].astype(jnp.float32)).astype(jnp.int32)
    weight_by = jnp.transpose(weights_ref[...])
    for k in range(routes_ref.shape[0]):
        named = named_by[:, k : k + 1] == lane
        hit = hit + jnp.where(named, 1.0, 0.0)
        weight = weight + jnp.where(named, weight_by[:, k : k + 1], 0.0)
    live = row < length
    hit = jnp.where(live, hit, 0.0)
    weight = jnp.where(live, weight, 0.0)
    before = jnp.where(iota((rows, rows), 1) < iota((rows, rows), 0), 1.0, 0.0)
    rank = jnp.dot(
        before.astype(jnp.bfloat16), hit.astype(jnp.bfloat16), preferred_element_type=jnp.float32
    )
    rows_ref[:, width:] = jnp.where(hit > 0.0, rank, -1.0).astype(jnp.bfloat16)
    for k in range(3):
        piece = weight.astype(jnp.bfloat16)
        pieces_ref[k * rows : (k + 1) * rows, :] = piece
        weight = weight - piece.astype(jnp.float32)


def pick(info, which, x_ref, width, place, slots):
    rows = x_ref.shape[0]
    ranks = x_ref[:, width:].astype(jnp.float32)
    lane = iota((rows, LANES), 1)
    source = (iota((rows, 1), 0) // LEN).astype(jnp.float32)
    rank = jnp.sum(jnp.where(lane == info[which], ranks, 0.0), axis=1, keepdims=True)
    slot = jnp.where(rank >= 0.0, place(source, rank), -1.0)
    slot_lane = iota((rows, slots), 1).astype(jnp.float32)
    one_hot = jnp.where(slot == slot_lane, 1.0, 0.0).astype(jnp.bfloat16)
    return lax.dot_general(
        one_hot, x_ref[:, :width], (((0,), (0,)), ((), ())), preferred_element_type=jnp.float32
    )


def activ(x, g_ref, u_ref):
    x = x.astype(jnp.bfloat16)
    gate = jnp.dot(x, g_ref[...], preferred_element_type=jnp.float32)
    up = jnp.dot(x, u_ref[...], preferred_element_type=jnp.float32)
    return (gate / (1.0 + jnp.exp(-gate)) * up).astype(jnp.bfloat16)


def own_kernel(info, x_ref, g_ref, u_ref, out_ref, late_ref, picked):
    step = pl.program_id(0)
    sources = x_ref.shape[0] // LEN
    more = CAP - FIRST
    early = sources * FIRST
    all_early = PLANE * early

    def place(source, rank):
        return jnp.where(
            rank < FIRST, source * FIRST + rank, early + source * more + (rank - FIRST)
        )

    chosen = pick(info, 0, x_ref, g_ref.shape[0], place, early + sources * more)
    for s in range(sources):
        start = pl.multiple_of((s * PLANE + step) * FIRST, FIRST)
        picked[pl.ds(start, FIRST), :] = chosen[s * FIRST : (s + 1) * FIRST]
    start = pl.multiple_of(all_early + step * sources * more, sources * more)
    picked[pl.ds(start, sources * more), :] = chosen[early:]

    @pl.when(step == PLANE - 1)
    def _():
        hidden = activ(picked[...], g_ref, u_ref)
        out_ref[...] = hidden[:all_early]
        rest = hidden[all_early:]
        shape = (late_ref.shape[0], rest.shape[0])
        column = iota(shape, 1)
        source = (column // more % sources) * PLANE + column // (more * sources)
        one_hot = jnp.where(iota(shape, 0) == source * SECOND + column % more, 1.0, 0.0)
        late_ref[...] = jnp.dot(
            one_hot.astype(jnp.bfloat16), rest, preferred_element_type=jnp.float32
        ).astype(jnp.bfloat16)


def oth_kernel(info, x_ref, g_ref, u_ref, _, out_ref, picked):
    step = pl.program_id(0)
    sources = x_ref.shape[0] // LEN

    def place(source, rank):
        return source * SECOND + (SECOND - CAP) + rank

    chosen = pick(info, 1, x_ref, g_ref.shape[0], place, sources * SECOND)
    for s in range(sources):
        start = pl.multiple_of((s * PLANE + step) * SECOND, SECOND)
        picked[pl.ds(start, SECOND), :] = chosen[s * SECOND : (s + 1) * SECOND]

    @pl.when(step == PLANE - 1)
    def _():
        out_ref[...] = activ(picked[...], g_ref, u_ref)


def down_kernel(*refs):
    out_ref = refs[-1]
    total = 0.0
    for hidden_ref, d_ref in zip(refs[0:-1:2], refs[1:-1:2]):
        total = total + lax.dot_general(
            hidden_ref[...],
            d_ref[...],
            (((1,), (1,)), ((), ())),
            preferred_element_type=jnp.float32,
        )
    out_ref[...] = total.astype(jnp.bfloat16)


def weigh(spans, stride, rank_ref, pieces_ref, back_ref, mix, step):
    slots = back_ref.shape[0]
    rows = rank_ref.shape[0]

    @pl.when(step == 0)
    def _():
        expert = iota((LANES, slots), 0)
        lane = iota((LANES, slots), 1)
        within = jnp.zeros((1, slots), jnp.float32)
        spread = jnp.zeros((LANES, slots), jnp.float32)
        for parity, offset, count, lowest in spans:
            start = jnp.where((expert & 1) == parity, (expert >> 1) * stride + offset, slots)
            inside = (lane >= start) & (lane < start + count)
            spread = spread + jnp.where(inside, 1.0, 0.0)
            ranks = jnp.where(inside, lane - start + lowest, 0)
            within = within + jnp.sum(ranks, axis=0, keepdims=True).astype(jnp.float32)
        spread = spread.astype(jnp.bfloat16)
        rank = jnp.dot(rank_ref[...], spread, preferred_element_type=jnp.float32)
        match = rank == within
        for k in range(3):
            part = jnp.dot(
                pieces_ref[k * rows : (k + 1) * rows, :], spread, preferred_element_type=jnp.float32
            )
            mix[k * rows : (k + 1) * rows, :] = jnp.where(match, part, 0.0).astype(jnp.bfloat16)

    parts = jnp.dot(mix[...], back_ref[...], preferred_element_type=jnp.float32)
    return parts[2 * rows :] + parts[rows : 2 * rows] + parts[:rows]


def first_kernel(info, rank_ref, pieces_ref, back_ref, moe_ref, mix):
    spans = ((info[2], 0, FIRST, 0),)
    moe_ref[...] = weigh(spans, FIRST, rank_ref, pieces_ref, back_ref, mix, pl.program_id(0))


def combine_kernel(
    info,
    rank_ref,
    pieces_ref,
    back_ref,
    moe_ref,
    resid_ref,
    _,
    out_ref,
    last_ref,
    square_ref,
    mix,
    squares,
):
    step = pl.program_id(0)
    length = info[3]
    late = SECOND - CAP
    spans = ((info[2], 0, late, FIRST), (1 - info[2], late, CAP, 0))
    moe = moe_ref[...] + weigh(spans, SECOND, rank_ref, pieces_ref, back_ref, mix, step)

    @pl.when(step == 0)
    def _():
        squares[...] = jnp.zeros_like(squares)

    out = (resid_ref[...].astype(jnp.float32) + moe).astype(jnp.bfloat16)
    out_ref[...] = out
    out_f = out.astype(jnp.float32)
    row = iota(out_f.shape, 0)
    last_ref[...] = jnp.sum(jnp.where(row == length - 1, out_f, 0.0), axis=0, keepdims=True)
    squares[...] += jnp.sum(jnp.where(row < length, out_f * out_f, 0.0), axis=0, keepdims=True)

    @pl.when(step == pl.num_programs(0) - 1)
    def _():
        square_ref[...] = jnp.broadcast_to(
            jnp.sum(squares[...], axis=1, keepdims=True), square_ref.shape
        )


def place_kernel(info, g_own, g_oth, u_own, u_oth, d_own, d_oth, _, out_ref):
    for k, (own, oth) in enumerate(((g_own, g_oth), (u_own, u_oth), (d_own, d_oth))):

        @pl.when(info[2] == 0)
        def _():
            out_ref[k, :, :FF] = own[...]
            out_ref[k, :, FF:] = oth[...]

        @pl.when(info[2] != 0)
        def _():
            out_ref[k, :, :FF] = oth[...]
            out_ref[k, :, FF:] = own[...]


def cast_kernel(blocks, x_ref, *refs):
    out_ref = refs[-1]
    rows = out_ref.shape[1]
    for b in range(blocks):
        out_ref[b] = x_ref[pl.ds(b, rows, stride=blocks), :].astype(jnp.bfloat16)


def tie_kernel(x_ref, _, out_ref):
    pass


def params():
    return pltpu.CompilerParams(vmem_limit_bytes=VMEM, dimension_semantics=("arbitrary",))


def whole(shape):
    return pl.BlockSpec(shape, lambda *_: tuple(0 for _ in shape))


def paired(
    hidden_in, lengths, routes, route_weights, norm_gain, master, unembed, final_gain, target_ids
):
    rows = hidden_in.shape[1]
    width = hidden_in.shape[2]
    blk_count = lax.axis_size("blk")
    blk = lax.axis_index("blk")
    rep = lax.axis_index("rep")
    first = blk_count * FIRST
    second = blk_count * SECOND
    resid = hidden_in[0]
    info = jnp.stack([2 * blk + rep, 2 * blk + 1 - rep, rep, lengths[blk]]).astype(jnp.int32)

    shard_rows = master.shape[1]
    flat = master.reshape(3 * shard_rows * blk_count, FF)

    def turned(k, *after):
        return pl.pallas_call(
            functools.partial(cast_kernel, blk_count),
            grid=(FF // LANES,),
            in_specs=[pl.BlockSpec((shard_rows * blk_count, LANES), lambda i: (k, i))]
            + [pl.BlockSpec(memory_space=pl.ANY)] * len(after),
            out_specs=pl.BlockSpec((blk_count, shard_rows, LANES), lambda i: (0, 0, i)),
            out_shape=jax.ShapeDtypeStruct((blk_count, shard_rows, FF), jnp.bfloat16),
            compiler_params=params(),
            name="cast",
        )(flat, *after)

    def moved(x):
        own = lax.all_to_all(x, "blk", split_axis=0, concat_axis=0, tiled=True)
        own = own.reshape(width, FF)
        return own, lax.ppermute(own, "rep", [(0, 1), (1, 0)])

    def tied(x, after):
        return pl.pallas_call(
            tie_kernel,
            in_specs=[pl.BlockSpec(memory_space=pl.ANY)] * 2,
            out_specs=pl.BlockSpec(memory_space=pl.ANY),
            out_shape=jax.ShapeDtypeStruct(x.shape, x.dtype),
            input_output_aliases={0: 0},
            name="tie",
        )(x, after)

    g_turned = turned(0)
    g_own, g_oth = moved(g_turned)
    u_own, u_oth = moved(turned(1))
    d_own, d_oth = moved(tied(turned(2), g_oth))

    row_ext, pieces = pl.pallas_call(
        prep_kernel,
        grid_spec=pltpu.PrefetchScalarGridSpec(
            num_scalar_prefetch=1,
            grid=(1,),
            in_specs=[
                whole((rows, width)),
                whole((routes.shape[2], rows)),
                whole((routes.shape[2], rows)),
                whole((1, width)),
                pl.BlockSpec(memory_space=pl.ANY),
            ],
            out_specs=[whole((rows, width + LANES)), whole((3 * rows, LANES))],
        ),
        out_shape=[
            jax.ShapeDtypeStruct((rows, width + LANES), jnp.bfloat16),
            jax.ShapeDtypeStruct((3 * rows, LANES), jnp.bfloat16),
        ],
        compiler_params=params(),
        name="prep",
    )(info, resid, routes[0].T, route_weights[0].T, norm_gain[None], g_turned)
    count = blk_count // PLANE
    lines = [[p + PLANE * q for q in range(count)] for p in range(PLANE)]
    planes = [[p + PLANE * q for p in range(PLANE)] for q in range(count)]
    line = lax.all_gather(row_ext, "blk", axis_index_groups=lines, axis=0, tiled=True)
    line = tied(line, g_own)
    tokens = lax.all_gather(line, "blk", axis_index_groups=planes, axis=0, tiled=True)

    def hidden_of(kernel, sizes, scratch, g, u, *after):
        return pl.pallas_call(
            kernel,
            grid_spec=pltpu.PrefetchScalarGridSpec(
                num_scalar_prefetch=1,
                grid=(PLANE,),
                in_specs=[pl.BlockSpec((count * rows, width + LANES), lambda i, *_: (i, 0))]
                + [whole((width, FF))] * 2
                + [pl.BlockSpec(memory_space=pl.ANY)] * len(after),
                out_specs=[whole((size, FF)) for size in sizes],
                scratch_shapes=[pltpu.VMEM((scratch, width), jnp.float32)],
            ),
            out_shape=[jax.ShapeDtypeStruct((size, FF), jnp.bfloat16) for size in sizes],
            compiler_params=params(),
            name="gate_up",
        )(info, tokens, g, u, *after)

    step = 512

    def outputs_of(size, *operands):
        return pl.pallas_call(
            down_kernel,
            grid=(width // step,),
            in_specs=[whole((size, FF)), pl.BlockSpec((step, FF), lambda i: (i, 0))]
            * (len(operands) // 2),
            out_specs=pl.BlockSpec((size, step), lambda i: (0, i)),
            out_shape=jax.ShapeDtypeStruct((size, width), jnp.bfloat16),
            compiler_params=params(),
            name="down",
        )(*operands)

    def returned(x):
        slots = x.shape[0]
        x = x.reshape(blk_count, slots // blk_count, width)
        x = lax.all_to_all(x, "blk", split_axis=0, concat_axis=0, tiled=True)
        return x.reshape(slots, width)

    extra = blk_count * (CAP - FIRST)
    own_hidden, late_hidden = hidden_of(own_kernel, (first, second), first + extra, g_own, u_own)
    own_out = tied(outputs_of(first, own_hidden, d_own), u_oth)
    own_back = returned(own_out)
    (oth_hidden,) = hidden_of(oth_kernel, (second,), second, g_oth, u_oth, own_out)
    oth_out = outputs_of(second, late_hidden, d_own, oth_hidden, d_oth)
    oth_back = returned(oth_out)

    part = width // 4
    server = pl.pallas_call(
        place_kernel,
        grid_spec=pltpu.PrefetchScalarGridSpec(
            num_scalar_prefetch=1,
            grid=(width // part,),
            in_specs=[pl.BlockSpec((part, FF), lambda i, *_: (i, 0))] * 6
            + [pl.BlockSpec(memory_space=pl.ANY)],
            out_specs=pl.BlockSpec((3, part, 2 * FF), lambda i, *_: (0, i, 0)),
        ),
        out_shape=jax.ShapeDtypeStruct((3, width, 2 * FF), jnp.bfloat16),
        compiler_params=params(),
        name="place",
    )(info, g_own, g_oth, u_own, u_oth, d_own, d_oth, oth_out)

    def weigh_specs(slots):
        return [
            pl.BlockSpec((rows, LANES), lambda i, *_: (0, width // LANES)),
            whole((3 * rows, LANES)),
            pl.BlockSpec((slots, step), lambda i, *_: (0, i)),
        ]

    column = pl.BlockSpec((rows, step), lambda i, *_: (0, i))
    moe = pl.pallas_call(
        first_kernel,
        grid_spec=pltpu.PrefetchScalarGridSpec(
            num_scalar_prefetch=1,
            grid=(width // step,),
            in_specs=weigh_specs(first),
            out_specs=column,
            scratch_shapes=[pltpu.VMEM((3 * rows, first), jnp.bfloat16)],
        ),
        out_shape=jax.ShapeDtypeStruct((rows, width), jnp.float32),
        compiler_params=params(),
        name="first",
    )(info, row_ext, pieces, own_back)
    out_rows, last, square = pl.pallas_call(
        combine_kernel,
        grid_spec=pltpu.PrefetchScalarGridSpec(
            num_scalar_prefetch=1,
            grid=(width // step,),
            in_specs=weigh_specs(second) + [column, column, pl.BlockSpec(memory_space=pl.ANY)],
            out_specs=[
                column,
                pl.BlockSpec((1, step), lambda i, *_: (0, i)),
                whole((1, LANES)),
            ],
            scratch_shapes=[
                pltpu.VMEM((3 * rows, second), jnp.bfloat16),
                pltpu.VMEM((1, step), jnp.float32),
            ],
        ),
        out_shape=[
            jax.ShapeDtypeStruct((rows, width), jnp.bfloat16),
            jax.ShapeDtypeStruct((1, width), jnp.float32),
            jax.ShapeDtypeStruct((1, LANES), jnp.float32),
        ],
        compiler_params=params(),
        name="combine",
    )(info, row_ext, pieces, oth_back, moe, resid, server)

    def everywhere(x):
        copies = jnp.broadcast_to(x[None], (blk_count,) + x.shape)
        return lax.all_to_all(copies, "blk", split_axis=0, concat_axis=0, tiled=True)

    gathered = everywhere(jnp.concatenate([last, square], axis=1))[:, 0]
    last_rows, square_total = gathered[:, :width], gathered[:, width]
    norms = jnp.sqrt(square_total / (lengths.astype(jnp.float32) * width) + 1e-06)
    final = (
        last_rows
        * lax.rsqrt(jnp.mean(last_rows * last_rows, axis=-1, keepdims=True) + 1e-05)
        * final_gain
    ).astype(jnp.bfloat16)
    logits = lax.dot_general(
        final, unembed, (((1,), (1,)), ((), ())), preferred_element_type=jnp.float32
    )
    vocab_base = blk * unembed.shape[0]
    target_hit = (
        target_ids[:, None] == vocab_base + jnp.arange(unembed.shape[0], dtype=jnp.int32)[None, :]
    )
    target_part = jnp.sum(jnp.where(target_hit, logits, 0.0), axis=1)
    top_part = jnp.max(logits, axis=1)
    parts = everywhere(jnp.stack([top_part, target_part]))
    request_stats = jnp.stack([norms, jnp.max(parts[:, 0], axis=0), jnp.sum(parts[:, 1], axis=0)])
    return (out_rows[None], server, request_stats)


def local(hidden_in, lengths, routes, route_weights, norm_gain, master, *rest):
    blk_count = lax.axis_size("blk")
    fits = (
        lax.axis_size("rep") == 2
        and master.shape[3] == FF
        and EXPERTS == 2 * blk_count
        and blk_count == PLANE * PLANE
        and hidden_in.shape[1] == LEN
        and lengths.shape[0] == blk_count
    )
    form = paired if fits else general
    return form(hidden_in, lengths, routes, route_weights, norm_gain, master, *rest)


def solution(mesh):
    return jax.shard_map(
        local,
        mesh=mesh,
        in_specs=(
            P("rep", "blk", None),
            P("rep"),
            P("rep", "blk", None),
            P("rep", "blk", None),
            P(),
            P(None, "blk", None, "rep"),
            P("blk", None),
            P(),
            P("rep"),
        ),
        out_specs=(P("rep", "blk", None), P(None, None, "blk"), P(None, "rep")),
        check_vma=False,
    )
```

```python
import functools

import jax
import jax.numpy as jnp
from jax import lax
from jax.experimental import pallas as pl
from jax.experimental.pallas import tpu as pltpu
from jax.sharding import PartitionSpec as P

FF = 512
EXPERTS = 32
LEN = 128
CAP = 36
FIRST = 32
SECOND = 40
GROUPS = 4
RING = (0, 1, 4, 5, 8, 9, 12, 13, 14, 15, 10, 11, 6, 7, 2, 3)
LANES = 128
VMEM = 56 * 1024 * 1024


def merged(x, axis, combine):
    everything = jax.tree.map(lambda part: lax.all_gather(part, axis), x)
    initial = jax.tree.map(lambda part: part[0], everything)

    def turn(k, so_far):
        return combine(so_far, jax.tree.map(lambda part: part[k], everything))

    return lax.fori_loop(1, lax.axis_size(axis), turn, initial)


def combine_stats(first, second):
    return (first[0] + second[0], jnp.maximum(first[1], second[1]))


def general(
    hidden_in, lengths, routes, route_weights, norm_gain, master, unembed, final_gain, target_ids
):
    rows_here = hidden_in.shape[1]
    width = hidden_in.shape[2]
    top_count = routes.shape[2]
    blk_count = lax.axis_size("blk")
    rep_count = lax.axis_size("rep")
    blk_index = lax.axis_index("blk")
    unit_count = master.shape[3] * rep_count
    split_ways = max(1, FF // unit_count)
    local_exp = max(1, unit_count // FF)
    group_width = min(unit_count, FF)
    capacity = CAP
    blocks = master.astype(jnp.bfloat16)
    arrived_blocks = lax.all_to_all(blocks, "blk", split_axis=2, concat_axis=1, tiled=True)
    server = lax.all_gather(arrived_blocks, "rep", axis=3, tiled=True)[:, :, 0, :]
    gate_w = server[0].reshape(width, local_exp, group_width)
    up_w = server[1].reshape(width, local_exp, group_width)
    down_w = server[2].reshape(width, local_exp, group_width)
    prompts_here = lengths.shape[0]
    slot_index = blk_index * rows_here + jnp.arange(rows_here, dtype=jnp.int32)
    prompt_of = slot_index // LEN
    position = slot_index % LEN
    prompt_match = prompt_of[:, None] == jnp.arange(prompts_here, dtype=jnp.int32)[None, :]
    row_len = jnp.sum(jnp.where(prompt_match, lengths[None, :], 0), axis=1)
    is_valid = position < row_len
    resid_f = hidden_in[0].astype(jnp.float32)
    normed = (
        resid_f * lax.rsqrt(jnp.mean(resid_f * resid_f, axis=-1, keepdims=True) + 1e-05) * norm_gain
    ).astype(jnp.bfloat16)
    expert_ids = routes[0].reshape(-1)
    pair_live = jnp.repeat(is_valid, top_count)
    pair_row = jnp.repeat(jnp.arange(rows_here, dtype=jnp.int32), top_count)
    expert_hits = (
        (expert_ids[:, None] == jnp.arange(EXPERTS, dtype=jnp.int32)[None, :]) & pair_live[:, None]
    ).astype(jnp.int32)
    slot_rank = jnp.sum((jnp.cumsum(expert_hits, axis=0) - 1) * expert_hits, axis=1)
    slot_id = jnp.where(pair_live, expert_ids * capacity + slot_rank, EXPERTS * capacity)
    source_row = jnp.zeros((EXPERTS * capacity + 1,), jnp.int32).at[slot_id].set(pair_row)[:-1]
    filled = jnp.zeros((EXPERTS * capacity + 1,), jnp.bfloat16).at[slot_id].set(1.0)[:-1]
    outgoing = (normed[source_row] * filled[:, None]).reshape(EXPERTS, capacity, width)
    sending = jnp.repeat(outgoing, split_ways, axis=0).reshape(
        blk_count, local_exp, capacity, width
    )
    arrived = lax.all_to_all(sending, "blk", split_axis=0, concat_axis=0, tiled=True)
    sources = arrived.shape[0]
    slot_count = arrived.shape[2]
    stride = sources
    while stride % 2 == 0 and stride * local_exp * slot_count > 1024:
        stride = stride // 2
    grouped = arrived.reshape(sources // stride, stride, local_exp, slot_count, width)

    def one_block(portion):
        gate_out = jnp.einsum("slnd,dlf->slnf", portion, gate_w, preferred_element_type=jnp.float32)
        up_out = jnp.einsum("slnd,dlf->slnf", portion, up_w, preferred_element_type=jnp.float32)
        hidden = (jax.nn.silu(gate_out) * up_out).astype(jnp.bfloat16)
        return jnp.einsum(
            "slnf,dlf->slnd", hidden, down_w, preferred_element_type=jnp.float32
        ).astype(jnp.bfloat16)

    returned = lax.all_to_all(
        lax.map(one_block, grouped).reshape(sources, local_exp, slot_count, width),
        "blk",
        split_axis=0,
        concat_axis=0,
        tiled=True,
    )
    summed_f = jnp.sum(
        returned.reshape(EXPERTS, split_ways, capacity, width).astype(jnp.float32), axis=1
    )
    expert_out = lax.optimization_barrier(summed_f.astype(jnp.bfloat16)).reshape(
        EXPERTS * capacity, width
    )
    gather_index = jnp.where(pair_live, expert_ids * capacity + slot_rank, 0)
    pair_weight = route_weights[0].reshape(-1) * pair_live.astype(jnp.float32)
    moe = jnp.sum(
        (expert_out[gather_index].astype(jnp.float32) * pair_weight[:, None]).reshape(
            rows_here, top_count, width
        ),
        axis=1,
    )
    out_rows = (resid_f + moe).astype(jnp.bfloat16)
    out_f = out_rows.astype(jnp.float32)
    row_squares = jnp.sum(out_f * out_f, axis=-1) * is_valid.astype(jnp.float32)
    square_local = jnp.sum(jnp.where(prompt_match, row_squares[:, None], 0.0), axis=0)
    is_last = is_valid & (position == row_len - 1)
    picker = (prompt_match & is_last[:, None]).astype(jnp.bfloat16)
    last_local = lax.dot_general(
        picker, out_rows, (((0,), (0,)), ((), ())), preferred_element_type=jnp.float32
    )
    last_rows, square_total = lax.psum((last_local, square_local), "blk")
    norms = jnp.sqrt(square_total / (lengths.astype(jnp.float32) * width) + 1e-06)
    final = (
        last_rows
        * lax.rsqrt(jnp.mean(last_rows * last_rows, axis=-1, keepdims=True) + 1e-05)
        * final_gain
    ).astype(jnp.bfloat16)
    logits = lax.dot_general(
        final, unembed, (((1,), (1,)), ((), ())), preferred_element_type=jnp.float32
    )
    vocab_base = blk_index * unembed.shape[0]
    target_hit = (
        target_ids[:, None] == vocab_base + jnp.arange(unembed.shape[0], dtype=jnp.int32)[None, :]
    )
    target_part = jnp.sum(jnp.where(target_hit, logits, 0.0), axis=1)
    top_part = jnp.max(logits, axis=1)
    target_logit, top_logit = merged((target_part, top_part), "blk", combine_stats)
    request_stats = jnp.stack([norms, top_logit, target_logit])
    return (out_rows[None], server, request_stats)


def iota(shape, dim):
    return lax.broadcasted_iota(jnp.int32, shape, dim)


def prep_kernel(info, hidden_ref, routes_ref, weights_ref, gain_ref, _, rows_ref, pieces_ref):
    rows, width = hidden_ref.shape
    length = info[3]
    x = hidden_ref[...].astype(jnp.float32)
    scale = lax.rsqrt(jnp.mean(x * x, axis=-1, keepdims=True) + 1e-05)
    rows_ref[:, :width] = (x * scale * gain_ref[...]).astype(jnp.bfloat16)
    lane = iota((rows, LANES), 1)
    row = iota((rows, LANES), 0)
    hit = jnp.zeros((rows, LANES), jnp.float32)
    weight = jnp.zeros((rows, LANES), jnp.float32)
    named_by = jnp.transpose(routes_ref[...].astype(jnp.float32)).astype(jnp.int32)
    weight_by = jnp.transpose(weights_ref[...])
    for k in range(routes_ref.shape[0]):
        named = named_by[:, k : k + 1] == lane
        hit = hit + jnp.where(named, 1.0, 0.0)
        weight = weight + jnp.where(named, weight_by[:, k : k + 1], 0.0)
    live = row < length
    hit = jnp.where(live, hit, 0.0)
    weight = jnp.where(live, weight, 0.0)
    before = jnp.where(iota((rows, rows), 1) < iota((rows, rows), 0), 1.0, 0.0)
    rank = jnp.dot(
        before.astype(jnp.bfloat16), hit.astype(jnp.bfloat16), preferred_element_type=jnp.float32
    )
    rows_ref[:, width:] = jnp.where(hit > 0.0, rank, -1.0).astype(jnp.bfloat16)
    for k in range(3):
        piece = weight.astype(jnp.bfloat16)
        pieces_ref[k * rows : (k + 1) * rows, :] = piece
        weight = weight - piece.astype(jnp.float32)


def pick(info, which, x_ref, width, place, slots):
    rows = x_ref.shape[0]
    ranks = x_ref[:, width:].astype(jnp.float32)
    lane = iota((rows, LANES), 1)
    source = (iota((rows, 1), 0) // LEN).astype(jnp.float32)
    rank = jnp.sum(jnp.where(lane == info[which], ranks, 0.0), axis=1, keepdims=True)
    slot = jnp.where(rank >= 0.0, place(source, rank), -1.0)
    slot_lane = iota((rows, slots), 1).astype(jnp.float32)
    one_hot = jnp.where(slot == slot_lane, 1.0, 0.0).astype(jnp.bfloat16)
    return lax.dot_general(
        one_hot, x_ref[:, :width], (((0,), (0,)), ((), ())), preferred_element_type=jnp.float32
    )


def activ(x, g_ref, u_ref):
    x = x.astype(jnp.bfloat16)
    gate = jnp.dot(x, g_ref[...], preferred_element_type=jnp.float32)
    up = jnp.dot(x, u_ref[...], preferred_element_type=jnp.float32)
    return (gate / (1.0 + jnp.exp(-gate)) * up).astype(jnp.bfloat16)


def own_kernel(info, x_ref, g_ref, u_ref, out_ref, late_ref, picked):
    step = pl.program_id(0)
    sources = x_ref.shape[0] // LEN
    more = CAP - FIRST
    early = sources * FIRST
    all_early = GROUPS * early

    def place(source, rank):
        return jnp.where(
            rank < FIRST, source * FIRST + rank, early + source * more + (rank - FIRST)
        )

    chosen = pick(info, 0, x_ref, g_ref.shape[0], place, early + sources * more)
    for s in range(sources):
        start = pl.multiple_of(info[4 + step * sources + s] * FIRST, FIRST)
        picked[pl.ds(start, FIRST), :] = chosen[s * FIRST : (s + 1) * FIRST]
    start = pl.multiple_of(all_early + step * sources * more, sources * more)
    picked[pl.ds(start, sources * more), :] = chosen[early:]

    @pl.when(step == GROUPS - 1)
    def _():
        hidden = activ(picked[...], g_ref, u_ref)
        out_ref[...] = hidden[:all_early]
        rest = hidden[all_early:]
        shape = (late_ref.shape[0], rest.shape[0])
        column = iota(shape, 1)
        source = jnp.zeros_like(column)
        for k, b in enumerate(RING):
            source = source + jnp.where(column // more == k, b, 0)
        one_hot = jnp.where(iota(shape, 0) == source * SECOND + column % more, 1.0, 0.0)
        late_ref[...] = jnp.dot(
            one_hot.astype(jnp.bfloat16), rest, preferred_element_type=jnp.float32
        ).astype(jnp.bfloat16)


def oth_kernel(info, x_ref, g_ref, u_ref, _, out_ref, picked):
    step = pl.program_id(0)
    sources = x_ref.shape[0] // LEN

    def place(source, rank):
        return source * SECOND + (SECOND - CAP) + rank

    chosen = pick(info, 1, x_ref, g_ref.shape[0], place, sources * SECOND)
    for s in range(sources):
        start = pl.multiple_of(info[4 + step * sources + s] * SECOND, SECOND)
        picked[pl.ds(start, SECOND), :] = chosen[s * SECOND : (s + 1) * SECOND]

    @pl.when(step == GROUPS - 1)
    def _():
        out_ref[...] = activ(picked[...], g_ref, u_ref)


def down_kernel(*refs):
    out_ref = refs[-1]
    total = 0.0
    for hidden_ref, d_ref in zip(refs[0:-1:2], refs[1:-1:2]):
        total = total + lax.dot_general(
            hidden_ref[...],
            d_ref[...],
            (((1,), (1,)), ((), ())),
            preferred_element_type=jnp.float32,
        )
    out_ref[...] = total.astype(jnp.bfloat16)


def mix_kernel(info, rank_ref, pieces_ref, first_ref, second_ref):
    rows = rank_ref.shape[0]
    late = SECOND - CAP
    own, oth = info[2], 1 - info[2]
    for mix_ref, stride, spans in (
        (first_ref, FIRST, ((own, 0, FIRST, 0),)),
        (second_ref, SECOND, ((own, 0, late, FIRST), (oth, late, CAP, 0))),
    ):
        slots = mix_ref.shape[1]
        expert = iota((LANES, slots), 0)
        lane = iota((LANES, slots), 1)
        within = jnp.zeros((1, slots), jnp.float32)
        spread = jnp.zeros((LANES, slots), jnp.float32)
        for parity, offset, count, lowest in spans:
            start = jnp.where((expert & 1) == parity, (expert >> 1) * stride + offset, slots)
            inside = (lane >= start) & (lane < start + count)
            spread = spread + jnp.where(inside, 1.0, 0.0)
            ranks = jnp.where(inside, lane - start + lowest, 0)
            within = within + jnp.sum(ranks, axis=0, keepdims=True).astype(jnp.float32)
        spread = spread.astype(jnp.bfloat16)
        rank = jnp.dot(rank_ref[...], spread, preferred_element_type=jnp.float32)
        match = rank == within
        for k in range(3):
            part = jnp.dot(
                pieces_ref[k * rows : (k + 1) * rows, :], spread, preferred_element_type=jnp.float32
            )
            mix_ref[k * rows : (k + 1) * rows, :] = jnp.where(match, part, 0.0).astype(jnp.bfloat16)


def weigh(mix_ref, back_ref):
    rows = mix_ref.shape[0] // 3
    parts = jnp.dot(mix_ref[...], back_ref[...], preferred_element_type=jnp.float32)
    return parts[2 * rows :] + parts[rows : 2 * rows] + parts[:rows]


def first_kernel(mix_ref, back_ref, moe_ref):
    moe_ref[...] = weigh(mix_ref, back_ref)


def combine_kernel(
    info, mix_ref, back_ref, moe_ref, resid_ref, _, out_ref, told_ref, lasts, squares
):
    step = pl.program_id(0)
    length = info[3]
    moe = moe_ref[...] + weigh(mix_ref, back_ref)

    @pl.when(step == 0)
    def _():
        squares[...] = jnp.zeros_like(squares)

    out = (resid_ref[...].astype(jnp.float32) + moe).astype(jnp.bfloat16)
    out_ref[...] = out
    out_f = out.astype(jnp.float32)
    row = iota(out_f.shape, 0)
    lasts[pl.ds(step, 1)] = jnp.sum(
        jnp.where(row == length - 1, out_f, 0.0), axis=0, keepdims=True
    )[None]
    squares[...] += jnp.sum(jnp.where(row < length, out_f * out_f, 0.0), axis=0, keepdims=True)

    @pl.when(step == pl.num_programs(0) - 1)
    def _():
        count = told_ref.shape[0]
        for k in range(lasts.shape[0]):
            size = lasts.shape[2]
            told_ref[:, :, k * size : (k + 1) * size] = jnp.broadcast_to(
                lasts[k : k + 1], (count, 1, size)
            )
        total = jnp.sum(squares[...], axis=1, keepdims=True)[None]
        told_ref[:, :, lasts.shape[0] * lasts.shape[2] :] = jnp.broadcast_to(
            total, (count, 1, LANES)
        )


def place_kernel(info, g_own, g_oth, u_own, u_oth, d_own, d_oth, _, out_ref):
    for k, (own, oth) in enumerate(((g_own, g_oth), (u_own, u_oth), (d_own, d_oth))):

        @pl.when(info[2] == 0)
        def _():
            out_ref[k, :, :FF] = own[...]
            out_ref[k, :, FF:] = oth[...]

        @pl.when(info[2] != 0)
        def _():
            out_ref[k, :, :FF] = oth[...]
            out_ref[k, :, FF:] = own[...]


def cast_kernel(blocks, x_ref, *refs):
    out_ref = refs[-1]
    rows = out_ref.shape[1]
    for b in range(blocks):
        out_ref[b] = x_ref[pl.ds(b, rows, stride=blocks), :].astype(jnp.bfloat16)


def tie_kernel(x_ref, _, out_ref):
    pass


def params():
    return pltpu.CompilerParams(vmem_limit_bytes=VMEM, dimension_semantics=("arbitrary",))


def whole(shape):
    return pl.BlockSpec(shape, lambda *_: tuple(0 for _ in shape))


def paired(
    hidden_in, lengths, routes, route_weights, norm_gain, master, unembed, final_gain, target_ids
):
    rows = hidden_in.shape[1]
    width = hidden_in.shape[2]
    blk_count = lax.axis_size("blk")
    blk = lax.axis_index("blk")
    rep = lax.axis_index("rep")
    first = blk_count * FIRST
    second = blk_count * SECOND
    resid = hidden_in[0]
    info = jnp.stack([2 * blk + rep, 2 * blk + 1 - rep, rep, lengths[blk]] + list(RING))
    info = info.astype(jnp.int32)

    shard_rows = master.shape[1]
    flat = master.reshape(3 * shard_rows * blk_count, FF)

    def turned(k, *after):
        return pl.pallas_call(
            functools.partial(cast_kernel, blk_count),
            grid=(FF // LANES,),
            in_specs=[pl.BlockSpec((shard_rows * blk_count, LANES), lambda i: (k, i))]
            + [pl.BlockSpec(memory_space=pl.ANY)] * len(after),
            out_specs=pl.BlockSpec((blk_count, shard_rows, LANES), lambda i: (0, 0, i)),
            out_shape=jax.ShapeDtypeStruct((blk_count, shard_rows, FF), jnp.bfloat16),
            compiler_params=params(),
            name="cast",
        )(flat, *after)

    def moved(x):
        own = lax.all_to_all(x, "blk", split_axis=0, concat_axis=0, tiled=True)
        own = own.reshape(width, FF)
        return own, lax.ppermute(own, "rep", [(0, 1), (1, 0)])

    def tied(x, after):
        return pl.pallas_call(
            tie_kernel,
            in_specs=[pl.BlockSpec(memory_space=pl.ANY)] * 2,
            out_specs=pl.BlockSpec(memory_space=pl.ANY),
            out_shape=jax.ShapeDtypeStruct(x.shape, x.dtype),
            input_output_aliases={0: 0},
            name="tie",
        )(x, after)

    g_turned = turned(0)
    g_own, g_oth = moved(g_turned)
    u_own, u_oth = moved(turned(1))
    d_own, d_oth = moved(tied(turned(2), g_oth))

    row_ext, pieces = pl.pallas_call(
        prep_kernel,
        grid_spec=pltpu.PrefetchScalarGridSpec(
            num_scalar_prefetch=1,
            grid=(1,),
            in_specs=[
                whole((rows, width)),
                whole((routes.shape[2], rows)),
                whole((routes.shape[2], rows)),
                whole((1, width)),
                pl.BlockSpec(memory_space=pl.ANY),
            ],
            out_specs=[whole((rows, width + LANES)), whole((3 * rows, LANES))],
        ),
        out_shape=[
            jax.ShapeDtypeStruct((rows, width + LANES), jnp.bfloat16),
            jax.ShapeDtypeStruct((3 * rows, LANES), jnp.bfloat16),
        ],
        compiler_params=params(),
        name="prep",
    )(info, resid, routes[0].T, route_weights[0].T, norm_gain[None], g_turned)
    tokens = lax.all_gather(row_ext, "blk", axis_index_groups=[list(RING)], axis=0, tiled=True)

    def hidden_of(kernel, sizes, scratch, g, u, *after):
        return pl.pallas_call(
            kernel,
            grid_spec=pltpu.PrefetchScalarGridSpec(
                num_scalar_prefetch=1,
                grid=(GROUPS,),
                in_specs=[pl.BlockSpec((blk_count // GROUPS * rows, width + LANES), lambda i, *_: (i, 0))]
                + [whole((width, FF))] * 2
                + [pl.BlockSpec(memory_space=pl.ANY)] * len(after),
                out_specs=[whole((size, FF)) for size in sizes],
                scratch_shapes=[pltpu.VMEM((scratch, width), jnp.float32)],
            ),
            out_shape=[jax.ShapeDtypeStruct((size, FF), jnp.bfloat16) for size in sizes],
            compiler_params=params(),
            name="gate_up",
        )(info, tokens, g, u, *after)

    step = 512

    def outputs_of(size, *operands):
        return pl.pallas_call(
            down_kernel,
            grid=(width // step,),
            in_specs=[whole((size, FF)), pl.BlockSpec((step, FF), lambda i: (i, 0))]
            * (len(operands) // 2),
            out_specs=pl.BlockSpec((size, step), lambda i: (0, i)),
            out_shape=jax.ShapeDtypeStruct((size, width), jnp.bfloat16),
            compiler_params=params(),
            name="down",
        )(*operands)

    def returned(x):
        slots = x.shape[0]
        x = x.reshape(blk_count, slots // blk_count, width)
        x = lax.all_to_all(x, "blk", split_axis=0, concat_axis=0, tiled=True)
        return x.reshape(slots, width)

    extra = blk_count * (CAP - FIRST)
    own_hidden, late_hidden = hidden_of(own_kernel, (first, second), first + extra, g_own, u_own)
    own_out = tied(outputs_of(first, own_hidden, d_own), u_oth)
    own_back = returned(own_out)
    (oth_hidden,) = hidden_of(oth_kernel, (second,), second, g_oth, u_oth, own_out)
    oth_out = outputs_of(second, late_hidden, d_own, oth_hidden, d_oth)
    oth_back = returned(oth_out)

    part = width // 4
    server = pl.pallas_call(
        place_kernel,
        grid_spec=pltpu.PrefetchScalarGridSpec(
            num_scalar_prefetch=1,
            grid=(width // part,),
            in_specs=[pl.BlockSpec((part, FF), lambda i, *_: (i, 0))] * 6
            + [pl.BlockSpec(memory_space=pl.ANY)],
            out_specs=pl.BlockSpec((3, part, 2 * FF), lambda i, *_: (0, i, 0)),
        ),
        out_shape=jax.ShapeDtypeStruct((3, width, 2 * FF), jnp.bfloat16),
        compiler_params=params(),
        name="place",
    )(info, g_own, g_oth, u_own, u_oth, d_own, d_oth, oth_out)

    first_mix, second_mix = pl.pallas_call(
        mix_kernel,
        grid_spec=pltpu.PrefetchScalarGridSpec(
            num_scalar_prefetch=1,
            grid=(1,),
            in_specs=[
                pl.BlockSpec((rows, LANES), lambda i, *_: (0, width // LANES)),
                whole((3 * rows, LANES)),
            ],
            out_specs=[whole((3 * rows, first)), whole((3 * rows, second))],
        ),
        out_shape=[
            jax.ShapeDtypeStruct((3 * rows, first), jnp.bfloat16),
            jax.ShapeDtypeStruct((3 * rows, second), jnp.bfloat16),
        ],
        compiler_params=params(),
        name="mix",
    )(info, row_ext, pieces)

    def weigh_specs(slots):
        return [whole((3 * rows, slots)), pl.BlockSpec((slots, step), lambda i, *_: (0, i))]

    column = pl.BlockSpec((rows, step), lambda i, *_: (0, i))
    moe = pl.pallas_call(
        first_kernel,
        grid=(width // step,),
        in_specs=weigh_specs(first),
        out_specs=column,
        out_shape=jax.ShapeDtypeStruct((rows, width), jnp.float32),
        compiler_params=params(),
        name="first",
    )(first_mix, own_back)
    out_rows, told = pl.pallas_call(
        combine_kernel,
        grid_spec=pltpu.PrefetchScalarGridSpec(
            num_scalar_prefetch=1,
            grid=(width // step,),
            in_specs=weigh_specs(second) + [column, column, pl.BlockSpec(memory_space=pl.ANY)],
            out_specs=[column, whole((blk_count, 1, width + LANES))],
            scratch_shapes=[
                pltpu.VMEM((width // step, 1, step), jnp.float32),
                pltpu.VMEM((1, step), jnp.float32),
            ],
        ),
        out_shape=[
            jax.ShapeDtypeStruct((rows, width), jnp.bfloat16),
            jax.ShapeDtypeStruct((blk_count, 1, width + LANES), jnp.float32),
        ],
        compiler_params=params(),
        name="combine",
    )(info, second_mix, oth_back, moe, resid, server)

    def everywhere(copies):
        return lax.all_to_all(copies, "blk", split_axis=0, concat_axis=0, tiled=True)

    gathered = everywhere(told)[:, 0]
    last_rows, square_total = gathered[:, :width], gathered[:, width]
    norms = jnp.sqrt(square_total / (lengths.astype(jnp.float32) * width) + 1e-06)
    final = (
        last_rows
        * lax.rsqrt(jnp.mean(last_rows * last_rows, axis=-1, keepdims=True) + 1e-05)
        * final_gain
    ).astype(jnp.bfloat16)
    logits = lax.dot_general(
        final, unembed, (((1,), (1,)), ((), ())), preferred_element_type=jnp.float32
    )
    vocab_base = blk * unembed.shape[0]
    target_hit = (
        target_ids[:, None] == vocab_base + jnp.arange(unembed.shape[0], dtype=jnp.int32)[None, :]
    )
    target_part = jnp.sum(jnp.where(target_hit, logits, 0.0), axis=1)
    top_part = jnp.max(logits, axis=1)
    stats = jnp.stack([top_part, target_part])
    parts = everywhere(jnp.broadcast_to(stats[None], (blk_count,) + stats.shape))
    request_stats = jnp.stack([norms, jnp.max(parts[:, 0], axis=0), jnp.sum(parts[:, 1], axis=0)])
    return (out_rows[None], server, request_stats)


def local(hidden_in, lengths, routes, route_weights, norm_gain, master, *rest):
    blk_count = lax.axis_size("blk")
    fits = (
        lax.axis_size("rep") == 2
        and master.shape[3] == FF
        and EXPERTS == 2 * blk_count
        and blk_count == len(RING)
        and hidden_in.shape[1] == LEN
        and lengths.shape[0] == blk_count
    )
    form = paired if fits else general
    return form(hidden_in, lengths, routes, route_weights, norm_gain, master, *rest)


def solution(mesh):
    return jax.shard_map(
        local,
        mesh=mesh,
        in_specs=(
            P("rep", "blk", None),
            P("rep"),
            P("rep", "blk", None),
            P("rep", "blk", None),
            P(),
            P(None, "blk", None, "rep"),
            P("blk", None),
            P(),
            P("rep"),
        ),
        out_specs=(P("rep", "blk", None), P(None, None, "blk"), P(None, "rep")),
        check_vma=False,
    )
```

```python
import functools

import jax
import jax.numpy as jnp
from jax import lax
from jax.experimental import pallas as pl
from jax.experimental.pallas import tpu as pltpu
from jax.sharding import PartitionSpec as P

FF = 512
EXPERTS = 32
LEN = 128
CAP = 36
FIRST = 32
SECOND = 40
GROUPS = 4
RING = (0, 1, 4, 5, 8, 9, 12, 13, 14, 15, 10, 11, 6, 7, 2, 3)
LANES = 128
VMEM = 56 * 1024 * 1024


def merged(x, axis, combine):
    everything = jax.tree.map(lambda part: lax.all_gather(part, axis), x)
    initial = jax.tree.map(lambda part: part[0], everything)

    def turn(k, so_far):
        return combine(so_far, jax.tree.map(lambda part: part[k], everything))

    return lax.fori_loop(1, lax.axis_size(axis), turn, initial)


def combine_stats(first, second):
    return (first[0] + second[0], jnp.maximum(first[1], second[1]))


def general(
    hidden_in, lengths, routes, route_weights, norm_gain, master, unembed, final_gain, target_ids
):
    rows_here = hidden_in.shape[1]
    width = hidden_in.shape[2]
    top_count = routes.shape[2]
    blk_count = lax.axis_size("blk")
    rep_count = lax.axis_size("rep")
    blk_index = lax.axis_index("blk")
    unit_count = master.shape[3] * rep_count
    split_ways = max(1, FF // unit_count)
    local_exp = max(1, unit_count // FF)
    group_width = min(unit_count, FF)
    capacity = CAP
    blocks = master.astype(jnp.bfloat16)
    arrived_blocks = lax.all_to_all(blocks, "blk", split_axis=2, concat_axis=1, tiled=True)
    server = lax.all_gather(arrived_blocks, "rep", axis=3, tiled=True)[:, :, 0, :]
    gate_w = server[0].reshape(width, local_exp, group_width)
    up_w = server[1].reshape(width, local_exp, group_width)
    down_w = server[2].reshape(width, local_exp, group_width)
    prompts_here = lengths.shape[0]
    slot_index = blk_index * rows_here + jnp.arange(rows_here, dtype=jnp.int32)
    prompt_of = slot_index // LEN
    position = slot_index % LEN
    prompt_match = prompt_of[:, None] == jnp.arange(prompts_here, dtype=jnp.int32)[None, :]
    row_len = jnp.sum(jnp.where(prompt_match, lengths[None, :], 0), axis=1)
    is_valid = position < row_len
    resid_f = hidden_in[0].astype(jnp.float32)
    normed = (
        resid_f * lax.rsqrt(jnp.mean(resid_f * resid_f, axis=-1, keepdims=True) + 1e-05) * norm_gain
    ).astype(jnp.bfloat16)
    expert_ids = routes[0].reshape(-1)
    pair_live = jnp.repeat(is_valid, top_count)
    pair_row = jnp.repeat(jnp.arange(rows_here, dtype=jnp.int32), top_count)
    expert_hits = (
        (expert_ids[:, None] == jnp.arange(EXPERTS, dtype=jnp.int32)[None, :]) & pair_live[:, None]
    ).astype(jnp.int32)
    slot_rank = jnp.sum((jnp.cumsum(expert_hits, axis=0) - 1) * expert_hits, axis=1)
    slot_id = jnp.where(pair_live, expert_ids * capacity + slot_rank, EXPERTS * capacity)
    source_row = jnp.zeros((EXPERTS * capacity + 1,), jnp.int32).at[slot_id].set(pair_row)[:-1]
    filled = jnp.zeros((EXPERTS * capacity + 1,), jnp.bfloat16).at[slot_id].set(1.0)[:-1]
    outgoing = (normed[source_row] * filled[:, None]).reshape(EXPERTS, capacity, width)
    sending = jnp.repeat(outgoing, split_ways, axis=0).reshape(
        blk_count, local_exp, capacity, width
    )
    arrived = lax.all_to_all(sending, "blk", split_axis=0, concat_axis=0, tiled=True)
    sources = arrived.shape[0]
    slot_count = arrived.shape[2]
    stride = sources
    while stride % 2 == 0 and stride * local_exp * slot_count > 1024:
        stride = stride // 2
    grouped = arrived.reshape(sources // stride, stride, local_exp, slot_count, width)

    def one_block(portion):
        gate_out = jnp.einsum("slnd,dlf->slnf", portion, gate_w, preferred_element_type=jnp.float32)
        up_out = jnp.einsum("slnd,dlf->slnf", portion, up_w, preferred_element_type=jnp.float32)
        hidden = (jax.nn.silu(gate_out) * up_out).astype(jnp.bfloat16)
        return jnp.einsum(
            "slnf,dlf->slnd", hidden, down_w, preferred_element_type=jnp.float32
        ).astype(jnp.bfloat16)

    returned = lax.all_to_all(
        lax.map(one_block, grouped).reshape(sources, local_exp, slot_count, width),
        "blk",
        split_axis=0,
        concat_axis=0,
        tiled=True,
    )
    summed_f = jnp.sum(
        returned.reshape(EXPERTS, split_ways, capacity, width).astype(jnp.float32), axis=1
    )
    expert_out = lax.optimization_barrier(summed_f.astype(jnp.bfloat16)).reshape(
        EXPERTS * capacity, width
    )
    gather_index = jnp.where(pair_live, expert_ids * capacity + slot_rank, 0)
    pair_weight = route_weights[0].reshape(-1) * pair_live.astype(jnp.float32)
    moe = jnp.sum(
        (expert_out[gather_index].astype(jnp.float32) * pair_weight[:, None]).reshape(
            rows_here, top_count, width
        ),
        axis=1,
    )
    out_rows = (resid_f + moe).astype(jnp.bfloat16)
    out_f = out_rows.astype(jnp.float32)
    row_squares = jnp.sum(out_f * out_f, axis=-1) * is_valid.astype(jnp.float32)
    square_local = jnp.sum(jnp.where(prompt_match, row_squares[:, None], 0.0), axis=0)
    is_last = is_valid & (position == row_len - 1)
    picker = (prompt_match & is_last[:, None]).astype(jnp.bfloat16)
    last_local = lax.dot_general(
        picker, out_rows, (((0,), (0,)), ((), ())), preferred_element_type=jnp.float32
    )
    last_rows, square_total = lax.psum((last_local, square_local), "blk")
    norms = jnp.sqrt(square_total / (lengths.astype(jnp.float32) * width) + 1e-06)
    final = (
        last_rows
        * lax.rsqrt(jnp.mean(last_rows * last_rows, axis=-1, keepdims=True) + 1e-05)
        * final_gain
    ).astype(jnp.bfloat16)
    logits = lax.dot_general(
        final, unembed, (((1,), (1,)), ((), ())), preferred_element_type=jnp.float32
    )
    vocab_base = blk_index * unembed.shape[0]
    target_hit = (
        target_ids[:, None] == vocab_base + jnp.arange(unembed.shape[0], dtype=jnp.int32)[None, :]
    )
    target_part = jnp.sum(jnp.where(target_hit, logits, 0.0), axis=1)
    top_part = jnp.max(logits, axis=1)
    target_logit, top_logit = merged((target_part, top_part), "blk", combine_stats)
    request_stats = jnp.stack([norms, top_logit, target_logit])
    return (out_rows[None], server, request_stats)


def iota(shape, dim):
    return lax.broadcasted_iota(jnp.int32, shape, dim)


def prep_kernel(info, hidden_ref, routes_ref, weights_ref, gain_ref, _, rows_ref, pieces_ref):
    rows, width = hidden_ref.shape
    length = info[3]
    x = hidden_ref[...].astype(jnp.float32)
    scale = lax.rsqrt(jnp.mean(x * x, axis=-1, keepdims=True) + 1e-05)
    rows_ref[:, :width] = (x * scale * gain_ref[...]).astype(jnp.bfloat16)
    lane = iota((rows, LANES), 1)
    row = iota((rows, LANES), 0)
    hit = jnp.zeros((rows, LANES), jnp.float32)
    weight = jnp.zeros((rows, LANES), jnp.float32)
    named_by = jnp.transpose(routes_ref[...].astype(jnp.float32)).astype(jnp.int32)
    weight_by = jnp.transpose(weights_ref[...])
    for k in range(routes_ref.shape[0]):
        named = named_by[:, k : k + 1] == lane
        hit = hit + jnp.where(named, 1.0, 0.0)
        weight = weight + jnp.where(named, weight_by[:, k : k + 1], 0.0)
    live = row < length
    hit = jnp.where(live, hit, 0.0)
    weight = jnp.where(live, weight, 0.0)
    before = jnp.where(iota((rows, rows), 1) < iota((rows, rows), 0), 1.0, 0.0)
    rank = jnp.dot(
        before.astype(jnp.bfloat16), hit.astype(jnp.bfloat16), preferred_element_type=jnp.float32
    )
    rows_ref[:, width:] = jnp.where(hit > 0.0, rank, -1.0).astype(jnp.bfloat16)
    for k in range(3):
        piece = weight.astype(jnp.bfloat16)
        pieces_ref[k * rows : (k + 1) * rows, :] = piece
        weight = weight - piece.astype(jnp.float32)


def pick(info, which, x_ref, width, place, slots):
    rows = x_ref.shape[0]
    ranks = x_ref[:, width:].astype(jnp.float32)
    lane = iota((rows, LANES), 1)
    source = (iota((rows, 1), 0) // LEN).astype(jnp.float32)
    rank = jnp.sum(jnp.where(lane == info[which], ranks, 0.0), axis=1, keepdims=True)
    slot = jnp.where(rank >= 0.0, place(source, rank), -1.0)
    slot_lane = iota((rows, slots), 1).astype(jnp.float32)
    one_hot = jnp.where(slot == slot_lane, 1.0, 0.0).astype(jnp.bfloat16)
    return lax.dot_general(
        one_hot, x_ref[:, :width], (((0,), (0,)), ((), ())), preferred_element_type=jnp.float32
    )


def activ(x, g_ref, u_ref):
    x = x.astype(jnp.bfloat16)
    gate = jnp.dot(x, g_ref[...], preferred_element_type=jnp.float32)
    up = jnp.dot(x, u_ref[...], preferred_element_type=jnp.float32)
    return (gate / (1.0 + jnp.exp(-gate)) * up).astype(jnp.bfloat16)


def own_kernel(info, x_ref, g_ref, u_ref, out_ref, late_ref, picked):
    step = pl.program_id(0)
    sources = x_ref.shape[0] // LEN
    more = CAP - FIRST
    early = sources * FIRST
    all_early = GROUPS * early

    def place(source, rank):
        return jnp.where(
            rank < FIRST, source * FIRST + rank, early + source * more + (rank - FIRST)
        )

    chosen = pick(info, 0, x_ref, g_ref.shape[0], place, early + sources * more)
    for s in range(sources):
        start = pl.multiple_of(info[4 + step * sources + s] * FIRST, FIRST)
        picked[pl.ds(start, FIRST), :] = chosen[s * FIRST : (s + 1) * FIRST]
    start = pl.multiple_of(all_early + step * sources * more, sources * more)
    picked[pl.ds(start, sources * more), :] = chosen[early:]

    @pl.when(step == GROUPS - 1)
    def _():
        hidden = activ(picked[...], g_ref, u_ref)
        out_ref[...] = hidden[:all_early]
        rest = hidden[all_early:]
        shape = (late_ref.shape[0], rest.shape[0])
        column = iota(shape, 1)
        source = jnp.zeros_like(column)
        for k, b in enumerate(RING):
            source = source + jnp.where(column // more == k, b, 0)
        one_hot = jnp.where(iota(shape, 0) == source * SECOND + column % more, 1.0, 0.0)
        late_ref[...] = jnp.dot(
            one_hot.astype(jnp.bfloat16), rest, preferred_element_type=jnp.float32
        ).astype(jnp.bfloat16)


def oth_kernel(info, x_ref, g_ref, u_ref, _, out_ref, picked):
    step = pl.program_id(0)
    sources = x_ref.shape[0] // LEN

    def place(source, rank):
        return source * SECOND + (SECOND - CAP) + rank

    chosen = pick(info, 1, x_ref, g_ref.shape[0], place, sources * SECOND)
    for s in range(sources):
        start = pl.multiple_of(info[4 + step * sources + s] * SECOND, SECOND)
        picked[pl.ds(start, SECOND), :] = chosen[s * SECOND : (s + 1) * SECOND]

    @pl.when(step == GROUPS - 1)
    def _():
        out_ref[...] = activ(picked[...], g_ref, u_ref)


def down_kernel(info, *refs):
    out_ref = refs[-1]
    total = 0.0
    for hidden_ref, d_ref in zip(refs[0:-1:2], refs[1:-1:2]):
        total = total + lax.dot_general(
            hidden_ref[...],
            d_ref[...],
            (((1,), (1,)), ((), ())),
            preferred_element_type=jnp.float32,
        )
    out_ref[...] = total.astype(jnp.bfloat16)


def mix_kernel(info, rank_ref, pieces_ref, first_ref, second_ref):
    rows = rank_ref.shape[0]
    late = SECOND - CAP
    own, oth = info[2], 1 - info[2]
    for mix_ref, stride, spans in (
        (first_ref, FIRST, ((own, 0, FIRST, 0),)),
        (second_ref, SECOND, ((own, 0, late, FIRST), (oth, late, CAP, 0))),
    ):
        slots = mix_ref.shape[1]
        expert = iota((LANES, slots), 0)
        lane = iota((LANES, slots), 1)
        within = jnp.zeros((1, slots), jnp.float32)
        spread = jnp.zeros((LANES, slots), jnp.float32)
        for parity, offset, count, lowest in spans:
            start = jnp.where((expert & 1) == parity, (expert >> 1) * stride + offset, slots)
            inside = (lane >= start) & (lane < start + count)
            spread = spread + jnp.where(inside, 1.0, 0.0)
            ranks = jnp.where(inside, lane - start + lowest, 0)
            within = within + jnp.sum(ranks, axis=0, keepdims=True).astype(jnp.float32)
        spread = spread.astype(jnp.bfloat16)
        rank = jnp.dot(rank_ref[...], spread, preferred_element_type=jnp.float32)
        match = rank == within
        for k in range(3):
            part = jnp.dot(
                pieces_ref[k * rows : (k + 1) * rows, :], spread, preferred_element_type=jnp.float32
            )
            mix_ref[k * rows : (k + 1) * rows, :] = jnp.where(match, part, 0.0).astype(jnp.bfloat16)


def weigh(mix_ref, back_ref):
    rows = mix_ref.shape[0] // 3
    parts = jnp.dot(mix_ref[...], back_ref[...], preferred_element_type=jnp.float32)
    return parts[2 * rows :] + parts[rows : 2 * rows] + parts[:rows]


def first_kernel(mix_ref, back_ref, resid_ref, base_ref):
    base_ref[...] = resid_ref[...].astype(jnp.float32) + weigh(mix_ref, back_ref)


def last_kernel(info, mix_ref, back_ref, base_ref, _, told_ref):
    rows = base_ref.shape[0]
    last = info[3] - 1
    shape = (8, mix_ref.shape[0])
    one_hot = jnp.where(iota(shape, 1) == iota(shape, 0) * rows + last, 1.0, 0.0)
    mix = jnp.dot(one_hot.astype(jnp.bfloat16), mix_ref[...], preferred_element_type=jnp.float32)
    parts = jnp.dot(mix.astype(jnp.bfloat16), back_ref[...], preferred_element_type=jnp.float32)
    moe = parts[2:3] + parts[1:2] + parts[0:1]
    out = (base_ref[pl.ds(last, 1), :] + moe).astype(jnp.bfloat16).astype(jnp.float32)
    told_ref[...] = jnp.broadcast_to(out[None], told_ref.shape)


def combine_kernel(info, mix_ref, back_ref, base_ref, _, out_ref, square_ref, squares):
    step = pl.program_id(0)

    @pl.when(step == 0)
    def _():
        squares[...] = jnp.zeros_like(squares)

    out = (base_ref[...] + weigh(mix_ref, back_ref)).astype(jnp.bfloat16)
    out_ref[...] = out
    out_f = out.astype(jnp.float32)
    row = iota(out_f.shape, 0)
    squares[...] += jnp.sum(jnp.where(row < info[3], out_f * out_f, 0.0), axis=0, keepdims=True)

    @pl.when(step == pl.num_programs(0) - 1)
    def _():
        total = jnp.sum(squares[...], axis=1, keepdims=True)
        square_ref[...] = jnp.broadcast_to(total, square_ref.shape)


def place_kernel(info, g_own, g_oth, u_own, u_oth, d_both, _, out_ref):
    for k, (own, oth) in enumerate(((g_own, g_oth), (u_own, u_oth))):

        @pl.when(info[2] == 0)
        def _():
            out_ref[k, :, :FF] = own[...]
            out_ref[k, :, FF:] = oth[...]

        @pl.when(info[2] != 0)
        def _():
            out_ref[k, :, :FF] = oth[...]
            out_ref[k, :, FF:] = own[...]

    out_ref[2, :, :FF] = d_both[0]
    out_ref[2, :, FF:] = d_both[1]


def cast_kernel(blocks, x_ref, *refs):
    out_ref = refs[-1]
    rows = out_ref.shape[1]
    for b in range(blocks):
        out_ref[b] = x_ref[pl.ds(b, rows, stride=blocks), :].astype(jnp.bfloat16)


def tie_kernel(x_ref, _, out_ref):
    pass


def params():
    return pltpu.CompilerParams(vmem_limit_bytes=VMEM, dimension_semantics=("arbitrary",))


def whole(shape):
    return pl.BlockSpec(shape, lambda *_: tuple(0 for _ in shape))


def paired(
    hidden_in, lengths, routes, route_weights, norm_gain, master, unembed, final_gain, target_ids
):
    rows = hidden_in.shape[1]
    width = hidden_in.shape[2]
    blk_count = lax.axis_size("blk")
    blk = lax.axis_index("blk")
    rep = lax.axis_index("rep")
    first = blk_count * FIRST
    second = blk_count * SECOND
    resid = hidden_in[0]
    info = jnp.stack([2 * blk + rep, 2 * blk + 1 - rep, rep, lengths[blk]] + list(RING))
    info = info.astype(jnp.int32)

    shard_rows = master.shape[1]
    flat = master.reshape(3 * shard_rows * blk_count, FF)

    def turned(k, *after):
        return pl.pallas_call(
            functools.partial(cast_kernel, blk_count),
            grid=(FF // LANES,),
            in_specs=[pl.BlockSpec((shard_rows * blk_count, LANES), lambda i: (k, i))]
            + [pl.BlockSpec(memory_space=pl.ANY)] * len(after),
            out_specs=pl.BlockSpec((blk_count, shard_rows, LANES), lambda i: (0, 0, i)),
            out_shape=jax.ShapeDtypeStruct((blk_count, shard_rows, FF), jnp.bfloat16),
            compiler_params=params(),
            name="cast",
        )(flat, *after)

    def moved(x):
        own = lax.all_to_all(x, "blk", split_axis=0, concat_axis=0, tiled=True)
        return own.reshape(width, FF)

    def swapped(x):
        return lax.ppermute(x, "rep", [(0, 1), (1, 0)])

    def tied(x, after):
        return pl.pallas_call(
            tie_kernel,
            in_specs=[pl.BlockSpec(memory_space=pl.ANY)] * 2,
            out_specs=pl.BlockSpec(memory_space=pl.ANY),
            out_shape=jax.ShapeDtypeStruct(x.shape, x.dtype),
            input_output_aliases={0: 0},
            name="tie",
        )(x, after)

    g_turned = turned(0)
    g_own = moved(g_turned)
    g_oth = swapped(g_own)
    u_own = moved(turned(1))
    u_oth = swapped(u_own)
    d_own = moved(tied(turned(2), g_oth))
    d_both = lax.all_gather(d_own, "rep", axis=0)

    row_ext, pieces = pl.pallas_call(
        prep_kernel,
        grid_spec=pltpu.PrefetchScalarGridSpec(
            num_scalar_prefetch=1,
            grid=(1,),
            in_specs=[
                whole((rows, width)),
                whole((routes.shape[2], rows)),
                whole((routes.shape[2], rows)),
                whole((1, width)),
                pl.BlockSpec(memory_space=pl.ANY),
            ],
            out_specs=[whole((rows, width + LANES)), whole((3 * rows, LANES))],
        ),
        out_shape=[
            jax.ShapeDtypeStruct((rows, width + LANES), jnp.bfloat16),
            jax.ShapeDtypeStruct((3 * rows, LANES), jnp.bfloat16),
        ],
        compiler_params=params(),
        name="prep",
    )(info, resid, routes[0].T, route_weights[0].T, norm_gain[None], g_turned)
    tokens = lax.all_gather(row_ext, "blk", axis_index_groups=[list(RING)], axis=0, tiled=True)

    def hidden_of(kernel, sizes, scratch, g, u, *after):
        return pl.pallas_call(
            kernel,
            grid_spec=pltpu.PrefetchScalarGridSpec(
                num_scalar_prefetch=1,
                grid=(GROUPS,),
                in_specs=[pl.BlockSpec((blk_count // GROUPS * rows, width + LANES), lambda i, *_: (i, 0))]
                + [whole((width, FF))] * 2
                + [pl.BlockSpec(memory_space=pl.ANY)] * len(after),
                out_specs=[whole((size, FF)) for size in sizes],
                scratch_shapes=[pltpu.VMEM((scratch, width), jnp.float32)],
            ),
            out_shape=[jax.ShapeDtypeStruct((size, FF), jnp.bfloat16) for size in sizes],
            compiler_params=params(),
            name="gate_up",
        )(info, tokens, g, u, *after)

    step = 512

    one = pl.BlockSpec((step, FF), lambda i, *_: (i, 0))
    other = pl.BlockSpec((None, step, FF), lambda i, info: (1 - info[2], i, 0))

    def outputs_of(size, halves, *operands):
        return pl.pallas_call(
            down_kernel,
            grid_spec=pltpu.PrefetchScalarGridSpec(
                num_scalar_prefetch=1,
                grid=(width // step,),
                in_specs=[spec for half in halves for spec in (whole((size, FF)), half)],
                out_specs=pl.BlockSpec((size, step), lambda i, *_: (0, i)),
            ),
            out_shape=jax.ShapeDtypeStruct((size, width), jnp.bfloat16),
            compiler_params=params(),
            name="down",
        )(info, *operands)

    def returned(x):
        slots = x.shape[0]
        x = x.reshape(blk_count, slots // blk_count, width)
        x = lax.all_to_all(x, "blk", split_axis=0, concat_axis=0, tiled=True)
        return x.reshape(slots, width)

    extra = blk_count * (CAP - FIRST)
    own_hidden, late_hidden = hidden_of(own_kernel, (first, second), first + extra, g_own, u_own)
    own_out = tied(outputs_of(first, (one,), own_hidden, d_own), u_oth)
    own_back = returned(own_out)
    (oth_hidden,) = hidden_of(oth_kernel, (second,), second, g_oth, u_oth, own_out)
    oth_out = outputs_of(second, (one, other), late_hidden, d_own, oth_hidden, d_both)
    oth_back = returned(oth_out)

    part = width // 4
    server = pl.pallas_call(
        place_kernel,
        grid_spec=pltpu.PrefetchScalarGridSpec(
            num_scalar_prefetch=1,
            grid=(width // part,),
            in_specs=[pl.BlockSpec((part, FF), lambda i, *_: (i, 0))] * 4
            + [
                pl.BlockSpec((2, part, FF), lambda i, *_: (0, i, 0)),
                pl.BlockSpec(memory_space=pl.ANY),
            ],
            out_specs=pl.BlockSpec((3, part, 2 * FF), lambda i, *_: (0, i, 0)),
        ),
        out_shape=jax.ShapeDtypeStruct((3, width, 2 * FF), jnp.bfloat16),
        compiler_params=params(),
        name="place",
    )(info, g_own, g_oth, u_own, u_oth, d_both, oth_out)

    first_mix, second_mix = pl.pallas_call(
        mix_kernel,
        grid_spec=pltpu.PrefetchScalarGridSpec(
            num_scalar_prefetch=1,
            grid=(1,),
            in_specs=[
                pl.BlockSpec((rows, LANES), lambda i, *_: (0, width // LANES)),
                whole((3 * rows, LANES)),
            ],
            out_specs=[whole((3 * rows, first)), whole((3 * rows, second))],
        ),
        out_shape=[
            jax.ShapeDtypeStruct((3 * rows, first), jnp.bfloat16),
            jax.ShapeDtypeStruct((3 * rows, second), jnp.bfloat16),
        ],
        compiler_params=params(),
        name="mix",
    )(info, row_ext, pieces)

    def weigh_specs(slots):
        return [whole((3 * rows, slots)), pl.BlockSpec((slots, step), lambda i, *_: (0, i))]

    column = pl.BlockSpec((rows, step), lambda i, *_: (0, i))
    base = pl.pallas_call(
        first_kernel,
        grid=(width // step,),
        in_specs=weigh_specs(first) + [column],
        out_specs=column,
        out_shape=jax.ShapeDtypeStruct((rows, width), jnp.float32),
        compiler_params=params(),
        name="first",
    )(first_mix, own_back, resid)
    told = pl.pallas_call(
        last_kernel,
        grid_spec=pltpu.PrefetchScalarGridSpec(
            num_scalar_prefetch=1,
            grid=(width // step,),
            in_specs=weigh_specs(second) + [column, pl.BlockSpec(memory_space=pl.ANY)],
            out_specs=pl.BlockSpec((blk_count, 1, step), lambda i, *_: (0, 0, i)),
        ),
        out_shape=jax.ShapeDtypeStruct((blk_count, 1, width), jnp.float32),
        compiler_params=params(),
        name="last",
    )(info, second_mix, oth_back, base, server)
    out_rows, square = pl.pallas_call(
        combine_kernel,
        grid_spec=pltpu.PrefetchScalarGridSpec(
            num_scalar_prefetch=1,
            grid=(width // step,),
            in_specs=weigh_specs(second) + [column, pl.BlockSpec(memory_space=pl.ANY)],
            out_specs=[column, whole((1, LANES))],
            scratch_shapes=[pltpu.VMEM((1, step), jnp.float32)],
        ),
        out_shape=[
            jax.ShapeDtypeStruct((rows, width), jnp.bfloat16),
            jax.ShapeDtypeStruct((1, LANES), jnp.float32),
        ],
        compiler_params=params(),
        name="combine",
    )(info, second_mix, oth_back, base, told)

    def everywhere(copies):
        return lax.all_to_all(copies, "blk", split_axis=0, concat_axis=0, tiled=True)

    last_rows = everywhere(told)[:, 0]
    final = (
        last_rows
        * lax.rsqrt(jnp.mean(last_rows * last_rows, axis=-1, keepdims=True) + 1e-05)
        * final_gain
    ).astype(jnp.bfloat16)
    logits = lax.dot_general(
        final, unembed, (((1,), (1,)), ((), ())), preferred_element_type=jnp.float32
    )
    vocab_base = blk * unembed.shape[0]
    target_hit = (
        target_ids[:, None] == vocab_base + jnp.arange(unembed.shape[0], dtype=jnp.int32)[None, :]
    )
    target_part = jnp.sum(jnp.where(target_hit, logits, 0.0), axis=1)
    top_part = jnp.max(logits, axis=1)
    prompt = jnp.arange(blk_count, dtype=jnp.int32)
    square_part = jnp.where(prompt == blk, square[0, :blk_count], 0.0)
    stats = jnp.stack([top_part, target_part, square_part])
    parts = everywhere(jnp.broadcast_to(stats[None], (blk_count,) + stats.shape))
    sums = jnp.sum(parts[:, 1:], axis=0)
    norms = jnp.sqrt(sums[1] / (lengths.astype(jnp.float32) * width) + 1e-06)
    request_stats = jnp.stack([norms, jnp.max(parts[:, 0], axis=0), sums[0]])
    return (out_rows[None], server, request_stats)


def local(hidden_in, lengths, routes, route_weights, norm_gain, master, *rest):
    blk_count = lax.axis_size("blk")
    fits = (
        lax.axis_size("rep") == 2
        and master.shape[3] == FF
        and EXPERTS == 2 * blk_count
        and blk_count == len(RING)
        and hidden_in.shape[1] == LEN
        and lengths.shape[0] == blk_count
    )
    form = paired if fits else general
    return form(hidden_in, lengths, routes, route_weights, norm_gain, master, *rest)


def solution(mesh):
    return jax.shard_map(
        local,
        mesh=mesh,
        in_specs=(
            P("rep", "blk", None),
            P("rep"),
            P("rep", "blk", None),
            P("rep", "blk", None),
            P(),
            P(None, "blk", None, "rep"),
            P("blk", None),
            P(),
            P("rep"),
        ),
        out_specs=(P("rep", "blk", None), P(None, None, "blk"), P(None, "rep")),
        check_vma=False,
    )
```

```python
import functools

import jax
import jax.numpy as jnp
from jax import lax
from jax.experimental import pallas as pl
from jax.experimental.pallas import tpu as pltpu
from jax.sharding import PartitionSpec as P

FF = 512
EXPERTS = 32
LEN = 128
CAP = 36
FIRST = 32
SECOND = 40
GROUPS = 4
RING = (0, 1, 4, 5, 8, 9, 12, 13, 14, 15, 10, 11, 6, 7, 2, 3)
LANES = 128
VMEM = 56 * 1024 * 1024


def merged(x, axis, combine):
    everything = jax.tree.map(lambda part: lax.all_gather(part, axis), x)
    initial = jax.tree.map(lambda part: part[0], everything)

    def turn(k, so_far):
        return combine(so_far, jax.tree.map(lambda part: part[k], everything))

    return lax.fori_loop(1, lax.axis_size(axis), turn, initial)


def combine_stats(first, second):
    return (first[0] + second[0], jnp.maximum(first[1], second[1]))


def general(
    hidden_in, lengths, routes, route_weights, norm_gain, master, unembed, final_gain, target_ids
):
    rows_here = hidden_in.shape[1]
    width = hidden_in.shape[2]
    top_count = routes.shape[2]
    blk_count = lax.axis_size("blk")
    rep_count = lax.axis_size("rep")
    blk_index = lax.axis_index("blk")
    unit_count = master.shape[3] * rep_count
    split_ways = max(1, FF // unit_count)
    local_exp = max(1, unit_count // FF)
    group_width = min(unit_count, FF)
    capacity = CAP
    blocks = master.astype(jnp.bfloat16)
    arrived_blocks = lax.all_to_all(blocks, "blk", split_axis=2, concat_axis=1, tiled=True)
    server = lax.all_gather(arrived_blocks, "rep", axis=3, tiled=True)[:, :, 0, :]
    gate_w = server[0].reshape(width, local_exp, group_width)
    up_w = server[1].reshape(width, local_exp, group_width)
    down_w = server[2].reshape(width, local_exp, group_width)
    prompts_here = lengths.shape[0]
    slot_index = blk_index * rows_here + jnp.arange(rows_here, dtype=jnp.int32)
    prompt_of = slot_index // LEN
    position = slot_index % LEN
    prompt_match = prompt_of[:, None] == jnp.arange(prompts_here, dtype=jnp.int32)[None, :]
    row_len = jnp.sum(jnp.where(prompt_match, lengths[None, :], 0), axis=1)
    is_valid = position < row_len
    resid_f = hidden_in[0].astype(jnp.float32)
    normed = (
        resid_f * lax.rsqrt(jnp.mean(resid_f * resid_f, axis=-1, keepdims=True) + 1e-05) * norm_gain
    ).astype(jnp.bfloat16)
    expert_ids = routes[0].reshape(-1)
    pair_live = jnp.repeat(is_valid, top_count)
    pair_row = jnp.repeat(jnp.arange(rows_here, dtype=jnp.int32), top_count)
    expert_hits = (
        (expert_ids[:, None] == jnp.arange(EXPERTS, dtype=jnp.int32)[None, :]) & pair_live[:, None]
    ).astype(jnp.int32)
    slot_rank = jnp.sum((jnp.cumsum(expert_hits, axis=0) - 1) * expert_hits, axis=1)
    slot_id = jnp.where(pair_live, expert_ids * capacity + slot_rank, EXPERTS * capacity)
    source_row = jnp.zeros((EXPERTS * capacity + 1,), jnp.int32).at[slot_id].set(pair_row)[:-1]
    filled = jnp.zeros((EXPERTS * capacity + 1,), jnp.bfloat16).at[slot_id].set(1.0)[:-1]
    outgoing = (normed[source_row] * filled[:, None]).reshape(EXPERTS, capacity, width)
    sending = jnp.repeat(outgoing, split_ways, axis=0).reshape(
        blk_count, local_exp, capacity, width
    )
    arrived = lax.all_to_all(sending, "blk", split_axis=0, concat_axis=0, tiled=True)
    sources = arrived.shape[0]
    slot_count = arrived.shape[2]
    stride = sources
    while stride % 2 == 0 and stride * local_exp * slot_count > 1024:
        stride = stride // 2
    grouped = arrived.reshape(sources // stride, stride, local_exp, slot_count, width)

    def one_block(portion):
        gate_out = jnp.einsum("slnd,dlf->slnf", portion, gate_w, preferred_element_type=jnp.float32)
        up_out = jnp.einsum("slnd,dlf->slnf", portion, up_w, preferred_element_type=jnp.float32)
        hidden = (jax.nn.silu(gate_out) * up_out).astype(jnp.bfloat16)
        return jnp.einsum(
            "slnf,dlf->slnd", hidden, down_w, preferred_element_type=jnp.float32
        ).astype(jnp.bfloat16)

    returned = lax.all_to_all(
        lax.map(one_block, grouped).reshape(sources, local_exp, slot_count, width),
        "blk",
        split_axis=0,
        concat_axis=0,
        tiled=True,
    )
    summed_f = jnp.sum(
        returned.reshape(EXPERTS, split_ways, capacity, width).astype(jnp.float32), axis=1
    )
    expert_out = lax.optimization_barrier(summed_f.astype(jnp.bfloat16)).reshape(
        EXPERTS * capacity, width
    )
    gather_index = jnp.where(pair_live, expert_ids * capacity + slot_rank, 0)
    pair_weight = route_weights[0].reshape(-1) * pair_live.astype(jnp.float32)
    moe = jnp.sum(
        (expert_out[gather_index].astype(jnp.float32) * pair_weight[:, None]).reshape(
            rows_here, top_count, width
        ),
        axis=1,
    )
    out_rows = (resid_f + moe).astype(jnp.bfloat16)
    out_f = out_rows.astype(jnp.float32)
    row_squares = jnp.sum(out_f * out_f, axis=-1) * is_valid.astype(jnp.float32)
    square_local = jnp.sum(jnp.where(prompt_match, row_squares[:, None], 0.0), axis=0)
    is_last = is_valid & (position == row_len - 1)
    picker = (prompt_match & is_last[:, None]).astype(jnp.bfloat16)
    last_local = lax.dot_general(
        picker, out_rows, (((0,), (0,)), ((), ())), preferred_element_type=jnp.float32
    )
    last_rows, square_total = lax.psum((last_local, square_local), "blk")
    norms = jnp.sqrt(square_total / (lengths.astype(jnp.float32) * width) + 1e-06)
    final = (
        last_rows
        * lax.rsqrt(jnp.mean(last_rows * last_rows, axis=-1, keepdims=True) + 1e-05)
        * final_gain
    ).astype(jnp.bfloat16)
    logits = lax.dot_general(
        final, unembed, (((1,), (1,)), ((), ())), preferred_element_type=jnp.float32
    )
    vocab_base = blk_index * unembed.shape[0]
    target_hit = (
        target_ids[:, None] == vocab_base + jnp.arange(unembed.shape[0], dtype=jnp.int32)[None, :]
    )
    target_part = jnp.sum(jnp.where(target_hit, logits, 0.0), axis=1)
    top_part = jnp.max(logits, axis=1)
    target_logit, top_logit = merged((target_part, top_part), "blk", combine_stats)
    request_stats = jnp.stack([norms, top_logit, target_logit])
    return (out_rows[None], server, request_stats)


def iota(shape, dim):
    return lax.broadcasted_iota(jnp.int32, shape, dim)


def prep_kernel(info, hidden_ref, routes_ref, weights_ref, gain_ref, _, rows_ref, pieces_ref):
    rows, width = hidden_ref.shape
    length = info[3]
    x = hidden_ref[...].astype(jnp.float32)
    scale = lax.rsqrt(jnp.mean(x * x, axis=-1, keepdims=True) + 1e-05)
    rows_ref[:, :width] = (x * scale * gain_ref[...]).astype(jnp.bfloat16)
    lane = iota((rows, LANES), 1)
    row = iota((rows, LANES), 0)
    hit = jnp.zeros((rows, LANES), jnp.float32)
    weight = jnp.zeros((rows, LANES), jnp.float32)
    named_by = jnp.transpose(routes_ref[...].astype(jnp.float32)).astype(jnp.int32)
    weight_by = jnp.transpose(weights_ref[...])
    for k in range(routes_ref.shape[0]):
        named = named_by[:, k : k + 1] == lane
        hit = hit + jnp.where(named, 1.0, 0.0)
        weight = weight + jnp.where(named, weight_by[:, k : k + 1], 0.0)
    live = row < length
    hit = jnp.where(live, hit, 0.0)
    weight = jnp.where(live, weight, 0.0)
    before = jnp.where(iota((rows, rows), 1) < iota((rows, rows), 0), 1.0, 0.0)
    rank = jnp.dot(
        before.astype(jnp.bfloat16), hit.astype(jnp.bfloat16), preferred_element_type=jnp.float32
    )
    rows_ref[:, width:] = jnp.where(hit > 0.0, rank, -1.0).astype(jnp.bfloat16)
    for k in range(3):
        piece = weight.astype(jnp.bfloat16)
        pieces_ref[k * rows : (k + 1) * rows, :] = piece
        weight = weight - piece.astype(jnp.float32)


def pick(info, which, x_ref, width, place, slots):
    rows = x_ref.shape[0]
    ranks = x_ref[:, width:].astype(jnp.float32)
    lane = iota((rows, LANES), 1)
    source = (iota((rows, 1), 0) // LEN).astype(jnp.float32)
    rank = jnp.sum(jnp.where(lane == info[which], ranks, 0.0), axis=1, keepdims=True)
    slot = jnp.where(rank >= 0.0, place(source, rank), -1.0)
    slot_lane = iota((rows, slots), 1).astype(jnp.float32)
    one_hot = jnp.where(slot == slot_lane, 1.0, 0.0).astype(jnp.bfloat16)
    return lax.dot_general(
        one_hot, x_ref[:, :width], (((0,), (0,)), ((), ())), preferred_element_type=jnp.float32
    )


def activ(x, g_ref, u_ref):
    x = x.astype(jnp.bfloat16)
    gate = jnp.dot(x, g_ref[...], preferred_element_type=jnp.float32)
    up = jnp.dot(x, u_ref[...], preferred_element_type=jnp.float32)
    return (gate / (1.0 + jnp.exp(-gate)) * up).astype(jnp.bfloat16)


def own_kernel(info, x_ref, g_ref, u_ref, out_ref, late_ref, picked):
    step = pl.program_id(0)
    sources = x_ref.shape[0] // LEN
    more = CAP - FIRST
    early = sources * FIRST
    all_early = GROUPS * early

    def place(source, rank):
        return jnp.where(
            rank < FIRST, source * FIRST + rank, early + source * more + (rank - FIRST)
        )

    chosen = pick(info, 0, x_ref, g_ref.shape[0], place, early + sources * more)
    for s in range(sources):
        start = pl.multiple_of(info[4 + step * sources + s] * FIRST, FIRST)
        picked[pl.ds(start, FIRST), :] = chosen[s * FIRST : (s + 1) * FIRST]
    start = pl.multiple_of(all_early + step * sources * more, sources * more)
    picked[pl.ds(start, sources * more), :] = chosen[early:]

    @pl.when(step == GROUPS - 1)
    def _():
        hidden = activ(picked[...], g_ref, u_ref)
        out_ref[...] = hidden[:all_early]
        rest = hidden[all_early:]
        shape = (late_ref.shape[0], rest.shape[0])
        column = iota(shape, 1)
        source = jnp.zeros_like(column)
        for k, b in enumerate(RING):
            source = source + jnp.where(column // more == k, b, 0)
        one_hot = jnp.where(iota(shape, 0) == source * SECOND + column % more, 1.0, 0.0)
        late_ref[...] = jnp.dot(
            one_hot.astype(jnp.bfloat16), rest, preferred_element_type=jnp.float32
        ).astype(jnp.bfloat16)


def oth_kernel(info, x_ref, g_ref, u_ref, _, out_ref, picked):
    step = pl.program_id(0)
    sources = x_ref.shape[0] // LEN

    def place(source, rank):
        return source * SECOND + (SECOND - CAP) + rank

    chosen = pick(info, 1, x_ref, g_ref.shape[0], place, sources * SECOND)
    for s in range(sources):
        start = pl.multiple_of(info[4 + step * sources + s] * SECOND, SECOND)
        picked[pl.ds(start, SECOND), :] = chosen[s * SECOND : (s + 1) * SECOND]

    @pl.when(step == GROUPS - 1)
    def _():
        out_ref[...] = activ(picked[...], g_ref, u_ref)


def down_kernel(*refs):
    out_ref = refs[-1]
    total = 0.0
    for hidden_ref, d_ref in zip(refs[0:-1:2], refs[1:-1:2]):
        total = total + lax.dot_general(
            hidden_ref[...],
            d_ref[...],
            (((1,), (1,)), ((), ())),
            preferred_element_type=jnp.float32,
        )
    out_ref[...] = total.astype(jnp.bfloat16)


def mix_kernel(info, rank_ref, pieces_ref, first_ref, second_ref):
    rows = rank_ref.shape[0]
    late = SECOND - CAP
    own, oth = info[2], 1 - info[2]
    for mix_ref, stride, spans in (
        (first_ref, FIRST, ((own, 0, FIRST, 0),)),
        (second_ref, SECOND, ((own, 0, late, FIRST), (oth, late, CAP, 0))),
    ):
        slots = mix_ref.shape[1]
        expert = iota((LANES, slots), 0)
        lane = iota((LANES, slots), 1)
        within = jnp.zeros((1, slots), jnp.float32)
        spread = jnp.zeros((LANES, slots), jnp.float32)
        for parity, offset, count, lowest in spans:
            start = jnp.where((expert & 1) == parity, (expert >> 1) * stride + offset, slots)
            inside = (lane >= start) & (lane < start + count)
            spread = spread + jnp.where(inside, 1.0, 0.0)
            ranks = jnp.where(inside, lane - start + lowest, 0)
            within = within + jnp.sum(ranks, axis=0, keepdims=True).astype(jnp.float32)
        spread = spread.astype(jnp.bfloat16)
        rank = jnp.dot(rank_ref[...], spread, preferred_element_type=jnp.float32)
        match = rank == within
        for k in range(3):
            part = jnp.dot(
                pieces_ref[k * rows : (k + 1) * rows, :], spread, preferred_element_type=jnp.float32
            )
            mix_ref[k * rows : (k + 1) * rows, :] = jnp.where(match, part, 0.0).astype(jnp.bfloat16)


def weigh(mix_ref, back_ref):
    rows = mix_ref.shape[0] // 3
    parts = jnp.dot(mix_ref[...], back_ref[...], preferred_element_type=jnp.float32)
    return parts[2 * rows :] + parts[rows : 2 * rows] + parts[:rows]


def first_kernel(mix_ref, back_ref, resid_ref, base_ref):
    base_ref[...] = resid_ref[...].astype(jnp.float32) + weigh(mix_ref, back_ref)


def last_kernel(info, mix_ref, back_ref, base_ref, _, told_ref):
    rows = base_ref.shape[0]
    last = info[3] - 1
    shape = (8, mix_ref.shape[0])
    one_hot = jnp.where(iota(shape, 1) == iota(shape, 0) * rows + last, 1.0, 0.0)
    mix = jnp.dot(one_hot.astype(jnp.bfloat16), mix_ref[...], preferred_element_type=jnp.float32)
    parts = jnp.dot(mix.astype(jnp.bfloat16), back_ref[...], preferred_element_type=jnp.float32)
    moe = parts[2:3] + parts[1:2] + parts[0:1]
    out = (base_ref[pl.ds(last, 1), :] + moe).astype(jnp.bfloat16).astype(jnp.float32)
    told_ref[...] = jnp.broadcast_to(out[None], told_ref.shape)


def combine_kernel(info, mix_ref, back_ref, base_ref, _, out_ref, square_ref, squares):
    step = pl.program_id(0)

    @pl.when(step == 0)
    def _():
        squares[...] = jnp.zeros_like(squares)

    out = (base_ref[...] + weigh(mix_ref, back_ref)).astype(jnp.bfloat16)
    out_ref[...] = out
    out_f = out.astype(jnp.float32)
    row = iota(out_f.shape, 0)
    squares[...] += jnp.sum(jnp.where(row < info[3], out_f * out_f, 0.0), axis=0, keepdims=True)

    @pl.when(step == pl.num_programs(0) - 1)
    def _():
        total = jnp.sum(squares[...], axis=1, keepdims=True)
        square_ref[...] = jnp.broadcast_to(total, square_ref.shape)


def place_kernel(info, g_own, g_oth, u_own, u_oth, d_own, d_oth, _, out_ref):
    for k, (own, oth) in enumerate(((g_own, g_oth), (u_own, u_oth), (d_own, d_oth))):

        @pl.when(info[2] == 0)
        def _():
            out_ref[k, :, :FF] = own[...]
            out_ref[k, :, FF:] = oth[...]

        @pl.when(info[2] != 0)
        def _():
            out_ref[k, :, :FF] = oth[...]
            out_ref[k, :, FF:] = own[...]


def cast_kernel(blocks, x_ref, *refs):
    out_ref = refs[-1]
    rows = out_ref.shape[1]
    for b in range(blocks):
        out_ref[b] = x_ref[pl.ds(b, rows, stride=blocks), :].astype(jnp.bfloat16)


def tie_kernel(x_ref, _, out_ref):
    pass


def params():
    return pltpu.CompilerParams(vmem_limit_bytes=VMEM, dimension_semantics=("arbitrary",))


def cost(macs, size):
    return pl.CostEstimate(flops=2 * macs, bytes_accessed=size, transcendentals=0)


def whole(shape):
    return pl.BlockSpec(shape, lambda *_: tuple(0 for _ in shape))


def paired(
    hidden_in, lengths, routes, route_weights, norm_gain, master, unembed, final_gain, target_ids
):
    rows = hidden_in.shape[1]
    width = hidden_in.shape[2]
    blk_count = lax.axis_size("blk")
    blk = lax.axis_index("blk")
    rep = lax.axis_index("rep")
    first = blk_count * FIRST
    second = blk_count * SECOND
    resid = hidden_in[0]
    info = jnp.stack([2 * blk + rep, 2 * blk + 1 - rep, rep, lengths[blk]] + list(RING))
    info = info.astype(jnp.int32)

    shard_rows = master.shape[1]
    flat = master.reshape(3 * shard_rows * blk_count, FF)

    def turned(k, *after):
        return pl.pallas_call(
            functools.partial(cast_kernel, blk_count),
            grid=(FF // LANES,),
            in_specs=[pl.BlockSpec((shard_rows * blk_count, LANES), lambda i: (k, i))]
            + [pl.BlockSpec(memory_space=pltpu.HBM)] * len(after),
            out_specs=pl.BlockSpec((blk_count, shard_rows, LANES), lambda i: (0, 0, i)),
            out_shape=jax.ShapeDtypeStruct((blk_count, shard_rows, FF), jnp.bfloat16),
            compiler_params=params(),
            cost_estimate=cost(0, 6 * shard_rows * blk_count * FF),
            name="cast",
        )(flat, *after)

    def moved(x):
        own = lax.all_to_all(x, "blk", split_axis=0, concat_axis=0, tiled=True)
        return own.reshape(width, FF)

    def swapped(x):
        return lax.ppermute(x, "rep", [(0, 1), (1, 0)])

    def tied(x, after):
        return pl.pallas_call(
            tie_kernel,
            in_specs=[pl.BlockSpec(memory_space=pltpu.HBM)] * 2,
            out_specs=pl.BlockSpec(memory_space=pltpu.HBM),
            out_shape=jax.ShapeDtypeStruct(x.shape, x.dtype),
            input_output_aliases={0: 0},
            cost_estimate=cost(0, 0),
            name="tie",
        )(x, after)

    g_turned = turned(0)
    g_own = moved(g_turned)
    g_oth = swapped(g_own)
    u_own = moved(turned(1))
    u_oth = swapped(u_own)
    d_own = moved(tied(turned(2), g_oth))

    row_ext, pieces = pl.pallas_call(
        prep_kernel,
        grid_spec=pltpu.PrefetchScalarGridSpec(
            num_scalar_prefetch=1,
            grid=(1,),
            in_specs=[
                whole((rows, width)),
                whole((routes.shape[2], rows)),
                whole((routes.shape[2], rows)),
                whole((1, width)),
                pl.BlockSpec(memory_space=pltpu.HBM),
            ],
            out_specs=[whole((rows, width + LANES)), whole((3 * rows, LANES))],
        ),
        out_shape=[
            jax.ShapeDtypeStruct((rows, width + LANES), jnp.bfloat16),
            jax.ShapeDtypeStruct((3 * rows, LANES), jnp.bfloat16),
        ],
        compiler_params=params(),
        cost_estimate=cost(rows * rows * LANES, 6 * rows * width),
        name="prep",
    )(info, resid, routes[0].T, route_weights[0].T, norm_gain[None], g_turned)
    tokens = lax.all_gather(row_ext, "blk", axis_index_groups=[list(RING)], axis=0, tiled=True)

    def hidden_of(kernel, sizes, scratch, g, u, *after):
        return pl.pallas_call(
            kernel,
            grid_spec=pltpu.PrefetchScalarGridSpec(
                num_scalar_prefetch=1,
                grid=(GROUPS,),
                in_specs=[pl.BlockSpec((blk_count // GROUPS * rows, width + LANES), lambda i, *_: (i, 0))]
                + [whole((width, FF))] * 2
                + [pl.BlockSpec(memory_space=pltpu.HBM)] * len(after),
                out_specs=[whole((size, FF)) for size in sizes],
                scratch_shapes=[pltpu.VMEM((scratch, width), jnp.float32)],
            ),
            out_shape=[jax.ShapeDtypeStruct((size, FF), jnp.bfloat16) for size in sizes],
            compiler_params=params(),
            cost_estimate=cost(2 * scratch * width * FF, 2 * (tokens.size + g.size + u.size)),
            name="gate_up",
        )(info, tokens, g, u, *after)

    step = 512

    def outputs_of(size, *operands):
        return pl.pallas_call(
            down_kernel,
            grid=(width // step,),
            in_specs=[whole((size, FF)), pl.BlockSpec((step, FF), lambda i: (i, 0))]
            * (len(operands) // 2),
            out_specs=pl.BlockSpec((size, step), lambda i: (0, i)),
            out_shape=jax.ShapeDtypeStruct((size, width), jnp.bfloat16),
            compiler_params=params(),
            cost_estimate=cost(size * FF * width * len(operands) // 2, size * 4 * width),
            name="down",
        )(*operands)

    def returned(x):
        slots = x.shape[0]
        x = x.reshape(blk_count, slots // blk_count, width)
        x = lax.all_to_all(x, "blk", split_axis=0, concat_axis=0, tiled=True)
        return x.reshape(slots, width)

    extra = blk_count * (CAP - FIRST)
    own_hidden, late_hidden = hidden_of(own_kernel, (first, second), first + extra, g_own, u_own)
    d_own = tied(d_own, own_hidden)
    d_oth = swapped(d_own)
    own_out = tied(outputs_of(first, own_hidden, d_own), u_oth)
    own_back = returned(own_out)
    (oth_hidden,) = hidden_of(oth_kernel, (second,), second, g_oth, u_oth, own_out)
    oth_out = outputs_of(second, late_hidden, d_own, oth_hidden, d_oth)
    oth_back = returned(oth_out)

    part = width // 4
    server = pl.pallas_call(
        place_kernel,
        grid_spec=pltpu.PrefetchScalarGridSpec(
            num_scalar_prefetch=1,
            grid=(width // part,),
            in_specs=[pl.BlockSpec((part, FF), lambda i, *_: (i, 0))] * 6
            + [pl.BlockSpec(memory_space=pltpu.HBM)],
            out_specs=pl.BlockSpec((3, part, 2 * FF), lambda i, *_: (0, i, 0)),
        ),
        out_shape=jax.ShapeDtypeStruct((3, width, 2 * FF), jnp.bfloat16),
        compiler_params=params(),
        cost_estimate=cost(0, 12 * width * FF * 2),
        name="place",
    )(info, g_own, g_oth, u_own, u_oth, d_own, d_oth, oth_out)

    first_mix, second_mix = pl.pallas_call(
        mix_kernel,
        grid_spec=pltpu.PrefetchScalarGridSpec(
            num_scalar_prefetch=1,
            grid=(1,),
            in_specs=[
                pl.BlockSpec((rows, LANES), lambda i, *_: (0, width // LANES)),
                whole((3 * rows, LANES)),
            ],
            out_specs=[whole((3 * rows, first)), whole((3 * rows, second))],
        ),
        out_shape=[
            jax.ShapeDtypeStruct((3 * rows, first), jnp.bfloat16),
            jax.ShapeDtypeStruct((3 * rows, second), jnp.bfloat16),
        ],
        compiler_params=params(),
        cost_estimate=cost(3 * rows * LANES * (first + second), 6 * rows * (first + second)),
        name="mix",
    )(info, row_ext, pieces)

    def weigh_specs(slots):
        return [whole((3 * rows, slots)), pl.BlockSpec((slots, step), lambda i, *_: (0, i))]

    column = pl.BlockSpec((rows, step), lambda i, *_: (0, i))
    base = pl.pallas_call(
        first_kernel,
        grid=(width // step,),
        in_specs=weigh_specs(first) + [column],
        out_specs=column,
        out_shape=jax.ShapeDtypeStruct((rows, width), jnp.float32),
        compiler_params=params(),
        cost_estimate=cost(3 * rows * first * width, 2 * first * width + 6 * rows * width),
        name="first",
    )(first_mix, own_back, resid)
    told = pl.pallas_call(
        last_kernel,
        grid_spec=pltpu.PrefetchScalarGridSpec(
            num_scalar_prefetch=1,
            grid=(width // step,),
            in_specs=weigh_specs(second) + [column, pl.BlockSpec(memory_space=pltpu.HBM)],
            out_specs=pl.BlockSpec((blk_count, 1, step), lambda i, *_: (0, 0, i)),
        ),
        out_shape=jax.ShapeDtypeStruct((blk_count, 1, width), jnp.float32),
        compiler_params=params(),
        cost_estimate=cost(8 * second * width, 2 * second * width + 4 * rows * width),
        name="last",
    )(info, second_mix, oth_back, base, server)
    out_rows, square = pl.pallas_call(
        combine_kernel,
        grid_spec=pltpu.PrefetchScalarGridSpec(
            num_scalar_prefetch=1,
            grid=(width // step,),
            in_specs=weigh_specs(second) + [column, pl.BlockSpec(memory_space=pltpu.HBM)],
            out_specs=[column, whole((1, LANES))],
            scratch_shapes=[pltpu.VMEM((1, step), jnp.float32)],
        ),
        out_shape=[
            jax.ShapeDtypeStruct((rows, width), jnp.bfloat16),
            jax.ShapeDtypeStruct((1, LANES), jnp.float32),
        ],
        compiler_params=params(),
        cost_estimate=cost(3 * rows * second * width, 2 * second * width + 6 * rows * width),
        name="combine",
    )(info, second_mix, oth_back, base, told)

    def everywhere(copies):
        return lax.all_to_all(copies, "blk", split_axis=0, concat_axis=0, tiled=True)

    last_rows = everywhere(told)[:, 0]
    final = (
        last_rows
        * lax.rsqrt(jnp.mean(last_rows * last_rows, axis=-1, keepdims=True) + 1e-05)
        * final_gain
    ).astype(jnp.bfloat16)
    logits = lax.dot_general(
        final, unembed, (((1,), (1,)), ((), ())), preferred_element_type=jnp.float32
    )
    vocab_base = blk * unembed.shape[0]
    target_hit = (
        target_ids[:, None] == vocab_base + jnp.arange(unembed.shape[0], dtype=jnp.int32)[None, :]
    )
    target_part = jnp.sum(jnp.where(target_hit, logits, 0.0), axis=1)
    top_part = jnp.max(logits, axis=1)
    prompt = jnp.arange(blk_count, dtype=jnp.int32)
    square_part = jnp.where(prompt == blk, square[0, :blk_count], 0.0)
    stats = jnp.stack([top_part, target_part, square_part])
    parts = everywhere(jnp.broadcast_to(stats[None], (blk_count,) + stats.shape))
    sums = jnp.sum(parts[:, 1:], axis=0)
    norms = jnp.sqrt(sums[1] / (lengths.astype(jnp.float32) * width) + 1e-06)
    request_stats = jnp.stack([norms, jnp.max(parts[:, 0], axis=0), sums[0]])
    return (out_rows[None], server, request_stats)


def local(hidden_in, lengths, routes, route_weights, norm_gain, master, *rest):
    blk_count = lax.axis_size("blk")
    fits = (
        lax.axis_size("rep") == 2
        and master.shape[3] == FF
        and EXPERTS == 2 * blk_count
        and blk_count == len(RING)
        and hidden_in.shape[1] == LEN
        and lengths.shape[0] == blk_count
    )
    form = paired if fits else general
    return form(hidden_in, lengths, routes, route_weights, norm_gain, master, *rest)


def solution(mesh):
    return jax.shard_map(
        local,
        mesh=mesh,
        in_specs=(
            P("rep", "blk", None),
            P("rep"),
            P("rep", "blk", None),
            P("rep", "blk", None),
            P(),
            P(None, "blk", None, "rep"),
            P("blk", None),
            P(),
            P("rep"),
        ),
        out_specs=(P("rep", "blk", None), P(None, None, "blk"), P(None, "rep")),
        check_vma=False,
    )
```

```python
import functools

import jax
import jax.numpy as jnp
from jax import lax
from jax.experimental import pallas as pl
from jax.experimental.pallas import tpu as pltpu
from jax.sharding import PartitionSpec as P

FF = 512
EXPERTS = 32
LEN = 128
CAP = 36
FIRST = 32
SECOND = 40
GROUPS = 4
RING = (0, 1, 4, 5, 8, 9, 12, 13, 14, 15, 10, 11, 6, 7, 2, 3)
LANES = 128
VMEM = 56 * 1024 * 1024


def merged(x, axis, combine):
    everything = jax.tree.map(lambda part: lax.all_gather(part, axis), x)
    initial = jax.tree.map(lambda part: part[0], everything)

    def turn(k, so_far):
        return combine(so_far, jax.tree.map(lambda part: part[k], everything))

    return lax.fori_loop(1, lax.axis_size(axis), turn, initial)


def combine_stats(first, second):
    return (first[0] + second[0], jnp.maximum(first[1], second[1]))


def general(
    hidden_in, lengths, routes, route_weights, norm_gain, master, unembed, final_gain, target_ids
):
    rows_here = hidden_in.shape[1]
    width = hidden_in.shape[2]
    top_count = routes.shape[2]
    blk_count = lax.axis_size("blk")
    rep_count = lax.axis_size("rep")
    blk_index = lax.axis_index("blk")
    unit_count = master.shape[3] * rep_count
    split_ways = max(1, FF // unit_count)
    local_exp = max(1, unit_count // FF)
    group_width = min(unit_count, FF)
    capacity = CAP
    blocks = master.astype(jnp.bfloat16)
    arrived_blocks = lax.all_to_all(blocks, "blk", split_axis=2, concat_axis=1, tiled=True)
    server = lax.all_gather(arrived_blocks, "rep", axis=3, tiled=True)[:, :, 0, :]
    gate_w = server[0].reshape(width, local_exp, group_width)
    up_w = server[1].reshape(width, local_exp, group_width)
    down_w = server[2].reshape(width, local_exp, group_width)
    prompts_here = lengths.shape[0]
    slot_index = blk_index * rows_here + jnp.arange(rows_here, dtype=jnp.int32)
    prompt_of = slot_index // LEN
    position = slot_index % LEN
    prompt_match = prompt_of[:, None] == jnp.arange(prompts_here, dtype=jnp.int32)[None, :]
    row_len = jnp.sum(jnp.where(prompt_match, lengths[None, :], 0), axis=1)
    is_valid = position < row_len
    resid_f = hidden_in[0].astype(jnp.float32)
    normed = (
        resid_f * lax.rsqrt(jnp.mean(resid_f * resid_f, axis=-1, keepdims=True) + 1e-05) * norm_gain
    ).astype(jnp.bfloat16)
    expert_ids = routes[0].reshape(-1)
    pair_live = jnp.repeat(is_valid, top_count)
    pair_row = jnp.repeat(jnp.arange(rows_here, dtype=jnp.int32), top_count)
    expert_hits = (
        (expert_ids[:, None] == jnp.arange(EXPERTS, dtype=jnp.int32)[None, :]) & pair_live[:, None]
    ).astype(jnp.int32)
    slot_rank = jnp.sum((jnp.cumsum(expert_hits, axis=0) - 1) * expert_hits, axis=1)
    slot_id = jnp.where(pair_live, expert_ids * capacity + slot_rank, EXPERTS * capacity)
    source_row = jnp.zeros((EXPERTS * capacity + 1,), jnp.int32).at[slot_id].set(pair_row)[:-1]
    filled = jnp.zeros((EXPERTS * capacity + 1,), jnp.bfloat16).at[slot_id].set(1.0)[:-1]
    outgoing = (normed[source_row] * filled[:, None]).reshape(EXPERTS, capacity, width)
    sending = jnp.repeat(outgoing, split_ways, axis=0).reshape(
        blk_count, local_exp, capacity, width
    )
    arrived = lax.all_to_all(sending, "blk", split_axis=0, concat_axis=0, tiled=True)
    sources = arrived.shape[0]
    slot_count = arrived.shape[2]
    stride = sources
    while stride % 2 == 0 and stride * local_exp * slot_count > 1024:
        stride = stride // 2
    grouped = arrived.reshape(sources // stride, stride, local_exp, slot_count, width)

    def one_block(portion):
        gate_out = jnp.einsum("slnd,dlf->slnf", portion, gate_w, preferred_element_type=jnp.float32)
        up_out = jnp.einsum("slnd,dlf->slnf", portion, up_w, preferred_element_type=jnp.float32)
        hidden = (jax.nn.silu(gate_out) * up_out).astype(jnp.bfloat16)
        return jnp.einsum(
            "slnf,dlf->slnd", hidden, down_w, preferred_element_type=jnp.float32
        ).astype(jnp.bfloat16)

    returned = lax.all_to_all(
        lax.map(one_block, grouped).reshape(sources, local_exp, slot_count, width),
        "blk",
        split_axis=0,
        concat_axis=0,
        tiled=True,
    )
    summed_f = jnp.sum(
        returned.reshape(EXPERTS, split_ways, capacity, width).astype(jnp.float32), axis=1
    )
    expert_out = lax.optimization_barrier(summed_f.astype(jnp.bfloat16)).reshape(
        EXPERTS * capacity, width
    )
    gather_index = jnp.where(pair_live, expert_ids * capacity + slot_rank, 0)
    pair_weight = route_weights[0].reshape(-1) * pair_live.astype(jnp.float32)
    moe = jnp.sum(
        (expert_out[gather_index].astype(jnp.float32) * pair_weight[:, None]).reshape(
            rows_here, top_count, width
        ),
        axis=1,
    )
    out_rows = (resid_f + moe).astype(jnp.bfloat16)
    out_f = out_rows.astype(jnp.float32)
    row_squares = jnp.sum(out_f * out_f, axis=-1) * is_valid.astype(jnp.float32)
    square_local = jnp.sum(jnp.where(prompt_match, row_squares[:, None], 0.0), axis=0)
    is_last = is_valid & (position == row_len - 1)
    picker = (prompt_match & is_last[:, None]).astype(jnp.bfloat16)
    last_local = lax.dot_general(
        picker, out_rows, (((0,), (0,)), ((), ())), preferred_element_type=jnp.float32
    )
    last_rows, square_total = lax.psum((last_local, square_local), "blk")
    norms = jnp.sqrt(square_total / (lengths.astype(jnp.float32) * width) + 1e-06)
    final = (
        last_rows
        * lax.rsqrt(jnp.mean(last_rows * last_rows, axis=-1, keepdims=True) + 1e-05)
        * final_gain
    ).astype(jnp.bfloat16)
    logits = lax.dot_general(
        final, unembed, (((1,), (1,)), ((), ())), preferred_element_type=jnp.float32
    )
    vocab_base = blk_index * unembed.shape[0]
    target_hit = (
        target_ids[:, None] == vocab_base + jnp.arange(unembed.shape[0], dtype=jnp.int32)[None, :]
    )
    target_part = jnp.sum(jnp.where(target_hit, logits, 0.0), axis=1)
    top_part = jnp.max(logits, axis=1)
    target_logit, top_logit = merged((target_part, top_part), "blk", combine_stats)
    request_stats = jnp.stack([norms, top_logit, target_logit])
    return (out_rows[None], server, request_stats)


def iota(shape, dim):
    return lax.broadcasted_iota(jnp.int32, shape, dim)


def prep_kernel(length_ref, hidden_ref, routes_ref, weights_ref, gain_ref, rows_ref, pieces_ref):
    rows, width = hidden_ref.shape
    length = length_ref[0]
    x = hidden_ref[...].astype(jnp.float32)
    scale = lax.rsqrt(jnp.mean(x * x, axis=-1, keepdims=True) + 1e-05)
    rows_ref[:, :width] = (x * scale * gain_ref[...][None]).astype(jnp.bfloat16)
    lane = iota((rows, LANES), 1)
    row = iota((rows, LANES), 0)
    hit = jnp.zeros((rows, LANES), jnp.float32)
    weight = jnp.zeros((rows, LANES), jnp.float32)
    named_by = jnp.transpose(routes_ref[...].astype(jnp.float32)).astype(jnp.int32)
    weight_by = jnp.transpose(weights_ref[...])
    for k in range(routes_ref.shape[0]):
        named = named_by[:, k : k + 1] == lane
        hit = hit + jnp.where(named, 1.0, 0.0)
        weight = weight + jnp.where(named, weight_by[:, k : k + 1], 0.0)
    live = row < length
    hit = jnp.where(live, hit, 0.0)
    weight = jnp.where(live, weight, 0.0)
    before = jnp.where(iota((rows, rows), 1) < iota((rows, rows), 0), 1.0, 0.0)
    rank = jnp.dot(
        before.astype(jnp.bfloat16), hit.astype(jnp.bfloat16), preferred_element_type=jnp.float32
    )
    rows_ref[:, width:] = jnp.where(hit > 0.0, rank, -1.0).astype(jnp.bfloat16)
    for k in range(3):
        piece = weight.astype(jnp.bfloat16)
        pieces_ref[k * rows : (k + 1) * rows, :] = piece
        weight = weight - piece.astype(jnp.float32)


def pick(info, which, x_ref, width, place, slots):
    rows = x_ref.shape[0]
    ranks = x_ref[:, width:].astype(jnp.float32)
    lane = iota((rows, LANES), 1)
    source = (iota((rows, 1), 0) // LEN).astype(jnp.float32)
    rank = jnp.sum(jnp.where(lane == info[which], ranks, 0.0), axis=1, keepdims=True)
    slot = jnp.where(rank >= 0.0, place(source, rank), -1.0)
    slot_lane = iota((rows, slots), 1).astype(jnp.float32)
    one_hot = jnp.where(slot == slot_lane, 1.0, 0.0).astype(jnp.bfloat16)
    return lax.dot_general(
        one_hot, x_ref[:, :width], (((0,), (0,)), ((), ())), preferred_element_type=jnp.float32
    )


def activ(x, g_ref, u_ref):
    x = x.astype(jnp.bfloat16)
    gate = jnp.dot(x, g_ref[...], preferred_element_type=jnp.float32)
    up = jnp.dot(x, u_ref[...], preferred_element_type=jnp.float32)
    return (gate / (1.0 + jnp.exp(-gate)) * up).astype(jnp.bfloat16)


def own_kernel(info, x_ref, g_ref, u_ref, out_ref, late_ref, picked):
    step = pl.program_id(0)
    sources = x_ref.shape[0] // LEN
    more = CAP - FIRST
    early = sources * FIRST
    all_early = GROUPS * early

    def place(source, rank):
        return jnp.where(
            rank < FIRST, source * FIRST + rank, early + source * more + (rank - FIRST)
        )

    chosen = pick(info, 0, x_ref, g_ref.shape[0], place, early + sources * more)
    for s in range(sources):
        start = pl.multiple_of(info[4 + step * sources + s] * FIRST, FIRST)
        picked[pl.ds(start, FIRST), :] = chosen[s * FIRST : (s + 1) * FIRST]
    start = pl.multiple_of(all_early + step * sources * more, sources * more)
    picked[pl.ds(start, sources * more), :] = chosen[early:]

    @pl.when(step == GROUPS - 1)
    def _():
        hidden = activ(picked[...], g_ref, u_ref)
        out_ref[...] = hidden[:all_early]
        rest = hidden[all_early:]
        shape = (late_ref.shape[0], rest.shape[0])
        column = iota(shape, 1)
        source = jnp.zeros_like(column)
        for k, b in enumerate(RING):
            source = source + jnp.where(column // more == k, b, 0)
        one_hot = jnp.where(iota(shape, 0) == source * SECOND + column % more, 1.0, 0.0)
        late_ref[...] = jnp.dot(
            one_hot.astype(jnp.bfloat16), rest, preferred_element_type=jnp.float32
        ).astype(jnp.bfloat16)


def oth_kernel(info, x_ref, g_ref, u_ref, _, out_ref, picked):
    step = pl.program_id(0)
    sources = x_ref.shape[0] // LEN

    def place(source, rank):
        return source * SECOND + (SECOND - CAP) + rank

    chosen = pick(info, 1, x_ref, g_ref.shape[0], place, sources * SECOND)
    for s in range(sources):
        start = pl.multiple_of(info[4 + step * sources + s] * SECOND, SECOND)
        picked[pl.ds(start, SECOND), :] = chosen[s * SECOND : (s + 1) * SECOND]

    @pl.when(step == GROUPS - 1)
    def _():
        out_ref[...] = activ(picked[...], g_ref, u_ref)


def matmul_nt(hidden_ref, d_ref):
    return lax.dot_general(
        hidden_ref[...], d_ref[...], (((1,), (1,)), ((), ())), preferred_element_type=jnp.float32
    )


def own_down_kernel(hidden_ref, d_ref, out_ref):
    out_ref[...] = matmul_nt(hidden_ref, d_ref).astype(jnp.bfloat16)


def oth_down_kernel(late_ref, d_ref, hidden_ref, d_a, d_b, out_ref):
    late = matmul_nt(late_ref, d_ref)
    in_a = pl.program_id(0) < pl.num_programs(0) // 2

    @pl.when(in_a)
    def _():
        out_ref[...] = (late + matmul_nt(hidden_ref, d_a)).astype(jnp.bfloat16)

    @pl.when(jnp.logical_not(in_a))
    def _():
        out_ref[...] = (late + matmul_nt(hidden_ref, d_b)).astype(jnp.bfloat16)


def mix_kernel(info, rank_ref, pieces_ref, first_ref, second_ref, last_ref):
    rows = rank_ref.shape[0]
    late = SECOND - CAP
    own, oth = info[2], 1 - info[2]
    for mix_ref, stride, spans in (
        (first_ref, FIRST, ((own, 0, FIRST, 0),)),
        (second_ref, SECOND, ((own, 0, late, FIRST), (oth, late, CAP, 0))),
    ):
        slots = mix_ref.shape[1]
        expert = iota((LANES, slots), 0)
        lane = iota((LANES, slots), 1)
        within = jnp.zeros((1, slots), jnp.float32)
        spread = jnp.zeros((LANES, slots), jnp.float32)
        for parity, offset, count, lowest in spans:
            start = jnp.where((expert & 1) == parity, (expert >> 1) * stride + offset, slots)
            inside = (lane >= start) & (lane < start + count)
            spread = spread + jnp.where(inside, 1.0, 0.0)
            ranks = jnp.where(inside, lane - start + lowest, 0)
            within = within + jnp.sum(ranks, axis=0, keepdims=True).astype(jnp.float32)
        spread = spread.astype(jnp.bfloat16)
        rank = jnp.dot(rank_ref[...], spread, preferred_element_type=jnp.float32)
        match = rank == within
        for k in range(3):
            part = jnp.dot(
                pieces_ref[k * rows : (k + 1) * rows, :], spread, preferred_element_type=jnp.float32
            )
            mix_ref[k * rows : (k + 1) * rows, :] = jnp.where(match, part, 0.0).astype(jnp.bfloat16)
    shape = (last_ref.shape[0], 3 * rows)
    one_hot = jnp.where(iota(shape, 1) == iota(shape, 0) * rows + info[3] - 1, 1.0, 0.0)
    last_ref[...] = jnp.dot(
        one_hot.astype(jnp.bfloat16), second_ref[...], preferred_element_type=jnp.float32
    ).astype(jnp.bfloat16)


def weigh(mix_ref, back_ref):
    rows = mix_ref.shape[0] // 3
    parts = jnp.dot(mix_ref[...], back_ref[...], preferred_element_type=jnp.float32)
    return parts[2 * rows :] + parts[rows : 2 * rows] + parts[:rows]


def first_kernel(info, mix_ref, back_ref, resid_ref, base_ref, last_ref):
    base = resid_ref[...].astype(jnp.float32) + weigh(mix_ref, back_ref)
    base_ref[...] = base
    is_last = iota(base.shape, 0) == info[3] - 1
    last_ref[...] = jnp.sum(jnp.where(is_last, base, 0.0), axis=0, keepdims=True)


def last_kernel(mix_ref, back_ref, base_ref, _, told_ref):
    parts = jnp.dot(mix_ref[...], back_ref[...], preferred_element_type=jnp.float32)
    moe = parts[2:3] + parts[1:2] + parts[0:1]
    out = (base_ref[...] + moe).astype(jnp.bfloat16).astype(jnp.float32)
    told_ref[...] = jnp.broadcast_to(out[None], told_ref.shape)


def combine_kernel(info, mix_ref, back_ref, base_ref, _, out_ref, square_ref, squares):
    step = pl.program_id(0)

    @pl.when(step == 0)
    def _():
        squares[...] = jnp.zeros_like(squares)

    out = (base_ref[...] + weigh(mix_ref, back_ref)).astype(jnp.bfloat16)
    out_ref[...] = out
    out_f = out.astype(jnp.float32)
    row = iota(out_f.shape, 0)
    squares[...] += jnp.sum(jnp.where(row < info[3], out_f * out_f, 0.0), axis=0, keepdims=True)

    @pl.when(step == pl.num_programs(0) - 1)
    def _():
        total = jnp.sum(squares[...], axis=1, keepdims=True)
        square_ref[...] = jnp.broadcast_to(total, square_ref.shape)


def place_kernel(info, g_own, g_oth, u_own, u_oth, d_own, d_a, d_b, _, out_ref):
    second_half = pl.program_id(0) >= pl.num_programs(0) // 2
    d_oth = jnp.where(second_half, d_b[...], d_a[...])
    for k, (own, oth) in enumerate(
        ((g_own[...], g_oth[...]), (u_own[...], u_oth[...]), (d_own[...], d_oth))
    ):
        left = info[2] == 0
        out_ref[k, :, :FF] = jnp.where(left, own, oth)
        out_ref[k, :, FF:] = jnp.where(left, oth, own)


def cast_kernel(blocks, x_ref, *refs):
    out_ref = refs[-1]
    rows = out_ref.shape[1]
    shape = (blocks * rows, blocks * rows)
    target = iota(shape, 0)
    one_hot = jnp.where(iota(shape, 1) == target % rows * blocks + target // rows, 1.0, 0.0)
    turned = jnp.dot(
        one_hot.astype(jnp.bfloat16),
        x_ref[...].astype(jnp.bfloat16),
        preferred_element_type=jnp.float32,
    ).astype(jnp.bfloat16)
    for b in range(blocks):
        out_ref[b] = turned[b * rows : (b + 1) * rows]


def tie_kernel(*_):
    pass


def params():
    return pltpu.CompilerParams(vmem_limit_bytes=VMEM, dimension_semantics=("arbitrary",))


def whole(shape):
    return pl.BlockSpec(shape, lambda *_: tuple(0 for _ in shape))


def paired(
    hidden_in, lengths, routes, route_weights, norm_gain, master, unembed, final_gain, target_ids
):
    rows = hidden_in.shape[1]
    width = hidden_in.shape[2]
    blk_count = lax.axis_size("blk")
    blk = lax.axis_index("blk")
    rep = lax.axis_index("rep")
    first = blk_count * FIRST
    second = blk_count * SECOND
    resid = hidden_in[0]
    length = lax.dynamic_slice(lengths, (blk,), (1,))
    info = jnp.stack([2 * blk + rep, 2 * blk + 1 - rep, rep, length[0]] + list(RING))
    info = info.astype(jnp.int32)

    shard_rows = master.shape[1]
    flat = master.reshape(3 * shard_rows * blk_count, FF)

    def turned(k, *after):
        return pl.pallas_call(
            functools.partial(cast_kernel, blk_count),
            grid=(shard_rows // 16,),
            in_specs=[pl.BlockSpec((16 * blk_count, FF), lambda i: (k * (shard_rows // 16) + i, 0))]
            + [pl.BlockSpec(memory_space=pl.ANY)] * len(after),
            out_specs=pl.BlockSpec((blk_count, 16, FF), lambda i: (0, i, 0)),
            out_shape=jax.ShapeDtypeStruct((blk_count, shard_rows, FF), jnp.bfloat16),
            compiler_params=params(),
            name="cast",
        )(flat, *after)

    def moved(x):
        own = lax.all_to_all(x, "blk", split_axis=0, concat_axis=0, tiled=True)
        return own.reshape(width, FF)

    def swapped(x):
        return lax.ppermute(x, "rep", [(0, 1), (1, 0)])

    def tied(x, *after):
        return pl.pallas_call(
            tie_kernel,
            in_specs=[pl.BlockSpec(memory_space=pl.ANY)] * (1 + len(after)),
            out_specs=pl.BlockSpec(memory_space=pl.ANY),
            out_shape=jax.ShapeDtypeStruct(x.shape, x.dtype),
            input_output_aliases={0: 0},
            name="tie",
        )(x, *after)

    row_ext, pieces = pl.pallas_call(
        prep_kernel,
        grid_spec=pltpu.PrefetchScalarGridSpec(
            num_scalar_prefetch=1,
            grid=(1,),
            in_specs=[
                whole((rows, width)),
                whole((routes.shape[2], rows)),
                whole((routes.shape[2], rows)),
                whole((width,)),
            ],
            out_specs=[whole((rows, width + LANES)), whole((3 * rows, LANES))],
        ),
        out_shape=[
            jax.ShapeDtypeStruct((rows, width + LANES), jnp.bfloat16),
            jax.ShapeDtypeStruct((3 * rows, LANES), jnp.bfloat16),
        ],
        compiler_params=params(),
        name="prep",
    )(length, resid, routes[0].T, route_weights[0].T, norm_gain)
    g_own = moved(turned(0, row_ext))
    g_oth = swapped(g_own)
    u_own = moved(turned(1))
    u_oth = swapped(u_own)
    d_own = moved(tied(turned(2), g_oth))

    tokens = lax.all_gather(row_ext, "blk", axis_index_groups=[list(RING)], axis=0, tiled=True)

    def hidden_of(kernel, sizes, scratch, g, u, *after):
        return pl.pallas_call(
            kernel,
            grid_spec=pltpu.PrefetchScalarGridSpec(
                num_scalar_prefetch=1,
                grid=(GROUPS,),
                in_specs=[pl.BlockSpec((blk_count // GROUPS * rows, width + LANES), lambda i, *_: (i, 0))]
                + [whole((width, FF))] * 2
                + [pl.BlockSpec(memory_space=pl.ANY)] * len(after),
                out_specs=[whole((size, FF)) for size in sizes],
                scratch_shapes=[pltpu.VMEM((scratch, width), jnp.float32)],
            ),
            out_shape=[jax.ShapeDtypeStruct((size, FF), jnp.bfloat16) for size in sizes],
            compiler_params=params(),
            name="gate_up",
        )(info, tokens, g, u, *after)

    step = 512

    quarter = width // 4
    in_a = pl.BlockSpec((quarter, FF), lambda i, *_: (jnp.minimum(i, 1), 0))
    in_b = pl.BlockSpec((quarter, FF), lambda i, *_: (jnp.maximum(i, 2) - 2, 0))

    def returned(x):
        slots = x.shape[0]
        x = x.reshape(blk_count, slots // blk_count, width)
        x = lax.all_to_all(x, "blk", split_axis=0, concat_axis=0, tiled=True)
        return x.reshape(slots, width)

    extra = blk_count * (CAP - FIRST)
    own_hidden, late_hidden = hidden_of(own_kernel, (first, second), first + extra, g_own, u_own)
    d_own = tied(d_own, own_hidden)
    half = width // 2
    d_oth_a = swapped(d_own[:half])
    own_out = pl.pallas_call(
        own_down_kernel,
        grid=(width // step,),
        in_specs=[whole((first, FF)), pl.BlockSpec((step, FF), lambda i: (i, 0))],
        out_specs=pl.BlockSpec((first, step), lambda i: (0, i)),
        out_shape=jax.ShapeDtypeStruct((first, width), jnp.bfloat16),
        compiler_params=params(),
        name="own_down",
    )(own_hidden, d_own)
    own_out = tied(own_out, u_oth)
    own_back = returned(own_out)
    (oth_hidden,) = hidden_of(oth_kernel, (second,), second, g_oth, u_oth, own_out)
    d_oth_b = swapped(tied(d_own[half:], d_oth_a, oth_hidden))
    oth_out = pl.pallas_call(
        oth_down_kernel,
        grid=(4,),
        in_specs=[
            whole((second, FF)),
            pl.BlockSpec((quarter, FF), lambda i: (i, 0)),
            whole((second, FF)),
            in_a,
            in_b,
        ],
        out_specs=pl.BlockSpec((second, quarter), lambda i: (0, i)),
        out_shape=jax.ShapeDtypeStruct((second, width), jnp.bfloat16),
        compiler_params=params(),
        name="oth_down",
    )(late_hidden, d_own, oth_hidden, d_oth_a, d_oth_b)
    oth_back = returned(oth_out)

    server = pl.pallas_call(
        place_kernel,
        grid_spec=pltpu.PrefetchScalarGridSpec(
            num_scalar_prefetch=1,
            grid=(4,),
            in_specs=[pl.BlockSpec((quarter, FF), lambda i, *_: (i, 0))] * 5
            + [in_a, in_b, pl.BlockSpec(memory_space=pl.ANY)],
            out_specs=pl.BlockSpec((3, quarter, 2 * FF), lambda i, *_: (0, i, 0)),
        ),
        out_shape=jax.ShapeDtypeStruct((3, width, 2 * FF), jnp.bfloat16),
        compiler_params=params(),
        name="place",
    )(info, g_own, g_oth, u_own, u_oth, d_own, d_oth_a, d_oth_b, oth_out)

    first_mix, second_mix, last_mix = pl.pallas_call(
        mix_kernel,
        grid_spec=pltpu.PrefetchScalarGridSpec(
            num_scalar_prefetch=1,
            grid=(1,),
            in_specs=[
                pl.BlockSpec((rows, LANES), lambda i, *_: (0, width // LANES)),
                whole((3 * rows, LANES)),
            ],
            out_specs=[whole((3 * rows, first)), whole((3 * rows, second)), whole((16, second))],
        ),
        out_shape=[
            jax.ShapeDtypeStruct((3 * rows, first), jnp.bfloat16),
            jax.ShapeDtypeStruct((3 * rows, second), jnp.bfloat16),
            jax.ShapeDtypeStruct((16, second), jnp.bfloat16),
        ],
        compiler_params=params(),
        name="mix",
    )(info, row_ext, pieces)

    def weigh_specs(slots):
        return [whole((3 * rows, slots)), pl.BlockSpec((slots, step), lambda i, *_: (0, i))]

    column = pl.BlockSpec((rows, step), lambda i, *_: (0, i))
    lane_row = pl.BlockSpec((1, step), lambda i, *_: (0, i))
    base, last_base = pl.pallas_call(
        first_kernel,
        grid_spec=pltpu.PrefetchScalarGridSpec(
            num_scalar_prefetch=1,
            grid=(width // step,),
            in_specs=weigh_specs(first) + [column],
            out_specs=[column, lane_row],
        ),
        out_shape=[
            jax.ShapeDtypeStruct((rows, width), jnp.float32),
            jax.ShapeDtypeStruct((1, width), jnp.float32),
        ],
        compiler_params=params(),
        name="first",
    )(info, first_mix, own_back, resid)
    told = pl.pallas_call(
        last_kernel,
        grid=(width // step,),
        in_specs=[
            whole((16, second)),
            pl.BlockSpec((second, step), lambda i: (0, i)),
            lane_row,
            pl.BlockSpec(memory_space=pl.ANY),
        ],
        out_specs=pl.BlockSpec((blk_count, 1, step), lambda i: (0, 0, i)),
        out_shape=jax.ShapeDtypeStruct((blk_count, 1, width), jnp.float32),
        compiler_params=params(),
        name="last",
    )(last_mix, oth_back, last_base, server)
    out_rows, square = pl.pallas_call(
        combine_kernel,
        grid_spec=pltpu.PrefetchScalarGridSpec(
            num_scalar_prefetch=1,
            grid=(width // step,),
            in_specs=weigh_specs(second) + [column, pl.BlockSpec(memory_space=pl.ANY)],
            out_specs=[column, whole((1, LANES))],
            scratch_shapes=[pltpu.VMEM((1, step), jnp.float32)],
        ),
        out_shape=[
            jax.ShapeDtypeStruct((rows, width), jnp.bfloat16),
            jax.ShapeDtypeStruct((1, LANES), jnp.float32),
        ],
        compiler_params=params(),
        name="combine",
    )(info, second_mix, oth_back, base, told)

    def everywhere(copies):
        return lax.all_to_all(copies, "blk", split_axis=0, concat_axis=0, tiled=True)

    last_rows = everywhere(told)[:, 0]
    final = (
        last_rows
        * lax.rsqrt(jnp.mean(last_rows * last_rows, axis=-1, keepdims=True) + 1e-05)
        * final_gain
    ).astype(jnp.bfloat16)
    logits = lax.dot_general(
        final, unembed, (((1,), (1,)), ((), ())), preferred_element_type=jnp.float32
    )
    vocab_base = blk * unembed.shape[0]
    target_hit = (
        target_ids[:, None] == vocab_base + jnp.arange(unembed.shape[0], dtype=jnp.int32)[None, :]
    )
    target_part = jnp.sum(jnp.where(target_hit, logits, 0.0), axis=1)
    top_part = jnp.max(logits, axis=1)
    prompt = jnp.arange(blk_count, dtype=jnp.int32)
    square_part = jnp.where(prompt == blk, square[0, :blk_count], 0.0)
    stats = jnp.stack([top_part, target_part, square_part])
    parts = everywhere(jnp.broadcast_to(stats[None], (blk_count,) + stats.shape))
    sums = jnp.sum(parts[:, 1:], axis=0)
    norms = jnp.sqrt(sums[1] / (lengths.astype(jnp.float32) * width) + 1e-06)
    request_stats = jnp.stack([norms, jnp.max(parts[:, 0], axis=0), sums[0]])
    return (out_rows[None], server, request_stats)


def local(hidden_in, lengths, routes, route_weights, norm_gain, master, *rest):
    blk_count = lax.axis_size("blk")
    fits = (
        lax.axis_size("rep") == 2
        and master.shape[3] == FF
        and EXPERTS == 2 * blk_count
        and blk_count == len(RING)
        and hidden_in.shape[1] == LEN
        and lengths.shape[0] == blk_count
    )
    form = paired if fits else general
    return form(hidden_in, lengths, routes, route_weights, norm_gain, master, *rest)


def solution(mesh):
    return jax.shard_map(
        local,
        mesh=mesh,
        in_specs=(
            P("rep", "blk", None),
            P("rep"),
            P("rep", "blk", None),
            P("rep", "blk", None),
            P(),
            P(None, "blk", None, "rep"),
            P("blk", None),
            P(),
            P("rep"),
        ),
        out_specs=(P("rep", "blk", None), P(None, None, "blk"), P(None, "rep")),
        check_vma=False,
    )
```

```python
import functools

import jax
import jax.numpy as jnp
from jax import lax
from jax.experimental import pallas as pl
from jax.experimental.pallas import tpu as pltpu
from jax.sharding import PartitionSpec as P

FF = 512
EXPERTS = 32
LEN = 128
CAP = 36
FIRST = 32
SECOND = 40
GROUPS = 4
RING = (0, 1, 4, 5, 8, 9, 12, 13, 14, 15, 10, 11, 6, 7, 2, 3)
LANES = 128
VMEM = 56 * 1024 * 1024


def merged(x, axis, combine):
    everything = jax.tree.map(lambda part: lax.all_gather(part, axis), x)
    initial = jax.tree.map(lambda part: part[0], everything)

    def turn(k, so_far):
        return combine(so_far, jax.tree.map(lambda part: part[k], everything))

    return lax.fori_loop(1, lax.axis_size(axis), turn, initial)


def combine_stats(first, second):
    return (first[0] + second[0], jnp.maximum(first[1], second[1]))


def general(
    hidden_in, lengths, routes, route_weights, norm_gain, master, unembed, final_gain, target_ids
):
    rows_here = hidden_in.shape[1]
    width = hidden_in.shape[2]
    top_count = routes.shape[2]
    blk_count = lax.axis_size("blk")
    rep_count = lax.axis_size("rep")
    blk_index = lax.axis_index("blk")
    unit_count = master.shape[3] * rep_count
    split_ways = max(1, FF // unit_count)
    local_exp = max(1, unit_count // FF)
    group_width = min(unit_count, FF)
    capacity = CAP
    blocks = master.astype(jnp.bfloat16)
    arrived_blocks = lax.all_to_all(blocks, "blk", split_axis=2, concat_axis=1, tiled=True)
    server = lax.all_gather(arrived_blocks, "rep", axis=3, tiled=True)[:, :, 0, :]
    gate_w = server[0].reshape(width, local_exp, group_width)
    up_w = server[1].reshape(width, local_exp, group_width)
    down_w = server[2].reshape(width, local_exp, group_width)
    prompts_here = lengths.shape[0]
    slot_index = blk_index * rows_here + jnp.arange(rows_here, dtype=jnp.int32)
    prompt_of = slot_index // LEN
    position = slot_index % LEN
    prompt_match = prompt_of[:, None] == jnp.arange(prompts_here, dtype=jnp.int32)[None, :]
    row_len = jnp.sum(jnp.where(prompt_match, lengths[None, :], 0), axis=1)
    is_valid = position < row_len
    resid_f = hidden_in[0].astype(jnp.float32)
    normed = (
        resid_f * lax.rsqrt(jnp.mean(resid_f * resid_f, axis=-1, keepdims=True) + 1e-05) * norm_gain
    ).astype(jnp.bfloat16)
    expert_ids = routes[0].reshape(-1)
    pair_live = jnp.repeat(is_valid, top_count)
    pair_row = jnp.repeat(jnp.arange(rows_here, dtype=jnp.int32), top_count)
    expert_hits = (
        (expert_ids[:, None] == jnp.arange(EXPERTS, dtype=jnp.int32)[None, :]) & pair_live[:, None]
    ).astype(jnp.int32)
    slot_rank = jnp.sum((jnp.cumsum(expert_hits, axis=0) - 1) * expert_hits, axis=1)
    slot_id = jnp.where(pair_live, expert_ids * capacity + slot_rank, EXPERTS * capacity)
    source_row = jnp.zeros((EXPERTS * capacity + 1,), jnp.int32).at[slot_id].set(pair_row)[:-1]
    filled = jnp.zeros((EXPERTS * capacity + 1,), jnp.bfloat16).at[slot_id].set(1.0)[:-1]
    outgoing = (normed[source_row] * filled[:, None]).reshape(EXPERTS, capacity, width)
    sending = jnp.repeat(outgoing, split_ways, axis=0).reshape(
        blk_count, local_exp, capacity, width
    )
    arrived = lax.all_to_all(sending, "blk", split_axis=0, concat_axis=0, tiled=True)
    sources = arrived.shape[0]
    slot_count = arrived.shape[2]
    stride = sources
    while stride % 2 == 0 and stride * local_exp * slot_count > 1024:
        stride = stride // 2
    grouped = arrived.reshape(sources // stride, stride, local_exp, slot_count, width)

    def one_block(portion):
        gate_out = jnp.einsum("slnd,dlf->slnf", portion, gate_w, preferred_element_type=jnp.float32)
        up_out = jnp.einsum("slnd,dlf->slnf", portion, up_w, preferred_element_type=jnp.float32)
        hidden = (jax.nn.silu(gate_out) * up_out).astype(jnp.bfloat16)
        return jnp.einsum(
            "slnf,dlf->slnd", hidden, down_w, preferred_element_type=jnp.float32
        ).astype(jnp.bfloat16)

    returned = lax.all_to_all(
        lax.map(one_block, grouped).reshape(sources, local_exp, slot_count, width),
        "blk",
        split_axis=0,
        concat_axis=0,
        tiled=True,
    )
    summed_f = jnp.sum(
        returned.reshape(EXPERTS, split_ways, capacity, width).astype(jnp.float32), axis=1
    )
    expert_out = lax.optimization_barrier(summed_f.astype(jnp.bfloat16)).reshape(
        EXPERTS * capacity, width
    )
    gather_index = jnp.where(pair_live, expert_ids * capacity + slot_rank, 0)
    pair_weight = route_weights[0].reshape(-1) * pair_live.astype(jnp.float32)
    moe = jnp.sum(
        (expert_out[gather_index].astype(jnp.float32) * pair_weight[:, None]).reshape(
            rows_here, top_count, width
        ),
        axis=1,
    )
    out_rows = (resid_f + moe).astype(jnp.bfloat16)
    out_f = out_rows.astype(jnp.float32)
    row_squares = jnp.sum(out_f * out_f, axis=-1) * is_valid.astype(jnp.float32)
    square_local = jnp.sum(jnp.where(prompt_match, row_squares[:, None], 0.0), axis=0)
    is_last = is_valid & (position == row_len - 1)
    picker = (prompt_match & is_last[:, None]).astype(jnp.bfloat16)
    last_local = lax.dot_general(
        picker, out_rows, (((0,), (0,)), ((), ())), preferred_element_type=jnp.float32
    )
    last_rows, square_total = lax.psum((last_local, square_local), "blk")
    norms = jnp.sqrt(square_total / (lengths.astype(jnp.float32) * width) + 1e-06)
    final = (
        last_rows
        * lax.rsqrt(jnp.mean(last_rows * last_rows, axis=-1, keepdims=True) + 1e-05)
        * final_gain
    ).astype(jnp.bfloat16)
    logits = lax.dot_general(
        final, unembed, (((1,), (1,)), ((), ())), preferred_element_type=jnp.float32
    )
    vocab_base = blk_index * unembed.shape[0]
    target_hit = (
        target_ids[:, None] == vocab_base + jnp.arange(unembed.shape[0], dtype=jnp.int32)[None, :]
    )
    target_part = jnp.sum(jnp.where(target_hit, logits, 0.0), axis=1)
    top_part = jnp.max(logits, axis=1)
    target_logit, top_logit = merged((target_part, top_part), "blk", combine_stats)
    request_stats = jnp.stack([norms, top_logit, target_logit])
    return (out_rows[None], server, request_stats)


def iota(shape, dim):
    return lax.broadcasted_iota(jnp.int32, shape, dim)


def prep_kernel(length_ref, hidden_ref, routes_ref, weights_ref, gain_ref, rows_ref, pieces_ref):
    rows, width = hidden_ref.shape
    length = length_ref[0]
    x = hidden_ref[...].astype(jnp.float32)
    scale = lax.rsqrt(jnp.mean(x * x, axis=-1, keepdims=True) + 1e-05)
    rows_ref[:, :width] = (x * scale * gain_ref[...][None]).astype(jnp.bfloat16)
    lane = iota((rows, LANES), 1)
    row = iota((rows, LANES), 0)
    hit = jnp.zeros((rows, LANES), jnp.float32)
    weight = jnp.zeros((rows, LANES), jnp.float32)
    named_by = jnp.transpose(routes_ref[...].astype(jnp.float32)).astype(jnp.int32)
    weight_by = jnp.transpose(weights_ref[...])
    for k in range(routes_ref.shape[0]):
        named = named_by[:, k : k + 1] == lane
        hit = hit + jnp.where(named, 1.0, 0.0)
        weight = weight + jnp.where(named, weight_by[:, k : k + 1], 0.0)
    live = row < length
    hit = jnp.where(live, hit, 0.0)
    weight = jnp.where(live, weight, 0.0)
    before = jnp.where(iota((rows, rows), 1) < iota((rows, rows), 0), 1.0, 0.0)
    rank = jnp.dot(
        before.astype(jnp.bfloat16), hit.astype(jnp.bfloat16), preferred_element_type=jnp.float32
    )
    rows_ref[:, width:] = jnp.where(hit > 0.0, rank, -1.0).astype(jnp.bfloat16)
    for k in range(3):
        piece = weight.astype(jnp.bfloat16)
        pieces_ref[k * rows : (k + 1) * rows, :] = piece
        weight = weight - piece.astype(jnp.float32)


def pick(info, which, x_ref, width, place, slots):
    rows = x_ref.shape[0]
    ranks = x_ref[:, width:].astype(jnp.float32)
    lane = iota((rows, LANES), 1)
    source = (iota((rows, 1), 0) // LEN).astype(jnp.float32)
    rank = jnp.sum(jnp.where(lane == info[which], ranks, 0.0), axis=1, keepdims=True)
    slot = jnp.where(rank >= 0.0, place(source, rank), -1.0)
    slot_lane = iota((rows, slots), 1).astype(jnp.float32)
    one_hot = jnp.where(slot == slot_lane, 1.0, 0.0).astype(jnp.bfloat16)
    return lax.dot_general(
        one_hot, x_ref[:, :width], (((0,), (0,)), ((), ())), preferred_element_type=jnp.float32
    )


def activ(x, g_ref, u_ref):
    x = x.astype(jnp.bfloat16)
    gate = jnp.dot(x, g_ref[...], preferred_element_type=jnp.float32)
    up = jnp.dot(x, u_ref[...], preferred_element_type=jnp.float32)
    return (gate / (1.0 + jnp.exp(-gate)) * up).astype(jnp.bfloat16)


def own_kernel(info, x_ref, g_ref, u_ref, out_ref, spot_ref, picked):
    step = pl.program_id(0)
    sources = x_ref.shape[0] // LEN
    more = CAP - FIRST
    early = sources * FIRST
    all_early = GROUPS * early

    def place(source, rank):
        return jnp.where(
            rank < FIRST, source * FIRST + rank, early + source * more + (rank - FIRST)
        )

    chosen = pick(info, 0, x_ref, g_ref.shape[0], place, early + sources * more)
    for s in range(sources):
        start = pl.multiple_of(info[4 + step * sources + s] * FIRST, FIRST)
        picked[pl.ds(start, FIRST), :] = chosen[s * FIRST : (s + 1) * FIRST]
    start = pl.multiple_of(all_early + step * sources * more, sources * more)
    picked[pl.ds(start, sources * more), :] = chosen[early:]

    @pl.when(step == GROUPS - 1)
    def _():
        out_ref[...] = activ(picked[...], g_ref, u_ref)
        column = iota(spot_ref.shape, 1)
        owner = lax.shift_right_logical(column, more.bit_length() - 1)
        source = jnp.zeros_like(column)
        for k, b in enumerate(RING):
            source = source + jnp.where(owner == k, b, 0)
        spot = source * SECOND + (column & (more - 1))
        spot_ref[...] = jnp.where(iota(spot_ref.shape, 0) == spot, 1.0, 0.0).astype(jnp.bfloat16)


def oth_kernel(info, x_ref, g_ref, u_ref, _, __, out_ref, picked):
    step = pl.program_id(0)
    sources = x_ref.shape[0] // LEN

    def place(source, rank):
        return source * SECOND + (SECOND - CAP) + rank

    chosen = pick(info, 1, x_ref, g_ref.shape[0], place, sources * SECOND)
    for s in range(sources):
        start = pl.multiple_of(info[4 + step * sources + s] * SECOND, SECOND)
        picked[pl.ds(start, SECOND), :] = chosen[s * SECOND : (s + 1) * SECOND]

    @pl.when(step == GROUPS - 1)
    def _():
        out_ref[...] = activ(picked[...], g_ref, u_ref)


def matmul_nt(hidden_ref, d_ref):
    return lax.dot_general(
        hidden_ref[...], d_ref[...], (((1,), (1,)), ((), ())), preferred_element_type=jnp.float32
    )


def own_down_kernel(hidden_ref, d_ref, out_ref, late_ref):
    out = matmul_nt(hidden_ref, d_ref).astype(jnp.bfloat16)
    rows = out_ref.shape[0]
    out_ref[...] = out[:rows]
    late_ref[...] = out[rows:]


def oth_down_kernel(hidden_ref, spot_ref, late_ref, d_a, d_b, out_ref):
    late = jnp.dot(spot_ref[...], late_ref[...], preferred_element_type=jnp.float32)
    in_a = pl.program_id(0) < pl.num_programs(0) // 2

    @pl.when(in_a)
    def _():
        out_ref[...] = (late + matmul_nt(hidden_ref, d_a)).astype(jnp.bfloat16)

    @pl.when(jnp.logical_not(in_a))
    def _():
        out_ref[...] = (late + matmul_nt(hidden_ref, d_b)).astype(jnp.bfloat16)


def mix_kernel(info, rank_ref, pieces_ref, first_ref, second_ref, last_ref):
    rows = rank_ref.shape[0]
    late = SECOND - CAP
    own, oth = info[2], 1 - info[2]
    for mix_ref, stride, spans in (
        (first_ref, FIRST, ((own, 0, FIRST, 0),)),
        (second_ref, SECOND, ((own, 0, late, FIRST), (oth, late, CAP, 0))),
    ):
        slots = mix_ref.shape[1]
        expert = iota((LANES, slots), 0)
        lane = iota((LANES, slots), 1)
        within = jnp.zeros((1, slots), jnp.float32)
        spread = jnp.zeros((LANES, slots), jnp.float32)
        for parity, offset, count, lowest in spans:
            start = jnp.where((expert & 1) == parity, (expert >> 1) * stride + offset, slots)
            inside = (lane >= start) & (lane < start + count)
            spread = spread + jnp.where(inside, 1.0, 0.0)
            ranks = jnp.where(inside, lane - start + lowest, 0)
            within = within + jnp.sum(ranks, axis=0, keepdims=True).astype(jnp.float32)
        spread = spread.astype(jnp.bfloat16)
        rank = jnp.dot(rank_ref[...], spread, preferred_element_type=jnp.float32)
        match = rank == within
        for k in range(3):
            part = jnp.dot(
                pieces_ref[k * rows : (k + 1) * rows, :], spread, preferred_element_type=jnp.float32
            )
            mix_ref[k * rows : (k + 1) * rows, :] = jnp.where(match, part, 0.0).astype(jnp.bfloat16)
    shape = (last_ref.shape[0], 3 * rows)
    one_hot = jnp.where(iota(shape, 1) == iota(shape, 0) * rows + info[3] - 1, 1.0, 0.0)
    last_ref[...] = jnp.dot(
        one_hot.astype(jnp.bfloat16), second_ref[...], preferred_element_type=jnp.float32
    ).astype(jnp.bfloat16)


def weigh(mix_ref, back_ref):
    rows = mix_ref.shape[0] // 3
    parts = jnp.dot(mix_ref[...], back_ref[...], preferred_element_type=jnp.float32)
    return parts[2 * rows :] + parts[rows : 2 * rows] + parts[:rows]


def first_kernel(info, mix_ref, back_ref, resid_ref, base_ref, last_ref):
    base = resid_ref[...].astype(jnp.float32) + weigh(mix_ref, back_ref)
    base_ref[...] = base
    is_last = iota(base.shape, 0) == info[3] - 1
    last_ref[...] = jnp.sum(jnp.where(is_last, base, 0.0), axis=0, keepdims=True)


def last_kernel(mix_ref, back_ref, base_ref, _, told_ref):
    parts = jnp.dot(mix_ref[...], back_ref[...], preferred_element_type=jnp.float32)
    moe = parts[2:3] + parts[1:2] + parts[0:1]
    out = (base_ref[...] + moe).astype(jnp.bfloat16).astype(jnp.float32)
    told_ref[...] = jnp.broadcast_to(out[None], told_ref.shape)


def combine_kernel(info, mix_ref, back_ref, base_ref, _, out_ref, square_ref, squares):
    step = pl.program_id(0)

    @pl.when(step == 0)
    def _():
        squares[...] = jnp.zeros_like(squares)

    out = (base_ref[...] + weigh(mix_ref, back_ref)).astype(jnp.bfloat16)
    out_ref[...] = out
    out_f = out.astype(jnp.float32)
    row = iota(out_f.shape, 0)
    squares[...] += jnp.sum(jnp.where(row < info[3], out_f * out_f, 0.0), axis=0, keepdims=True)

    @pl.when(step == pl.num_programs(0) - 1)
    def _():
        total = jnp.sum(squares[...], axis=1, keepdims=True)
        square_ref[...] = jnp.broadcast_to(total, square_ref.shape)


def place_kernel(info, g_own, g_oth, u_own, u_oth, d_own, d_a, d_b, _, out_ref):
    second_half = pl.program_id(0) >= pl.num_programs(0) // 2
    d_oth = jnp.where(second_half, d_b[...], d_a[...])
    for k, (own, oth) in enumerate(
        ((g_own[...], g_oth[...]), (u_own[...], u_oth[...]), (d_own[...], d_oth))
    ):
        left = info[2] == 0
        out_ref[k, :, :FF] = jnp.where(left, own, oth)
        out_ref[k, :, FF:] = jnp.where(left, oth, own)


def cast_kernel(blocks, x_ref, *refs):
    out_ref, order = refs[-2:]
    rows = out_ref.shape[1]

    @pl.when(pl.program_id(0) == 0)
    def _():
        target = iota(order.shape, 0)
        source = (target & (rows - 1)) * blocks + lax.shift_right_logical(target, 4)
        order[...] = jnp.where(iota(order.shape, 1) == source, 1.0, 0.0).astype(jnp.bfloat16)

    turned = jnp.dot(
        order[...], x_ref[...].astype(jnp.bfloat16), preferred_element_type=jnp.float32
    ).astype(jnp.bfloat16)
    for b in range(blocks):
        out_ref[b] = turned[b * rows : (b + 1) * rows]


def tie_kernel(*_):
    pass


def params():
    return pltpu.CompilerParams(vmem_limit_bytes=VMEM, dimension_semantics=("arbitrary",))


def whole(shape):
    return pl.BlockSpec(shape, lambda *_: tuple(0 for _ in shape))


def paired(
    hidden_in, lengths, routes, route_weights, norm_gain, master, unembed, final_gain, target_ids
):
    rows = hidden_in.shape[1]
    width = hidden_in.shape[2]
    blk_count = lax.axis_size("blk")
    blk = lax.axis_index("blk")
    rep = lax.axis_index("rep")
    first = blk_count * FIRST
    second = blk_count * SECOND
    resid = hidden_in[0]
    length = lax.dynamic_slice(lengths, (blk,), (1,))
    info = jnp.stack([2 * blk + rep, 2 * blk + 1 - rep, rep, length[0]] + list(RING))
    info = info.astype(jnp.int32)

    shard_rows = master.shape[1]
    flat = master.reshape(3 * shard_rows * blk_count, FF)

    def turned(k, *after):
        return pl.pallas_call(
            functools.partial(cast_kernel, blk_count),
            grid=(shard_rows // 16,),
            in_specs=[pl.BlockSpec((16 * blk_count, FF), lambda i: (k * (shard_rows // 16) + i, 0))]
            + [pl.BlockSpec(memory_space=pl.ANY)] * len(after),
            out_specs=pl.BlockSpec((blk_count, 16, FF), lambda i: (0, i, 0)),
            out_shape=jax.ShapeDtypeStruct((blk_count, shard_rows, FF), jnp.bfloat16),
            scratch_shapes=[pltpu.VMEM((16 * blk_count, 16 * blk_count), jnp.bfloat16)],
            compiler_params=params(),
            name="cast",
        )(flat, *after)

    def moved(x):
        own = lax.all_to_all(x, "blk", split_axis=0, concat_axis=0, tiled=True)
        return own.reshape(width, FF)

    def swapped(x):
        return lax.ppermute(x, "rep", [(0, 1), (1, 0)])

    def tied(x, *after):
        return pl.pallas_call(
            tie_kernel,
            in_specs=[pl.BlockSpec(memory_space=pl.ANY)] * (1 + len(after)),
            out_specs=pl.BlockSpec(memory_space=pl.ANY),
            out_shape=jax.ShapeDtypeStruct(x.shape, x.dtype),
            input_output_aliases={0: 0},
            name="tie",
        )(x, *after)

    row_ext, pieces = pl.pallas_call(
        prep_kernel,
        grid_spec=pltpu.PrefetchScalarGridSpec(
            num_scalar_prefetch=1,
            grid=(1,),
            in_specs=[
                whole((rows, width)),
                whole((routes.shape[2], rows)),
                whole((routes.shape[2], rows)),
                whole((width,)),
            ],
            out_specs=[whole((rows, width + LANES)), whole((3 * rows, LANES))],
        ),
        out_shape=[
            jax.ShapeDtypeStruct((rows, width + LANES), jnp.bfloat16),
            jax.ShapeDtypeStruct((3 * rows, LANES), jnp.bfloat16),
        ],
        compiler_params=params(),
        name="prep",
    )(length, resid, routes[0].T, route_weights[0].T, norm_gain)
    g_own = moved(turned(0, row_ext))
    g_oth = swapped(g_own)
    u_own = moved(turned(1))
    u_oth = swapped(u_own)
    d_own = moved(tied(turned(2), g_oth))

    tokens = lax.all_gather(row_ext, "blk", axis_index_groups=[list(RING)], axis=0, tiled=True)

    def hidden_of(kernel, sizes, scratch, g, u, *after):
        return pl.pallas_call(
            kernel,
            grid_spec=pltpu.PrefetchScalarGridSpec(
                num_scalar_prefetch=1,
                grid=(GROUPS,),
                in_specs=[pl.BlockSpec((blk_count // GROUPS * rows, width + LANES), lambda i, *_: (i, 0))]
                + [whole((width, FF))] * 2
                + [pl.BlockSpec(memory_space=pl.ANY)] * len(after),
                out_specs=[whole(size) for size in sizes],
                scratch_shapes=[pltpu.VMEM((scratch, width), jnp.float32)],
            ),
            out_shape=[jax.ShapeDtypeStruct(size, jnp.bfloat16) for size in sizes],
            compiler_params=params(),
            name="gate_up",
        )(info, tokens, g, u, *after)

    step = 512

    quarter = width // 4
    in_a = pl.BlockSpec((quarter, FF), lambda i, *_: (jnp.minimum(i, 1), 0))
    in_b = pl.BlockSpec((quarter, FF), lambda i, *_: (jnp.maximum(i, 2) - 2, 0))

    def returned(x):
        slots = x.shape[0]
        x = x.reshape(blk_count, slots // blk_count, width)
        x = lax.all_to_all(x, "blk", split_axis=0, concat_axis=0, tiled=True)
        return x.reshape(slots, width)

    extra = blk_count * (CAP - FIRST)
    own_hidden, spot = hidden_of(
        own_kernel, ((first + extra, FF), (second, extra)), first + extra, g_own, u_own
    )
    d_own = tied(d_own, own_hidden)
    half = width // 2
    d_oth_a = swapped(d_own[:half])
    d_oth_b = swapped(tied(d_own[half:], d_oth_a))
    own_out, late_out = pl.pallas_call(
        own_down_kernel,
        grid=(width // step,),
        in_specs=[whole((first + extra, FF)), pl.BlockSpec((step, FF), lambda i: (i, 0))],
        out_specs=[
            pl.BlockSpec((first, step), lambda i: (0, i)),
            pl.BlockSpec((extra, step), lambda i: (0, i)),
        ],
        out_shape=[
            jax.ShapeDtypeStruct((first, width), jnp.bfloat16),
            jax.ShapeDtypeStruct((extra, width), jnp.bfloat16),
        ],
        compiler_params=params(),
        name="own_down",
    )(own_hidden, d_own)
    own_out = tied(own_out, u_oth)
    own_back = returned(own_out)
    (oth_hidden,) = hidden_of(
        oth_kernel, ((second, FF),), second, g_oth, u_oth, own_out, d_oth_a
    )
    oth_out = pl.pallas_call(
        oth_down_kernel,
        grid=(4,),
        in_specs=[
            whole((second, FF)),
            whole((second, extra)),
            pl.BlockSpec((extra, quarter), lambda i: (0, i)),
            in_a,
            in_b,
        ],
        out_specs=pl.BlockSpec((second, quarter), lambda i: (0, i)),
        out_shape=jax.ShapeDtypeStruct((second, width), jnp.bfloat16),
        compiler_params=params(),
        name="oth_down",
    )(oth_hidden, spot, late_out, d_oth_a, d_oth_b)
    oth_back = returned(oth_out)

    server = pl.pallas_call(
        place_kernel,
        grid_spec=pltpu.PrefetchScalarGridSpec(
            num_scalar_prefetch=1,
            grid=(4,),
            in_specs=[pl.BlockSpec((quarter, FF), lambda i, *_: (i, 0))] * 5
            + [in_a, in_b, pl.BlockSpec(memory_space=pl.ANY)],
            out_specs=pl.BlockSpec((3, quarter, 2 * FF), lambda i, *_: (0, i, 0)),
        ),
        out_shape=jax.ShapeDtypeStruct((3, width, 2 * FF), jnp.bfloat16),
        compiler_params=params(),
        name="place",
    )(info, g_own, g_oth, u_own, u_oth, d_own, d_oth_a, d_oth_b, oth_out)

    first_mix, second_mix, last_mix = pl.pallas_call(
        mix_kernel,
        grid_spec=pltpu.PrefetchScalarGridSpec(
            num_scalar_prefetch=1,
            grid=(1,),
            in_specs=[
                pl.BlockSpec((rows, LANES), lambda i, *_: (0, width // LANES)),
                whole((3 * rows, LANES)),
            ],
            out_specs=[whole((3 * rows, first)), whole((3 * rows, second)), whole((16, second))],
        ),
        out_shape=[
            jax.ShapeDtypeStruct((3 * rows, first), jnp.bfloat16),
            jax.ShapeDtypeStruct((3 * rows, second), jnp.bfloat16),
            jax.ShapeDtypeStruct((16, second), jnp.bfloat16),
        ],
        compiler_params=params(),
        name="mix",
    )(info, row_ext, pieces)

    def weigh_specs(slots):
        return [whole((3 * rows, slots)), pl.BlockSpec((slots, step), lambda i, *_: (0, i))]

    column = pl.BlockSpec((rows, step), lambda i, *_: (0, i))
    lane_row = pl.BlockSpec((1, step), lambda i, *_: (0, i))
    base, last_base = pl.pallas_call(
        first_kernel,
        grid_spec=pltpu.PrefetchScalarGridSpec(
            num_scalar_prefetch=1,
            grid=(width // step,),
            in_specs=weigh_specs(first) + [column],
            out_specs=[column, lane_row],
        ),
        out_shape=[
            jax.ShapeDtypeStruct((rows, width), jnp.float32),
            jax.ShapeDtypeStruct((1, width), jnp.float32),
        ],
        compiler_params=params(),
        name="first",
    )(info, first_mix, own_back, resid)
    told = pl.pallas_call(
        last_kernel,
        grid=(width // step,),
        in_specs=[
            whole((16, second)),
            pl.BlockSpec((second, step), lambda i: (0, i)),
            lane_row,
            pl.BlockSpec(memory_space=pl.ANY),
        ],
        out_specs=pl.BlockSpec((blk_count, 1, step), lambda i: (0, 0, i)),
        out_shape=jax.ShapeDtypeStruct((blk_count, 1, width), jnp.float32),
        compiler_params=params(),
        name="last",
    )(last_mix, oth_back, last_base, server)
    out_rows, square = pl.pallas_call(
        combine_kernel,
        grid_spec=pltpu.PrefetchScalarGridSpec(
            num_scalar_prefetch=1,
            grid=(width // step,),
            in_specs=weigh_specs(second) + [column, pl.BlockSpec(memory_space=pl.ANY)],
            out_specs=[column, whole((1, LANES))],
            scratch_shapes=[pltpu.VMEM((1, step), jnp.float32)],
        ),
        out_shape=[
            jax.ShapeDtypeStruct((rows, width), jnp.bfloat16),
            jax.ShapeDtypeStruct((1, LANES), jnp.float32),
        ],
        compiler_params=params(),
        name="combine",
    )(info, second_mix, oth_back, base, told)

    def everywhere(copies):
        return lax.all_to_all(copies, "blk", split_axis=0, concat_axis=0, tiled=True)

    last_rows = everywhere(told)[:, 0]
    final = (
        last_rows
        * lax.rsqrt(jnp.mean(last_rows * last_rows, axis=-1, keepdims=True) + 1e-05)
        * final_gain
    ).astype(jnp.bfloat16)
    logits = lax.dot_general(
        final, unembed, (((1,), (1,)), ((), ())), preferred_element_type=jnp.float32
    )
    vocab_base = blk * unembed.shape[0]
    target_hit = (
        target_ids[:, None] == vocab_base + jnp.arange(unembed.shape[0], dtype=jnp.int32)[None, :]
    )
    target_part = jnp.sum(jnp.where(target_hit, logits, 0.0), axis=1)
    top_part = jnp.max(logits, axis=1)
    prompt = jnp.arange(blk_count, dtype=jnp.int32)
    square_part = jnp.where(prompt == blk, square[0, :blk_count], 0.0)
    stats = jnp.stack([top_part, target_part, square_part])
    parts = everywhere(jnp.broadcast_to(stats[None], (blk_count,) + stats.shape))
    sums = jnp.sum(parts[:, 1:], axis=0)
    norms = jnp.sqrt(sums[1] / (lengths.astype(jnp.float32) * width) + 1e-06)
    request_stats = jnp.stack([norms, jnp.max(parts[:, 0], axis=0), sums[0]])
    return (out_rows[None], server, request_stats)


def local(hidden_in, lengths, routes, route_weights, norm_gain, master, *rest):
    blk_count = lax.axis_size("blk")
    fits = (
        lax.axis_size("rep") == 2
        and master.shape[3] == FF
        and EXPERTS == 2 * blk_count
        and blk_count == len(RING)
        and hidden_in.shape[1] == LEN
        and lengths.shape[0] == blk_count
    )
    form = paired if fits else general
    return form(hidden_in, lengths, routes, route_weights, norm_gain, master, *rest)


def solution(mesh):
    return jax.shard_map(
        local,
        mesh=mesh,
        in_specs=(
            P("rep", "blk", None),
            P("rep"),
            P("rep", "blk", None),
            P("rep", "blk", None),
            P(),
            P(None, "blk", None, "rep"),
            P("blk", None),
            P(),
            P("rep"),
        ),
        out_specs=(P("rep", "blk", None), P(None, None, "blk"), P(None, "rep")),
        check_vma=False,
    )
```

```python
import functools

import jax
import jax.numpy as jnp
from jax import lax
from jax.experimental import pallas as pl
from jax.experimental.pallas import tpu as pltpu
from jax.sharding import PartitionSpec as P

FF = 512
EXPERTS = 32
LEN = 128
CAP = 36
FIRST = 32
SECOND = 40
GROUPS = 4
RING = (0, 1, 4, 5, 8, 9, 12, 13, 14, 15, 10, 11, 6, 7, 2, 3)
LANES = 128
VMEM = 36 * 1024 * 1024


def merged(x, axis, combine):
    everything = jax.tree.map(lambda part: lax.all_gather(part, axis), x)
    initial = jax.tree.map(lambda part: part[0], everything)

    def turn(k, so_far):
        return combine(so_far, jax.tree.map(lambda part: part[k], everything))

    return lax.fori_loop(1, lax.axis_size(axis), turn, initial)


def combine_stats(first, second):
    return (first[0] + second[0], jnp.maximum(first[1], second[1]))


def general(
    hidden_in, lengths, routes, route_weights, norm_gain, master, unembed, final_gain, target_ids
):
    rows_here = hidden_in.shape[1]
    width = hidden_in.shape[2]
    top_count = routes.shape[2]
    blk_count = lax.axis_size("blk")
    rep_count = lax.axis_size("rep")
    blk_index = lax.axis_index("blk")
    unit_count = master.shape[3] * rep_count
    split_ways = max(1, FF // unit_count)
    local_exp = max(1, unit_count // FF)
    group_width = min(unit_count, FF)
    capacity = CAP
    blocks = master.astype(jnp.bfloat16)
    arrived_blocks = lax.all_to_all(blocks, "blk", split_axis=2, concat_axis=1, tiled=True)
    server = lax.all_gather(arrived_blocks, "rep", axis=3, tiled=True)[:, :, 0, :]
    gate_w = server[0].reshape(width, local_exp, group_width)
    up_w = server[1].reshape(width, local_exp, group_width)
    down_w = server[2].reshape(width, local_exp, group_width)
    prompts_here = lengths.shape[0]
    slot_index = blk_index * rows_here + jnp.arange(rows_here, dtype=jnp.int32)
    prompt_of = slot_index // LEN
    position = slot_index % LEN
    prompt_match = prompt_of[:, None] == jnp.arange(prompts_here, dtype=jnp.int32)[None, :]
    row_len = jnp.sum(jnp.where(prompt_match, lengths[None, :], 0), axis=1)
    is_valid = position < row_len
    resid_f = hidden_in[0].astype(jnp.float32)
    normed = (
        resid_f * lax.rsqrt(jnp.mean(resid_f * resid_f, axis=-1, keepdims=True) + 1e-05) * norm_gain
    ).astype(jnp.bfloat16)
    expert_ids = routes[0].reshape(-1)
    pair_live = jnp.repeat(is_valid, top_count)
    pair_row = jnp.repeat(jnp.arange(rows_here, dtype=jnp.int32), top_count)
    expert_hits = (
        (expert_ids[:, None] == jnp.arange(EXPERTS, dtype=jnp.int32)[None, :]) & pair_live[:, None]
    ).astype(jnp.int32)
    slot_rank = jnp.sum((jnp.cumsum(expert_hits, axis=0) - 1) * expert_hits, axis=1)
    slot_id = jnp.where(pair_live, expert_ids * capacity + slot_rank, EXPERTS * capacity)
    source_row = jnp.zeros((EXPERTS * capacity + 1,), jnp.int32).at[slot_id].set(pair_row)[:-1]
    filled = jnp.zeros((EXPERTS * capacity + 1,), jnp.bfloat16).at[slot_id].set(1.0)[:-1]
    outgoing = (normed[source_row] * filled[:, None]).reshape(EXPERTS, capacity, width)
    sending = jnp.repeat(outgoing, split_ways, axis=0).reshape(
        blk_count, local_exp, capacity, width
    )
    arrived = lax.all_to_all(sending, "blk", split_axis=0, concat_axis=0, tiled=True)
    sources = arrived.shape[0]
    slot_count = arrived.shape[2]
    stride = sources
    while stride % 2 == 0 and stride * local_exp * slot_count > 1024:
        stride = stride // 2
    grouped = arrived.reshape(sources // stride, stride, local_exp, slot_count, width)

    def one_block(portion):
        gate_out = jnp.einsum("slnd,dlf->slnf", portion, gate_w, preferred_element_type=jnp.float32)
        up_out = jnp.einsum("slnd,dlf->slnf", portion, up_w, preferred_element_type=jnp.float32)
        hidden = (jax.nn.silu(gate_out) * up_out).astype(jnp.bfloat16)
        return jnp.einsum(
            "slnf,dlf->slnd", hidden, down_w, preferred_element_type=jnp.float32
        ).astype(jnp.bfloat16)

    returned = lax.all_to_all(
        lax.map(one_block, grouped).reshape(sources, local_exp, slot_count, width),
        "blk",
        split_axis=0,
        concat_axis=0,
        tiled=True,
    )
    summed_f = jnp.sum(
        returned.reshape(EXPERTS, split_ways, capacity, width).astype(jnp.float32), axis=1
    )
    expert_out = lax.optimization_barrier(summed_f.astype(jnp.bfloat16)).reshape(
        EXPERTS * capacity, width
    )
    gather_index = jnp.where(pair_live, expert_ids * capacity + slot_rank, 0)
    pair_weight = route_weights[0].reshape(-1) * pair_live.astype(jnp.float32)
    moe = jnp.sum(
        (expert_out[gather_index].astype(jnp.float32) * pair_weight[:, None]).reshape(
            rows_here, top_count, width
        ),
        axis=1,
    )
    out_rows = (resid_f + moe).astype(jnp.bfloat16)
    out_f = out_rows.astype(jnp.float32)
    row_squares = jnp.sum(out_f * out_f, axis=-1) * is_valid.astype(jnp.float32)
    square_local = jnp.sum(jnp.where(prompt_match, row_squares[:, None], 0.0), axis=0)
    is_last = is_valid & (position == row_len - 1)
    picker = (prompt_match & is_last[:, None]).astype(jnp.bfloat16)
    last_local = lax.dot_general(
        picker, out_rows, (((0,), (0,)), ((), ())), preferred_element_type=jnp.float32
    )
    last_rows, square_total = lax.psum((last_local, square_local), "blk")
    norms = jnp.sqrt(square_total / (lengths.astype(jnp.float32) * width) + 1e-06)
    final = (
        last_rows
        * lax.rsqrt(jnp.mean(last_rows * last_rows, axis=-1, keepdims=True) + 1e-05)
        * final_gain
    ).astype(jnp.bfloat16)
    logits = lax.dot_general(
        final, unembed, (((1,), (1,)), ((), ())), preferred_element_type=jnp.float32
    )
    vocab_base = blk_index * unembed.shape[0]
    target_hit = (
        target_ids[:, None] == vocab_base + jnp.arange(unembed.shape[0], dtype=jnp.int32)[None, :]
    )
    target_part = jnp.sum(jnp.where(target_hit, logits, 0.0), axis=1)
    top_part = jnp.max(logits, axis=1)
    target_logit, top_logit = merged((target_part, top_part), "blk", combine_stats)
    request_stats = jnp.stack([norms, top_logit, target_logit])
    return (out_rows[None], server, request_stats)


def iota(shape, dim):
    return lax.broadcasted_iota(jnp.int32, shape, dim)


def prep_kernel(length_ref, hidden_ref, routes_ref, weights_ref, gain_ref, rows_ref, pieces_ref):
    rows, width = hidden_ref.shape
    length = length_ref[0]
    x = hidden_ref[...].astype(jnp.float32)
    scale = lax.rsqrt(jnp.mean(x * x, axis=-1, keepdims=True) + 1e-05)
    rows_ref[:, :width] = (x * scale * gain_ref[...][None]).astype(jnp.bfloat16)
    lane = iota((rows, LANES), 1)
    row = iota((rows, LANES), 0)
    hit = jnp.zeros((rows, LANES), jnp.float32)
    weight = jnp.zeros((rows, LANES), jnp.float32)
    named_by = jnp.transpose(routes_ref[...].astype(jnp.float32)).astype(jnp.int32)
    weight_by = jnp.transpose(weights_ref[...])
    for k in range(routes_ref.shape[0]):
        named = named_by[:, k : k + 1] == lane
        hit = hit + jnp.where(named, 1.0, 0.0)
        weight = weight + jnp.where(named, weight_by[:, k : k + 1], 0.0)
    live = row < length
    hit = jnp.where(live, hit, 0.0)
    weight = jnp.where(live, weight, 0.0)
    before = jnp.where(iota((rows, rows), 1) < iota((rows, rows), 0), 1.0, 0.0)
    rank = jnp.dot(
        before.astype(jnp.bfloat16), hit.astype(jnp.bfloat16), preferred_element_type=jnp.float32
    )
    rows_ref[:, width:] = jnp.where(hit > 0.0, rank, -1.0).astype(jnp.bfloat16)
    for k in range(3):
        piece = weight.astype(jnp.bfloat16)
        pieces_ref[k * rows : (k + 1) * rows, :] = piece
        weight = weight - piece.astype(jnp.float32)


def pick(info, which, x_ref, width, place, slots):
    rows = x_ref.shape[0]
    ranks = x_ref[:, width:].astype(jnp.float32)
    lane = iota((rows, LANES), 1)
    source = (iota((rows, 1), 0) // LEN).astype(jnp.float32)
    rank = jnp.sum(jnp.where(lane == info[which], ranks, 0.0), axis=1, keepdims=True)
    slot = jnp.where(rank >= 0.0, place(source, rank), -1.0)
    slot_lane = iota((rows, slots), 1).astype(jnp.float32)
    one_hot = jnp.where(slot == slot_lane, 1.0, 0.0).astype(jnp.bfloat16)
    return lax.dot_general(
        one_hot, x_ref[:, :width], (((0,), (0,)), ((), ())), preferred_element_type=jnp.float32
    )


def activ(x, g_ref, u_ref):
    x = x.astype(jnp.bfloat16)
    gate = jnp.dot(x, g_ref[...], preferred_element_type=jnp.float32)
    up = jnp.dot(x, u_ref[...], preferred_element_type=jnp.float32)
    return (gate / (1.0 + jnp.exp(-gate)) * up).astype(jnp.bfloat16)


def own_kernel(info, x_ref, g_ref, u_ref, out_ref, spot_ref, picked):
    step = pl.program_id(0)
    sources = x_ref.shape[0] // LEN
    more = CAP - FIRST
    early = sources * FIRST
    all_early = GROUPS * early

    def place(source, rank):
        return jnp.where(
            rank < FIRST, source * FIRST + rank, early + source * more + (rank - FIRST)
        )

    chosen = pick(info, 0, x_ref, g_ref.shape[0], place, early + sources * more)
    for s in range(sources):
        start = pl.multiple_of(info[4 + step * sources + s] * FIRST, FIRST)
        picked[pl.ds(start, FIRST), :] = chosen[s * FIRST : (s + 1) * FIRST]
    start = pl.multiple_of(all_early + step * sources * more, sources * more)
    picked[pl.ds(start, sources * more), :] = chosen[early:]

    @pl.when(step == GROUPS - 1)
    def _():
        out_ref[...] = activ(picked[...], g_ref, u_ref)
        column = iota(spot_ref.shape, 1)
        owner = lax.shift_right_logical(column, more.bit_length() - 1)
        source = jnp.zeros_like(column)
        for k, b in enumerate(RING):
            source = source + jnp.where(owner == k, b, 0)
        spot = source * SECOND + (column & (more - 1))
        spot_ref[...] = jnp.where(iota(spot_ref.shape, 0) == spot, 1.0, 0.0).astype(jnp.bfloat16)


def oth_kernel(info, x_ref, g_ref, u_ref, _, out_ref, picked):
    step = pl.program_id(0)
    sources = x_ref.shape[0] // LEN

    def place(source, rank):
        return source * SECOND + (SECOND - CAP) + rank

    chosen = pick(info, 1, x_ref, g_ref.shape[0], place, sources * SECOND)
    for s in range(sources):
        start = pl.multiple_of(info[4 + step * sources + s] * SECOND, SECOND)
        picked[pl.ds(start, SECOND), :] = chosen[s * SECOND : (s + 1) * SECOND]

    @pl.when(step == GROUPS - 1)
    def _():
        out_ref[...] = activ(picked[...], g_ref, u_ref)


def matmul_nt(hidden_ref, d):
    return lax.dot_general(
        hidden_ref[...], d, (((1,), (1,)), ((), ())), preferred_element_type=jnp.float32
    )


def fetched(sources, held, sems):
    step = pl.program_id(0)
    rows = held.shape[1]

    @pl.when(step == 0)
    def _():
        for k, source in enumerate(sources):
            pltpu.make_async_copy(source, held.at[k], sems.at[k]).start()

    for k, source in enumerate(sources):

        @pl.when(step == k)
        def _():
            pltpu.make_async_copy(source, held.at[k], sems.at[k]).wait()

    return held[step]


def own_down_kernel(hidden_ref, d_ref, out_ref, late_ref, held, sems):
    size = held.shape[1]
    d = fetched([d_ref.at[k * size : (k + 1) * size] for k in range(held.shape[0])], held, sems)
    out = matmul_nt(hidden_ref, d).astype(jnp.bfloat16)
    rows = out_ref.shape[0]
    out_ref[...] = out[:rows]
    late_ref[...] = out[rows:]


def oth_down_kernel(info, hidden_ref, spot_ref, late_ref, d_a, d_b, out_ref, held, sems):
    size = held.shape[1]
    other = 1 - info[2]
    sources = [d_a.at[other, :size], d_a.at[other, size:], d_b.at[:size], d_b.at[size:]]
    d = fetched(sources, held, sems)
    late = jnp.dot(spot_ref[...], late_ref[...], preferred_element_type=jnp.float32)
    out_ref[...] = (late + matmul_nt(hidden_ref, d)).astype(jnp.bfloat16)


def mix_kernel(info, rank_ref, pieces_ref, first_ref, second_ref, last_ref):
    rows = rank_ref.shape[0]
    late = SECOND - CAP
    own, oth = info[2], 1 - info[2]
    for mix_ref, stride, spans in (
        (first_ref, FIRST, ((own, 0, FIRST, 0),)),
        (second_ref, SECOND, ((own, 0, late, FIRST), (oth, late, CAP, 0))),
    ):
        slots = mix_ref.shape[1]
        expert = iota((LANES, slots), 0)
        lane = iota((LANES, slots), 1)
        within = jnp.zeros((1, slots), jnp.float32)
        spread = jnp.zeros((LANES, slots), jnp.float32)
        for parity, offset, count, lowest in spans:
            start = jnp.where((expert & 1) == parity, (expert >> 1) * stride + offset, slots)
            inside = (lane >= start) & (lane < start + count)
            spread = spread + jnp.where(inside, 1.0, 0.0)
            ranks = jnp.where(inside, lane - start + lowest, 0)
            within = within + jnp.sum(ranks, axis=0, keepdims=True).astype(jnp.float32)
        spread = spread.astype(jnp.bfloat16)
        rank = jnp.dot(rank_ref[...], spread, preferred_element_type=jnp.float32)
        match = rank == within
        for k in range(3):
            part = jnp.dot(
                pieces_ref[k * rows : (k + 1) * rows, :], spread, preferred_element_type=jnp.float32
            )
            mix_ref[k * rows : (k + 1) * rows, :] = jnp.where(match, part, 0.0).astype(jnp.bfloat16)
    shape = (last_ref.shape[0], 3 * rows)
    one_hot = jnp.where(iota(shape, 1) == iota(shape, 0) * rows + info[3] - 1, 1.0, 0.0)
    last_ref[...] = jnp.dot(
        one_hot.astype(jnp.bfloat16), second_ref[...], preferred_element_type=jnp.float32
    ).astype(jnp.bfloat16)


def weigh(mix_ref, back_ref):
    rows = mix_ref.shape[0] // 3
    parts = jnp.dot(mix_ref[...], back_ref[...], preferred_element_type=jnp.float32)
    return parts[2 * rows :] + parts[rows : 2 * rows] + parts[:rows]


def first_kernel(info, mix_ref, back_ref, resid_ref, base_ref, last_ref):
    base = resid_ref[...].astype(jnp.float32) + weigh(mix_ref, back_ref)
    base_ref[...] = base
    is_last = iota(base.shape, 0) == info[3] - 1
    last_ref[...] = jnp.sum(jnp.where(is_last, base, 0.0), axis=0, keepdims=True)


def last_kernel(mix_ref, base_ref, back_ref, _, told_ref, held, sems):
    size = held.shape[1]
    copies = [
        pltpu.make_async_copy(back_ref.at[k * size : (k + 1) * size], held.at[k], sems.at[k])
        for k in range(held.shape[0])
    ]
    for copy in copies:
        copy.start()
    parts = jnp.zeros((mix_ref.shape[0], held.shape[2]), jnp.float32)
    for k, copy in enumerate(copies):
        copy.wait()
        parts = parts + jnp.dot(
            mix_ref[:, k * size : (k + 1) * size], held[k], preferred_element_type=jnp.float32
        )
    moe = parts[2:3] + parts[1:2] + parts[0:1]
    out = (base_ref[...] + moe).astype(jnp.bfloat16).astype(jnp.float32)
    told_ref[...] = jnp.broadcast_to(out[None], told_ref.shape)


def combine_kernel(info, mix_ref, back_ref, base_ref, _, out_ref, square_ref, squares):
    step = pl.program_id(0)

    @pl.when(step == 0)
    def _():
        squares[...] = jnp.zeros_like(squares)

    out = (base_ref[...] + weigh(mix_ref, back_ref)).astype(jnp.bfloat16)
    out_ref[...] = out
    out_f = out.astype(jnp.float32)
    row = iota(out_f.shape, 0)
    squares[...] += jnp.sum(jnp.where(row < info[3], out_f * out_f, 0.0), axis=0, keepdims=True)

    @pl.when(step == pl.num_programs(0) - 1)
    def _():
        total = jnp.sum(squares[...], axis=1, keepdims=True)
        square_ref[...] = jnp.broadcast_to(total, square_ref.shape)


def place_kernel(info, g_own, g_oth, u_own, u_oth, d_own, d_a, d_b, _, out_ref):
    second_half = pl.program_id(0) >= pl.num_programs(0) // 2
    d_oth = jnp.where(second_half, d_b[...], d_a[...])
    for k, (own, oth) in enumerate(
        ((g_own[...], g_oth[...]), (u_own[...], u_oth[...]), (d_own[...], d_oth))
    ):
        left = info[2] == 0
        out_ref[k, :, :FF] = jnp.where(left, own, oth)
        out_ref[k, :, FF:] = jnp.where(left, oth, own)


def cast_kernel(blocks, x_ref, *refs):
    out_ref, order = refs[-2:]

    @pl.when(pl.program_id(0) == 0)
    def _():
        target = iota(order.shape, 0)
        source = (target & 15) * blocks + lax.shift_right_logical(target, 4)
        order[...] = jnp.where(iota(order.shape, 1) == source, 1.0, 0.0).astype(jnp.bfloat16)

    size = order.shape[0]
    for group in range(x_ref.shape[0] // size):
        x = x_ref[group * size : (group + 1) * size].astype(jnp.bfloat16)
        turned = jnp.dot(order[...], x, preferred_element_type=jnp.float32).astype(jnp.bfloat16)
        for b in range(blocks):
            out_ref[b, group * 16 : (group + 1) * 16] = turned[b * 16 : (b + 1) * 16]


def tie_kernel(*_):
    pass


def params():
    return pltpu.CompilerParams(vmem_limit_bytes=VMEM, dimension_semantics=("arbitrary",))


def whole(shape):
    return pl.BlockSpec(shape, lambda *_: tuple(0 for _ in shape))


def paired(
    hidden_in, lengths, routes, route_weights, norm_gain, master, unembed, final_gain, target_ids
):
    rows = hidden_in.shape[1]
    width = hidden_in.shape[2]
    blk_count = lax.axis_size("blk")
    blk = lax.axis_index("blk")
    rep = lax.axis_index("rep")
    first = blk_count * FIRST
    second = blk_count * SECOND
    resid = hidden_in[0]
    length = lax.dynamic_slice(lengths, (blk,), (1,))
    info = jnp.stack([2 * blk + rep, 2 * blk + 1 - rep, rep, length[0]] + list(RING))
    info = info.astype(jnp.int32)

    shard_rows = master.shape[1]
    flat = master.reshape(3 * shard_rows * blk_count, FF)

    def turned(k, *after):
        return pl.pallas_call(
            functools.partial(cast_kernel, blk_count),
            grid=(2,),
            in_specs=[pl.BlockSpec((shard_rows // 2 * blk_count, FF), lambda i: (2 * k + i, 0))]
            + [pl.BlockSpec(memory_space=pl.ANY)] * len(after),
            out_specs=pl.BlockSpec((blk_count, shard_rows // 2, FF), lambda i: (0, i, 0)),
            out_shape=jax.ShapeDtypeStruct((blk_count, shard_rows, FF), jnp.bfloat16),
            scratch_shapes=[pltpu.VMEM((16 * blk_count, 16 * blk_count), jnp.bfloat16)],
            compiler_params=params(),
            name="cast",
        )(flat, *after)

    def moved(x):
        own = lax.all_to_all(x, "blk", split_axis=0, concat_axis=0, tiled=True)
        return own.reshape(width, FF)

    def swapped(x):
        return lax.ppermute(x, "rep", [(0, 1), (1, 0)])

    def tied(x, *after):
        return pl.pallas_call(
            tie_kernel,
            in_specs=[pl.BlockSpec(memory_space=pl.ANY)] * (1 + len(after)),
            out_specs=pl.BlockSpec(memory_space=pl.ANY),
            out_shape=jax.ShapeDtypeStruct(x.shape, x.dtype),
            input_output_aliases={0: 0},
            name="tie",
        )(x, *after)

    row_ext, pieces = pl.pallas_call(
        prep_kernel,
        grid_spec=pltpu.PrefetchScalarGridSpec(
            num_scalar_prefetch=1,
            grid=(1,),
            in_specs=[
                whole((rows, width)),
                whole((routes.shape[2], rows)),
                whole((routes.shape[2], rows)),
                whole((width,)),
            ],
            out_specs=[whole((rows, width + LANES)), whole((3 * rows, LANES))],
        ),
        out_shape=[
            jax.ShapeDtypeStruct((rows, width + LANES), jnp.bfloat16),
            jax.ShapeDtypeStruct((3 * rows, LANES), jnp.bfloat16),
        ],
        compiler_params=params(),
        name="prep",
    )(length, resid, routes[0].T, route_weights[0].T, norm_gain)
    g_own = moved(turned(0, row_ext))
    g_oth = swapped(g_own)
    u_own = moved(turned(1))
    u_oth = swapped(u_own)
    d_own = moved(tied(turned(2), g_oth))

    tokens = lax.all_gather(row_ext, "blk", axis_index_groups=[list(RING)], axis=0, tiled=True)

    def hidden_of(kernel, sizes, scratch, g, u, *after):
        return pl.pallas_call(
            kernel,
            grid_spec=pltpu.PrefetchScalarGridSpec(
                num_scalar_prefetch=1,
                grid=(GROUPS,),
                in_specs=[pl.BlockSpec((blk_count // GROUPS * rows, width + LANES), lambda i, *_: (i, 0))]
                + [whole((width, FF))] * 2
                + [pl.BlockSpec(memory_space=pl.ANY)] * len(after),
                out_specs=[whole(size) for size in sizes],
                scratch_shapes=[pltpu.VMEM((scratch, width), jnp.float32)],
            ),
            out_shape=[jax.ShapeDtypeStruct(size, jnp.bfloat16) for size in sizes],
            compiler_params=params(),
            name="gate_up",
        )(info, tokens, g, u, *after)

    step = 512

    quarter = width // 4
    in_a = pl.BlockSpec((None, quarter, FF), lambda i, info: (1 - info[2], jnp.minimum(i, 1), 0))
    in_b = pl.BlockSpec((quarter, FF), lambda i, *_: (jnp.maximum(i, 2) - 2, 0))
    anywhere = pl.BlockSpec(memory_space=pl.ANY)

    def returned(x):
        slots = x.shape[0]
        x = x.reshape(blk_count, slots // blk_count, width)
        x = lax.all_to_all(x, "blk", split_axis=0, concat_axis=0, tiled=True)
        return x.reshape(slots, width)

    extra = blk_count * (CAP - FIRST)
    own_hidden, spot = hidden_of(
        own_kernel, ((first + extra, FF), (second, extra)), first + extra, g_own, u_own
    )
    d_own = tied(d_own, own_hidden)
    half = width // 2
    d_oth_a = lax.all_gather(d_own[:half], "rep", axis=0)
    d_oth_b = swapped(d_own[half:])
    own_out, late_out = pl.pallas_call(
        own_down_kernel,
        grid=(width // step,),
        in_specs=[whole((first + extra, FF)), anywhere],
        out_specs=[
            pl.BlockSpec((first, step), lambda i: (0, i)),
            pl.BlockSpec((extra, step), lambda i: (0, i)),
        ],
        out_shape=[
            jax.ShapeDtypeStruct((first, width), jnp.bfloat16),
            jax.ShapeDtypeStruct((extra, width), jnp.bfloat16),
        ],
        scratch_shapes=[
            pltpu.VMEM((width // step, step, FF), jnp.bfloat16),
            pltpu.SemaphoreType.DMA((width // step,)),
        ],
        compiler_params=params(),
        name="own_down",
    )(own_hidden, d_own)
    own_out = tied(own_out, u_oth)
    own_back = returned(own_out)
    (oth_hidden,) = hidden_of(
        oth_kernel, ((second, FF),), second, g_oth, u_oth, own_out
    )
    oth_out = pl.pallas_call(
        oth_down_kernel,
        grid_spec=pltpu.PrefetchScalarGridSpec(
            num_scalar_prefetch=1,
            grid=(4,),
            in_specs=[
                whole((second, FF)),
                whole((second, extra)),
                pl.BlockSpec((extra, quarter), lambda i, *_: (0, i)),
                anywhere,
                anywhere,
            ],
            out_specs=pl.BlockSpec((second, quarter), lambda i, *_: (0, i)),
            scratch_shapes=[
                pltpu.VMEM((4, quarter, FF), jnp.bfloat16),
                pltpu.SemaphoreType.DMA((4,)),
            ],
        ),
        out_shape=jax.ShapeDtypeStruct((second, width), jnp.bfloat16),
        compiler_params=params(),
        name="oth_down",
    )(info, oth_hidden, spot, late_out, d_oth_a, d_oth_b)
    oth_back = returned(oth_out)

    server = pl.pallas_call(
        place_kernel,
        grid_spec=pltpu.PrefetchScalarGridSpec(
            num_scalar_prefetch=1,
            grid=(4,),
            in_specs=[pl.BlockSpec((quarter, FF), lambda i, *_: (i, 0))] * 5
            + [in_a, in_b, pl.BlockSpec(memory_space=pl.ANY)],
            out_specs=pl.BlockSpec((3, quarter, 2 * FF), lambda i, *_: (0, i, 0)),
        ),
        out_shape=jax.ShapeDtypeStruct((3, width, 2 * FF), jnp.bfloat16),
        compiler_params=params(),
        name="place",
    )(info, g_own, g_oth, u_own, u_oth, d_own, d_oth_a, d_oth_b, oth_out)

    first_mix, second_mix, last_mix = pl.pallas_call(
        mix_kernel,
        grid_spec=pltpu.PrefetchScalarGridSpec(
            num_scalar_prefetch=1,
            grid=(1,),
            in_specs=[
                pl.BlockSpec((rows, LANES), lambda i, *_: (0, width // LANES)),
                whole((3 * rows, LANES)),
            ],
            out_specs=[whole((3 * rows, first)), whole((3 * rows, second)), whole((16, second))],
        ),
        out_shape=[
            jax.ShapeDtypeStruct((3 * rows, first), jnp.bfloat16),
            jax.ShapeDtypeStruct((3 * rows, second), jnp.bfloat16),
            jax.ShapeDtypeStruct((16, second), jnp.bfloat16),
        ],
        compiler_params=params(),
        name="mix",
    )(info, row_ext, pieces)

    def weigh_specs(slots):
        return [whole((3 * rows, slots)), pl.BlockSpec((slots, step), lambda i, *_: (0, i))]

    column = pl.BlockSpec((rows, step), lambda i, *_: (0, i))
    lane_row = pl.BlockSpec((1, step), lambda i, *_: (0, i))
    base, last_base = pl.pallas_call(
        first_kernel,
        grid_spec=pltpu.PrefetchScalarGridSpec(
            num_scalar_prefetch=1,
            grid=(width // step,),
            in_specs=weigh_specs(first) + [column],
            out_specs=[column, lane_row],
        ),
        out_shape=[
            jax.ShapeDtypeStruct((rows, width), jnp.float32),
            jax.ShapeDtypeStruct((1, width), jnp.float32),
        ],
        compiler_params=params(),
        name="first",
    )(info, first_mix, own_back, resid)
    told = pl.pallas_call(
        last_kernel,
        grid=(1,),
        in_specs=[whole((16, second)), whole((1, width)), anywhere, anywhere],
        out_specs=whole((blk_count, 1, width)),
        out_shape=jax.ShapeDtypeStruct((blk_count, 1, width), jnp.float32),
        scratch_shapes=[
            pltpu.VMEM((second // LANES, LANES, width), jnp.bfloat16),
            pltpu.SemaphoreType.DMA((second // LANES,)),
        ],
        compiler_params=params(),
        name="last",
    )(last_mix, last_base, oth_back, server)
    out_rows, square = pl.pallas_call(
        combine_kernel,
        grid_spec=pltpu.PrefetchScalarGridSpec(
            num_scalar_prefetch=1,
            grid=(width // step,),
            in_specs=weigh_specs(second) + [column, pl.BlockSpec(memory_space=pl.ANY)],
            out_specs=[column, whole((1, LANES))],
            scratch_shapes=[pltpu.VMEM((1, step), jnp.float32)],
        ),
        out_shape=[
            jax.ShapeDtypeStruct((rows, width), jnp.bfloat16),
            jax.ShapeDtypeStruct((1, LANES), jnp.float32),
        ],
        compiler_params=params(),
        name="combine",
    )(info, second_mix, oth_back, base, told)

    def everywhere(copies):
        return lax.all_to_all(copies, "blk", split_axis=0, concat_axis=0, tiled=True)

    last_rows = everywhere(told)[:, 0]
    final = (
        last_rows
        * lax.rsqrt(jnp.mean(last_rows * last_rows, axis=-1, keepdims=True) + 1e-05)
        * final_gain
    ).astype(jnp.bfloat16)
    logits = lax.dot_general(
        final, unembed, (((1,), (1,)), ((), ())), preferred_element_type=jnp.float32
    )
    vocab_base = blk * unembed.shape[0]
    target_hit = (
        target_ids[:, None] == vocab_base + jnp.arange(unembed.shape[0], dtype=jnp.int32)[None, :]
    )
    target_part = jnp.sum(jnp.where(target_hit, logits, 0.0), axis=1)
    top_part = jnp.max(logits, axis=1)
    prompt = jnp.arange(blk_count, dtype=jnp.int32)
    square_part = jnp.where(prompt == blk, square[0, :blk_count], 0.0)
    stats = jnp.stack([top_part, target_part, square_part])
    parts = everywhere(jnp.broadcast_to(stats[None], (blk_count,) + stats.shape))
    sums = jnp.sum(parts[:, 1:], axis=0)
    norms = jnp.sqrt(sums[1] / (lengths.astype(jnp.float32) * width) + 1e-06)
    request_stats = jnp.stack([norms, jnp.max(parts[:, 0], axis=0), sums[0]])
    return (out_rows[None], server, request_stats)


def local(hidden_in, lengths, routes, route_weights, norm_gain, master, *rest):
    blk_count = lax.axis_size("blk")
    fits = (
        lax.axis_size("rep") == 2
        and master.shape[3] == FF
        and EXPERTS == 2 * blk_count
        and blk_count == len(RING)
        and hidden_in.shape[1] == LEN
        and lengths.shape[0] == blk_count
    )
    form = paired if fits else general
    return form(hidden_in, lengths, routes, route_weights, norm_gain, master, *rest)


def solution(mesh):
    return jax.shard_map(
        local,
        mesh=mesh,
        in_specs=(
            P("rep", "blk", None),
            P("rep"),
            P("rep", "blk", None),
            P("rep", "blk", None),
            P(),
            P(None, "blk", None, "rep"),
            P("blk", None),
            P(),
            P("rep"),
        ),
        out_specs=(P("rep", "blk", None), P(None, None, "blk"), P(None, "rep")),
        check_vma=False,
    )
```

```python
import functools

import jax
import jax.numpy as jnp
from jax import lax
from jax.experimental import pallas as pl
from jax.experimental.pallas import tpu as pltpu
from jax.sharding import PartitionSpec as P

FF = 512
EXPERTS = 32
LEN = 128
CAP = 36
FIRST = 32
SECOND = 40
GROUPS = 4
RING = (0, 1, 4, 5, 8, 9, 12, 13, 14, 15, 10, 11, 6, 7, 2, 3)
LANES = 128
VMEM = 56 * 1024 * 1024


def merged(x, axis, combine):
    everything = jax.tree.map(lambda part: lax.all_gather(part, axis), x)
    initial = jax.tree.map(lambda part: part[0], everything)

    def turn(k, so_far):
        return combine(so_far, jax.tree.map(lambda part: part[k], everything))

    return lax.fori_loop(1, lax.axis_size(axis), turn, initial)


def combine_stats(first, second):
    return (first[0] + second[0], jnp.maximum(first[1], second[1]))


def general(
    hidden_in, lengths, routes, route_weights, norm_gain, master, unembed, final_gain, target_ids
):
    rows_here = hidden_in.shape[1]
    width = hidden_in.shape[2]
    top_count = routes.shape[2]
    blk_count = lax.axis_size("blk")
    rep_count = lax.axis_size("rep")
    blk_index = lax.axis_index("blk")
    unit_count = master.shape[3] * rep_count
    split_ways = max(1, FF // unit_count)
    local_exp = max(1, unit_count // FF)
    group_width = min(unit_count, FF)
    capacity = CAP
    blocks = master.astype(jnp.bfloat16)
    arrived_blocks = lax.all_to_all(blocks, "blk", split_axis=2, concat_axis=1, tiled=True)
    server = lax.all_gather(arrived_blocks, "rep", axis=3, tiled=True)[:, :, 0, :]
    gate_w = server[0].reshape(width, local_exp, group_width)
    up_w = server[1].reshape(width, local_exp, group_width)
    down_w = server[2].reshape(width, local_exp, group_width)
    prompts_here = lengths.shape[0]
    slot_index = blk_index * rows_here + jnp.arange(rows_here, dtype=jnp.int32)
    prompt_of = slot_index // LEN
    position = slot_index % LEN
    prompt_match = prompt_of[:, None] == jnp.arange(prompts_here, dtype=jnp.int32)[None, :]
    row_len = jnp.sum(jnp.where(prompt_match, lengths[None, :], 0), axis=1)
    is_valid = position < row_len
    resid_f = hidden_in[0].astype(jnp.float32)
    normed = (
        resid_f * lax.rsqrt(jnp.mean(resid_f * resid_f, axis=-1, keepdims=True) + 1e-05) * norm_gain
    ).astype(jnp.bfloat16)
    expert_ids = routes[0].reshape(-1)
    pair_live = jnp.repeat(is_valid, top_count)
    pair_row = jnp.repeat(jnp.arange(rows_here, dtype=jnp.int32), top_count)
    expert_hits = (
        (expert_ids[:, None] == jnp.arange(EXPERTS, dtype=jnp.int32)[None, :]) & pair_live[:, None]
    ).astype(jnp.int32)
    slot_rank = jnp.sum((jnp.cumsum(expert_hits, axis=0) - 1) * expert_hits, axis=1)
    slot_id = jnp.where(pair_live, expert_ids * capacity + slot_rank, EXPERTS * capacity)
    source_row = jnp.zeros((EXPERTS * capacity + 1,), jnp.int32).at[slot_id].set(pair_row)[:-1]
    filled = jnp.zeros((EXPERTS * capacity + 1,), jnp.bfloat16).at[slot_id].set(1.0)[:-1]
    outgoing = (normed[source_row] * filled[:, None]).reshape(EXPERTS, capacity, width)
    sending = jnp.repeat(outgoing, split_ways, axis=0).reshape(
        blk_count, local_exp, capacity, width
    )
    arrived = lax.all_to_all(sending, "blk", split_axis=0, concat_axis=0, tiled=True)
    sources = arrived.shape[0]
    slot_count = arrived.shape[2]
    stride = sources
    while stride % 2 == 0 and stride * local_exp * slot_count > 1024:
        stride = stride // 2
    grouped = arrived.reshape(sources // stride, stride, local_exp, slot_count, width)

    def one_block(portion):
        gate_out = jnp.einsum("slnd,dlf->slnf", portion, gate_w, preferred_element_type=jnp.float32)
        up_out = jnp.einsum("slnd,dlf->slnf", portion, up_w, preferred_element_type=jnp.float32)
        hidden = (jax.nn.silu(gate_out) * up_out).astype(jnp.bfloat16)
        return jnp.einsum(
            "slnf,dlf->slnd", hidden, down_w, preferred_element_type=jnp.float32
        ).astype(jnp.bfloat16)

    returned = lax.all_to_all(
        lax.map(one_block, grouped).reshape(sources, local_exp, slot_count, width),
        "blk",
        split_axis=0,
        concat_axis=0,
        tiled=True,
    )
    summed_f = jnp.sum(
        returned.reshape(EXPERTS, split_ways, capacity, width).astype(jnp.float32), axis=1
    )
    expert_out = lax.optimization_barrier(summed_f.astype(jnp.bfloat16)).reshape(
        EXPERTS * capacity, width
    )
    gather_index = jnp.where(pair_live, expert_ids * capacity + slot_rank, 0)
    pair_weight = route_weights[0].reshape(-1) * pair_live.astype(jnp.float32)
    moe = jnp.sum(
        (expert_out[gather_index].astype(jnp.float32) * pair_weight[:, None]).reshape(
            rows_here, top_count, width
        ),
        axis=1,
    )
    out_rows = (resid_f + moe).astype(jnp.bfloat16)
    out_f = out_rows.astype(jnp.float32)
    row_squares = jnp.sum(out_f * out_f, axis=-1) * is_valid.astype(jnp.float32)
    square_local = jnp.sum(jnp.where(prompt_match, row_squares[:, None], 0.0), axis=0)
    is_last = is_valid & (position == row_len - 1)
    picker = (prompt_match & is_last[:, None]).astype(jnp.bfloat16)
    last_local = lax.dot_general(
        picker, out_rows, (((0,), (0,)), ((), ())), preferred_element_type=jnp.float32
    )
    last_rows, square_total = lax.psum((last_local, square_local), "blk")
    norms = jnp.sqrt(square_total / (lengths.astype(jnp.float32) * width) + 1e-06)
    final = (
        last_rows
        * lax.rsqrt(jnp.mean(last_rows * last_rows, axis=-1, keepdims=True) + 1e-05)
        * final_gain
    ).astype(jnp.bfloat16)
    logits = lax.dot_general(
        final, unembed, (((1,), (1,)), ((), ())), preferred_element_type=jnp.float32
    )
    vocab_base = blk_index * unembed.shape[0]
    target_hit = (
        target_ids[:, None] == vocab_base + jnp.arange(unembed.shape[0], dtype=jnp.int32)[None, :]
    )
    target_part = jnp.sum(jnp.where(target_hit, logits, 0.0), axis=1)
    top_part = jnp.max(logits, axis=1)
    target_logit, top_logit = merged((target_part, top_part), "blk", combine_stats)
    request_stats = jnp.stack([norms, top_logit, target_logit])
    return (out_rows[None], server, request_stats)


def iota(shape, dim):
    return lax.broadcasted_iota(jnp.int32, shape, dim)


def prep_kernel(length_ref, hidden_ref, routes_ref, weights_ref, gain_ref, rows_ref, pieces_ref):
    rows, width = hidden_ref.shape
    length = length_ref[0]
    x = hidden_ref[...].astype(jnp.float32)
    scale = lax.rsqrt(jnp.mean(x * x, axis=-1, keepdims=True) + 1e-05)
    rows_ref[:, :width] = (x * scale * gain_ref[...][None]).astype(jnp.bfloat16)
    lane = iota((rows, LANES), 1)
    row = iota((rows, LANES), 0)
    hit = jnp.zeros((rows, LANES), jnp.float32)
    weight = jnp.zeros((rows, LANES), jnp.float32)
    named_by = jnp.transpose(routes_ref[...].astype(jnp.float32)).astype(jnp.int32)
    weight_by = jnp.transpose(weights_ref[...])
    for k in range(routes_ref.shape[0]):
        named = named_by[:, k : k + 1] == lane
        hit = hit + jnp.where(named, 1.0, 0.0)
        weight = weight + jnp.where(named, weight_by[:, k : k + 1], 0.0)
    live = row < length
    hit = jnp.where(live, hit, 0.0)
    weight = jnp.where(live, weight, 0.0)
    before = jnp.where(iota((rows, rows), 1) < iota((rows, rows), 0), 1.0, 0.0)
    rank = jnp.dot(
        before.astype(jnp.bfloat16), hit.astype(jnp.bfloat16), preferred_element_type=jnp.float32
    )
    rows_ref[:, width:] = jnp.where(hit > 0.0, rank, -1.0).astype(jnp.bfloat16)
    for k in range(3):
        piece = weight.astype(jnp.bfloat16)
        pieces_ref[k * rows : (k + 1) * rows, :] = piece
        weight = weight - piece.astype(jnp.float32)


def pick(info, which, x_ref, width, place, slots):
    rows = x_ref.shape[0]
    ranks = x_ref[:, width:].astype(jnp.float32)
    lane = iota((rows, LANES), 1)
    source = (iota((rows, 1), 0) // LEN).astype(jnp.float32)
    rank = jnp.sum(jnp.where(lane == info[which], ranks, 0.0), axis=1, keepdims=True)
    slot = jnp.where(rank >= 0.0, place(source, rank), -1.0)
    slot_lane = iota((rows, slots), 1).astype(jnp.float32)
    one_hot = jnp.where(slot == slot_lane, 1.0, 0.0).astype(jnp.bfloat16)
    return lax.dot_general(
        one_hot, x_ref[:, :width], (((0,), (0,)), ((), ())), preferred_element_type=jnp.float32
    )


def activ(x, g_ref, u_ref):
    x = x.astype(jnp.bfloat16)
    gate = jnp.dot(x, g_ref[...], preferred_element_type=jnp.float32)
    up = jnp.dot(x, u_ref[...], preferred_element_type=jnp.float32)
    return (gate / (1.0 + jnp.exp(-gate)) * up).astype(jnp.bfloat16)


def own_kernel(info, x_ref, g_ref, u_ref, out_ref, spot_ref, picked):
    step = pl.program_id(0)
    sources = x_ref.shape[0] // LEN
    more = CAP - FIRST
    early = sources * FIRST
    all_early = GROUPS * early

    def place(source, rank):
        return jnp.where(
            rank < FIRST, source * FIRST + rank, early + source * more + (rank - FIRST)
        )

    chosen = pick(info, 0, x_ref, g_ref.shape[0], place, early + sources * more)
    for s in range(sources):
        start = pl.multiple_of(info[4 + step * sources + s] * FIRST, FIRST)
        picked[pl.ds(start, FIRST), :] = chosen[s * FIRST : (s + 1) * FIRST]
    start = pl.multiple_of(all_early + step * sources * more, sources * more)
    picked[pl.ds(start, sources * more), :] = chosen[early:]

    @pl.when(step == GROUPS - 1)
    def _():
        out_ref[...] = activ(picked[...], g_ref, u_ref)
        column = iota(spot_ref.shape, 1)
        owner = lax.shift_right_logical(column, more.bit_length() - 1)
        source = jnp.zeros_like(column)
        for k, b in enumerate(RING):
            source = source + jnp.where(owner == k, b, 0)
        spot = source * SECOND + (column & (more - 1))
        spot_ref[...] = jnp.where(iota(spot_ref.shape, 0) == spot, 1.0, 0.0).astype(jnp.bfloat16)


def oth_kernel(info, x_ref, g_ref, u_ref, _, out_ref, picked):
    step = pl.program_id(0)
    sources = x_ref.shape[0] // LEN

    def place(source, rank):
        return source * SECOND + (SECOND - CAP) + rank

    chosen = pick(info, 1, x_ref, g_ref.shape[0], place, sources * SECOND)
    for s in range(sources):
        start = pl.multiple_of(info[4 + step * sources + s] * SECOND, SECOND)
        picked[pl.ds(start, SECOND), :] = chosen[s * SECOND : (s + 1) * SECOND]

    @pl.when(step == GROUPS - 1)
    def _():
        out_ref[...] = activ(picked[...], g_ref, u_ref)


def matmul_nt(hidden_ref, d):
    return lax.dot_general(
        hidden_ref[...], d, (((1,), (1,)), ((), ())), preferred_element_type=jnp.float32
    )


def fetched(sources, held, sems):
    step = pl.program_id(0)
    rows = held.shape[1]

    @pl.when(step == 0)
    def _():
        for k, source in enumerate(sources):
            pltpu.make_async_copy(source, held.at[k], sems.at[k]).start()

    for k, source in enumerate(sources):

        @pl.when(step == k)
        def _():
            pltpu.make_async_copy(source, held.at[k], sems.at[k]).wait()

    return held[step]


def own_down_kernel(hidden_ref, d_ref, out_ref, late_ref, held, sems):
    size = held.shape[1]
    d = fetched([d_ref.at[k * size : (k + 1) * size] for k in range(held.shape[0])], held, sems)
    out = matmul_nt(hidden_ref, d).astype(jnp.bfloat16)
    rows = out_ref.shape[0]
    out_ref[...] = out[:rows]
    late_ref[...] = out[rows:]


def oth_down_kernel(info, hidden_ref, spot_ref, late_ref, d_ref, out_ref, held, sems):
    size = held.shape[1]
    other = 1 - info[2]
    sources = [d_ref.at[other, k * size : (k + 1) * size] for k in range(held.shape[0])]
    d = fetched(sources, held, sems)
    late = jnp.dot(spot_ref[...], late_ref[...], preferred_element_type=jnp.float32)
    out_ref[...] = (late + matmul_nt(hidden_ref, d)).astype(jnp.bfloat16)


def mix_kernel(info, rank_ref, pieces_ref, first_ref, second_ref, last_ref):
    rows = rank_ref.shape[0]
    late = SECOND - CAP
    own, oth = info[2], 1 - info[2]
    for mix_ref, stride, spans in (
        (first_ref, FIRST, ((own, 0, FIRST, 0),)),
        (second_ref, SECOND, ((own, 0, late, FIRST), (oth, late, CAP, 0))),
    ):
        slots = mix_ref.shape[1]
        expert = iota((LANES, slots), 0)
        lane = iota((LANES, slots), 1)
        within = jnp.zeros((1, slots), jnp.float32)
        spread = jnp.zeros((LANES, slots), jnp.float32)
        for parity, offset, count, lowest in spans:
            start = jnp.where((expert & 1) == parity, (expert >> 1) * stride + offset, slots)
            inside = (lane >= start) & (lane < start + count)
            spread = spread + jnp.where(inside, 1.0, 0.0)
            ranks = jnp.where(inside, lane - start + lowest, 0)
            within = within + jnp.sum(ranks, axis=0, keepdims=True).astype(jnp.float32)
        spread = spread.astype(jnp.bfloat16)
        rank = jnp.dot(rank_ref[...], spread, preferred_element_type=jnp.float32)
        match = rank == within
        for k in range(3):
            part = jnp.dot(
                pieces_ref[k * rows : (k + 1) * rows, :], spread, preferred_element_type=jnp.float32
            )
            mix_ref[k * rows : (k + 1) * rows, :] = jnp.where(match, part, 0.0).astype(jnp.bfloat16)
    shape = (last_ref.shape[0], 3 * rows)
    one_hot = jnp.where(iota(shape, 1) == iota(shape, 0) * rows + info[3] - 1, 1.0, 0.0)
    last_ref[...] = jnp.dot(
        one_hot.astype(jnp.bfloat16), second_ref[...], preferred_element_type=jnp.float32
    ).astype(jnp.bfloat16)


def weigh(mix_ref, back_ref):
    rows = mix_ref.shape[0] // 3
    parts = jnp.dot(mix_ref[...], back_ref[...], preferred_element_type=jnp.float32)
    return parts[2 * rows :] + parts[rows : 2 * rows] + parts[:rows]


def first_kernel(info, mix_ref, back_ref, resid_ref, base_ref, last_ref):
    base = resid_ref[...].astype(jnp.float32) + weigh(mix_ref, back_ref)
    base_ref[...] = base
    is_last = iota(base.shape, 0) == info[3] - 1
    last_ref[...] = jnp.sum(jnp.where(is_last, base, 0.0), axis=0, keepdims=True)


def last_kernel(mix_ref, base_ref, back_ref, _, told_ref, held, sems):
    size = held.shape[1]
    copies = [
        pltpu.make_async_copy(back_ref.at[k * size : (k + 1) * size], held.at[k], sems.at[k])
        for k in range(held.shape[0])
    ]
    for copy in copies:
        copy.start()
    parts = jnp.zeros((mix_ref.shape[0], held.shape[2]), jnp.float32)
    for k, copy in enumerate(copies):
        copy.wait()
        parts = parts + jnp.dot(
            mix_ref[:, k * size : (k + 1) * size], held[k], preferred_element_type=jnp.float32
        )
    moe = parts[2:3] + parts[1:2] + parts[0:1]
    out = (base_ref[...] + moe).astype(jnp.bfloat16).astype(jnp.float32)
    told_ref[...] = jnp.broadcast_to(out[None], told_ref.shape)


def combine_kernel(info, mix_ref, back_ref, base_ref, _, out_ref, square_ref, squares):
    step = pl.program_id(0)

    @pl.when(step == 0)
    def _():
        squares[...] = jnp.zeros_like(squares)

    out = (base_ref[...] + weigh(mix_ref, back_ref)).astype(jnp.bfloat16)
    out_ref[...] = out
    out_f = out.astype(jnp.float32)
    row = iota(out_f.shape, 0)
    squares[...] += jnp.sum(jnp.where(row < info[3], out_f * out_f, 0.0), axis=0, keepdims=True)

    @pl.when(step == pl.num_programs(0) - 1)
    def _():
        total = jnp.sum(squares[...], axis=1, keepdims=True)
        square_ref[...] = jnp.broadcast_to(total, square_ref.shape)


def place_kernel(info, g_own, g_oth, u_own, u_oth, d_both, _, out_ref):
    left = info[2] == 0
    for k, (own, oth) in enumerate(((g_own[...], g_oth[...]), (u_own[...], u_oth[...]))):
        out_ref[k, :, :FF] = jnp.where(left, own, oth)
        out_ref[k, :, FF:] = jnp.where(left, oth, own)
    out_ref[2, :, :FF] = d_both[0]
    out_ref[2, :, FF:] = d_both[1]


def cast_kernel(first_row, blocks, x_ref, *refs):
    out_ref, held, turned, sems_in, sems_out = refs[-5:]
    groups, size = held.shape[:2]
    fetches, stores = [], []
    for g in range(groups):
        rows = pl.ds(first_row + g * size, size)
        fetches.append(pltpu.make_async_copy(x_ref.at[rows], held.at[g], sems_in.at[g]))
        target = out_ref.at[:, g * 16 : (g + 1) * 16]
        stores.append(pltpu.make_async_copy(turned.at[g], target, sems_out.at[g]))
    for fetch in fetches:
        fetch.start()
    target = iota((size, size), 0)
    source = (target & 15) * blocks + lax.shift_right_logical(target, 4)
    order = jnp.where(iota((size, size), 1) == source, 1.0, 0.0).astype(jnp.bfloat16)
    for g in range(groups):
        fetches[g].wait()
        rows = jnp.dot(order, held[g].astype(jnp.bfloat16), preferred_element_type=jnp.float32)
        turned[g] = rows.astype(jnp.bfloat16).reshape(turned.shape[1:])
        stores[g].start()
    for store in stores:
        store.wait()


def tie_kernel(*_):
    pass


def params():
    return pltpu.CompilerParams(vmem_limit_bytes=VMEM, dimension_semantics=("arbitrary",))


def whole(shape):
    return pl.BlockSpec(shape, lambda *_: tuple(0 for _ in shape))


def paired(
    hidden_in, lengths, routes, route_weights, norm_gain, master, unembed, final_gain, target_ids
):
    rows = hidden_in.shape[1]
    width = hidden_in.shape[2]
    blk_count = lax.axis_size("blk")
    blk = lax.axis_index("blk")
    rep = lax.axis_index("rep")
    first = blk_count * FIRST
    second = blk_count * SECOND
    resid = hidden_in[0]
    length = lax.dynamic_slice(lengths, (blk,), (1,))
    info = jnp.stack([2 * blk + rep, 2 * blk + 1 - rep, rep, length[0]] + list(RING))
    info = info.astype(jnp.int32)

    shard_rows = master.shape[1]
    flat = master.reshape(3 * shard_rows * blk_count, FF)

    groups = shard_rows // 16

    def turned(k, *after):
        return pl.pallas_call(
            functools.partial(cast_kernel, k * shard_rows * blk_count, blk_count),
            in_specs=[pl.BlockSpec(memory_space=pl.ANY)] * (1 + len(after)),
            out_specs=pl.BlockSpec(memory_space=pl.ANY),
            out_shape=jax.ShapeDtypeStruct((blk_count, shard_rows, FF), jnp.bfloat16),
            scratch_shapes=[
                pltpu.VMEM((groups, 16 * blk_count, FF), jnp.float32),
                pltpu.VMEM((groups, blk_count, 16, FF), jnp.bfloat16),
                pltpu.SemaphoreType.DMA((groups,)),
                pltpu.SemaphoreType.DMA((groups,)),
            ],
            compiler_params=pltpu.CompilerParams(vmem_limit_bytes=VMEM),
            name="cast",
        )(flat, *after)

    def moved(x):
        own = lax.all_to_all(x, "blk", split_axis=0, concat_axis=0, tiled=True)
        return own.reshape(width, FF)

    def swapped(x):
        return lax.ppermute(x, "rep", [(0, 1), (1, 0)])

    def tied(x, *after):
        return pl.pallas_call(
            tie_kernel,
            in_specs=[pl.BlockSpec(memory_space=pl.ANY)] * (1 + len(after)),
            out_specs=pl.BlockSpec(memory_space=pl.ANY),
            out_shape=jax.ShapeDtypeStruct(x.shape, x.dtype),
            input_output_aliases={0: 0},
            name="tie",
        )(x, *after)

    row_ext, pieces = pl.pallas_call(
        prep_kernel,
        grid_spec=pltpu.PrefetchScalarGridSpec(
            num_scalar_prefetch=1,
            grid=(1,),
            in_specs=[
                whole((rows, width)),
                whole((routes.shape[2], rows)),
                whole((routes.shape[2], rows)),
                whole((width,)),
            ],
            out_specs=[whole((rows, width + LANES)), whole((3 * rows, LANES))],
        ),
        out_shape=[
            jax.ShapeDtypeStruct((rows, width + LANES), jnp.bfloat16),
            jax.ShapeDtypeStruct((3 * rows, LANES), jnp.bfloat16),
        ],
        compiler_params=params(),
        name="prep",
    )(length, resid, routes[0].T, route_weights[0].T, norm_gain)
    g_own = moved(turned(0, row_ext))
    g_oth = swapped(g_own)
    u_own = moved(turned(1))
    u_oth = swapped(u_own)
    d_own = moved(tied(turned(2), g_oth))

    tokens = lax.all_gather(row_ext, "blk", axis_index_groups=[list(RING)], axis=0, tiled=True)

    def hidden_of(kernel, sizes, scratch, g, u, *after):
        return pl.pallas_call(
            kernel,
            grid_spec=pltpu.PrefetchScalarGridSpec(
                num_scalar_prefetch=1,
                grid=(GROUPS,),
                in_specs=[pl.BlockSpec((blk_count // GROUPS * rows, width + LANES), lambda i, *_: (i, 0))]
                + [whole((width, FF))] * 2
                + [pl.BlockSpec(memory_space=pl.ANY)] * len(after),
                out_specs=[whole(size) for size in sizes],
                scratch_shapes=[pltpu.VMEM((scratch, width), jnp.float32)],
            ),
            out_shape=[jax.ShapeDtypeStruct(size, jnp.bfloat16) for size in sizes],
            compiler_params=params(),
            name="gate_up",
        )(info, tokens, g, u, *after)

    step = 512

    quarter = width // 4
    anywhere = pl.BlockSpec(memory_space=pl.ANY)

    def returned(x):
        slots = x.shape[0]
        x = x.reshape(blk_count, slots // blk_count, width)
        x = lax.all_to_all(x, "blk", split_axis=0, concat_axis=0, tiled=True)
        return x.reshape(slots, width)

    extra = blk_count * (CAP - FIRST)
    own_hidden, spot = hidden_of(
        own_kernel, ((first + extra, FF), (second, extra)), first + extra, g_own, u_own
    )
    d_own = tied(d_own, own_hidden)
    d_both = lax.all_gather(d_own, "rep", axis=0)
    own_out, late_out = pl.pallas_call(
        own_down_kernel,
        grid=(width // step,),
        in_specs=[whole((first + extra, FF)), anywhere],
        out_specs=[
            pl.BlockSpec((first, step), lambda i: (0, i)),
            pl.BlockSpec((extra, step), lambda i: (0, i)),
        ],
        out_shape=[
            jax.ShapeDtypeStruct((first, width), jnp.bfloat16),
            jax.ShapeDtypeStruct((extra, width), jnp.bfloat16),
        ],
        scratch_shapes=[
            pltpu.VMEM((width // step, step, FF), jnp.bfloat16),
            pltpu.SemaphoreType.DMA((width // step,)),
        ],
        compiler_params=params(),
        name="own_down",
    )(own_hidden, d_own)
    own_out = tied(own_out, u_oth)
    own_back = returned(own_out)
    (oth_hidden,) = hidden_of(
        oth_kernel, ((second, FF),), second, g_oth, u_oth, own_out
    )
    oth_out = pl.pallas_call(
        oth_down_kernel,
        grid_spec=pltpu.PrefetchScalarGridSpec(
            num_scalar_prefetch=1,
            grid=(4,),
            in_specs=[
                whole((second, FF)),
                whole((second, extra)),
                pl.BlockSpec((extra, quarter), lambda i, *_: (0, i)),
                anywhere,
            ],
            out_specs=pl.BlockSpec((second, quarter), lambda i, *_: (0, i)),
            scratch_shapes=[
                pltpu.VMEM((4, quarter, FF), jnp.bfloat16),
                pltpu.SemaphoreType.DMA((4,)),
            ],
        ),
        out_shape=jax.ShapeDtypeStruct((second, width), jnp.bfloat16),
        compiler_params=params(),
        name="oth_down",
    )(info, oth_hidden, spot, late_out, d_both)
    oth_back = returned(oth_out)

    server = pl.pallas_call(
        place_kernel,
        grid_spec=pltpu.PrefetchScalarGridSpec(
            num_scalar_prefetch=1,
            grid=(4,),
            in_specs=[pl.BlockSpec((quarter, FF), lambda i, *_: (i, 0))] * 4
            + [pl.BlockSpec((2, quarter, FF), lambda i, *_: (0, i, 0)), anywhere],
            out_specs=pl.BlockSpec((3, quarter, 2 * FF), lambda i, *_: (0, i, 0)),
        ),
        out_shape=jax.ShapeDtypeStruct((3, width, 2 * FF), jnp.bfloat16),
        compiler_params=params(),
        name="place",
    )(info, g_own, g_oth, u_own, u_oth, d_both, oth_out)

    first_mix, second_mix, last_mix = pl.pallas_call(
        mix_kernel,
        grid_spec=pltpu.PrefetchScalarGridSpec(
            num_scalar_prefetch=1,
            grid=(1,),
            in_specs=[
                pl.BlockSpec((rows, LANES), lambda i, *_: (0, width // LANES)),
                whole((3 * rows, LANES)),
            ],
            out_specs=[whole((3 * rows, first)), whole((3 * rows, second)), whole((16, second))],
        ),
        out_shape=[
            jax.ShapeDtypeStruct((3 * rows, first), jnp.bfloat16),
            jax.ShapeDtypeStruct((3 * rows, second), jnp.bfloat16),
            jax.ShapeDtypeStruct((16, second), jnp.bfloat16),
        ],
        compiler_params=params(),
        name="mix",
    )(info, row_ext, pieces)

    def weigh_specs(slots):
        return [whole((3 * rows, slots)), pl.BlockSpec((slots, step), lambda i, *_: (0, i))]

    column = pl.BlockSpec((rows, step), lambda i, *_: (0, i))
    lane_row = pl.BlockSpec((1, step), lambda i, *_: (0, i))
    base, last_base = pl.pallas_call(
        first_kernel,
        grid_spec=pltpu.PrefetchScalarGridSpec(
            num_scalar_prefetch=1,
            grid=(width // step,),
            in_specs=weigh_specs(first) + [column],
            out_specs=[column, lane_row],
        ),
        out_shape=[
            jax.ShapeDtypeStruct((rows, width), jnp.float32),
            jax.ShapeDtypeStruct((1, width), jnp.float32),
        ],
        compiler_params=params(),
        name="first",
    )(info, first_mix, own_back, resid)
    told = pl.pallas_call(
        last_kernel,
        grid=(1,),
        in_specs=[whole((16, second)), whole((1, width)), anywhere, anywhere],
        out_specs=whole((blk_count, 1, width)),
        out_shape=jax.ShapeDtypeStruct((blk_count, 1, width), jnp.float32),
        scratch_shapes=[
            pltpu.VMEM((second // LANES, LANES, width), jnp.bfloat16),
            pltpu.SemaphoreType.DMA((second // LANES,)),
        ],
        compiler_params=params(),
        name="last",
    )(last_mix, last_base, oth_back, server)
    out_rows, square = pl.pallas_call(
        combine_kernel,
        grid_spec=pltpu.PrefetchScalarGridSpec(
            num_scalar_prefetch=1,
            grid=(width // step,),
            in_specs=weigh_specs(second) + [column, pl.BlockSpec(memory_space=pl.ANY)],
            out_specs=[column, whole((1, LANES))],
            scratch_shapes=[pltpu.VMEM((1, step), jnp.float32)],
        ),
        out_shape=[
            jax.ShapeDtypeStruct((rows, width), jnp.bfloat16),
            jax.ShapeDtypeStruct((1, LANES), jnp.float32),
        ],
        compiler_params=params(),
        name="combine",
    )(info, second_mix, oth_back, base, told)

    def everywhere(copies):
        return lax.all_to_all(copies, "blk", split_axis=0, concat_axis=0, tiled=True)

    last_rows = everywhere(told)[:, 0]
    final = (
        last_rows
        * lax.rsqrt(jnp.mean(last_rows * last_rows, axis=-1, keepdims=True) + 1e-05)
        * final_gain
    ).astype(jnp.bfloat16)
    logits = lax.dot_general(
        final, unembed, (((1,), (1,)), ((), ())), preferred_element_type=jnp.float32
    )
    vocab_base = blk * unembed.shape[0]
    target_hit = (
        target_ids[:, None] == vocab_base + jnp.arange(unembed.shape[0], dtype=jnp.int32)[None, :]
    )
    target_part = jnp.sum(jnp.where(target_hit, logits, 0.0), axis=1)
    top_part = jnp.max(logits, axis=1)
    prompt = jnp.arange(blk_count, dtype=jnp.int32)
    square_part = jnp.where(prompt == blk, square[0, :blk_count], 0.0)
    stats = jnp.stack([top_part, target_part, square_part])
    parts = everywhere(jnp.broadcast_to(stats[None], (blk_count,) + stats.shape))
    sums = jnp.sum(parts[:, 1:], axis=0)
    norms = jnp.sqrt(sums[1] / (lengths.astype(jnp.float32) * width) + 1e-06)
    request_stats = jnp.stack([norms, jnp.max(parts[:, 0], axis=0), sums[0]])
    return (out_rows[None], server, request_stats)


def local(hidden_in, lengths, routes, route_weights, norm_gain, master, *rest):
    blk_count = lax.axis_size("blk")
    fits = (
        lax.axis_size("rep") == 2
        and master.shape[3] == FF
        and EXPERTS == 2 * blk_count
        and blk_count == len(RING)
        and hidden_in.shape[1] == LEN
        and lengths.shape[0] == blk_count
    )
    form = paired if fits else general
    return form(hidden_in, lengths, routes, route_weights, norm_gain, master, *rest)


def solution(mesh):
    return jax.shard_map(
        local,
        mesh=mesh,
        in_specs=(
            P("rep", "blk", None),
            P("rep"),
            P("rep", "blk", None),
            P("rep", "blk", None),
            P(),
            P(None, "blk", None, "rep"),
            P("blk", None),
            P(),
            P("rep"),
        ),
        out_specs=(P("rep", "blk", None), P(None, None, "blk"), P(None, "rep")),
        check_vma=False,
    )
```

```python
import functools

import jax
import jax.numpy as jnp
from jax import lax
from jax.experimental import pallas as pl
from jax.experimental.pallas import tpu as pltpu
from jax.sharding import PartitionSpec as P

FF = 512
EXPERTS = 32
LEN = 128
CAP = 36
FIRST = 32
SECOND = 40
GROUPS = 4
RING = (0, 1, 4, 5, 8, 9, 12, 13, 14, 15, 10, 11, 6, 7, 2, 3)
LANES = 128
VMEM = 56 * 1024 * 1024


def merged(x, axis, combine):
    everything = jax.tree.map(lambda part: lax.all_gather(part, axis), x)
    initial = jax.tree.map(lambda part: part[0], everything)

    def turn(k, so_far):
        return combine(so_far, jax.tree.map(lambda part: part[k], everything))

    return lax.fori_loop(1, lax.axis_size(axis), turn, initial)


def combine_stats(first, second):
    return (first[0] + second[0], jnp.maximum(first[1], second[1]))


def general(
    hidden_in, lengths, routes, route_weights, norm_gain, master, unembed, final_gain, target_ids
):
    rows_here = hidden_in.shape[1]
    width = hidden_in.shape[2]
    top_count = routes.shape[2]
    blk_count = lax.axis_size("blk")
    rep_count = lax.axis_size("rep")
    blk_index = lax.axis_index("blk")
    unit_count = master.shape[3] * rep_count
    split_ways = max(1, FF // unit_count)
    local_exp = max(1, unit_count // FF)
    group_width = min(unit_count, FF)
    capacity = CAP
    blocks = master.astype(jnp.bfloat16)
    arrived_blocks = lax.all_to_all(blocks, "blk", split_axis=2, concat_axis=1, tiled=True)
    server = lax.all_gather(arrived_blocks, "rep", axis=3, tiled=True)[:, :, 0, :]
    gate_w = server[0].reshape(width, local_exp, group_width)
    up_w = server[1].reshape(width, local_exp, group_width)
    down_w = server[2].reshape(width, local_exp, group_width)
    prompts_here = lengths.shape[0]
    slot_index = blk_index * rows_here + jnp.arange(rows_here, dtype=jnp.int32)
    prompt_of = slot_index // LEN
    position = slot_index % LEN
    prompt_match = prompt_of[:, None] == jnp.arange(prompts_here, dtype=jnp.int32)[None, :]
    row_len = jnp.sum(jnp.where(prompt_match, lengths[None, :], 0), axis=1)
    is_valid = position < row_len
    resid_f = hidden_in[0].astype(jnp.float32)
    normed = (
        resid_f * lax.rsqrt(jnp.mean(resid_f * resid_f, axis=-1, keepdims=True) + 1e-05) * norm_gain
    ).astype(jnp.bfloat16)
    expert_ids = routes[0].reshape(-1)
    pair_live = jnp.repeat(is_valid, top_count)
    pair_row = jnp.repeat(jnp.arange(rows_here, dtype=jnp.int32), top_count)
    expert_hits = (
        (expert_ids[:, None] == jnp.arange(EXPERTS, dtype=jnp.int32)[None, :]) & pair_live[:, None]
    ).astype(jnp.int32)
    slot_rank = jnp.sum((jnp.cumsum(expert_hits, axis=0) - 1) * expert_hits, axis=1)
    slot_id = jnp.where(pair_live, expert_ids * capacity + slot_rank, EXPERTS * capacity)
    source_row = jnp.zeros((EXPERTS * capacity + 1,), jnp.int32).at[slot_id].set(pair_row)[:-1]
    filled = jnp.zeros((EXPERTS * capacity + 1,), jnp.bfloat16).at[slot_id].set(1.0)[:-1]
    outgoing = (normed[source_row] * filled[:, None]).reshape(EXPERTS, capacity, width)
    sending = jnp.repeat(outgoing, split_ways, axis=0).reshape(
        blk_count, local_exp, capacity, width
    )
    arrived = lax.all_to_all(sending, "blk", split_axis=0, concat_axis=0, tiled=True)
    sources = arrived.shape[0]
    slot_count = arrived.shape[2]
    stride = sources
    while stride % 2 == 0 and stride * local_exp * slot_count > 1024:
        stride = stride // 2
    grouped = arrived.reshape(sources // stride, stride, local_exp, slot_count, width)

    def one_block(portion):
        gate_out = jnp.einsum("slnd,dlf->slnf", portion, gate_w, preferred_element_type=jnp.float32)
        up_out = jnp.einsum("slnd,dlf->slnf", portion, up_w, preferred_element_type=jnp.float32)
        hidden = (jax.nn.silu(gate_out) * up_out).astype(jnp.bfloat16)
        return jnp.einsum(
            "slnf,dlf->slnd", hidden, down_w, preferred_element_type=jnp.float32
        ).astype(jnp.bfloat16)

    returned = lax.all_to_all(
        lax.map(one_block, grouped).reshape(sources, local_exp, slot_count, width),
        "blk",
        split_axis=0,
        concat_axis=0,
        tiled=True,
    )
    summed_f = jnp.sum(
        returned.reshape(EXPERTS, split_ways, capacity, width).astype(jnp.float32), axis=1
    )
    expert_out = lax.optimization_barrier(summed_f.astype(jnp.bfloat16)).reshape(
        EXPERTS * capacity, width
    )
    gather_index = jnp.where(pair_live, expert_ids * capacity + slot_rank, 0)
    pair_weight = route_weights[0].reshape(-1) * pair_live.astype(jnp.float32)
    moe = jnp.sum(
        (expert_out[gather_index].astype(jnp.float32) * pair_weight[:, None]).reshape(
            rows_here, top_count, width
        ),
        axis=1,
    )
    out_rows = (resid_f + moe).astype(jnp.bfloat16)
    out_f = out_rows.astype(jnp.float32)
    row_squares = jnp.sum(out_f * out_f, axis=-1) * is_valid.astype(jnp.float32)
    square_local = jnp.sum(jnp.where(prompt_match, row_squares[:, None], 0.0), axis=0)
    is_last = is_valid & (position == row_len - 1)
    picker = (prompt_match & is_last[:, None]).astype(jnp.bfloat16)
    last_local = lax.dot_general(
        picker, out_rows, (((0,), (0,)), ((), ())), preferred_element_type=jnp.float32
    )
    last_rows, square_total = lax.psum((last_local, square_local), "blk")
    norms = jnp.sqrt(square_total / (lengths.astype(jnp.float32) * width) + 1e-06)
    final = (
        last_rows
        * lax.rsqrt(jnp.mean(last_rows * last_rows, axis=-1, keepdims=True) + 1e-05)
        * final_gain
    ).astype(jnp.bfloat16)
    logits = lax.dot_general(
        final, unembed, (((1,), (1,)), ((), ())), preferred_element_type=jnp.float32
    )
    vocab_base = blk_index * unembed.shape[0]
    target_hit = (
        target_ids[:, None] == vocab_base + jnp.arange(unembed.shape[0], dtype=jnp.int32)[None, :]
    )
    target_part = jnp.sum(jnp.where(target_hit, logits, 0.0), axis=1)
    top_part = jnp.max(logits, axis=1)
    target_logit, top_logit = merged((target_part, top_part), "blk", combine_stats)
    request_stats = jnp.stack([norms, top_logit, target_logit])
    return (out_rows[None], server, request_stats)


def iota(shape, dim):
    return lax.broadcasted_iota(jnp.int32, shape, dim)


def prep_kernel(lengths_ref, blk_ref, hidden_ref, routes_ref, weights_ref, gain_ref, rows_ref, pieces_ref):
    rows, width = hidden_ref.shape
    length = lengths_ref[blk_ref[0]]
    x = hidden_ref[...].astype(jnp.float32)
    scale = lax.rsqrt(jnp.mean(x * x, axis=-1, keepdims=True) + 1e-05)
    rows_ref[:, :width] = (x * scale * gain_ref[...][None]).astype(jnp.bfloat16)
    lane = iota((rows, LANES), 1)
    row = iota((rows, LANES), 0)
    hit = jnp.zeros((rows, LANES), jnp.float32)
    weight = jnp.zeros((rows, LANES), jnp.float32)
    named_by = jnp.transpose(routes_ref[...].astype(jnp.float32)).astype(jnp.int32)
    weight_by = jnp.transpose(weights_ref[...])
    for k in range(routes_ref.shape[0]):
        named = named_by[:, k : k + 1] == lane
        hit = hit + jnp.where(named, 1.0, 0.0)
        weight = weight + jnp.where(named, weight_by[:, k : k + 1], 0.0)
    live = row < length
    hit = jnp.where(live, hit, 0.0)
    weight = jnp.where(live, weight, 0.0)
    before = jnp.where(iota((rows, rows), 1) < iota((rows, rows), 0), 1.0, 0.0)
    rank = jnp.dot(
        before.astype(jnp.bfloat16), hit.astype(jnp.bfloat16), preferred_element_type=jnp.float32
    )
    rows_ref[:, width:] = jnp.where(hit > 0.0, rank, -1.0).astype(jnp.bfloat16)
    for k in range(3):
        piece = weight.astype(jnp.bfloat16)
        pieces_ref[k * rows : (k + 1) * rows, :] = piece
        weight = weight - piece.astype(jnp.float32)


def pick(info, which, x_ref, width, place, slots):
    rows = x_ref.shape[0]
    ranks = x_ref[:, width:].astype(jnp.float32)
    lane = iota((rows, LANES), 1)
    source = (iota((rows, 1), 0) // LEN).astype(jnp.float32)
    rank = jnp.sum(jnp.where(lane == info[which], ranks, 0.0), axis=1, keepdims=True)
    slot = jnp.where(rank >= 0.0, place(source, rank), -1.0)
    slot_lane = iota((rows, slots), 1).astype(jnp.float32)
    one_hot = jnp.where(slot == slot_lane, 1.0, 0.0).astype(jnp.bfloat16)
    return lax.dot_general(
        one_hot, x_ref[:, :width], (((0,), (0,)), ((), ())), preferred_element_type=jnp.float32
    )


def activ(x, g_ref, u_ref):
    x = x.astype(jnp.bfloat16)
    gate = jnp.dot(x, g_ref[...], preferred_element_type=jnp.float32)
    up = jnp.dot(x, u_ref[...], preferred_element_type=jnp.float32)
    return (gate / (1.0 + jnp.exp(-gate)) * up).astype(jnp.bfloat16)


def own_kernel(info, x_ref, g_ref, u_ref, out_ref, spot_ref, picked):
    step = pl.program_id(0)
    sources = x_ref.shape[0] // LEN
    more = CAP - FIRST
    early = sources * FIRST
    all_early = GROUPS * early

    def place(source, rank):
        return jnp.where(
            rank < FIRST, source * FIRST + rank, early + source * more + (rank - FIRST)
        )

    chosen = pick(info, 0, x_ref, g_ref.shape[0], place, early + sources * more)
    for s in range(sources):
        start = pl.multiple_of(info[4 + step * sources + s] * FIRST, FIRST)
        picked[pl.ds(start, FIRST), :] = chosen[s * FIRST : (s + 1) * FIRST]
    start = pl.multiple_of(all_early + step * sources * more, sources * more)
    picked[pl.ds(start, sources * more), :] = chosen[early:]

    @pl.when(step == GROUPS - 1)
    def _():
        out_ref[...] = activ(picked[...], g_ref, u_ref)
        column = iota(spot_ref.shape, 1)
        owner = lax.shift_right_logical(column, more.bit_length() - 1)
        source = jnp.zeros_like(column)
        for k, b in enumerate(RING):
            source = source + jnp.where(owner == k, b, 0)
        spot = source * SECOND + (column & (more - 1))
        spot_ref[...] = jnp.where(iota(spot_ref.shape, 0) == spot, 1.0, 0.0).astype(jnp.bfloat16)


def oth_kernel(info, x_ref, g_ref, u_ref, _, out_ref, picked):
    step = pl.program_id(0)
    sources = x_ref.shape[0] // LEN

    def place(source, rank):
        return source * SECOND + (SECOND - CAP) + rank

    chosen = pick(info, 1, x_ref, g_ref.shape[0], place, sources * SECOND)
    for s in range(sources):
        start = pl.multiple_of(info[4 + step * sources + s] * SECOND, SECOND)
        picked[pl.ds(start, SECOND), :] = chosen[s * SECOND : (s + 1) * SECOND]

    @pl.when(step == GROUPS - 1)
    def _():
        out_ref[...] = activ(picked[...], g_ref, u_ref)


def matmul_nt(hidden_ref, d):
    return lax.dot_general(
        hidden_ref[...], d, (((1,), (1,)), ((), ())), preferred_element_type=jnp.float32
    )


def fetched(sources, held, sems):
    step = pl.program_id(0)
    rows = held.shape[1]

    @pl.when(step == 0)
    def _():
        for k, source in enumerate(sources):
            pltpu.make_async_copy(source, held.at[k], sems.at[k]).start()

    for k, source in enumerate(sources):

        @pl.when(step == k)
        def _():
            pltpu.make_async_copy(source, held.at[k], sems.at[k]).wait()

    return held[step]


def own_down_kernel(hidden_ref, d_ref, out_ref, late_ref, a_ref, b_ref, held, sems):
    step = pl.program_id(0)
    size = held.shape[1]
    d = fetched([d_ref.at[k * size : (k + 1) * size] for k in range(held.shape[0])], held, sems)

    @pl.when(step < held.shape[0] // 2)
    def _():
        a_ref[...] = d

    @pl.when(step >= held.shape[0] // 2)
    def _():
        b_ref[...] = d

    out = matmul_nt(hidden_ref, d).astype(jnp.bfloat16)
    rows = out_ref.shape[0]
    out_ref[...] = out[:rows]
    late_ref[...] = out[rows:]


def oth_down_kernel(info, hidden_ref, spot_ref, late_ref, d_a, d_b, out_ref, held, sems):
    size = held.shape[1]
    other = 1 - info[2]
    sources = [d_a.at[other, :size], d_a.at[other, size:], d_b.at[:size], d_b.at[size:]]
    d = fetched(sources, held, sems)
    late = jnp.dot(spot_ref[...], late_ref[...], preferred_element_type=jnp.float32)
    out_ref[...] = (late + matmul_nt(hidden_ref, d)).astype(jnp.bfloat16)


def mix_kernel(info, rank_ref, pieces_ref, first_ref, second_ref, last_ref):
    rows = rank_ref.shape[0]
    late = SECOND - CAP
    own, oth = info[2], 1 - info[2]
    for mix_ref, stride, spans in (
        (first_ref, FIRST, ((own, 0, FIRST, 0),)),
        (second_ref, SECOND, ((own, 0, late, FIRST), (oth, late, CAP, 0))),
    ):
        slots = mix_ref.shape[1]
        expert = iota((LANES, slots), 0)
        lane = iota((LANES, slots), 1)
        within = jnp.zeros((1, slots), jnp.float32)
        spread = jnp.zeros((LANES, slots), jnp.float32)
        for parity, offset, count, lowest in spans:
            start = jnp.where((expert & 1) == parity, (expert >> 1) * stride + offset, slots)
            inside = (lane >= start) & (lane < start + count)
            spread = spread + jnp.where(inside, 1.0, 0.0)
            ranks = jnp.where(inside, lane - start + lowest, 0)
            within = within + jnp.sum(ranks, axis=0, keepdims=True).astype(jnp.float32)
        spread = spread.astype(jnp.bfloat16)
        rank = jnp.dot(rank_ref[...], spread, preferred_element_type=jnp.float32)
        match = rank == within
        for k in range(3):
            part = jnp.dot(
                pieces_ref[k * rows : (k + 1) * rows, :], spread, preferred_element_type=jnp.float32
            )
            mix_ref[k * rows : (k + 1) * rows, :] = jnp.where(match, part, 0.0).astype(jnp.bfloat16)
    shape = (last_ref.shape[0], 3 * rows)
    one_hot = jnp.where(iota(shape, 1) == iota(shape, 0) * rows + info[3] - 1, 1.0, 0.0)
    last_ref[...] = jnp.dot(
        one_hot.astype(jnp.bfloat16), second_ref[...], preferred_element_type=jnp.float32
    ).astype(jnp.bfloat16)


def weigh(mix_ref, back):
    rows = mix_ref.shape[0] // 3
    parts = jnp.dot(mix_ref[...], back, preferred_element_type=jnp.float32)
    return parts[2 * rows :] + parts[rows : 2 * rows] + parts[:rows]


def columns(ref, held):
    size = held.shape[2]
    return [ref.at[:, k * size : (k + 1) * size] for k in range(held.shape[0])]


def first_kernel(info, mix_ref, back_ref, resid_ref, base_ref, last_ref, held, sems):
    back = fetched(columns(back_ref, held), held, sems)
    base = resid_ref[...].astype(jnp.float32) + weigh(mix_ref, back)
    base_ref[...] = base
    is_last = iota(base.shape, 0) == info[3] - 1
    last_ref[...] = jnp.sum(jnp.where(is_last, base, 0.0), axis=0, keepdims=True)


def last_kernel(mix_ref, base_ref, back_ref, _, told_ref, held, sems):
    size = held.shape[1]
    copies = [
        pltpu.make_async_copy(back_ref.at[k * size : (k + 1) * size], held.at[k], sems.at[k])
        for k in range(held.shape[0])
    ]
    for copy in copies:
        copy.start()
    parts = jnp.zeros((mix_ref.shape[0], held.shape[2]), jnp.float32)
    for k, copy in enumerate(copies):
        copy.wait()
        parts = parts + jnp.dot(
            mix_ref[:, k * size : (k + 1) * size], held[k], preferred_element_type=jnp.float32
        )
    moe = parts[2:3] + parts[1:2] + parts[0:1]
    out = (base_ref[...] + moe).astype(jnp.bfloat16).astype(jnp.float32)
    told_ref[...] = jnp.broadcast_to(out[None], told_ref.shape)


def combine_kernel(info, mix_ref, back_ref, base_ref, _, out_ref, square_ref, squares, held, sems):
    step = pl.program_id(0)

    @pl.when(step == 0)
    def _():
        squares[...] = jnp.zeros_like(squares)

    back = fetched(columns(back_ref, held), held, sems)
    out = (base_ref[...] + weigh(mix_ref, back)).astype(jnp.bfloat16)
    out_ref[...] = out
    out_f = out.astype(jnp.float32)
    row = iota(out_f.shape, 0)
    squares[...] += jnp.sum(jnp.where(row < info[3], out_f * out_f, 0.0), axis=0, keepdims=True)

    @pl.when(step == pl.num_programs(0) - 1)
    def _():
        total = jnp.sum(squares[...], axis=1, keepdims=True)
        square_ref[...] = jnp.broadcast_to(total, square_ref.shape)


def place_kernel(info, g_own, g_oth, u_own, u_oth, d_a, b_own, b_oth, _, out_ref):
    left = info[2] == 0
    for k, (own, oth) in enumerate(((g_own[...], g_oth[...]), (u_own[...], u_oth[...]))):
        out_ref[k, :, :FF] = jnp.where(left, own, oth)
        out_ref[k, :, FF:] = jnp.where(left, oth, own)
    in_a = pl.program_id(0) < pl.num_programs(0) // 2
    out_ref[2, :, :FF] = jnp.where(in_a, d_a[0], jnp.where(left, b_own[...], b_oth[...]))
    out_ref[2, :, FF:] = jnp.where(in_a, d_a[1], jnp.where(left, b_oth[...], b_own[...]))


def cast_kernel(first_row, blocks, x_ref, *refs):
    out_ref, held, turned, sems_in, sems_out = refs[-5:]
    groups, size = held.shape[:2]
    fetches, stores = [], []
    for g in range(groups):
        rows = pl.ds(first_row + g * size, size)
        fetches.append(pltpu.make_async_copy(x_ref.at[rows], held.at[g], sems_in.at[g]))
        target = out_ref.at[:, g * 16 : (g + 1) * 16]
        stores.append(pltpu.make_async_copy(turned.at[g], target, sems_out.at[g]))
    for fetch in fetches:
        fetch.start()
    target = iota((size, size), 0)
    source = (target & 15) * blocks + lax.shift_right_logical(target, 4)
    order = jnp.where(iota((size, size), 1) == source, 1.0, 0.0).astype(jnp.bfloat16)
    for g in range(groups):
        fetches[g].wait()
        rows = jnp.dot(order, held[g].astype(jnp.bfloat16), preferred_element_type=jnp.float32)
        turned[g] = rows.astype(jnp.bfloat16).reshape(turned.shape[1:])
        stores[g].start()
    for store in stores:
        store.wait()


def tie_kernel(*_):
    pass


def params():
    return pltpu.CompilerParams(vmem_limit_bytes=VMEM, dimension_semantics=("arbitrary",))


def whole(shape):
    return pl.BlockSpec(shape, lambda *_: tuple(0 for _ in shape))


def paired(
    hidden_in, lengths, routes, route_weights, norm_gain, master, unembed, final_gain, target_ids
):
    rows = hidden_in.shape[1]
    width = hidden_in.shape[2]
    blk_count = lax.axis_size("blk")
    blk = lax.axis_index("blk")
    rep = lax.axis_index("rep")
    first = blk_count * FIRST
    second = blk_count * SECOND
    resid = hidden_in[0]
    info = jnp.stack([2 * blk + rep, 2 * blk + 1 - rep, rep, lengths[blk]] + list(RING))
    info = info.astype(jnp.int32)

    shard_rows = master.shape[1]
    flat = master.reshape(3 * shard_rows * blk_count, FF)

    groups = shard_rows // 16

    def turned(k, *after):
        return pl.pallas_call(
            functools.partial(cast_kernel, k * shard_rows * blk_count, blk_count),
            in_specs=[pl.BlockSpec(memory_space=pl.ANY)] * (1 + len(after)),
            out_specs=pl.BlockSpec(memory_space=pl.ANY),
            out_shape=jax.ShapeDtypeStruct((blk_count, shard_rows, FF), jnp.bfloat16),
            scratch_shapes=[
                pltpu.VMEM((groups, 16 * blk_count, FF), jnp.float32),
                pltpu.VMEM((groups, blk_count, 16, FF), jnp.bfloat16),
                pltpu.SemaphoreType.DMA((groups,)),
                pltpu.SemaphoreType.DMA((groups,)),
            ],
            compiler_params=pltpu.CompilerParams(vmem_limit_bytes=VMEM),
            name="cast",
        )(flat, *after)

    def moved(x):
        own = lax.all_to_all(x, "blk", split_axis=0, concat_axis=0, tiled=True)
        return own.reshape(width, FF)

    def swapped(x):
        return lax.ppermute(x, "rep", [(0, 1), (1, 0)])

    def tied(x, *after):
        return pl.pallas_call(
            tie_kernel,
            in_specs=[pl.BlockSpec(memory_space=pl.ANY)] * (1 + len(after)),
            out_specs=pl.BlockSpec(memory_space=pl.ANY),
            out_shape=jax.ShapeDtypeStruct(x.shape, x.dtype),
            input_output_aliases={0: 0},
            name="tie",
        )(x, *after)

    row_ext, pieces = pl.pallas_call(
        prep_kernel,
        grid_spec=pltpu.PrefetchScalarGridSpec(
            num_scalar_prefetch=2,
            grid=(1,),
            in_specs=[
                whole((rows, width)),
                whole((routes.shape[2], rows)),
                whole((routes.shape[2], rows)),
                whole((width,)),
            ],
            out_specs=[whole((rows, width + LANES)), whole((3 * rows, LANES))],
        ),
        out_shape=[
            jax.ShapeDtypeStruct((rows, width + LANES), jnp.bfloat16),
            jax.ShapeDtypeStruct((3 * rows, LANES), jnp.bfloat16),
        ],
        compiler_params=params(),
        name="prep",
    )(lengths, blk[None].astype(jnp.int32), resid, routes[0].T, route_weights[0].T, norm_gain)
    g_own = moved(turned(0, row_ext))
    g_oth = swapped(g_own)
    u_own = moved(turned(1))
    u_oth = swapped(u_own)
    d_own = moved(tied(turned(2), g_oth))

    tokens = lax.all_gather(row_ext, "blk", axis_index_groups=[list(RING)], axis=0, tiled=True)

    def hidden_of(kernel, sizes, scratch, g, u, *after):
        return pl.pallas_call(
            kernel,
            grid_spec=pltpu.PrefetchScalarGridSpec(
                num_scalar_prefetch=1,
                grid=(GROUPS,),
                in_specs=[pl.BlockSpec((blk_count // GROUPS * rows, width + LANES), lambda i, *_: (i, 0))]
                + [whole((width, FF))] * 2
                + [pl.BlockSpec(memory_space=pl.ANY)] * len(after),
                out_specs=[whole(size) for size in sizes],
                scratch_shapes=[pltpu.VMEM((scratch, width), jnp.float32)],
            ),
            out_shape=[jax.ShapeDtypeStruct(size, jnp.bfloat16) for size in sizes],
            compiler_params=params(),
            name="gate_up",
        )(info, tokens, g, u, *after)

    step = 512

    quarter = width // 4
    anywhere = pl.BlockSpec(memory_space=pl.ANY)

    def returned(x):
        slots = x.shape[0]
        x = x.reshape(blk_count, slots // blk_count, width)
        x = lax.all_to_all(x, "blk", split_axis=0, concat_axis=0, tiled=True)
        return x.reshape(slots, width)

    extra = blk_count * (CAP - FIRST)
    own_hidden, spot = hidden_of(
        own_kernel, ((first + extra, FF), (second, extra)), first + extra, g_own, u_own
    )
    half = width // 2
    in_a = pl.BlockSpec((quarter, FF), lambda i, *_: (jnp.minimum(i, 1), 0))
    in_b = pl.BlockSpec((quarter, FF), lambda i, *_: (jnp.maximum(i, 2) - 2, 0))
    own_out, late_out, d_a, d_b = pl.pallas_call(
        own_down_kernel,
        grid=(4,),
        in_specs=[whole((first + extra, FF)), anywhere],
        out_specs=[
            pl.BlockSpec((first, quarter), lambda i: (0, i)),
            pl.BlockSpec((extra, quarter), lambda i: (0, i)),
            in_a,
            in_b,
        ],
        out_shape=[
            jax.ShapeDtypeStruct((first, width), jnp.bfloat16),
            jax.ShapeDtypeStruct((extra, width), jnp.bfloat16),
            jax.ShapeDtypeStruct((half, FF), jnp.bfloat16),
            jax.ShapeDtypeStruct((half, FF), jnp.bfloat16),
        ],
        scratch_shapes=[
            pltpu.VMEM((4, quarter, FF), jnp.bfloat16),
            pltpu.SemaphoreType.DMA((4,)),
        ],
        compiler_params=params(),
        name="own_down",
    )(own_hidden, d_own)
    both_a = lax.all_gather(d_a, "rep", axis=0)
    oth_b = swapped(d_b)
    own_out = tied(own_out, u_oth)
    own_back = returned(own_out)
    (oth_hidden,) = hidden_of(
        oth_kernel, ((second, FF),), second, g_oth, u_oth, own_out
    )
    oth_out = pl.pallas_call(
        oth_down_kernel,
        grid_spec=pltpu.PrefetchScalarGridSpec(
            num_scalar_prefetch=1,
            grid=(4,),
            in_specs=[
                whole((second, FF)),
                whole((second, extra)),
                pl.BlockSpec((extra, quarter), lambda i, *_: (0, i)),
                anywhere,
                anywhere,
            ],
            out_specs=pl.BlockSpec((second, quarter), lambda i, *_: (0, i)),
            scratch_shapes=[
                pltpu.VMEM((4, quarter, FF), jnp.bfloat16),
                pltpu.SemaphoreType.DMA((4,)),
            ],
        ),
        out_shape=jax.ShapeDtypeStruct((second, width), jnp.bfloat16),
        compiler_params=params(),
        name="oth_down",
    )(info, oth_hidden, spot, late_out, both_a, oth_b)
    oth_back = returned(oth_out)

    server = pl.pallas_call(
        place_kernel,
        grid_spec=pltpu.PrefetchScalarGridSpec(
            num_scalar_prefetch=1,
            grid=(4,),
            in_specs=[pl.BlockSpec((quarter, FF), lambda i, *_: (i, 0))] * 4
            + [
                pl.BlockSpec((2, quarter, FF), lambda i, *_: (0, jnp.minimum(i, 1), 0)),
                in_b,
                in_b,
                anywhere,
            ],
            out_specs=pl.BlockSpec((3, quarter, 2 * FF), lambda i, *_: (0, i, 0)),
        ),
        out_shape=jax.ShapeDtypeStruct((3, width, 2 * FF), jnp.bfloat16),
        compiler_params=params(),
        name="place",
    )(info, g_own, g_oth, u_own, u_oth, both_a, d_b, oth_b, oth_out)

    first_mix, second_mix, last_mix = pl.pallas_call(
        mix_kernel,
        grid_spec=pltpu.PrefetchScalarGridSpec(
            num_scalar_prefetch=1,
            grid=(1,),
            in_specs=[
                pl.BlockSpec((rows, LANES), lambda i, *_: (0, width // LANES)),
                whole((3 * rows, LANES)),
            ],
            out_specs=[whole((3 * rows, first)), whole((3 * rows, second)), whole((16, second))],
        ),
        out_shape=[
            jax.ShapeDtypeStruct((3 * rows, first), jnp.bfloat16),
            jax.ShapeDtypeStruct((3 * rows, second), jnp.bfloat16),
            jax.ShapeDtypeStruct((16, second), jnp.bfloat16),
        ],
        compiler_params=params(),
        name="mix",
    )(info, row_ext, pieces)

    def weigh_specs(slots):
        return [whole((3 * rows, slots)), anywhere]

    def hold(slots):
        return [
            pltpu.VMEM((width // step, slots, step), jnp.bfloat16),
            pltpu.SemaphoreType.DMA((width // step,)),
        ]

    column = pl.BlockSpec((rows, step), lambda i, *_: (0, i))
    lane_row = pl.BlockSpec((1, step), lambda i, *_: (0, i))
    base, last_base = pl.pallas_call(
        first_kernel,
        grid_spec=pltpu.PrefetchScalarGridSpec(
            num_scalar_prefetch=1,
            grid=(width // step,),
            in_specs=weigh_specs(first) + [column],
            out_specs=[column, lane_row],
            scratch_shapes=hold(first),
        ),
        out_shape=[
            jax.ShapeDtypeStruct((rows, width), jnp.float32),
            jax.ShapeDtypeStruct((1, width), jnp.float32),
        ],
        compiler_params=params(),
        name="first",
    )(info, first_mix, own_back, resid)
    told = pl.pallas_call(
        last_kernel,
        grid=(1,),
        in_specs=[whole((16, second)), whole((1, width)), anywhere, anywhere],
        out_specs=whole((blk_count, 1, width)),
        out_shape=jax.ShapeDtypeStruct((blk_count, 1, width), jnp.float32),
        scratch_shapes=[
            pltpu.VMEM((second // LANES, LANES, width), jnp.bfloat16),
            pltpu.SemaphoreType.DMA((second // LANES,)),
        ],
        compiler_params=params(),
        name="last",
    )(last_mix, last_base, oth_back, server)
    out_rows, square = pl.pallas_call(
        combine_kernel,
        grid_spec=pltpu.PrefetchScalarGridSpec(
            num_scalar_prefetch=1,
            grid=(width // step,),
            in_specs=weigh_specs(second) + [column, pl.BlockSpec(memory_space=pl.ANY)],
            out_specs=[column, whole((1, LANES))],
            scratch_shapes=[pltpu.VMEM((1, step), jnp.float32)] + hold(second),
        ),
        out_shape=[
            jax.ShapeDtypeStruct((rows, width), jnp.bfloat16),
            jax.ShapeDtypeStruct((1, LANES), jnp.float32),
        ],
        compiler_params=params(),
        name="combine",
    )(info, second_mix, oth_back, base, told)

    def everywhere(copies):
        return lax.all_to_all(copies, "blk", split_axis=0, concat_axis=0, tiled=True)

    last_rows = everywhere(told)[:, 0]
    final = (
        last_rows
        * lax.rsqrt(jnp.mean(last_rows * last_rows, axis=-1, keepdims=True) + 1e-05)
        * final_gain
    ).astype(jnp.bfloat16)
    logits = lax.dot_general(
        final, unembed, (((1,), (1,)), ((), ())), preferred_element_type=jnp.float32
    )
    vocab_base = blk * unembed.shape[0]
    target_hit = (
        target_ids[:, None] == vocab_base + jnp.arange(unembed.shape[0], dtype=jnp.int32)[None, :]
    )
    target_part = jnp.sum(jnp.where(target_hit, logits, 0.0), axis=1)
    top_part = jnp.max(logits, axis=1)
    prompt = jnp.arange(blk_count, dtype=jnp.int32)
    square_part = jnp.where(prompt == blk, square[0, :blk_count], 0.0)
    stats = jnp.stack([top_part, target_part, square_part])
    parts = everywhere(jnp.broadcast_to(stats[None], (blk_count,) + stats.shape))
    sums = jnp.sum(parts[:, 1:], axis=0)
    norms = jnp.sqrt(sums[1] / (lengths.astype(jnp.float32) * width) + 1e-06)
    request_stats = jnp.stack([norms, jnp.max(parts[:, 0], axis=0), sums[0]])
    return (out_rows[None], server, request_stats)


def local(hidden_in, lengths, routes, route_weights, norm_gain, master, *rest):
    blk_count = lax.axis_size("blk")
    fits = (
        lax.axis_size("rep") == 2
        and master.shape[3] == FF
        and EXPERTS == 2 * blk_count
        and blk_count == len(RING)
        and hidden_in.shape[1] == LEN
        and lengths.shape[0] == blk_count
    )
    form = paired if fits else general
    return form(hidden_in, lengths, routes, route_weights, norm_gain, master, *rest)


def solution(mesh):
    return jax.shard_map(
        local,
        mesh=mesh,
        in_specs=(
            P("rep", "blk", None),
            P("rep"),
            P("rep", "blk", None),
            P("rep", "blk", None),
            P(),
            P(None, "blk", None, "rep"),
            P("blk", None),
            P(),
            P("rep"),
        ),
        out_specs=(P("rep", "blk", None), P(None, None, "blk"), P(None, "rep")),
        check_vma=False,
    )
```

```python
import functools

import jax
import jax.numpy as jnp
from jax import lax
from jax.experimental import pallas as pl
from jax.experimental.pallas import tpu as pltpu
from jax.sharding import PartitionSpec as P

FF = 512
EXPERTS = 32
LEN = 128
CAP = 36
FIRST = 32
SECOND = 40
GROUPS = 4
RING = (0, 1, 4, 5, 8, 9, 12, 13, 14, 15, 10, 11, 6, 7, 2, 3)
LANES = 128
VMEM = 56 * 1024 * 1024


def merged(x, axis, combine):
    everything = jax.tree.map(lambda part: lax.all_gather(part, axis), x)
    initial = jax.tree.map(lambda part: part[0], everything)

    def turn(k, so_far):
        return combine(so_far, jax.tree.map(lambda part: part[k], everything))

    return lax.fori_loop(1, lax.axis_size(axis), turn, initial)


def combine_stats(first, second):
    return (first[0] + second[0], jnp.maximum(first[1], second[1]))


def general(
    hidden_in, lengths, routes, route_weights, norm_gain, master, unembed, final_gain, target_ids
):
    rows_here = hidden_in.shape[1]
    width = hidden_in.shape[2]
    top_count = routes.shape[2]
    blk_count = lax.axis_size("blk")
    rep_count = lax.axis_size("rep")
    blk_index = lax.axis_index("blk")
    unit_count = master.shape[3] * rep_count
    split_ways = max(1, FF // unit_count)
    local_exp = max(1, unit_count // FF)
    group_width = min(unit_count, FF)
    capacity = CAP
    blocks = master.astype(jnp.bfloat16)
    arrived_blocks = lax.all_to_all(blocks, "blk", split_axis=2, concat_axis=1, tiled=True)
    server = lax.all_gather(arrived_blocks, "rep", axis=3, tiled=True)[:, :, 0, :]
    gate_w = server[0].reshape(width, local_exp, group_width)
    up_w = server[1].reshape(width, local_exp, group_width)
    down_w = server[2].reshape(width, local_exp, group_width)
    prompts_here = lengths.shape[0]
    slot_index = blk_index * rows_here + jnp.arange(rows_here, dtype=jnp.int32)
    prompt_of = slot_index // LEN
    position = slot_index % LEN
    prompt_match = prompt_of[:, None] == jnp.arange(prompts_here, dtype=jnp.int32)[None, :]
    row_len = jnp.sum(jnp.where(prompt_match, lengths[None, :], 0), axis=1)
    is_valid = position < row_len
    resid_f = hidden_in[0].astype(jnp.float32)
    normed = (
        resid_f * lax.rsqrt(jnp.mean(resid_f * resid_f, axis=-1, keepdims=True) + 1e-05) * norm_gain
    ).astype(jnp.bfloat16)
    expert_ids = routes[0].reshape(-1)
    pair_live = jnp.repeat(is_valid, top_count)
    pair_row = jnp.repeat(jnp.arange(rows_here, dtype=jnp.int32), top_count)
    expert_hits = (
        (expert_ids[:, None] == jnp.arange(EXPERTS, dtype=jnp.int32)[None, :]) & pair_live[:, None]
    ).astype(jnp.int32)
    slot_rank = jnp.sum((jnp.cumsum(expert_hits, axis=0) - 1) * expert_hits, axis=1)
    slot_id = jnp.where(pair_live, expert_ids * capacity + slot_rank, EXPERTS * capacity)
    source_row = jnp.zeros((EXPERTS * capacity + 1,), jnp.int32).at[slot_id].set(pair_row)[:-1]
    filled = jnp.zeros((EXPERTS * capacity + 1,), jnp.bfloat16).at[slot_id].set(1.0)[:-1]
    outgoing = (normed[source_row] * filled[:, None]).reshape(EXPERTS, capacity, width)
    sending = jnp.repeat(outgoing, split_ways, axis=0).reshape(
        blk_count, local_exp, capacity, width
    )
    arrived = lax.all_to_all(sending, "blk", split_axis=0, concat_axis=0, tiled=True)
    sources = arrived.shape[0]
    slot_count = arrived.shape[2]
    stride = sources
    while stride % 2 == 0 and stride * local_exp * slot_count > 1024:
        stride = stride // 2
    grouped = arrived.reshape(sources // stride, stride, local_exp, slot_count, width)

    def one_block(portion):
        gate_out = jnp.einsum("slnd,dlf->slnf", portion, gate_w, preferred_element_type=jnp.float32)
        up_out = jnp.einsum("slnd,dlf->slnf", portion, up_w, preferred_element_type=jnp.float32)
        hidden = (jax.nn.silu(gate_out) * up_out).astype(jnp.bfloat16)
        return jnp.einsum(
            "slnf,dlf->slnd", hidden, down_w, preferred_element_type=jnp.float32
        ).astype(jnp.bfloat16)

    returned = lax.all_to_all(
        lax.map(one_block, grouped).reshape(sources, local_exp, slot_count, width),
        "blk",
        split_axis=0,
        concat_axis=0,
        tiled=True,
    )
    summed_f = jnp.sum(
        returned.reshape(EXPERTS, split_ways, capacity, width).astype(jnp.float32), axis=1
    )
    expert_out = lax.optimization_barrier(summed_f.astype(jnp.bfloat16)).reshape(
        EXPERTS * capacity, width
    )
    gather_index = jnp.where(pair_live, expert_ids * capacity + slot_rank, 0)
    pair_weight = route_weights[0].reshape(-1) * pair_live.astype(jnp.float32)
    moe = jnp.sum(
        (expert_out[gather_index].astype(jnp.float32) * pair_weight[:, None]).reshape(
            rows_here, top_count, width
        ),
        axis=1,
    )
    out_rows = (resid_f + moe).astype(jnp.bfloat16)
    out_f = out_rows.astype(jnp.float32)
    row_squares = jnp.sum(out_f * out_f, axis=-1) * is_valid.astype(jnp.float32)
    square_local = jnp.sum(jnp.where(prompt_match, row_squares[:, None], 0.0), axis=0)
    is_last = is_valid & (position == row_len - 1)
    picker = (prompt_match & is_last[:, None]).astype(jnp.bfloat16)
    last_local = lax.dot_general(
        picker, out_rows, (((0,), (0,)), ((), ())), preferred_element_type=jnp.float32
    )
    last_rows, square_total = lax.psum((last_local, square_local), "blk")
    norms = jnp.sqrt(square_total / (lengths.astype(jnp.float32) * width) + 1e-06)
    final = (
        last_rows
        * lax.rsqrt(jnp.mean(last_rows * last_rows, axis=-1, keepdims=True) + 1e-05)
        * final_gain
    ).astype(jnp.bfloat16)
    logits = lax.dot_general(
        final, unembed, (((1,), (1,)), ((), ())), preferred_element_type=jnp.float32
    )
    vocab_base = blk_index * unembed.shape[0]
    target_hit = (
        target_ids[:, None] == vocab_base + jnp.arange(unembed.shape[0], dtype=jnp.int32)[None, :]
    )
    target_part = jnp.sum(jnp.where(target_hit, logits, 0.0), axis=1)
    top_part = jnp.max(logits, axis=1)
    target_logit, top_logit = merged((target_part, top_part), "blk", combine_stats)
    request_stats = jnp.stack([norms, top_logit, target_logit])
    return (out_rows[None], server, request_stats)


def iota(shape, dim):
    return lax.broadcasted_iota(jnp.int32, shape, dim)


def prep_kernel(lengths_ref, blk_ref, hidden_ref, routes_ref, weights_ref, gain_ref, rows_ref, pieces_ref):
    rows, width = hidden_ref.shape
    length = lengths_ref[blk_ref[0]]
    x = hidden_ref[...].astype(jnp.float32)
    scale = lax.rsqrt(jnp.mean(x * x, axis=-1, keepdims=True) + 1e-05)
    rows_ref[:, :width] = (x * scale * gain_ref[...][None]).astype(jnp.bfloat16)
    column = iota((rows, LANES), 1)
    lane = column & (EXPERTS - 1)
    row = iota((rows, LANES), 0)
    hit = jnp.zeros((rows, LANES), jnp.float32)
    weight = jnp.zeros((rows, LANES), jnp.float32)
    named_by = jnp.transpose(routes_ref[...].astype(jnp.float32)).astype(jnp.int32)
    weight_by = jnp.transpose(weights_ref[...])
    for k in range(routes_ref.shape[0]):
        named = named_by[:, k : k + 1] == lane
        hit = hit + jnp.where(named, 1.0, 0.0)
        weight = weight + jnp.where(named, weight_by[:, k : k + 1], 0.0)
    live = row < length
    hit = jnp.where(live, hit, 0.0)
    weight = jnp.where(live, weight, 0.0)
    before = jnp.where(iota((rows, rows), 1) < iota((rows, rows), 0), 1.0, 0.0)
    rank = jnp.dot(
        before.astype(jnp.bfloat16), hit.astype(jnp.bfloat16), preferred_element_type=jnp.float32
    )
    told = jnp.where(hit > 0.0, rank, -1.0)
    for k in range(3):
        piece = weight.astype(jnp.bfloat16)
        pieces_ref[k * rows : (k + 1) * rows, :] = piece
        value = piece.astype(jnp.float32)
        told = jnp.where(column >= (k + 1) * EXPERTS, value, told)
        weight = weight - value
    rows_ref[:, width:] = told.astype(jnp.bfloat16)


def pick(info, lengths_ref, ring_ref, which, x_ref, width, place, slots, lasts):
    step = pl.program_id(0)
    rows = x_ref.shape[0]
    sources = rows // LEN
    ranks = x_ref[:, width:].astype(jnp.float32)
    lane = iota((rows, LANES), 1)
    row = iota((rows, 1), 0)
    source = row // LEN
    rank = jnp.sum(jnp.where(lane == info[which], ranks, 0.0), axis=1, keepdims=True)
    slot = jnp.where(rank >= 0.0, place(source.astype(jnp.float32), rank), -1.0)
    slot_lane = iota((rows, slots), 1).astype(jnp.float32)
    one_hot = jnp.where(slot == slot_lane, 1.0, 0.0).astype(jnp.bfloat16)
    dims = (((0,), (0,)), ((), ()))
    chosen = lax.dot_general(
        one_hot, x_ref[:, :width], dims, preferred_element_type=jnp.float32
    )
    home = jnp.full_like(row, -1)
    for s in range(sources):
        owner = ring_ref[step * sources + s]
        home = jnp.where(row == s * LEN + lengths_ref[owner] - 1, owner, home)
    home = jnp.where(rank >= 0.0, home, -1)
    count = lasts.shape[0]
    one_hot = jnp.where(home == iota((rows, count), 1), 1.0, 0.0).astype(jnp.bfloat16)
    last = lax.dot_general(one_hot, x_ref[...], dims, preferred_element_type=jnp.float32)

    @pl.when(step == 0)
    def _():
        lasts[...] = last

    @pl.when(step != 0)
    def _():
        lasts[...] += last

    return chosen


def share_of(info, which, lasts, width):
    ext = lasts[:, width:]
    lane = iota(ext.shape, 1)
    is_own = (lane >= EXPERTS) & ((lane & (EXPERTS - 1)) == info[which])
    return jnp.broadcast_to(
        jnp.sum(jnp.where(is_own, ext, 0.0), axis=1, keepdims=True), ext.shape
    )


def activ(x, g_ref, u_ref):
    x = x.astype(jnp.bfloat16)
    gate = jnp.dot(x, g_ref[...], preferred_element_type=jnp.float32)
    up = jnp.dot(x, u_ref[...], preferred_element_type=jnp.float32)
    return (gate / (1.0 + jnp.exp(-gate)) * up).astype(jnp.bfloat16)


def own_kernel(
    info, lengths_ref, ring_ref, x_ref, g_ref, u_ref, out_ref, spot_ref, share_ref, picked, lasts
):
    step = pl.program_id(0)
    sources = x_ref.shape[0] // LEN
    width = g_ref.shape[0]
    more = CAP - FIRST
    early = sources * FIRST
    all_early = GROUPS * early
    all_rows = all_early + GROUPS * sources * more

    def place(source, rank):
        return jnp.where(
            rank < FIRST, source * FIRST + rank, early + source * more + (rank - FIRST)
        )

    chosen = pick(
        info, lengths_ref, ring_ref, 0, x_ref, width, place, early + sources * more, lasts
    )
    for s in range(sources):
        start = pl.multiple_of(ring_ref[step * sources + s] * FIRST, FIRST)
        picked[pl.ds(start, FIRST), :] = chosen[s * FIRST : (s + 1) * FIRST]
    start = pl.multiple_of(all_early + step * sources * more, sources * more)
    picked[pl.ds(start, sources * more), :] = chosen[early:]

    @pl.when(step == GROUPS - 1)
    def _():
        picked[all_rows:, :] = lasts[:, :width]
        out_ref[...] = activ(picked[...], g_ref, u_ref)
        share_ref[...] = share_of(info, 0, lasts, width)
        column = iota(spot_ref.shape, 1)
        owner = lax.shift_right_logical(column, more.bit_length() - 1)
        source = jnp.full_like(column, -1)
        for k, b in enumerate(RING):
            source = jnp.where(owner == k, b, source)
        spot = jnp.where(source >= 0, source * SECOND + (column & (more - 1)), -1)
        spot_ref[...] = jnp.where(iota(spot_ref.shape, 0) == spot, 1.0, 0.0).astype(jnp.bfloat16)


def oth_kernel(
    info,
    lengths_ref,
    ring_ref,
    x_ref,
    g_ref,
    u_ref,
    resid_ref,
    _,
    out_ref,
    share_ref,
    base_ref,
    picked,
    lasts,
):
    step = pl.program_id(0)
    sources = x_ref.shape[0] // LEN
    width = g_ref.shape[0]
    all_rows = GROUPS * sources * SECOND

    def place(source, rank):
        return source * SECOND + (SECOND - CAP) + rank

    chosen = pick(info, lengths_ref, ring_ref, 1, x_ref, width, place, sources * SECOND, lasts)
    for s in range(sources):
        start = pl.multiple_of(ring_ref[step * sources + s] * SECOND, SECOND)
        picked[pl.ds(start, SECOND), :] = chosen[s * SECOND : (s + 1) * SECOND]

    @pl.when(step == GROUPS - 1)
    def _():
        picked[all_rows:, :] = lasts[:, :width]
        out_ref[...] = activ(picked[...], g_ref, u_ref)
        share_ref[...] = share_of(info, 1, lasts, width)
        resid = resid_ref[...].astype(jnp.float32)
        is_last = iota(resid.shape, 0) == info[3] - 1
        last = jnp.sum(jnp.where(is_last, resid, 0.0), axis=0, keepdims=True)
        base_ref[...] = jnp.where(iota(base_ref.shape, 0) == info[4], last, 0.0)


def matmul_nt(hidden_ref, d):
    return lax.dot_general(
        hidden_ref[...], d, (((1,), (1,)), ((), ())), preferred_element_type=jnp.float32
    )


def fetched(sources, held, sems):
    step = pl.program_id(0)
    rows = held.shape[1]

    @pl.when(step == 0)
    def _():
        for k, source in enumerate(sources):
            pltpu.make_async_copy(source, held.at[k], sems.at[k]).start()

    for k, source in enumerate(sources):

        @pl.when(step == k)
        def _():
            pltpu.make_async_copy(source, held.at[k], sems.at[k]).wait()

    return held[step]


def own_down_kernel(hidden_ref, share_ref, d_ref, out_ref, late_ref, part_ref, held, sems):
    size = held.shape[1]
    d = fetched([d_ref.at[k * size : (k + 1) * size] for k in range(held.shape[0])], held, sems)
    out = matmul_nt(hidden_ref, d).astype(jnp.bfloat16)
    rows = out_ref.shape[0]
    out_ref[...] = out[:rows]
    late_ref[...] = out[rows:]
    count = part_ref.shape[0]
    part_ref[...] = share_ref[:, :1] * out[-count:].astype(jnp.float32)


def oth_down_kernel(
    info,
    hidden_ref,
    share_ref,
    spot_ref,
    late_ref,
    base_ref,
    part_ref,
    d_ref,
    out_ref,
    sum_ref,
    held,
    sems,
):
    size = held.shape[1]
    other = 1 - info[2]
    sources = [d_ref.at[other, k * size : (k + 1) * size] for k in range(held.shape[0])]
    d = fetched(sources, held, sems)
    late = jnp.dot(spot_ref[...], late_ref[...], preferred_element_type=jnp.float32)
    out = matmul_nt(hidden_ref, d)
    rows = out_ref.shape[0]
    out_ref[...] = (late + out[:rows]).astype(jnp.bfloat16)
    last = out[rows:].astype(jnp.bfloat16).astype(jnp.float32)
    sum_ref[...] = base_ref[...] + part_ref[...] + share_ref[:, :1] * last


def mix_kernel(info, rank_ref, pieces_ref, first_ref, second_ref):
    rows = rank_ref.shape[0]
    late = SECOND - CAP
    own, oth = info[2], 1 - info[2]
    for mix_ref, stride, spans in (
        (first_ref, FIRST, ((own, 0, FIRST, 0),)),
        (second_ref, SECOND, ((own, 0, late, FIRST), (oth, late, CAP, 0))),
    ):
        slots = mix_ref.shape[1]
        expert = iota((LANES, slots), 0)
        lane = iota((LANES, slots), 1)
        within = jnp.zeros((1, slots), jnp.float32)
        spread = jnp.zeros((LANES, slots), jnp.float32)
        for parity, offset, count, lowest in spans:
            start = jnp.where((expert & 1) == parity, (expert >> 1) * stride + offset, slots)
            inside = (lane >= start) & (lane < start + count)
            spread = spread + jnp.where(inside, 1.0, 0.0)
            ranks = jnp.where(inside, lane - start + lowest, 0)
            within = within + jnp.sum(ranks, axis=0, keepdims=True).astype(jnp.float32)
        spread = spread.astype(jnp.bfloat16)
        rank = jnp.dot(rank_ref[...], spread, preferred_element_type=jnp.float32)
        match = rank == within
        for k in range(3):
            part = jnp.dot(
                pieces_ref[k * rows : (k + 1) * rows, :], spread, preferred_element_type=jnp.float32
            )
            mix_ref[k * rows : (k + 1) * rows, :] = jnp.where(match, part, 0.0).astype(jnp.bfloat16)


def weigh(mix_ref, back_ref):
    rows = mix_ref.shape[0] // 3
    parts = jnp.dot(mix_ref[...], back_ref[...], preferred_element_type=jnp.float32)
    return parts[2 * rows :] + parts[rows : 2 * rows] + parts[:rows]


def first_kernel(mix_ref, back_ref, resid_ref, base_ref):
    base_ref[...] = resid_ref[...].astype(jnp.float32) + weigh(mix_ref, back_ref)


def combine_kernel(info, mix_ref, back_ref, base_ref, _, __, out_ref, square_ref, squares):
    step = pl.program_id(0)

    @pl.when(step == 0)
    def _():
        squares[...] = jnp.zeros_like(squares)

    out = (base_ref[...] + weigh(mix_ref, back_ref)).astype(jnp.bfloat16)
    out_ref[...] = out
    out_f = out.astype(jnp.float32)
    row = iota(out_f.shape, 0)
    squares[...] += jnp.sum(jnp.where(row < info[3], out_f * out_f, 0.0), axis=0, keepdims=True)

    @pl.when(step == pl.num_programs(0) - 1)
    def _():
        total = jnp.sum(squares[...], axis=1, keepdims=True)
        square_ref[...] = jnp.broadcast_to(total, square_ref.shape)


def place_kernel(info, g_own, g_oth, u_own, u_oth, d_both, _, out_ref):
    left = info[2] == 0
    for k, (own, oth) in enumerate(((g_own[...], g_oth[...]), (u_own[...], u_oth[...]))):
        out_ref[k, :, :FF] = jnp.where(left, own, oth)
        out_ref[k, :, FF:] = jnp.where(left, oth, own)
    out_ref[2, :, :FF] = d_both[0]
    out_ref[2, :, FF:] = d_both[1]


def cast_kernel(first_row, blocks, x_ref, *refs):
    out_ref, held, turned, sems_in, sems_out = refs[-5:]
    groups, size = held.shape[:2]
    fetches, stores = [], []
    for g in range(groups):
        rows = pl.ds(first_row + g * size, size)
        fetches.append(pltpu.make_async_copy(x_ref.at[rows], held.at[g], sems_in.at[g]))
        target = out_ref.at[:, g * 16 : (g + 1) * 16]
        stores.append(pltpu.make_async_copy(turned.at[g], target, sems_out.at[g]))
    for fetch in fetches:
        fetch.start()
    target = iota((size, size), 0)
    source = (target & 15) * blocks + lax.shift_right_logical(target, 4)
    order = jnp.where(iota((size, size), 1) == source, 1.0, 0.0).astype(jnp.bfloat16)
    for g in range(groups):
        fetches[g].wait()
        rows = jnp.dot(order, held[g].astype(jnp.bfloat16), preferred_element_type=jnp.float32)
        turned[g] = rows.astype(jnp.bfloat16).reshape(turned.shape[1:])
        stores[g].start()
    for store in stores:
        store.wait()


def tie_kernel(*_):
    pass


def params():
    return pltpu.CompilerParams(vmem_limit_bytes=VMEM, dimension_semantics=("arbitrary",))


def whole(shape):
    return pl.BlockSpec(shape, lambda *_: tuple(0 for _ in shape))


def paired(
    hidden_in, lengths, routes, route_weights, norm_gain, master, unembed, final_gain, target_ids
):
    rows = hidden_in.shape[1]
    width = hidden_in.shape[2]
    blk_count = lax.axis_size("blk")
    blk = lax.axis_index("blk")
    rep = lax.axis_index("rep")
    first = blk_count * FIRST
    second = blk_count * SECOND
    resid = hidden_in[0]
    info = jnp.stack([2 * blk + rep, 2 * blk + 1 - rep, rep, lengths[blk], blk])
    info = info.astype(jnp.int32)

    shard_rows = master.shape[1]
    flat = master.reshape(3 * shard_rows * blk_count, FF)

    groups = shard_rows // 16

    def turned(k, *after):
        return pl.pallas_call(
            functools.partial(cast_kernel, k * shard_rows * blk_count, blk_count),
            in_specs=[pl.BlockSpec(memory_space=pl.ANY)] * (1 + len(after)),
            out_specs=pl.BlockSpec(memory_space=pl.ANY),
            out_shape=jax.ShapeDtypeStruct((blk_count, shard_rows, FF), jnp.bfloat16),
            scratch_shapes=[
                pltpu.VMEM((groups, 16 * blk_count, FF), jnp.float32),
                pltpu.VMEM((groups, blk_count, 16, FF), jnp.bfloat16),
                pltpu.SemaphoreType.DMA((groups,)),
                pltpu.SemaphoreType.DMA((groups,)),
            ],
            compiler_params=pltpu.CompilerParams(vmem_limit_bytes=VMEM),
            name="cast",
        )(flat, *after)

    def moved(x):
        own = lax.all_to_all(x, "blk", split_axis=0, concat_axis=0, tiled=True)
        return own.reshape(width, FF)

    def swapped(x):
        return lax.ppermute(x, "rep", [(0, 1), (1, 0)])

    def tied(x, *after):
        return pl.pallas_call(
            tie_kernel,
            in_specs=[pl.BlockSpec(memory_space=pl.ANY)] * (1 + len(after)),
            out_specs=pl.BlockSpec(memory_space=pl.ANY),
            out_shape=jax.ShapeDtypeStruct(x.shape, x.dtype),
            input_output_aliases={0: 0},
            name="tie",
        )(x, *after)

    row_ext, pieces = pl.pallas_call(
        prep_kernel,
        grid_spec=pltpu.PrefetchScalarGridSpec(
            num_scalar_prefetch=2,
            grid=(1,),
            in_specs=[
                whole((rows, width)),
                whole((routes.shape[2], rows)),
                whole((routes.shape[2], rows)),
                whole((width,)),
            ],
            out_specs=[whole((rows, width + LANES)), whole((3 * rows, LANES))],
        ),
        out_shape=[
            jax.ShapeDtypeStruct((rows, width + LANES), jnp.bfloat16),
            jax.ShapeDtypeStruct((3 * rows, LANES), jnp.bfloat16),
        ],
        compiler_params=params(),
        name="prep",
    )(lengths, blk[None].astype(jnp.int32), resid, routes[0].T, route_weights[0].T, norm_gain)
    g_own = moved(turned(0, row_ext))
    g_oth = swapped(g_own)
    u_own = moved(turned(1))
    u_oth = swapped(u_own)
    d_own = moved(tied(turned(2), g_oth))

    tokens = lax.all_gather(row_ext, "blk", axis_index_groups=[list(RING)], axis=0, tiled=True)

    ring = jnp.array(RING, jnp.int32)

    def hidden_of(kernel, outs, picked, operands, specs):
        return pl.pallas_call(
            kernel,
            grid_spec=pltpu.PrefetchScalarGridSpec(
                num_scalar_prefetch=3,
                grid=(GROUPS,),
                in_specs=[pl.BlockSpec((blk_count // GROUPS * rows, width + LANES), lambda i, *_: (i, 0))]
                + [whole((width, FF))] * 2
                + specs,
                out_specs=[whole(out.shape) for out in outs],
                scratch_shapes=[
                    pltpu.VMEM((picked, width), jnp.float32),
                    pltpu.VMEM((blk_count, width + LANES), jnp.float32),
                ],
            ),
            out_shape=outs,
            compiler_params=params(),
            name="gate_up",
        )(info, lengths, ring, tokens, *operands)

    step = 512
    quarter = width // 4
    anywhere = pl.BlockSpec(memory_space=pl.ANY)

    def returned(x):
        slots = x.shape[0]
        x = x.reshape(blk_count, slots // blk_count, width)
        x = lax.all_to_all(x, "blk", split_axis=0, concat_axis=0, tiled=True)
        return x.reshape(slots, width)

    def bf16(*shape):
        return jax.ShapeDtypeStruct(shape, jnp.bfloat16)

    def f32(*shape):
        return jax.ShapeDtypeStruct(shape, jnp.float32)

    extra = blk_count * (CAP - FIRST) + blk_count
    own_hidden, spot, own_share = hidden_of(
        own_kernel,
        [bf16(first + extra, FF), bf16(second, extra), f32(blk_count, LANES)],
        first + extra,
        (g_own, u_own),
        [],
    )
    d_own = tied(d_own, own_hidden)
    d_both = lax.all_gather(d_own, "rep", axis=0)
    own_out, late_out, own_part = pl.pallas_call(
        own_down_kernel,
        grid=(width // step,),
        in_specs=[whole((first + extra, FF)), whole((blk_count, LANES)), anywhere],
        out_specs=[
            pl.BlockSpec((first, step), lambda i: (0, i)),
            pl.BlockSpec((extra, step), lambda i: (0, i)),
            pl.BlockSpec((blk_count, step), lambda i: (0, i)),
        ],
        out_shape=[bf16(first, width), bf16(extra, width), f32(blk_count, width)],
        scratch_shapes=[
            pltpu.VMEM((width // step, step, FF), jnp.bfloat16),
            pltpu.SemaphoreType.DMA((width // step,)),
        ],
        compiler_params=params(),
        name="own_down",
    )(own_hidden, own_share, d_own)
    own_out = tied(own_out, u_oth)
    own_back = returned(own_out)
    oth_hidden, oth_share, base_part = hidden_of(
        oth_kernel,
        [bf16(second + blk_count, FF), f32(blk_count, LANES), f32(blk_count, width)],
        second + blk_count,
        (g_oth, u_oth, resid, own_out),
        [whole((rows, width)), anywhere],
    )
    part_spec = pl.BlockSpec((blk_count, quarter), lambda i, *_: (0, i))
    oth_out, last_part = pl.pallas_call(
        oth_down_kernel,
        grid_spec=pltpu.PrefetchScalarGridSpec(
            num_scalar_prefetch=1,
            grid=(4,),
            in_specs=[
                whole((second + blk_count, FF)),
                whole((blk_count, LANES)),
                whole((second, extra)),
                pl.BlockSpec((extra, quarter), lambda i, *_: (0, i)),
                part_spec,
                part_spec,
                anywhere,
            ],
            out_specs=[pl.BlockSpec((second, quarter), lambda i, *_: (0, i)), part_spec],
            scratch_shapes=[
                pltpu.VMEM((4, quarter, FF), jnp.bfloat16),
                pltpu.SemaphoreType.DMA((4,)),
            ],
        ),
        out_shape=[bf16(second, width), f32(blk_count, width)],
        compiler_params=params(),
        name="oth_down",
    )(info, oth_hidden, oth_share, spot, late_out, base_part, own_part, d_both)
    last_parts = lax.all_gather(last_part, "blk", axis_index_groups=[list(RING)], axis=0)
    oth_back = returned(oth_out)

    server = pl.pallas_call(
        place_kernel,
        grid_spec=pltpu.PrefetchScalarGridSpec(
            num_scalar_prefetch=1,
            grid=(4,),
            in_specs=[pl.BlockSpec((quarter, FF), lambda i, *_: (i, 0))] * 4
            + [pl.BlockSpec((2, quarter, FF), lambda i, *_: (0, i, 0)), anywhere],
            out_specs=pl.BlockSpec((3, quarter, 2 * FF), lambda i, *_: (0, i, 0)),
        ),
        out_shape=jax.ShapeDtypeStruct((3, width, 2 * FF), jnp.bfloat16),
        compiler_params=params(),
        name="place",
    )(info, g_own, g_oth, u_own, u_oth, d_both, oth_out)

    first_mix, second_mix = pl.pallas_call(
        mix_kernel,
        grid_spec=pltpu.PrefetchScalarGridSpec(
            num_scalar_prefetch=1,
            grid=(1,),
            in_specs=[
                pl.BlockSpec((rows, LANES), lambda i, *_: (0, width // LANES)),
                whole((3 * rows, LANES)),
            ],
            out_specs=[whole((3 * rows, first)), whole((3 * rows, second))],
        ),
        out_shape=[
            jax.ShapeDtypeStruct((3 * rows, first), jnp.bfloat16),
            jax.ShapeDtypeStruct((3 * rows, second), jnp.bfloat16),
        ],
        compiler_params=params(),
        name="mix",
    )(info, row_ext, pieces)

    def weigh_specs(slots):
        return [whole((3 * rows, slots)), pl.BlockSpec((slots, step), lambda i, *_: (0, i))]

    column = pl.BlockSpec((rows, step), lambda i, *_: (0, i))
    base = pl.pallas_call(
        first_kernel,
        grid=(width // step,),
        in_specs=weigh_specs(first) + [column],
        out_specs=column,
        out_shape=f32(rows, width),
        compiler_params=params(),
        name="first",
    )(first_mix, own_back, resid)
    last_rows = lax.reduce_precision(jnp.sum(last_parts, axis=0), 8, 7)
    final = (
        last_rows
        * lax.rsqrt(jnp.mean(last_rows * last_rows, axis=-1, keepdims=True) + 1e-05)
        * final_gain
    ).astype(jnp.bfloat16)
    logits = lax.dot_general(
        final, unembed, (((1,), (1,)), ((), ())), preferred_element_type=jnp.float32
    )
    vocab_base = blk * unembed.shape[0]
    target_hit = (
        target_ids[:, None] == vocab_base + jnp.arange(unembed.shape[0], dtype=jnp.int32)[None, :]
    )
    target_part = jnp.sum(jnp.where(target_hit, logits, 0.0), axis=1)
    top_part = jnp.max(logits, axis=1)

    out_rows, square = pl.pallas_call(
        combine_kernel,
        grid_spec=pltpu.PrefetchScalarGridSpec(
            num_scalar_prefetch=1,
            grid=(width // step,),
            in_specs=weigh_specs(second) + [column, anywhere, anywhere],
            out_specs=[column, whole((1, LANES))],
            scratch_shapes=[pltpu.VMEM((1, step), jnp.float32)],
        ),
        out_shape=[
            jax.ShapeDtypeStruct((rows, width), jnp.bfloat16),
            jax.ShapeDtypeStruct((1, LANES), jnp.float32),
        ],
        compiler_params=params(),
        name="combine",
    )(info, second_mix, oth_back, base, server, top_part[None])

    def everywhere(copies):
        return lax.all_to_all(copies, "blk", split_axis=0, concat_axis=0, tiled=True)

    prompt = jnp.arange(blk_count, dtype=jnp.int32)
    square_part = jnp.where(prompt == blk, square[0, :blk_count], 0.0)
    stats = jnp.stack([top_part, target_part, square_part])
    parts = everywhere(jnp.broadcast_to(stats[None], (blk_count,) + stats.shape))
    sums = jnp.sum(parts[:, 1:], axis=0)
    norms = jnp.sqrt(sums[1] / (lengths.astype(jnp.float32) * width) + 1e-06)
    request_stats = jnp.stack([norms, jnp.max(parts[:, 0], axis=0), sums[0]])
    return (out_rows[None], server, request_stats)


def local(hidden_in, lengths, routes, route_weights, norm_gain, master, *rest):
    blk_count = lax.axis_size("blk")
    fits = (
        lax.axis_size("rep") == 2
        and master.shape[3] == FF
        and EXPERTS == 2 * blk_count
        and blk_count == len(RING)
        and hidden_in.shape[1] == LEN
        and lengths.shape[0] == blk_count
    )
    form = paired if fits else general
    return form(hidden_in, lengths, routes, route_weights, norm_gain, master, *rest)


def solution(mesh):
    return jax.shard_map(
        local,
        mesh=mesh,
        in_specs=(
            P("rep", "blk", None),
            P("rep"),
            P("rep", "blk", None),
            P("rep", "blk", None),
            P(),
            P(None, "blk", None, "rep"),
            P("blk", None),
            P(),
            P("rep"),
        ),
        out_specs=(P("rep", "blk", None), P(None, None, "blk"), P(None, "rep")),
        check_vma=False,
    )
```

```python
import functools

import jax
import jax.numpy as jnp
from jax import lax
from jax.experimental import pallas as pl
from jax.experimental.pallas import tpu as pltpu
from jax.sharding import PartitionSpec as P

FF = 512
EXPERTS = 32
LEN = 128
CAP = 36
FIRST = 32
SECOND = 40
GROUPS = 4
RING = (0, 1, 4, 5, 8, 9, 12, 13, 14, 15, 10, 11, 6, 7, 2, 3)
LANES = 128
VMEM = 62 * 1024 * 1024


def merged(x, axis, combine):
    everything = jax.tree.map(lambda part: lax.all_gather(part, axis), x)
    initial = jax.tree.map(lambda part: part[0], everything)

    def turn(k, so_far):
        return combine(so_far, jax.tree.map(lambda part: part[k], everything))

    return lax.fori_loop(1, lax.axis_size(axis), turn, initial)


def combine_stats(first, second):
    return (first[0] + second[0], jnp.maximum(first[1], second[1]))


def general(
    hidden_in, lengths, routes, route_weights, norm_gain, master, unembed, final_gain, target_ids
):
    rows_here = hidden_in.shape[1]
    width = hidden_in.shape[2]
    top_count = routes.shape[2]
    blk_count = lax.axis_size("blk")
    rep_count = lax.axis_size("rep")
    blk_index = lax.axis_index("blk")
    unit_count = master.shape[3] * rep_count
    split_ways = max(1, FF // unit_count)
    local_exp = max(1, unit_count // FF)
    group_width = min(unit_count, FF)
    capacity = CAP
    blocks = master.astype(jnp.bfloat16)
    arrived_blocks = lax.all_to_all(blocks, "blk", split_axis=2, concat_axis=1, tiled=True)
    server = lax.all_gather(arrived_blocks, "rep", axis=3, tiled=True)[:, :, 0, :]
    gate_w = server[0].reshape(width, local_exp, group_width)
    up_w = server[1].reshape(width, local_exp, group_width)
    down_w = server[2].reshape(width, local_exp, group_width)
    prompts_here = lengths.shape[0]
    slot_index = blk_index * rows_here + jnp.arange(rows_here, dtype=jnp.int32)
    prompt_of = slot_index // LEN
    position = slot_index % LEN
    prompt_match = prompt_of[:, None] == jnp.arange(prompts_here, dtype=jnp.int32)[None, :]
    row_len = jnp.sum(jnp.where(prompt_match, lengths[None, :], 0), axis=1)
    is_valid = position < row_len
    resid_f = hidden_in[0].astype(jnp.float32)
    normed = (
        resid_f * lax.rsqrt(jnp.mean(resid_f * resid_f, axis=-1, keepdims=True) + 1e-05) * norm_gain
    ).astype(jnp.bfloat16)
    expert_ids = routes[0].reshape(-1)
    pair_live = jnp.repeat(is_valid, top_count)
    pair_row = jnp.repeat(jnp.arange(rows_here, dtype=jnp.int32), top_count)
    expert_hits = (
        (expert_ids[:, None] == jnp.arange(EXPERTS, dtype=jnp.int32)[None, :]) & pair_live[:, None]
    ).astype(jnp.int32)
    slot_rank = jnp.sum((jnp.cumsum(expert_hits, axis=0) - 1) * expert_hits, axis=1)
    slot_id = jnp.where(pair_live, expert_ids * capacity + slot_rank, EXPERTS * capacity)
    source_row = jnp.zeros((EXPERTS * capacity + 1,), jnp.int32).at[slot_id].set(pair_row)[:-1]
    filled = jnp.zeros((EXPERTS * capacity + 1,), jnp.bfloat16).at[slot_id].set(1.0)[:-1]
    outgoing = (normed[source_row] * filled[:, None]).reshape(EXPERTS, capacity, width)
    sending = jnp.repeat(outgoing, split_ways, axis=0).reshape(
        blk_count, local_exp, capacity, width
    )
    arrived = lax.all_to_all(sending, "blk", split_axis=0, concat_axis=0, tiled=True)
    sources = arrived.shape[0]
    slot_count = arrived.shape[2]
    stride = sources
    while stride % 2 == 0 and stride * local_exp * slot_count > 1024:
        stride = stride // 2
    grouped = arrived.reshape(sources // stride, stride, local_exp, slot_count, width)

    def one_block(portion):
        gate_out = jnp.einsum("slnd,dlf->slnf", portion, gate_w, preferred_element_type=jnp.float32)
        up_out = jnp.einsum("slnd,dlf->slnf", portion, up_w, preferred_element_type=jnp.float32)
        hidden = (jax.nn.silu(gate_out) * up_out).astype(jnp.bfloat16)
        return jnp.einsum(
            "slnf,dlf->slnd", hidden, down_w, preferred_element_type=jnp.float32
        ).astype(jnp.bfloat16)

    returned = lax.all_to_all(
        lax.map(one_block, grouped).reshape(sources, local_exp, slot_count, width),
        "blk",
        split_axis=0,
        concat_axis=0,
        tiled=True,
    )
    summed_f = jnp.sum(
        returned.reshape(EXPERTS, split_ways, capacity, width).astype(jnp.float32), axis=1
    )
    expert_out = lax.optimization_barrier(summed_f.astype(jnp.bfloat16)).reshape(
        EXPERTS * capacity, width
    )
    gather_index = jnp.where(pair_live, expert_ids * capacity + slot_rank, 0)
    pair_weight = route_weights[0].reshape(-1) * pair_live.astype(jnp.float32)
    moe = jnp.sum(
        (expert_out[gather_index].astype(jnp.float32) * pair_weight[:, None]).reshape(
            rows_here, top_count, width
        ),
        axis=1,
    )
    out_rows = (resid_f + moe).astype(jnp.bfloat16)
    out_f = out_rows.astype(jnp.float32)
    row_squares = jnp.sum(out_f * out_f, axis=-1) * is_valid.astype(jnp.float32)
    square_local = jnp.sum(jnp.where(prompt_match, row_squares[:, None], 0.0), axis=0)
    is_last = is_valid & (position == row_len - 1)
    picker = (prompt_match & is_last[:, None]).astype(jnp.bfloat16)
    last_local = lax.dot_general(
        picker, out_rows, (((0,), (0,)), ((), ())), preferred_element_type=jnp.float32
    )
    last_rows, square_total = lax.psum((last_local, square_local), "blk")
    norms = jnp.sqrt(square_total / (lengths.astype(jnp.float32) * width) + 1e-06)
    final = (
        last_rows
        * lax.rsqrt(jnp.mean(last_rows * last_rows, axis=-1, keepdims=True) + 1e-05)
        * final_gain
    ).astype(jnp.bfloat16)
    logits = lax.dot_general(
        final, unembed, (((1,), (1,)), ((), ())), preferred_element_type=jnp.float32
    )
    vocab_base = blk_index * unembed.shape[0]
    target_hit = (
        target_ids[:, None] == vocab_base + jnp.arange(unembed.shape[0], dtype=jnp.int32)[None, :]
    )
    target_part = jnp.sum(jnp.where(target_hit, logits, 0.0), axis=1)
    top_part = jnp.max(logits, axis=1)
    target_logit, top_logit = merged((target_part, top_part), "blk", combine_stats)
    request_stats = jnp.stack([norms, top_logit, target_logit])
    return (out_rows[None], server, request_stats)


def iota(shape, dim):
    return lax.broadcasted_iota(jnp.int32, shape, dim)


def prep_kernel(lengths_ref, blk_ref, hidden_ref, routes_ref, weights_ref, gain_ref, rows_ref, pieces_ref):
    rows, width = hidden_ref.shape
    length = lengths_ref[blk_ref[0]]
    x = hidden_ref[...].astype(jnp.float32)
    scale = lax.rsqrt(jnp.mean(x * x, axis=-1, keepdims=True) + 1e-05)
    rows_ref[:, :width] = (x * scale * gain_ref[...][None]).astype(jnp.bfloat16)
    column = iota((rows, LANES), 1)
    lane = column & (EXPERTS - 1)
    row = iota((rows, LANES), 0)
    hit = jnp.zeros((rows, LANES), jnp.float32)
    weight = jnp.zeros((rows, LANES), jnp.float32)
    named_by = jnp.transpose(routes_ref[...].astype(jnp.float32)).astype(jnp.int32)
    weight_by = jnp.transpose(weights_ref[...])
    for k in range(routes_ref.shape[0]):
        named = named_by[:, k : k + 1] == lane
        hit = hit + jnp.where(named, 1.0, 0.0)
        weight = weight + jnp.where(named, weight_by[:, k : k + 1], 0.0)
    live = row < length
    hit = jnp.where(live, hit, 0.0)
    weight = jnp.where(live, weight, 0.0)
    before = jnp.where(iota((rows, rows), 1) < iota((rows, rows), 0), 1.0, 0.0)
    rank = jnp.dot(
        before.astype(jnp.bfloat16), hit.astype(jnp.bfloat16), preferred_element_type=jnp.float32
    )
    told = jnp.where(hit > 0.0, rank, -1.0)
    for k in range(3):
        piece = weight.astype(jnp.bfloat16)
        pieces_ref[k * rows : (k + 1) * rows, :] = piece
        value = piece.astype(jnp.float32)
        told = jnp.where(column >= (k + 1) * EXPERTS, value, told)
        weight = weight - value
    rows_ref[:, width:] = told.astype(jnp.bfloat16)


def pick(info, lengths_ref, ring_ref, which, x_ref, width, place, slots, lasts):
    step = pl.program_id(0)
    rows = x_ref.shape[0]
    sources = rows // LEN
    ranks = x_ref[:, width:].astype(jnp.float32)
    lane = iota((rows, LANES), 1)
    row = iota((rows, 1), 0)
    source = row // LEN
    rank = jnp.sum(jnp.where(lane == info[which], ranks, 0.0), axis=1, keepdims=True)
    slot = jnp.where(rank >= 0.0, place(source.astype(jnp.float32), rank), -1.0)
    slot_lane = iota((rows, slots), 1).astype(jnp.float32)
    one_hot = jnp.where(slot == slot_lane, 1.0, 0.0).astype(jnp.bfloat16)
    dims = (((0,), (0,)), ((), ()))
    chosen = lax.dot_general(
        one_hot, x_ref[:, :width], dims, preferred_element_type=jnp.float32
    )
    home = jnp.full_like(row, -1)
    for s in range(sources):
        owner = ring_ref[step * sources + s]
        home = jnp.where(row == s * LEN + lengths_ref[owner] - 1, owner, home)
    home = jnp.where(rank >= 0.0, home, -1)
    count = lasts.shape[0]
    one_hot = jnp.where(home == iota((rows, count), 1), 1.0, 0.0).astype(jnp.bfloat16)
    last = lax.dot_general(one_hot, x_ref[...], dims, preferred_element_type=jnp.float32)

    @pl.when(step == 0)
    def _():
        lasts[...] = last

    @pl.when(step != 0)
    def _():
        lasts[...] += last

    return chosen


def share_of(info, which, lasts, width):
    ext = lasts[:, width:]
    lane = iota(ext.shape, 1)
    is_own = (lane >= EXPERTS) & ((lane & (EXPERTS - 1)) == info[which])
    return jnp.broadcast_to(
        jnp.sum(jnp.where(is_own, ext, 0.0), axis=1, keepdims=True), ext.shape
    )


def activ(x, g_ref, u_ref):
    x = x.astype(jnp.bfloat16)
    gate = jnp.dot(x, g_ref[...], preferred_element_type=jnp.float32)
    up = jnp.dot(x, u_ref[...], preferred_element_type=jnp.float32)
    return (gate / (1.0 + jnp.exp(-gate)) * up).astype(jnp.bfloat16)


def own_kernel(
    info, lengths_ref, ring_ref, x_ref, g_ref, u_ref, out_ref, spot_ref, share_ref, picked, lasts
):
    step = pl.program_id(0)
    sources = x_ref.shape[0] // LEN
    width = g_ref.shape[0]
    more = CAP - FIRST
    early = sources * FIRST
    all_early = GROUPS * early
    all_rows = all_early + GROUPS * sources * more

    def place(source, rank):
        return jnp.where(
            rank < FIRST, source * FIRST + rank, early + source * more + (rank - FIRST)
        )

    chosen = pick(
        info, lengths_ref, ring_ref, 0, x_ref, width, place, early + sources * more, lasts
    )
    for s in range(sources):
        start = pl.multiple_of(ring_ref[step * sources + s] * FIRST, FIRST)
        picked[pl.ds(start, FIRST), :] = chosen[s * FIRST : (s + 1) * FIRST]
    start = pl.multiple_of(all_early + step * sources * more, sources * more)
    picked[pl.ds(start, sources * more), :] = chosen[early:]

    @pl.when(step == GROUPS - 1)
    def _():
        picked[all_rows:, :] = lasts[:, :width]
        out_ref[...] = activ(picked[...], g_ref, u_ref)
        share_ref[...] = share_of(info, 0, lasts, width)
        column = iota(spot_ref.shape, 1)
        owner = lax.shift_right_logical(column, more.bit_length() - 1)
        source = jnp.full_like(column, -1)
        for k, b in enumerate(RING):
            source = jnp.where(owner == k, b, source)
        spot = jnp.where(source >= 0, source * SECOND + (column & (more - 1)), -1)
        spot_ref[...] = jnp.where(iota(spot_ref.shape, 0) == spot, 1.0, 0.0).astype(jnp.bfloat16)


def oth_kernel(
    info,
    lengths_ref,
    ring_ref,
    x_ref,
    g_ref,
    u_ref,
    resid_ref,
    _,
    out_ref,
    share_ref,
    base_ref,
    picked,
    lasts,
):
    step = pl.program_id(0)
    sources = x_ref.shape[0] // LEN
    width = g_ref.shape[0]
    all_rows = GROUPS * sources * SECOND

    def place(source, rank):
        return source * SECOND + (SECOND - CAP) + rank

    chosen = pick(info, lengths_ref, ring_ref, 1, x_ref, width, place, sources * SECOND, lasts)
    for s in range(sources):
        start = pl.multiple_of(ring_ref[step * sources + s] * SECOND, SECOND)
        picked[pl.ds(start, SECOND), :] = chosen[s * SECOND : (s + 1) * SECOND]

    @pl.when(step == GROUPS - 1)
    def _():
        picked[all_rows:, :] = lasts[:, :width]
        out_ref[...] = activ(picked[...], g_ref, u_ref)
        share_ref[...] = share_of(info, 1, lasts, width)
        resid = resid_ref[...].astype(jnp.float32)
        is_last = iota(resid.shape, 0) == info[3] - 1
        last = jnp.sum(jnp.where(is_last, resid, 0.0), axis=0, keepdims=True)
        base_ref[...] = jnp.where(iota(base_ref.shape, 0) == info[4], last, 0.0)


def matmul_nt(hidden_ref, d):
    return lax.dot_general(
        hidden_ref[...], d, (((1,), (1,)), ((), ())), preferred_element_type=jnp.float32
    )


def fetched(sources, held, sems):
    step = pl.program_id(0)
    rows = held.shape[1]

    @pl.when(step == 0)
    def _():
        for k, source in enumerate(sources):
            pltpu.make_async_copy(source, held.at[k], sems.at[k]).start()

    for k, source in enumerate(sources):

        @pl.when(step == k)
        def _():
            pltpu.make_async_copy(source, held.at[k], sems.at[k]).wait()

    return held[step]


def own_down_kernel(hidden_ref, share_ref, d_ref, out_ref, late_ref, part_ref, held, sems):
    size = held.shape[1]
    d = fetched([d_ref.at[k * size : (k + 1) * size] for k in range(held.shape[0])], held, sems)
    out = matmul_nt(hidden_ref, d).astype(jnp.bfloat16)
    rows = out_ref.shape[0]
    out_ref[...] = out[:rows]
    late_ref[...] = out[rows:]
    count = part_ref.shape[0]
    part_ref[...] = share_ref[:, :1] * out[-count:].astype(jnp.float32)


def oth_down_kernel(
    info,
    hidden_ref,
    share_ref,
    spot_ref,
    late_ref,
    base_ref,
    part_ref,
    d_ref,
    out_ref,
    sum_ref,
    held,
    sems,
):
    size = held.shape[1]
    other = 1 - info[2]
    sources = [d_ref.at[other, k * size : (k + 1) * size] for k in range(held.shape[0])]
    d = fetched(sources, held, sems)
    late = jnp.dot(spot_ref[...], late_ref[...], preferred_element_type=jnp.float32)
    out = matmul_nt(hidden_ref, d)
    rows = out_ref.shape[0]
    out_ref[...] = (late + out[:rows]).astype(jnp.bfloat16)
    last = out[rows:].astype(jnp.bfloat16).astype(jnp.float32)
    total = base_ref[...] + part_ref[...] + share_ref[:, :1] * last
    high = total.astype(jnp.bfloat16)
    low = jnp.where(iota(total.shape, 0) == info[4], total - high.astype(jnp.float32), 0.0)
    low = jnp.sum(low, axis=0, keepdims=True)
    count = total.shape[0]
    sum_ref[:count, :] = high
    rest = (sum_ref.shape[0] - count, total.shape[1])
    sum_ref[count:, :] = jnp.where(iota(rest, 0) == 0, low, 0.0).astype(jnp.bfloat16)


def mix_kernel(info, rank_ref, pieces_ref, first_ref, second_ref):
    rows = rank_ref.shape[0]
    late = SECOND - CAP
    own, oth = info[2], 1 - info[2]
    for mix_ref, stride, spans in (
        (first_ref, FIRST, ((own, 0, FIRST, 0),)),
        (second_ref, SECOND, ((own, 0, late, FIRST), (oth, late, CAP, 0))),
    ):
        slots = mix_ref.shape[1]
        expert = iota((LANES, slots), 0)
        lane = iota((LANES, slots), 1)
        within = jnp.zeros((1, slots), jnp.float32)
        spread = jnp.zeros((LANES, slots), jnp.float32)
        for parity, offset, count, lowest in spans:
            start = jnp.where((expert & 1) == parity, (expert >> 1) * stride + offset, slots)
            inside = (lane >= start) & (lane < start + count)
            spread = spread + jnp.where(inside, 1.0, 0.0)
            ranks = jnp.where(inside, lane - start + lowest, 0)
            within = within + jnp.sum(ranks, axis=0, keepdims=True).astype(jnp.float32)
        spread = spread.astype(jnp.bfloat16)
        rank = jnp.dot(rank_ref[...], spread, preferred_element_type=jnp.float32)
        match = rank == within
        for k in range(3):
            part = jnp.dot(
                pieces_ref[k * rows : (k + 1) * rows, :], spread, preferred_element_type=jnp.float32
            )
            mix_ref[k * rows : (k + 1) * rows, :] = jnp.where(match, part, 0.0).astype(jnp.bfloat16)


def weigh(mix_ref, back_ref):
    rows = mix_ref.shape[0] // 3
    parts = jnp.dot(mix_ref[...], back_ref[...], preferred_element_type=jnp.float32)
    return parts[2 * rows :] + parts[rows : 2 * rows] + parts[:rows]


def first_kernel(mix_ref, back_ref, resid_ref, base_ref):
    base_ref[...] = resid_ref[...].astype(jnp.float32) + weigh(mix_ref, back_ref)


def combine_kernel(info, mix_ref, back_ref, base_ref, _, __, out_ref, square_ref, squares):
    step = pl.program_id(0)

    @pl.when(step == 0)
    def _():
        squares[...] = jnp.zeros_like(squares)

    out = (base_ref[...] + weigh(mix_ref, back_ref)).astype(jnp.bfloat16)
    out_ref[...] = out
    out_f = out.astype(jnp.float32)
    row = iota(out_f.shape, 0)
    squares[...] += jnp.sum(jnp.where(row < info[3], out_f * out_f, 0.0), axis=0, keepdims=True)

    @pl.when(step == pl.num_programs(0) - 1)
    def _():
        total = jnp.sum(squares[...], axis=1, keepdims=True)
        square_ref[...] = jnp.broadcast_to(total, square_ref.shape)


def place_kernel(info, g_own, g_oth, u_own, u_oth, d_both, _, out_ref):
    left = info[2] == 0
    for k, (own, oth) in enumerate(((g_own[...], g_oth[...]), (u_own[...], u_oth[...]))):
        out_ref[k, :, :FF] = jnp.where(left, own, oth)
        out_ref[k, :, FF:] = jnp.where(left, oth, own)
    out_ref[2, :, :FF] = d_both[0]
    out_ref[2, :, FF:] = d_both[1]


def cast_kernel(first_row, blocks, x_ref, *refs):
    out_ref, held, turned, sems_in, sems_out = refs[-5:]
    groups, size = held.shape[:2]
    fetches, stores = [], []
    for g in range(groups):
        rows = pl.ds(first_row + g * size, size)
        fetches.append(pltpu.make_async_copy(x_ref.at[rows], held.at[g], sems_in.at[g]))
        target = out_ref.at[:, g * 16 : (g + 1) * 16]
        stores.append(pltpu.make_async_copy(turned.at[g], target, sems_out.at[g]))
    for fetch in fetches:
        fetch.start()
    target = iota((size, size), 0)
    source = (target & 15) * blocks + lax.shift_right_logical(target, 4)
    order = jnp.where(iota((size, size), 1) == source, 1.0, 0.0).astype(jnp.bfloat16)
    for g in range(groups):
        fetches[g].wait()
        rows = jnp.dot(order, held[g].astype(jnp.bfloat16), preferred_element_type=jnp.float32)
        turned[g] = rows.astype(jnp.bfloat16).reshape(turned.shape[1:])
        stores[g].start()
    for store in stores:
        store.wait()


def tie_kernel(*_):
    pass


def params():
    return pltpu.CompilerParams(vmem_limit_bytes=VMEM, dimension_semantics=("arbitrary",))


def whole(shape):
    return pl.BlockSpec(shape, lambda *_: tuple(0 for _ in shape))


def paired(
    hidden_in, lengths, routes, route_weights, norm_gain, master, unembed, final_gain, target_ids
):
    rows = hidden_in.shape[1]
    width = hidden_in.shape[2]
    blk_count = lax.axis_size("blk")
    blk = lax.axis_index("blk")
    rep = lax.axis_index("rep")
    first = blk_count * FIRST
    second = blk_count * SECOND
    resid = hidden_in[0]
    info = jnp.stack([2 * blk + rep, 2 * blk + 1 - rep, rep, lengths[blk], blk])
    info = info.astype(jnp.int32)

    shard_rows = master.shape[1]
    flat = master.reshape(3 * shard_rows * blk_count, FF)

    groups = shard_rows // 16

    def turned(k, *after):
        return pl.pallas_call(
            functools.partial(cast_kernel, k * shard_rows * blk_count, blk_count),
            in_specs=[pl.BlockSpec(memory_space=pl.ANY)] * (1 + len(after)),
            out_specs=pl.BlockSpec(memory_space=pl.ANY),
            out_shape=jax.ShapeDtypeStruct((blk_count, shard_rows, FF), jnp.bfloat16),
            scratch_shapes=[
                pltpu.VMEM((groups, 16 * blk_count, FF), jnp.float32),
                pltpu.VMEM((groups, blk_count, 16, FF), jnp.bfloat16),
                pltpu.SemaphoreType.DMA((groups,)),
                pltpu.SemaphoreType.DMA((groups,)),
            ],
            compiler_params=pltpu.CompilerParams(vmem_limit_bytes=VMEM),
            name="cast",
        )(flat, *after)

    def moved(x):
        own = lax.all_to_all(x, "blk", split_axis=0, concat_axis=0, tiled=True)
        return own.reshape(width, FF)

    def swapped(x):
        return lax.ppermute(x, "rep", [(0, 1), (1, 0)])

    def tied(x, *after):
        return pl.pallas_call(
            tie_kernel,
            in_specs=[pl.BlockSpec(memory_space=pl.ANY)] * (1 + len(after)),
            out_specs=pl.BlockSpec(memory_space=pl.ANY),
            out_shape=jax.ShapeDtypeStruct(x.shape, x.dtype),
            input_output_aliases={0: 0},
            name="tie",
        )(x, *after)

    row_ext, pieces = pl.pallas_call(
        prep_kernel,
        grid_spec=pltpu.PrefetchScalarGridSpec(
            num_scalar_prefetch=2,
            grid=(1,),
            in_specs=[
                whole((rows, width)),
                whole((routes.shape[2], rows)),
                whole((routes.shape[2], rows)),
                whole((width,)),
            ],
            out_specs=[whole((rows, width + LANES)), whole((3 * rows, LANES))],
        ),
        out_shape=[
            jax.ShapeDtypeStruct((rows, width + LANES), jnp.bfloat16),
            jax.ShapeDtypeStruct((3 * rows, LANES), jnp.bfloat16),
        ],
        compiler_params=params(),
        name="prep",
    )(lengths, blk[None].astype(jnp.int32), resid, routes[0].T, route_weights[0].T, norm_gain)
    g_own = moved(turned(0, row_ext))
    g_oth = swapped(g_own)
    u_own = moved(turned(1))
    u_oth = swapped(u_own)
    d_own = moved(tied(turned(2), g_oth))

    tokens = lax.all_gather(row_ext, "blk", axis_index_groups=[list(RING)], axis=0, tiled=True)

    ring = jnp.array(RING, jnp.int32)

    def hidden_of(kernel, outs, picked, operands, specs):
        return pl.pallas_call(
            kernel,
            grid_spec=pltpu.PrefetchScalarGridSpec(
                num_scalar_prefetch=3,
                grid=(GROUPS,),
                in_specs=[pl.BlockSpec((blk_count // GROUPS * rows, width + LANES), lambda i, *_: (i, 0))]
                + [whole((width, FF))] * 2
                + specs,
                out_specs=[whole(out.shape) for out in outs],
                scratch_shapes=[
                    pltpu.VMEM((picked, width), jnp.float32),
                    pltpu.VMEM((blk_count, width + LANES), jnp.float32),
                ],
            ),
            out_shape=outs,
            compiler_params=params(),
            name="gate_up",
        )(info, lengths, ring, tokens, *operands)

    step = 512
    quarter = width // 4
    anywhere = pl.BlockSpec(memory_space=pl.ANY)

    def returned(x):
        slots = x.shape[0]
        x = x.reshape(blk_count, slots // blk_count, width)
        x = lax.all_to_all(x, "blk", split_axis=0, concat_axis=0, tiled=True)
        return x.reshape(slots, width)

    def bf16(*shape):
        return jax.ShapeDtypeStruct(shape, jnp.bfloat16)

    def f32(*shape):
        return jax.ShapeDtypeStruct(shape, jnp.float32)

    extra = blk_count * (CAP - FIRST) + blk_count
    own_hidden, spot, own_share = hidden_of(
        own_kernel,
        [bf16(first + extra, FF), bf16(second, extra), f32(blk_count, LANES)],
        first + extra,
        (g_own, u_own),
        [],
    )
    d_own = tied(d_own, own_hidden)
    d_both = lax.all_gather(d_own, "rep", axis=0)
    own_out, late_out, own_part = pl.pallas_call(
        own_down_kernel,
        grid=(width // step,),
        in_specs=[whole((first + extra, FF)), whole((blk_count, LANES)), anywhere],
        out_specs=[
            pl.BlockSpec((first, step), lambda i: (0, i)),
            pl.BlockSpec((extra, step), lambda i: (0, i)),
            pl.BlockSpec((blk_count, step), lambda i: (0, i)),
        ],
        out_shape=[bf16(first, width), bf16(extra, width), f32(blk_count, width)],
        scratch_shapes=[
            pltpu.VMEM((width // step, step, FF), jnp.bfloat16),
            pltpu.SemaphoreType.DMA((width // step,)),
        ],
        compiler_params=params(),
        name="own_down",
    )(own_hidden, own_share, d_own)
    own_out = tied(own_out, u_oth)
    own_back = returned(own_out)
    oth_hidden, oth_share, base_part = hidden_of(
        oth_kernel,
        [bf16(second + blk_count, FF), f32(blk_count, LANES), f32(blk_count, width)],
        second + blk_count,
        (g_oth, u_oth, resid, own_out),
        [whole((rows, width)), anywhere],
    )
    part_spec = pl.BlockSpec((blk_count, quarter), lambda i, *_: (0, i))
    oth_out, last_part = pl.pallas_call(
        oth_down_kernel,
        grid_spec=pltpu.PrefetchScalarGridSpec(
            num_scalar_prefetch=1,
            grid=(4,),
            in_specs=[
                whole((second + blk_count, FF)),
                whole((blk_count, LANES)),
                whole((second, extra)),
                pl.BlockSpec((extra, quarter), lambda i, *_: (0, i)),
                part_spec,
                part_spec,
                anywhere,
            ],
            out_specs=[
                pl.BlockSpec((second, quarter), lambda i, *_: (0, i)),
                pl.BlockSpec((blk_count + 8, quarter), lambda i, *_: (0, i)),
            ],
            scratch_shapes=[
                pltpu.VMEM((4, quarter, FF), jnp.bfloat16),
                pltpu.SemaphoreType.DMA((4,)),
            ],
        ),
        out_shape=[bf16(second, width), bf16(blk_count + 8, width)],
        compiler_params=params(),
        name="oth_down",
    )(info, oth_hidden, oth_share, spot, late_out, base_part, own_part, d_both)
    last_parts = lax.all_gather(last_part, "blk", axis=0).astype(jnp.float32)
    last_total = jnp.sum(last_parts[:, :blk_count], axis=0) + last_parts[:, blk_count]
    oth_back = returned(oth_out)

    server = pl.pallas_call(
        place_kernel,
        grid_spec=pltpu.PrefetchScalarGridSpec(
            num_scalar_prefetch=1,
            grid=(4,),
            in_specs=[pl.BlockSpec((quarter, FF), lambda i, *_: (i, 0))] * 4
            + [pl.BlockSpec((2, quarter, FF), lambda i, *_: (0, i, 0)), anywhere],
            out_specs=pl.BlockSpec((3, quarter, 2 * FF), lambda i, *_: (0, i, 0)),
        ),
        out_shape=jax.ShapeDtypeStruct((3, width, 2 * FF), jnp.bfloat16),
        compiler_params=params(),
        name="place",
    )(info, g_own, g_oth, u_own, u_oth, d_both, oth_out)

    first_mix, second_mix = pl.pallas_call(
        mix_kernel,
        grid_spec=pltpu.PrefetchScalarGridSpec(
            num_scalar_prefetch=1,
            grid=(1,),
            in_specs=[
                pl.BlockSpec((rows, LANES), lambda i, *_: (0, width // LANES)),
                whole((3 * rows, LANES)),
            ],
            out_specs=[whole((3 * rows, first)), whole((3 * rows, second))],
        ),
        out_shape=[
            jax.ShapeDtypeStruct((3 * rows, first), jnp.bfloat16),
            jax.ShapeDtypeStruct((3 * rows, second), jnp.bfloat16),
        ],
        compiler_params=params(),
        name="mix",
    )(info, row_ext, pieces)

    def weigh_specs(slots):
        return [whole((3 * rows, slots)), pl.BlockSpec((slots, step), lambda i, *_: (0, i))]

    column = pl.BlockSpec((rows, step), lambda i, *_: (0, i))
    base = pl.pallas_call(
        first_kernel,
        grid=(width // step,),
        in_specs=weigh_specs(first) + [column],
        out_specs=column,
        out_shape=f32(rows, width),
        compiler_params=params(),
        name="first",
    )(first_mix, own_back, resid)
    last_rows = lax.reduce_precision(last_total, 8, 7)
    final = (
        last_rows
        * lax.rsqrt(jnp.mean(last_rows * last_rows, axis=-1, keepdims=True) + 1e-05)
        * final_gain
    ).astype(jnp.bfloat16)
    logits = lax.dot_general(
        final, unembed, (((1,), (1,)), ((), ())), preferred_element_type=jnp.float32
    )
    vocab_base = blk * unembed.shape[0]
    target_hit = (
        target_ids[:, None] == vocab_base + jnp.arange(unembed.shape[0], dtype=jnp.int32)[None, :]
    )
    target_part = jnp.sum(jnp.where(target_hit, logits, 0.0), axis=1)
    top_part = jnp.max(logits, axis=1)

    out_rows, square = pl.pallas_call(
        combine_kernel,
        grid_spec=pltpu.PrefetchScalarGridSpec(
            num_scalar_prefetch=1,
            grid=(width // step,),
            in_specs=weigh_specs(second) + [column, anywhere, anywhere],
            out_specs=[column, whole((1, LANES))],
            scratch_shapes=[pltpu.VMEM((1, step), jnp.float32)],
        ),
        out_shape=[
            jax.ShapeDtypeStruct((rows, width), jnp.bfloat16),
            jax.ShapeDtypeStruct((1, LANES), jnp.float32),
        ],
        compiler_params=params(),
        name="combine",
    )(info, second_mix, oth_back, base, server, top_part[None])

    def everywhere(copies):
        return lax.all_to_all(copies, "blk", split_axis=0, concat_axis=0, tiled=True)

    prompt = jnp.arange(blk_count, dtype=jnp.int32)
    square_part = jnp.where(prompt == blk, square[0, :blk_count], 0.0)
    stats = jnp.stack([top_part, target_part, square_part])
    parts = everywhere(jnp.broadcast_to(stats[None], (blk_count,) + stats.shape))
    sums = jnp.sum(parts[:, 1:], axis=0)
    norms = jnp.sqrt(sums[1] / (lengths.astype(jnp.float32) * width) + 1e-06)
    request_stats = jnp.stack([norms, jnp.max(parts[:, 0], axis=0), sums[0]])
    return (out_rows[None], server, request_stats)


def local(hidden_in, lengths, routes, route_weights, norm_gain, master, *rest):
    blk_count = lax.axis_size("blk")
    fits = (
        lax.axis_size("rep") == 2
        and master.shape[3] == FF
        and EXPERTS == 2 * blk_count
        and blk_count == len(RING)
        and hidden_in.shape[1] == LEN
        and lengths.shape[0] == blk_count
    )
    form = paired if fits else general
    return form(hidden_in, lengths, routes, route_weights, norm_gain, master, *rest)


def solution(mesh):
    return jax.shard_map(
        local,
        mesh=mesh,
        in_specs=(
            P("rep", "blk", None),
            P("rep"),
            P("rep", "blk", None),
            P("rep", "blk", None),
            P(),
            P(None, "blk", None, "rep"),
            P("blk", None),
            P(),
            P("rep"),
        ),
        out_specs=(P("rep", "blk", None), P(None, None, "blk"), P(None, "rep")),
        check_vma=False,
    )
```

```python
import functools

import jax
import jax.numpy as jnp
from jax import lax
from jax.experimental import pallas as pl
from jax.experimental.pallas import tpu as pltpu
from jax.sharding import PartitionSpec as P

FF = 512
EXPERTS = 32
LEN = 128
CAP = 36
FIRST = 32
SECOND = 40
GROUPS = 4
RING = (0, 1, 4, 5, 8, 9, 12, 13, 14, 15, 10, 11, 6, 7, 2, 3)
LANES = 128
VMEM = 56 * 1024 * 1024


def merged(x, axis, combine):
    everything = jax.tree.map(lambda part: lax.all_gather(part, axis), x)
    initial = jax.tree.map(lambda part: part[0], everything)

    def turn(k, so_far):
        return combine(so_far, jax.tree.map(lambda part: part[k], everything))

    return lax.fori_loop(1, lax.axis_size(axis), turn, initial)


def combine_stats(first, second):
    return (first[0] + second[0], jnp.maximum(first[1], second[1]))


def general(
    hidden_in, lengths, routes, route_weights, norm_gain, master, unembed, final_gain, target_ids
):
    rows_here = hidden_in.shape[1]
    width = hidden_in.shape[2]
    top_count = routes.shape[2]
    blk_count = lax.axis_size("blk")
    rep_count = lax.axis_size("rep")
    blk_index = lax.axis_index("blk")
    unit_count = master.shape[3] * rep_count
    split_ways = max(1, FF // unit_count)
    local_exp = max(1, unit_count // FF)
    group_width = min(unit_count, FF)
    capacity = CAP
    blocks = master.astype(jnp.bfloat16)
    arrived_blocks = lax.all_to_all(blocks, "blk", split_axis=2, concat_axis=1, tiled=True)
    server = lax.all_gather(arrived_blocks, "rep", axis=3, tiled=True)[:, :, 0, :]
    gate_w = server[0].reshape(width, local_exp, group_width)
    up_w = server[1].reshape(width, local_exp, group_width)
    down_w = server[2].reshape(width, local_exp, group_width)
    prompts_here = lengths.shape[0]
    slot_index = blk_index * rows_here + jnp.arange(rows_here, dtype=jnp.int32)
    prompt_of = slot_index // LEN
    position = slot_index % LEN
    prompt_match = prompt_of[:, None] == jnp.arange(prompts_here, dtype=jnp.int32)[None, :]
    row_len = jnp.sum(jnp.where(prompt_match, lengths[None, :], 0), axis=1)
    is_valid = position < row_len
    resid_f = hidden_in[0].astype(jnp.float32)
    normed = (
        resid_f * lax.rsqrt(jnp.mean(resid_f * resid_f, axis=-1, keepdims=True) + 1e-05) * norm_gain
    ).astype(jnp.bfloat16)
    expert_ids = routes[0].reshape(-1)
    pair_live = jnp.repeat(is_valid, top_count)
    pair_row = jnp.repeat(jnp.arange(rows_here, dtype=jnp.int32), top_count)
    expert_hits = (
        (expert_ids[:, None] == jnp.arange(EXPERTS, dtype=jnp.int32)[None, :]) & pair_live[:, None]
    ).astype(jnp.int32)
    slot_rank = jnp.sum((jnp.cumsum(expert_hits, axis=0) - 1) * expert_hits, axis=1)
    slot_id = jnp.where(pair_live, expert_ids * capacity + slot_rank, EXPERTS * capacity)
    source_row = jnp.zeros((EXPERTS * capacity + 1,), jnp.int32).at[slot_id].set(pair_row)[:-1]
    filled = jnp.zeros((EXPERTS * capacity + 1,), jnp.bfloat16).at[slot_id].set(1.0)[:-1]
    outgoing = (normed[source_row] * filled[:, None]).reshape(EXPERTS, capacity, width)
    sending = jnp.repeat(outgoing, split_ways, axis=0).reshape(
        blk_count, local_exp, capacity, width
    )
    arrived = lax.all_to_all(sending, "blk", split_axis=0, concat_axis=0, tiled=True)
    sources = arrived.shape[0]
    slot_count = arrived.shape[2]
    stride = sources
    while stride % 2 == 0 and stride * local_exp * slot_count > 1024:
        stride = stride // 2
    grouped = arrived.reshape(sources // stride, stride, local_exp, slot_count, width)

    def one_block(portion):
        gate_out = jnp.einsum("slnd,dlf->slnf", portion, gate_w, preferred_element_type=jnp.float32)
        up_out = jnp.einsum("slnd,dlf->slnf", portion, up_w, preferred_element_type=jnp.float32)
        hidden = (jax.nn.silu(gate_out) * up_out).astype(jnp.bfloat16)
        return jnp.einsum(
            "slnf,dlf->slnd", hidden, down_w, preferred_element_type=jnp.float32
        ).astype(jnp.bfloat16)

    returned = lax.all_to_all(
        lax.map(one_block, grouped).reshape(sources, local_exp, slot_count, width),
        "blk",
        split_axis=0,
        concat_axis=0,
        tiled=True,
    )
    summed_f = jnp.sum(
        returned.reshape(EXPERTS, split_ways, capacity, width).astype(jnp.float32), axis=1
    )
    expert_out = lax.optimization_barrier(summed_f.astype(jnp.bfloat16)).reshape(
        EXPERTS * capacity, width
    )
    gather_index = jnp.where(pair_live, expert_ids * capacity + slot_rank, 0)
    pair_weight = route_weights[0].reshape(-1) * pair_live.astype(jnp.float32)
    moe = jnp.sum(
        (expert_out[gather_index].astype(jnp.float32) * pair_weight[:, None]).reshape(
            rows_here, top_count, width
        ),
        axis=1,
    )
    out_rows = (resid_f + moe).astype(jnp.bfloat16)
    out_f = out_rows.astype(jnp.float32)
    row_squares = jnp.sum(out_f * out_f, axis=-1) * is_valid.astype(jnp.float32)
    square_local = jnp.sum(jnp.where(prompt_match, row_squares[:, None], 0.0), axis=0)
    is_last = is_valid & (position == row_len - 1)
    picker = (prompt_match & is_last[:, None]).astype(jnp.bfloat16)
    last_local = lax.dot_general(
        picker, out_rows, (((0,), (0,)), ((), ())), preferred_element_type=jnp.float32
    )
    last_rows, square_total = lax.psum((last_local, square_local), "blk")
    norms = jnp.sqrt(square_total / (lengths.astype(jnp.float32) * width) + 1e-06)
    final = (
        last_rows
        * lax.rsqrt(jnp.mean(last_rows * last_rows, axis=-1, keepdims=True) + 1e-05)
        * final_gain
    ).astype(jnp.bfloat16)
    logits = lax.dot_general(
        final, unembed, (((1,), (1,)), ((), ())), preferred_element_type=jnp.float32
    )
    vocab_base = blk_index * unembed.shape[0]
    target_hit = (
        target_ids[:, None] == vocab_base + jnp.arange(unembed.shape[0], dtype=jnp.int32)[None, :]
    )
    target_part = jnp.sum(jnp.where(target_hit, logits, 0.0), axis=1)
    top_part = jnp.max(logits, axis=1)
    target_logit, top_logit = merged((target_part, top_part), "blk", combine_stats)
    request_stats = jnp.stack([norms, top_logit, target_logit])
    return (out_rows[None], server, request_stats)


def iota(shape, dim):
    return lax.broadcasted_iota(jnp.int32, shape, dim)


def prep_kernel(lengths_ref, blk_ref, hidden_ref, routes_ref, weights_ref, gain_ref, rows_ref, pieces_ref):
    rows, width = hidden_ref.shape
    length = lengths_ref[blk_ref[0]]
    x = hidden_ref[...].astype(jnp.float32)
    scale = lax.rsqrt(jnp.mean(x * x, axis=-1, keepdims=True) + 1e-05)
    rows_ref[:, :width] = (x * scale * gain_ref[...][None]).astype(jnp.bfloat16)
    column = iota((rows, LANES), 1)
    lane = column & (EXPERTS - 1)
    row = iota((rows, LANES), 0)
    hit = jnp.zeros((rows, LANES), jnp.float32)
    weight = jnp.zeros((rows, LANES), jnp.float32)
    named_by = jnp.transpose(routes_ref[...].astype(jnp.float32)).astype(jnp.int32)
    weight_by = jnp.transpose(weights_ref[...])
    for k in range(routes_ref.shape[0]):
        named = named_by[:, k : k + 1] == lane
        hit = hit + jnp.where(named, 1.0, 0.0)
        weight = weight + jnp.where(named, weight_by[:, k : k + 1], 0.0)
    live = row < length
    hit = jnp.where(live, hit, 0.0)
    weight = jnp.where(live, weight, 0.0)
    before = jnp.where(iota((rows, rows), 1) < iota((rows, rows), 0), 1.0, 0.0)
    rank = jnp.dot(
        before.astype(jnp.bfloat16), hit.astype(jnp.bfloat16), preferred_element_type=jnp.float32
    )
    told = jnp.where(hit > 0.0, rank, -1.0)
    for k in range(3):
        piece = weight.astype(jnp.bfloat16)
        pieces_ref[k * rows : (k + 1) * rows, :] = piece
        value = piece.astype(jnp.float32)
        told = jnp.where(column >= (k + 1) * EXPERTS, value, told)
        weight = weight - value
    rows_ref[:, width:] = told.astype(jnp.bfloat16)


def pick(info, lengths_ref, ring_ref, which, x_ref, width, place, slots, lasts):
    step = pl.program_id(0)
    rows = x_ref.shape[0]
    sources = rows // LEN
    ranks = x_ref[:, width:].astype(jnp.float32)
    lane = iota((rows, LANES), 1)
    row = iota((rows, 1), 0)
    source = row // LEN
    rank = jnp.sum(jnp.where(lane == info[which], ranks, 0.0), axis=1, keepdims=True)
    slot = jnp.where(rank >= 0.0, place(source.astype(jnp.float32), rank), -1.0)
    slot_lane = iota((rows, slots), 1).astype(jnp.float32)
    one_hot = jnp.where(slot == slot_lane, 1.0, 0.0).astype(jnp.bfloat16)
    dims = (((0,), (0,)), ((), ()))
    chosen = lax.dot_general(
        one_hot, x_ref[:, :width], dims, preferred_element_type=jnp.float32
    )
    home = jnp.full_like(row, -1)
    for s in range(sources):
        owner = ring_ref[step * sources + s]
        home = jnp.where(row == s * LEN + lengths_ref[owner] - 1, owner, home)
    home = jnp.where(rank >= 0.0, home, -1)
    count = lasts.shape[0]
    one_hot = jnp.where(home == iota((rows, count), 1), 1.0, 0.0).astype(jnp.bfloat16)
    last = lax.dot_general(one_hot, x_ref[...], dims, preferred_element_type=jnp.float32)

    @pl.when(step == 0)
    def _():
        lasts[...] = last

    @pl.when(step != 0)
    def _():
        lasts[...] += last

    return chosen


def share_of(info, which, lasts, width):
    ext = lasts[:, width:]
    lane = iota(ext.shape, 1)
    is_own = (lane >= EXPERTS) & ((lane & (EXPERTS - 1)) == info[which])
    return jnp.broadcast_to(
        jnp.sum(jnp.where(is_own, ext, 0.0), axis=1, keepdims=True), ext.shape
    )


def activ(x, g_ref, u_ref):
    x = x.astype(jnp.bfloat16)
    gate = jnp.dot(x, g_ref[...], preferred_element_type=jnp.float32)
    up = jnp.dot(x, u_ref[...], preferred_element_type=jnp.float32)
    return (gate / (1.0 + jnp.exp(-gate)) * up).astype(jnp.bfloat16)


def own_kernel(
    info, lengths_ref, ring_ref, x_ref, g_ref, u_ref, out_ref, spot_ref, share_ref, picked, lasts
):
    step = pl.program_id(0)
    sources = x_ref.shape[0] // LEN
    width = g_ref.shape[0]
    more = CAP - FIRST
    early = sources * FIRST
    all_early = GROUPS * early
    all_rows = all_early + GROUPS * sources * more

    def place(source, rank):
        return jnp.where(
            rank < FIRST, source * FIRST + rank, early + source * more + (rank - FIRST)
        )

    chosen = pick(
        info, lengths_ref, ring_ref, 0, x_ref, width, place, early + sources * more, lasts
    )
    for s in range(sources):
        start = pl.multiple_of(ring_ref[step * sources + s] * FIRST, FIRST)
        picked[pl.ds(start, FIRST), :] = chosen[s * FIRST : (s + 1) * FIRST]
    start = pl.multiple_of(all_early + step * sources * more, sources * more)
    picked[pl.ds(start, sources * more), :] = chosen[early:]

    @pl.when(step == GROUPS - 1)
    def _():
        count = lasts.shape[0]
        picked[all_rows : all_rows + count, :] = lasts[:, :width]
        blank = picked.shape[0] - all_rows - count
        picked[all_rows + count :, :] = jnp.zeros((blank, width), jnp.float32)
        out_ref[...] = activ(picked[...], g_ref, u_ref)
        share_ref[...] = share_of(info, 0, lasts, width)
        column = iota(spot_ref.shape, 1)
        owner = lax.shift_right_logical(column, more.bit_length() - 1)
        source = jnp.full_like(column, -1)
        for k, b in enumerate(RING):
            source = jnp.where(owner == k, b, source)
        spot = jnp.where(source >= 0, source * SECOND + (column & (more - 1)), -1)
        spot_ref[...] = jnp.where(iota(spot_ref.shape, 0) == spot, 1.0, 0.0).astype(jnp.bfloat16)


def oth_kernel(
    info,
    lengths_ref,
    ring_ref,
    x_ref,
    g_ref,
    u_ref,
    resid_ref,
    _,
    out_ref,
    share_ref,
    base_ref,
    picked,
    lasts,
):
    step = pl.program_id(0)
    sources = x_ref.shape[0] // LEN
    width = g_ref.shape[0]
    all_rows = GROUPS * sources * SECOND

    def place(source, rank):
        return source * SECOND + (SECOND - CAP) + rank

    chosen = pick(info, lengths_ref, ring_ref, 1, x_ref, width, place, sources * SECOND, lasts)
    for s in range(sources):
        start = pl.multiple_of(ring_ref[step * sources + s] * SECOND, SECOND)
        picked[pl.ds(start, SECOND), :] = chosen[s * SECOND : (s + 1) * SECOND]

    @pl.when(step == GROUPS - 1)
    def _():
        picked[all_rows:, :] = lasts[:, :width]
        out_ref[...] = activ(picked[...], g_ref, u_ref)
        share_ref[...] = share_of(info, 1, lasts, width)
        resid = resid_ref[...].astype(jnp.float32)
        is_last = iota(resid.shape, 0) == info[3] - 1
        last = jnp.sum(jnp.where(is_last, resid, 0.0), axis=0, keepdims=True)
        base_ref[...] = jnp.where(iota(base_ref.shape, 0) == info[4], last, 0.0)


def matmul_nt(hidden_ref, d):
    return lax.dot_general(
        hidden_ref[...], d, (((1,), (1,)), ((), ())), preferred_element_type=jnp.float32
    )


def started(copies):
    for copy in copies:
        copy.start()
    return copies


def waited(copies):
    for copy in copies:
        copy.wait()


def own_down_kernel(
    hidden_any, share_any, d_any, out_any, late_any, part_any, hidden, share, d, out, part, sems
):
    chunks, size = d.shape[:2]
    rows, count = out_any.shape[0], part.shape[1]
    at = rows + count * (CAP - FIRST)
    copy = pltpu.make_async_copy
    first = started(
        [copy(hidden_any, hidden, sems.at[0, 0]), copy(share_any, share, sems.at[0, 1])]
    )
    downs = started(
        [
            copy(d_any.at[k * size : (k + 1) * size], d.at[k], sems.at[1, k])
            for k in range(chunks)
        ]
    )
    waited(first)
    stores = []
    for k in range(chunks):
        downs[k].wait()
        out[k] = matmul_nt(hidden, d[k]).astype(jnp.bfloat16)
        part[k] = share[:, :1] * out[k, at : at + count].astype(jnp.float32)
        columns = slice(k * size, (k + 1) * size)
        stores += started(
            [
                copy(out.at[k, :rows], out_any.at[:, columns], sems.at[2, k]),
                copy(out.at[k, rows:], late_any.at[:, columns], sems.at[3, k]),
                copy(part.at[k], part_any.at[:, columns], sems.at[4, k]),
            ]
        )
    waited(stores)


def oth_down_kernel(
    info,
    hidden_any,
    share_any,
    spot_any,
    late_any,
    base_any,
    part_any,
    d_any,
    out_any,
    sum_any,
    hidden,
    share,
    spot,
    late,
    base,
    part,
    d,
    out,
    total,
    sems,
):
    chunks, size = d.shape[:2]
    rows = out_any.shape[0]
    copy = pltpu.make_async_copy
    other = 1 - info[2]
    sources = (hidden_any, share_any, spot_any, late_any, base_any, part_any)
    targets = (hidden, share, spot, late, base, part)
    downs = started(
        [
            copy(d_any.at[other, k * size : (k + 1) * size], d.at[k], sems.at[1, k])
            for k in range(chunks)
        ]
    )
    first = started([copy(x, y, sems.at[0, k]) for k, (x, y) in enumerate(zip(sources, targets))])
    waited(first)
    stores = []
    for k in range(chunks):
        downs[k].wait()
        columns = slice(k * size, (k + 1) * size)
        placed = jnp.dot(spot[...], late[:, columns], preferred_element_type=jnp.float32)
        value = matmul_nt(hidden, d[k])
        out[k] = (placed + value[:rows]).astype(jnp.bfloat16)
        last = value[rows:].astype(jnp.bfloat16).astype(jnp.float32)
        total[k] = base[:, columns] + part[:, columns] + share[:, :1] * last
        stores += started(
            [
                copy(total.at[k], sum_any.at[:, columns], sems.at[3, k]),
                copy(out.at[k], out_any.at[:, columns], sems.at[2, k]),
            ]
        )
    waited(stores)


def mix_kernel(info, rank_ref, pieces_ref, first_ref, second_ref):
    rows = rank_ref.shape[0]
    late = SECOND - CAP
    own, oth = info[2], 1 - info[2]
    for mix_ref, stride, spans in (
        (first_ref, FIRST, ((own, 0, FIRST, 0),)),
        (second_ref, SECOND, ((own, 0, late, FIRST), (oth, late, CAP, 0))),
    ):
        slots = mix_ref.shape[1]
        expert = iota((LANES, slots), 0)
        lane = iota((LANES, slots), 1)
        within = jnp.zeros((1, slots), jnp.float32)
        spread = jnp.zeros((LANES, slots), jnp.float32)
        for parity, offset, count, lowest in spans:
            start = jnp.where((expert & 1) == parity, (expert >> 1) * stride + offset, slots)
            inside = (lane >= start) & (lane < start + count)
            spread = spread + jnp.where(inside, 1.0, 0.0)
            ranks = jnp.where(inside, lane - start + lowest, 0)
            within = within + jnp.sum(ranks, axis=0, keepdims=True).astype(jnp.float32)
        spread = spread.astype(jnp.bfloat16)
        rank = jnp.dot(rank_ref[...], spread, preferred_element_type=jnp.float32)
        match = rank == within
        for k in range(3):
            part = jnp.dot(
                pieces_ref[k * rows : (k + 1) * rows, :], spread, preferred_element_type=jnp.float32
            )
            mix_ref[k * rows : (k + 1) * rows, :] = jnp.where(match, part, 0.0).astype(jnp.bfloat16)


def weigh(mix_ref, back_ref):
    rows = mix_ref.shape[0] // 3
    parts = jnp.dot(mix_ref[...], back_ref[...], preferred_element_type=jnp.float32)
    return parts[2 * rows :] + parts[rows : 2 * rows] + parts[:rows]


def first_kernel(mix_ref, back_ref, resid_ref, base_ref):
    base_ref[...] = resid_ref[...].astype(jnp.float32) + weigh(mix_ref, back_ref)


def combine_kernel(
    info, mix_any, back_any, base_any, _, __, out_ref, square_ref, mix, back, base, sems
):
    chunks, size = back.shape[:2]
    rows = base.shape[0]
    copy = pltpu.make_async_copy
    first = started([copy(mix_any, mix, sems.at[chunks])])
    backs = started(
        [copy(back_any.at[k * size : (k + 1) * size], back.at[k], sems.at[k]) for k in range(chunks)]
    )
    late = started([copy(base_any, base, sems.at[chunks + 1])])
    waited(first)
    parts = jnp.zeros((mix.shape[0], base.shape[1]), jnp.float32)
    for k in range(chunks):
        backs[k].wait()
        parts = parts + jnp.dot(
            mix[:, k * size : (k + 1) * size], back[k], preferred_element_type=jnp.float32
        )
    waited(late)
    moe = parts[2 * rows :] + parts[rows : 2 * rows] + parts[:rows]
    out = (base[...] + moe).astype(jnp.bfloat16)
    out_ref[...] = out
    out_f = out.astype(jnp.float32)
    row = iota(out_f.shape, 0)
    total = jnp.sum(jnp.where(row < info[3], out_f * out_f, 0.0), axis=0, keepdims=True)
    square_ref[...] = jnp.broadcast_to(
        jnp.sum(total, axis=1, keepdims=True), square_ref.shape
    )


def place_kernel(info, g_own, g_oth, u_own, u_oth, d_both, _, out_ref):
    left = info[2] == 0
    for k, (own, oth) in enumerate(((g_own[...], g_oth[...]), (u_own[...], u_oth[...]))):
        out_ref[k, :, :FF] = jnp.where(left, own, oth)
        out_ref[k, :, FF:] = jnp.where(left, oth, own)
    out_ref[2, :, :FF] = d_both[0]
    out_ref[2, :, FF:] = d_both[1]


def cast_kernel(first_row, blocks, x_ref, *refs):
    out_ref, held, turned, sems_in, sems_out = refs[-5:]
    groups, size = held.shape[:2]
    fetches, stores = [], []
    for g in range(groups):
        rows = pl.ds(first_row + g * size, size)
        fetches.append(pltpu.make_async_copy(x_ref.at[rows], held.at[g], sems_in.at[g]))
        target = out_ref.at[:, g * 16 : (g + 1) * 16]
        stores.append(pltpu.make_async_copy(turned.at[g], target, sems_out.at[g]))
    for fetch in fetches:
        fetch.start()
    target = iota((size, size), 0)
    source = (target & 15) * blocks + lax.shift_right_logical(target, 4)
    order = jnp.where(iota((size, size), 1) == source, 1.0, 0.0).astype(jnp.bfloat16)
    for g in range(groups):
        fetches[g].wait()
        rows = jnp.dot(order, held[g].astype(jnp.bfloat16), preferred_element_type=jnp.float32)
        turned[g] = rows.astype(jnp.bfloat16).reshape(turned.shape[1:])
        stores[g].start()
    for store in stores:
        store.wait()


def tie_kernel(*_):
    pass


def params():
    return pltpu.CompilerParams(vmem_limit_bytes=VMEM, dimension_semantics=("arbitrary",))


def whole(shape):
    return pl.BlockSpec(shape, lambda *_: tuple(0 for _ in shape))


def paired(
    hidden_in, lengths, routes, route_weights, norm_gain, master, unembed, final_gain, target_ids
):
    rows = hidden_in.shape[1]
    width = hidden_in.shape[2]
    blk_count = lax.axis_size("blk")
    blk = lax.axis_index("blk")
    rep = lax.axis_index("rep")
    first = blk_count * FIRST
    second = blk_count * SECOND
    resid = hidden_in[0]
    info = jnp.stack([2 * blk + rep, 2 * blk + 1 - rep, rep, lengths[blk], blk])
    info = info.astype(jnp.int32)

    shard_rows = master.shape[1]
    flat = master.reshape(3 * shard_rows * blk_count, FF)

    groups = shard_rows // 16

    def turned(k, *after):
        return pl.pallas_call(
            functools.partial(cast_kernel, k * shard_rows * blk_count, blk_count),
            in_specs=[pl.BlockSpec(memory_space=pl.ANY)] * (1 + len(after)),
            out_specs=pl.BlockSpec(memory_space=pl.ANY),
            out_shape=jax.ShapeDtypeStruct((blk_count, shard_rows, FF), jnp.bfloat16),
            scratch_shapes=[
                pltpu.VMEM((groups, 16 * blk_count, FF), jnp.float32),
                pltpu.VMEM((groups, blk_count, 16, FF), jnp.bfloat16),
                pltpu.SemaphoreType.DMA((groups,)),
                pltpu.SemaphoreType.DMA((groups,)),
            ],
            compiler_params=pltpu.CompilerParams(vmem_limit_bytes=VMEM),
            name="cast",
        )(flat, *after)

    def moved(x):
        own = lax.all_to_all(x, "blk", split_axis=0, concat_axis=0, tiled=True)
        return own.reshape(width, FF)

    def swapped(x):
        return lax.ppermute(x, "rep", [(0, 1), (1, 0)])

    def tied(x, *after):
        return pl.pallas_call(
            tie_kernel,
            in_specs=[pl.BlockSpec(memory_space=pl.ANY)] * (1 + len(after)),
            out_specs=pl.BlockSpec(memory_space=pl.ANY),
            out_shape=jax.ShapeDtypeStruct(x.shape, x.dtype),
            input_output_aliases={0: 0},
            name="tie",
        )(x, *after)

    row_ext, pieces = pl.pallas_call(
        prep_kernel,
        grid_spec=pltpu.PrefetchScalarGridSpec(
            num_scalar_prefetch=2,
            grid=(1,),
            in_specs=[
                whole((rows, width)),
                whole((routes.shape[2], rows)),
                whole((routes.shape[2], rows)),
                whole((width,)),
            ],
            out_specs=[whole((rows, width + LANES)), whole((3 * rows, LANES))],
        ),
        out_shape=[
            jax.ShapeDtypeStruct((rows, width + LANES), jnp.bfloat16),
            jax.ShapeDtypeStruct((3 * rows, LANES), jnp.bfloat16),
        ],
        compiler_params=params(),
        name="prep",
    )(lengths, blk[None].astype(jnp.int32), resid, routes[0].T, route_weights[0].T, norm_gain)
    g_own = moved(turned(0, row_ext))
    g_oth = swapped(g_own)
    u_own = moved(turned(1))
    u_oth = swapped(u_own)
    d_own = moved(tied(turned(2), g_oth))

    tokens = lax.all_gather(row_ext, "blk", axis_index_groups=[list(RING)], axis=0, tiled=True)

    ring = jnp.array(RING, jnp.int32)

    def hidden_of(kernel, outs, picked, operands, specs):
        return pl.pallas_call(
            kernel,
            grid_spec=pltpu.PrefetchScalarGridSpec(
                num_scalar_prefetch=3,
                grid=(GROUPS,),
                in_specs=[pl.BlockSpec((blk_count // GROUPS * rows, width + LANES), lambda i, *_: (i, 0))]
                + [whole((width, FF))] * 2
                + specs,
                out_specs=[whole(out.shape) for out in outs],
                scratch_shapes=[
                    pltpu.VMEM((picked, width), jnp.float32),
                    pltpu.VMEM((blk_count, width + LANES), jnp.float32),
                ],
            ),
            out_shape=outs,
            compiler_params=params(),
            name="gate_up",
        )(info, lengths, ring, tokens, *operands)

    step = 512
    quarter = width // 4
    anywhere = pl.BlockSpec(memory_space=pl.ANY)

    def returned(x):
        slots = x.shape[0]
        x = x.reshape(blk_count, slots // blk_count, width)
        x = lax.all_to_all(x, "blk", split_axis=0, concat_axis=0, tiled=True)
        return x.reshape(slots, width)

    def bf16(*shape):
        return jax.ShapeDtypeStruct(shape, jnp.bfloat16)

    def f32(*shape):
        return jax.ShapeDtypeStruct(shape, jnp.float32)

    extra = LANES
    own_hidden, spot, own_share = hidden_of(
        own_kernel,
        [bf16(first + extra, FF), bf16(second, extra), f32(blk_count, LANES)],
        first + extra,
        (g_own, u_own),
        [],
    )
    d_own = tied(d_own, own_hidden)
    d_both = lax.all_gather(d_own, "rep", axis=0)
    own_out, late_out, own_part = pl.pallas_call(
        own_down_kernel,
        in_specs=[anywhere] * 3,
        out_specs=[anywhere] * 3,
        out_shape=[bf16(first, width), bf16(extra, width), f32(blk_count, width)],
        scratch_shapes=[
            pltpu.VMEM((first + extra, FF), jnp.bfloat16),
            pltpu.VMEM((blk_count, LANES), jnp.float32),
            pltpu.VMEM((4, quarter, FF), jnp.bfloat16),
            pltpu.VMEM((4, first + extra, quarter), jnp.bfloat16),
            pltpu.VMEM((4, blk_count, quarter), jnp.float32),
            pltpu.SemaphoreType.DMA((5, 4)),
        ],
        compiler_params=pltpu.CompilerParams(vmem_limit_bytes=VMEM),
        name="own_down",
    )(own_hidden, own_share, d_own)
    own_out = tied(own_out, u_oth)
    own_back = returned(own_out)
    oth_hidden, oth_share, base_part = hidden_of(
        oth_kernel,
        [bf16(second + blk_count, FF), f32(blk_count, LANES), f32(blk_count, width)],
        second + blk_count,
        (g_oth, u_oth, resid, own_out),
        [whole((rows, width)), anywhere],
    )
    oth_out, last_part = pl.pallas_call(
        oth_down_kernel,
        grid_spec=pltpu.PrefetchScalarGridSpec(
            num_scalar_prefetch=1,
            grid=(1,),
            in_specs=[anywhere] * 7,
            out_specs=[anywhere] * 2,
            scratch_shapes=[
                pltpu.VMEM((second + blk_count, FF), jnp.bfloat16),
                pltpu.VMEM((blk_count, LANES), jnp.float32),
                pltpu.VMEM((second, extra), jnp.bfloat16),
                pltpu.VMEM((extra, width), jnp.bfloat16),
                pltpu.VMEM((blk_count, width), jnp.float32),
                pltpu.VMEM((blk_count, width), jnp.float32),
                pltpu.VMEM((4, quarter, FF), jnp.bfloat16),
                pltpu.VMEM((4, second, quarter), jnp.bfloat16),
                pltpu.VMEM((4, blk_count, quarter), jnp.float32),
                pltpu.SemaphoreType.DMA((4, 6)),
            ],
        ),
        out_shape=[bf16(second, width), f32(blk_count, width)],
        compiler_params=params(),
        name="oth_down",
    )(info, oth_hidden, oth_share, spot, late_out, base_part, own_part, d_both)
    last_parts = lax.all_gather(last_part, "blk", axis_index_groups=[list(RING)], axis=0)
    oth_back = returned(oth_out)

    server = pl.pallas_call(
        place_kernel,
        grid_spec=pltpu.PrefetchScalarGridSpec(
            num_scalar_prefetch=1,
            grid=(4,),
            in_specs=[pl.BlockSpec((quarter, FF), lambda i, *_: (i, 0))] * 4
            + [pl.BlockSpec((2, quarter, FF), lambda i, *_: (0, i, 0)), anywhere],
            out_specs=pl.BlockSpec((3, quarter, 2 * FF), lambda i, *_: (0, i, 0)),
        ),
        out_shape=jax.ShapeDtypeStruct((3, width, 2 * FF), jnp.bfloat16),
        compiler_params=params(),
        name="place",
    )(info, g_own, g_oth, u_own, u_oth, d_both, oth_out)

    first_mix, second_mix = pl.pallas_call(
        mix_kernel,
        grid_spec=pltpu.PrefetchScalarGridSpec(
            num_scalar_prefetch=1,
            grid=(1,),
            in_specs=[
                pl.BlockSpec((rows, LANES), lambda i, *_: (0, width // LANES)),
                whole((3 * rows, LANES)),
            ],
            out_specs=[whole((3 * rows, first)), whole((3 * rows, second))],
        ),
        out_shape=[
            jax.ShapeDtypeStruct((3 * rows, first), jnp.bfloat16),
            jax.ShapeDtypeStruct((3 * rows, second), jnp.bfloat16),
        ],
        compiler_params=params(),
        name="mix",
    )(info, row_ext, pieces)

    def weigh_specs(slots):
        return [whole((3 * rows, slots)), pl.BlockSpec((slots, step), lambda i, *_: (0, i))]

    column = pl.BlockSpec((rows, step), lambda i, *_: (0, i))
    base = pl.pallas_call(
        first_kernel,
        grid=(width // step,),
        in_specs=weigh_specs(first) + [column],
        out_specs=column,
        out_shape=f32(rows, width),
        compiler_params=params(),
        name="first",
    )(first_mix, own_back, resid)
    last_rows = lax.reduce_precision(jnp.sum(last_parts, axis=0), 8, 7)
    final = (
        last_rows
        * lax.rsqrt(jnp.mean(last_rows * last_rows, axis=-1, keepdims=True) + 1e-05)
        * final_gain
    ).astype(jnp.bfloat16)
    logits = lax.dot_general(
        final, unembed, (((1,), (1,)), ((), ())), preferred_element_type=jnp.float32
    )
    vocab_base = blk * unembed.shape[0]
    target_hit = (
        target_ids[:, None] == vocab_base + jnp.arange(unembed.shape[0], dtype=jnp.int32)[None, :]
    )
    target_part = jnp.sum(jnp.where(target_hit, logits, 0.0), axis=1)
    top_part = jnp.max(logits, axis=1)

    out_rows, square = pl.pallas_call(
        combine_kernel,
        grid_spec=pltpu.PrefetchScalarGridSpec(
            num_scalar_prefetch=1,
            grid=(1,),
            in_specs=[anywhere] * 5,
            out_specs=[whole((rows, width)), whole((1, LANES))],
            scratch_shapes=[
                pltpu.VMEM((3 * rows, second), jnp.bfloat16),
                pltpu.VMEM((second // LANES, LANES, width), jnp.bfloat16),
                pltpu.VMEM((rows, width), jnp.float32),
                pltpu.SemaphoreType.DMA((second // LANES + 2,)),
            ],
        ),
        out_shape=[bf16(rows, width), f32(1, LANES)],
        compiler_params=params(),
        name="combine",
    )(info, second_mix, oth_back, base, server, top_part[None])

    def everywhere(copies):
        return lax.all_to_all(copies, "blk", split_axis=0, concat_axis=0, tiled=True)

    prompt = jnp.arange(blk_count, dtype=jnp.int32)
    square_part = jnp.where(prompt == blk, square[0, :blk_count], 0.0)
    stats = jnp.stack([top_part, target_part, square_part])
    parts = everywhere(jnp.broadcast_to(stats[None], (blk_count,) + stats.shape))
    sums = jnp.sum(parts[:, 1:], axis=0)
    norms = jnp.sqrt(sums[1] / (lengths.astype(jnp.float32) * width) + 1e-06)
    request_stats = jnp.stack([norms, jnp.max(parts[:, 0], axis=0), sums[0]])
    return (out_rows[None], server, request_stats)


def local(hidden_in, lengths, routes, route_weights, norm_gain, master, *rest):
    blk_count = lax.axis_size("blk")
    fits = (
        lax.axis_size("rep") == 2
        and master.shape[3] == FF
        and EXPERTS == 2 * blk_count
        and blk_count == len(RING)
        and hidden_in.shape[1] == LEN
        and lengths.shape[0] == blk_count
    )
    form = paired if fits else general
    return form(hidden_in, lengths, routes, route_weights, norm_gain, master, *rest)


def solution(mesh):
    return jax.shard_map(
        local,
        mesh=mesh,
        in_specs=(
            P("rep", "blk", None),
            P("rep"),
            P("rep", "blk", None),
            P("rep", "blk", None),
            P(),
            P(None, "blk", None, "rep"),
            P("blk", None),
            P(),
            P("rep"),
        ),
        out_specs=(P("rep", "blk", None), P(None, None, "blk"), P(None, "rep")),
        check_vma=False,
    )
```

```python
import functools

import jax
import jax.numpy as jnp
from jax import lax
from jax.experimental import pallas as pl
from jax.experimental.pallas import tpu as pltpu
from jax.sharding import PartitionSpec as P

FF = 512
EXPERTS = 32
LEN = 128
CAP = 36
FIRST = 32
SECOND = 40
GROUPS = 4
RING = (0, 1, 4, 5, 8, 9, 12, 13, 14, 15, 10, 11, 6, 7, 2, 3)
LANES = 128
VMEM = 56 * 1024 * 1024


def merged(x, axis, combine):
    everything = jax.tree.map(lambda part: lax.all_gather(part, axis), x)
    initial = jax.tree.map(lambda part: part[0], everything)

    def turn(k, so_far):
        return combine(so_far, jax.tree.map(lambda part: part[k], everything))

    return lax.fori_loop(1, lax.axis_size(axis), turn, initial)


def combine_stats(first, second):
    return (first[0] + second[0], jnp.maximum(first[1], second[1]))


def general(
    hidden_in, lengths, routes, route_weights, norm_gain, master, unembed, final_gain, target_ids
):
    rows_here = hidden_in.shape[1]
    width = hidden_in.shape[2]
    top_count = routes.shape[2]
    blk_count = lax.axis_size("blk")
    rep_count = lax.axis_size("rep")
    blk_index = lax.axis_index("blk")
    unit_count = master.shape[3] * rep_count
    split_ways = max(1, FF // unit_count)
    local_exp = max(1, unit_count // FF)
    group_width = min(unit_count, FF)
    capacity = CAP
    blocks = master.astype(jnp.bfloat16)
    arrived_blocks = lax.all_to_all(blocks, "blk", split_axis=2, concat_axis=1, tiled=True)
    server = lax.all_gather(arrived_blocks, "rep", axis=3, tiled=True)[:, :, 0, :]
    gate_w = server[0].reshape(width, local_exp, group_width)
    up_w = server[1].reshape(width, local_exp, group_width)
    down_w = server[2].reshape(width, local_exp, group_width)
    prompts_here = lengths.shape[0]
    slot_index = blk_index * rows_here + jnp.arange(rows_here, dtype=jnp.int32)
    prompt_of = slot_index // LEN
    position = slot_index % LEN
    prompt_match = prompt_of[:, None] == jnp.arange(prompts_here, dtype=jnp.int32)[None, :]
    row_len = jnp.sum(jnp.where(prompt_match, lengths[None, :], 0), axis=1)
    is_valid = position < row_len
    resid_f = hidden_in[0].astype(jnp.float32)
    normed = (
        resid_f * lax.rsqrt(jnp.mean(resid_f * resid_f, axis=-1, keepdims=True) + 1e-05) * norm_gain
    ).astype(jnp.bfloat16)
    expert_ids = routes[0].reshape(-1)
    pair_live = jnp.repeat(is_valid, top_count)
    pair_row = jnp.repeat(jnp.arange(rows_here, dtype=jnp.int32), top_count)
    expert_hits = (
        (expert_ids[:, None] == jnp.arange(EXPERTS, dtype=jnp.int32)[None, :]) & pair_live[:, None]
    ).astype(jnp.int32)
    slot_rank = jnp.sum((jnp.cumsum(expert_hits, axis=0) - 1) * expert_hits, axis=1)
    slot_id = jnp.where(pair_live, expert_ids * capacity + slot_rank, EXPERTS * capacity)
    source_row = jnp.zeros((EXPERTS * capacity + 1,), jnp.int32).at[slot_id].set(pair_row)[:-1]
    filled = jnp.zeros((EXPERTS * capacity + 1,), jnp.bfloat16).at[slot_id].set(1.0)[:-1]
    outgoing = (normed[source_row] * filled[:, None]).reshape(EXPERTS, capacity, width)
    sending = jnp.repeat(outgoing, split_ways, axis=0).reshape(
        blk_count, local_exp, capacity, width
    )
    arrived = lax.all_to_all(sending, "blk", split_axis=0, concat_axis=0, tiled=True)
    sources = arrived.shape[0]
    slot_count = arrived.shape[2]
    stride = sources
    while stride % 2 == 0 and stride * local_exp * slot_count > 1024:
        stride = stride // 2
    grouped = arrived.reshape(sources // stride, stride, local_exp, slot_count, width)

    def one_block(portion):
        gate_out = jnp.einsum("slnd,dlf->slnf", portion, gate_w, preferred_element_type=jnp.float32)
        up_out = jnp.einsum("slnd,dlf->slnf", portion, up_w, preferred_element_type=jnp.float32)
        hidden = (jax.nn.silu(gate_out) * up_out).astype(jnp.bfloat16)
        return jnp.einsum(
            "slnf,dlf->slnd", hidden, down_w, preferred_element_type=jnp.float32
        ).astype(jnp.bfloat16)

    returned = lax.all_to_all(
        lax.map(one_block, grouped).reshape(sources, local_exp, slot_count, width),
        "blk",
        split_axis=0,
        concat_axis=0,
        tiled=True,
    )
    summed_f = jnp.sum(
        returned.reshape(EXPERTS, split_ways, capacity, width).astype(jnp.float32), axis=1
    )
    expert_out = lax.optimization_barrier(summed_f.astype(jnp.bfloat16)).reshape(
        EXPERTS * capacity, width
    )
    gather_index = jnp.where(pair_live, expert_ids * capacity + slot_rank, 0)
    pair_weight = route_weights[0].reshape(-1) * pair_live.astype(jnp.float32)
    moe = jnp.sum(
        (expert_out[gather_index].astype(jnp.float32) * pair_weight[:, None]).reshape(
            rows_here, top_count, width
        ),
        axis=1,
    )
    out_rows = (resid_f + moe).astype(jnp.bfloat16)
    out_f = out_rows.astype(jnp.float32)
    row_squares = jnp.sum(out_f * out_f, axis=-1) * is_valid.astype(jnp.float32)
    square_local = jnp.sum(jnp.where(prompt_match, row_squares[:, None], 0.0), axis=0)
    is_last = is_valid & (position == row_len - 1)
    picker = (prompt_match & is_last[:, None]).astype(jnp.bfloat16)
    last_local = lax.dot_general(
        picker, out_rows, (((0,), (0,)), ((), ())), preferred_element_type=jnp.float32
    )
    last_rows, square_total = lax.psum((last_local, square_local), "blk")
    norms = jnp.sqrt(square_total / (lengths.astype(jnp.float32) * width) + 1e-06)
    final = (
        last_rows
        * lax.rsqrt(jnp.mean(last_rows * last_rows, axis=-1, keepdims=True) + 1e-05)
        * final_gain
    ).astype(jnp.bfloat16)
    logits = lax.dot_general(
        final, unembed, (((1,), (1,)), ((), ())), preferred_element_type=jnp.float32
    )
    vocab_base = blk_index * unembed.shape[0]
    target_hit = (
        target_ids[:, None] == vocab_base + jnp.arange(unembed.shape[0], dtype=jnp.int32)[None, :]
    )
    target_part = jnp.sum(jnp.where(target_hit, logits, 0.0), axis=1)
    top_part = jnp.max(logits, axis=1)
    target_logit, top_logit = merged((target_part, top_part), "blk", combine_stats)
    request_stats = jnp.stack([norms, top_logit, target_logit])
    return (out_rows[None], server, request_stats)


def iota(shape, dim):
    return lax.broadcasted_iota(jnp.int32, shape, dim)


def prep_kernel(lengths_ref, blk_ref, hidden_ref, routes_ref, weights_ref, gain_ref, rows_ref, pieces_ref):
    rows, width = hidden_ref.shape
    length = lengths_ref[blk_ref[0]]
    x = hidden_ref[...].astype(jnp.float32)
    scale = lax.rsqrt(jnp.mean(x * x, axis=-1, keepdims=True) + 1e-05)
    rows_ref[:, :width] = (x * scale * gain_ref[...][None]).astype(jnp.bfloat16)
    column = iota((rows, LANES), 1)
    lane = column & (EXPERTS - 1)
    row = iota((rows, LANES), 0)
    hit = jnp.zeros((rows, LANES), jnp.float32)
    weight = jnp.zeros((rows, LANES), jnp.float32)
    named_by = jnp.transpose(routes_ref[...].astype(jnp.float32)).astype(jnp.int32)
    weight_by = jnp.transpose(weights_ref[...])
    for k in range(routes_ref.shape[0]):
        named = named_by[:, k : k + 1] == lane
        hit = hit + jnp.where(named, 1.0, 0.0)
        weight = weight + jnp.where(named, weight_by[:, k : k + 1], 0.0)
    live = row < length
    hit = jnp.where(live, hit, 0.0)
    weight = jnp.where(live, weight, 0.0)
    before = jnp.where(iota((rows, rows), 1) < iota((rows, rows), 0), 1.0, 0.0)
    rank = jnp.dot(
        before.astype(jnp.bfloat16), hit.astype(jnp.bfloat16), preferred_element_type=jnp.float32
    )
    told = jnp.where(hit > 0.0, rank, -1.0)
    for k in range(3):
        piece = weight.astype(jnp.bfloat16)
        pieces_ref[k * rows : (k + 1) * rows, :] = piece
        value = piece.astype(jnp.float32)
        told = jnp.where(column >= (k + 1) * EXPERTS, value, told)
        weight = weight - value
    rows_ref[:, width:] = told.astype(jnp.bfloat16)


def pick(info, lengths_ref, ring_ref, which, x_ref, width, place, slots, lasts):
    step = pl.program_id(0)
    rows = x_ref.shape[0]
    sources = rows // LEN
    ranks = x_ref[:, width:].astype(jnp.float32)
    lane = iota((rows, LANES), 1)
    row = iota((rows, 1), 0)
    source = row // LEN
    rank = jnp.sum(jnp.where(lane == info[which], ranks, 0.0), axis=1, keepdims=True)
    slot = jnp.where(rank >= 0.0, place(source.astype(jnp.float32), rank), -1.0)
    slot_lane = iota((rows, slots), 1).astype(jnp.float32)
    one_hot = jnp.where(slot == slot_lane, 1.0, 0.0).astype(jnp.bfloat16)
    dims = (((0,), (0,)), ((), ()))
    chosen = lax.dot_general(
        one_hot, x_ref[:, :width], dims, preferred_element_type=jnp.float32
    )
    home = jnp.full_like(row, -1)
    for s in range(sources):
        owner = ring_ref[step * sources + s]
        home = jnp.where(row == s * LEN + lengths_ref[owner] - 1, owner, home)
    home = jnp.where(rank >= 0.0, home, -1)
    count = lasts.shape[0]
    one_hot = jnp.where(home == iota((rows, count), 1), 1.0, 0.0).astype(jnp.bfloat16)
    last = lax.dot_general(one_hot, x_ref[...], dims, preferred_element_type=jnp.float32)

    @pl.when(step == 0)
    def _():
        lasts[...] = last

    @pl.when(step != 0)
    def _():
        lasts[...] += last

    return chosen


def share_of(info, which, lasts, width):
    ext = lasts[:, width:]
    lane = iota(ext.shape, 1)
    is_own = (lane >= EXPERTS) & ((lane & (EXPERTS - 1)) == info[which])
    return jnp.broadcast_to(
        jnp.sum(jnp.where(is_own, ext, 0.0), axis=1, keepdims=True), ext.shape
    )


def activ(x, g_ref, u_ref):
    x = x.astype(jnp.bfloat16)
    gate = jnp.dot(x, g_ref[...], preferred_element_type=jnp.float32)
    up = jnp.dot(x, u_ref[...], preferred_element_type=jnp.float32)
    return (gate / (1.0 + jnp.exp(-gate)) * up).astype(jnp.bfloat16)


def own_kernel(
    info, lengths_ref, ring_ref, x_ref, g_ref, u_ref, out_ref, spot_ref, share_ref, picked, lasts
):
    step = pl.program_id(0)
    sources = x_ref.shape[0] // LEN
    width = g_ref.shape[0]
    more = CAP - FIRST
    early = sources * FIRST
    all_early = GROUPS * early
    all_rows = all_early + GROUPS * sources * more

    def place(source, rank):
        return jnp.where(
            rank < FIRST, source * FIRST + rank, early + source * more + (rank - FIRST)
        )

    chosen = pick(
        info, lengths_ref, ring_ref, 0, x_ref, width, place, early + sources * more, lasts
    )
    for s in range(sources):
        start = pl.multiple_of(ring_ref[step * sources + s] * FIRST, FIRST)
        picked[pl.ds(start, FIRST), :] = chosen[s * FIRST : (s + 1) * FIRST]
    start = pl.multiple_of(all_early + step * sources * more, sources * more)
    picked[pl.ds(start, sources * more), :] = chosen[early:]

    @pl.when(step == GROUPS - 1)
    def _():
        count = lasts.shape[0]
        picked[all_rows : all_rows + count, :] = lasts[:, :width]
        blank = picked.shape[0] - all_rows - count
        picked[all_rows + count :, :] = jnp.zeros((blank, width), jnp.float32)
        out_ref[...] = activ(picked[...], g_ref, u_ref)
        share_ref[...] = share_of(info, 0, lasts, width)
        column = iota(spot_ref.shape, 1)
        owner = lax.shift_right_logical(column, more.bit_length() - 1)
        source = jnp.full_like(column, -1)
        for k, b in enumerate(RING):
            source = jnp.where(owner == k, b, source)
        spot = jnp.where(source >= 0, source * SECOND + (column & (more - 1)), -1)
        spot_ref[...] = jnp.where(iota(spot_ref.shape, 0) == spot, 1.0, 0.0).astype(jnp.bfloat16)


def oth_kernel(
    info,
    lengths_ref,
    ring_ref,
    x_ref,
    g_ref,
    u_ref,
    resid_ref,
    _,
    out_ref,
    share_ref,
    base_ref,
    picked,
    lasts,
):
    step = pl.program_id(0)
    sources = x_ref.shape[0] // LEN
    width = g_ref.shape[0]
    all_rows = GROUPS * sources * SECOND

    def place(source, rank):
        return source * SECOND + (SECOND - CAP) + rank

    chosen = pick(info, lengths_ref, ring_ref, 1, x_ref, width, place, sources * SECOND, lasts)
    for s in range(sources):
        start = pl.multiple_of(ring_ref[step * sources + s] * SECOND, SECOND)
        picked[pl.ds(start, SECOND), :] = chosen[s * SECOND : (s + 1) * SECOND]

    @pl.when(step == GROUPS - 1)
    def _():
        picked[all_rows:, :] = lasts[:, :width]
        out_ref[...] = activ(picked[...], g_ref, u_ref)
        share_ref[...] = share_of(info, 1, lasts, width)
        resid = resid_ref[...].astype(jnp.float32)
        is_last = iota(resid.shape, 0) == info[3] - 1
        last = jnp.sum(jnp.where(is_last, resid, 0.0), axis=0, keepdims=True)
        base_ref[...] = jnp.where(iota(base_ref.shape, 0) == info[4], last, 0.0)


def matmul_nt(hidden, d):
    return lax.dot_general(
        hidden[...], d, (((1,), (1,)), ((), ())), preferred_element_type=jnp.float32
    )


def started(copies):
    for copy in copies:
        copy.start()
    return copies


def waited(copies):
    for copy in copies:
        copy.wait()


def own_down_kernel(
    hidden_any, share_any, d_any, out_any, late_any, part_any, hidden, share, d, out, part, sems
):
    chunks, size = d.shape[:2]
    rows, count = out_any.shape[0], part.shape[1]
    at = rows + count * (CAP - FIRST)
    copy = pltpu.make_async_copy
    first = started(
        [copy(hidden_any, hidden, sems.at[0, 0]), copy(share_any, share, sems.at[0, 1])]
    )
    downs = started(
        [
            copy(d_any.at[k * size : (k + 1) * size], d.at[k], sems.at[1, k])
            for k in range(chunks)
        ]
    )
    waited(first)
    stores = []
    for k in range(chunks):
        downs[k].wait()
        out[k] = matmul_nt(hidden, d[k]).astype(jnp.bfloat16)
        part[k] = share[:, :1] * out[k, at : at + count].astype(jnp.float32)
        columns = slice(k * size, (k + 1) * size)
        stores += started(
            [
                copy(out.at[k, :rows], out_any.at[:, columns], sems.at[2, k]),
                copy(out.at[k, rows:], late_any.at[:, columns], sems.at[3, k]),
                copy(part.at[k], part_any.at[:, columns], sems.at[4, k]),
            ]
        )
    waited(stores)


def oth_down_kernel(
    info,
    hidden_any,
    share_any,
    spot_any,
    late_any,
    base_any,
    part_any,
    d_any,
    out_any,
    sum_any,
    hidden,
    share,
    spot,
    late,
    base,
    part,
    d,
    out,
    total,
    sems,
):
    chunks, size = d.shape[:2]
    rows = out_any.shape[0]
    copy = pltpu.make_async_copy
    other = 1 - info[2]
    sources = (hidden_any, share_any, spot_any, late_any, base_any, part_any)
    targets = (hidden, share, spot, late, base, part)
    downs = started(
        [
            copy(d_any.at[other, k * size : (k + 1) * size], d.at[k], sems.at[1, k])
            for k in range(chunks)
        ]
    )
    first = started([copy(x, y, sems.at[0, k]) for k, (x, y) in enumerate(zip(sources, targets))])
    waited(first)
    stores = []
    for k in range(chunks):
        downs[k].wait()
        columns = slice(k * size, (k + 1) * size)
        placed = jnp.dot(spot[...], late[:, columns], preferred_element_type=jnp.float32)
        value = matmul_nt(hidden, d[k])
        out[k] = (placed + value[:rows]).astype(jnp.bfloat16)
        last = value[rows:].astype(jnp.bfloat16).astype(jnp.float32)
        value = base[:, columns] + part[:, columns] + share[:, :1] * last
        high = value.astype(jnp.bfloat16)
        low = jnp.where(iota(value.shape, 0) == info[4], value - high.astype(jnp.float32), 0.0)
        count = value.shape[0]
        total[k, :count] = high
        low = jnp.sum(low, axis=0, keepdims=True)
        rest = (total.shape[1] - count, size)
        total[k, count:] = jnp.where(iota(rest, 0) == 0, low, 0.0).astype(jnp.bfloat16)
        stores += started(
            [
                copy(total.at[k], sum_any.at[:, columns], sems.at[3, k]),
                copy(out.at[k], out_any.at[:, columns], sems.at[2, k]),
            ]
        )
    waited(stores)


def mix_kernel(info, rank_ref, pieces_ref, first_ref, second_ref):
    rows = rank_ref.shape[0]
    late = SECOND - CAP
    own, oth = info[2], 1 - info[2]
    for mix_ref, stride, spans in (
        (first_ref, FIRST, ((own, 0, FIRST, 0),)),
        (second_ref, SECOND, ((own, 0, late, FIRST), (oth, late, CAP, 0))),
    ):
        slots = mix_ref.shape[1]
        expert = iota((LANES, slots), 0)
        lane = iota((LANES, slots), 1)
        within = jnp.zeros((1, slots), jnp.float32)
        spread = jnp.zeros((LANES, slots), jnp.float32)
        for parity, offset, count, lowest in spans:
            start = jnp.where((expert & 1) == parity, (expert >> 1) * stride + offset, slots)
            inside = (lane >= start) & (lane < start + count)
            spread = spread + jnp.where(inside, 1.0, 0.0)
            ranks = jnp.where(inside, lane - start + lowest, 0)
            within = within + jnp.sum(ranks, axis=0, keepdims=True).astype(jnp.float32)
        spread = spread.astype(jnp.bfloat16)
        rank = jnp.dot(rank_ref[...], spread, preferred_element_type=jnp.float32)
        match = rank == within
        for k in range(3):
            part = jnp.dot(
                pieces_ref[k * rows : (k + 1) * rows, :], spread, preferred_element_type=jnp.float32
            )
            mix_ref[k * rows : (k + 1) * rows, :] = jnp.where(match, part, 0.0).astype(jnp.bfloat16)


def weigh(mix_ref, back_ref):
    rows = mix_ref.shape[0] // 3
    parts = jnp.dot(mix_ref[...], back_ref[...], preferred_element_type=jnp.float32)
    return parts[2 * rows :] + parts[rows : 2 * rows] + parts[:rows]


def first_kernel(mix_ref, back_ref, resid_ref, base_ref):
    base_ref[...] = resid_ref[...].astype(jnp.float32) + weigh(mix_ref, back_ref)


def combine_kernel(
    info, mix_any, back_any, base_any, _, __, out_ref, square_ref, mix, back, base, sems
):
    chunks, size = back.shape[:2]
    rows = base.shape[0]
    copy = pltpu.make_async_copy
    first = started([copy(mix_any, mix, sems.at[chunks])])
    backs = started(
        [copy(back_any.at[k * size : (k + 1) * size], back.at[k], sems.at[k]) for k in range(chunks)]
    )
    late = started([copy(base_any, base, sems.at[chunks + 1])])
    waited(first)
    parts = jnp.zeros((mix.shape[0], base.shape[1]), jnp.float32)
    for k in range(chunks):
        backs[k].wait()
        parts = parts + jnp.dot(
            mix[:, k * size : (k + 1) * size], back[k], preferred_element_type=jnp.float32
        )
    waited(late)
    moe = parts[2 * rows :] + parts[rows : 2 * rows] + parts[:rows]
    out = (base[...] + moe).astype(jnp.bfloat16)
    out_ref[...] = out
    out_f = out.astype(jnp.float32)
    row = iota(out_f.shape, 0)
    total = jnp.sum(jnp.where(row < info[3], out_f * out_f, 0.0), axis=0, keepdims=True)
    total = jnp.sum(total, axis=1, keepdims=True)
    square_ref[...] = jnp.where(iota(square_ref.shape, 1) == info[4], total, 0.0)


def logits_kernel(info, parts_any, gain_ref, target_ref, unembed_any, out_ref, parts, unembed, sems):
    chunks, size = unembed.shape[:2]
    copy = pltpu.make_async_copy
    first = copy(parts_any, parts, sems.at[chunks])
    first.start()
    rows = started(
        [
            copy(unembed_any.at[k * size : (k + 1) * size], unembed.at[k], sems.at[k])
            for k in range(chunks)
        ]
    )
    first.wait()
    count = out_ref.shape[0]
    shares = parts[...].astype(jnp.float32)
    last = jnp.zeros((count, parts.shape[1]), jnp.float32)
    place = iota(last.shape, 0)
    for k, owner in enumerate(RING):
        at = k * (count + 8)
        last = last + shares[at : at + count]
        last = last + jnp.where(place == owner, shares[at + count : at + count + 1], 0.0)
    last = last.astype(jnp.bfloat16).astype(jnp.float32)
    scale = lax.rsqrt(jnp.mean(last * last, axis=-1, keepdims=True) + 1e-05)
    final = (last * scale * gain_ref[...][None]).astype(jnp.bfloat16)
    lane = iota((count, size), 1)
    top = jnp.full((count, 1), -jnp.inf, jnp.float32)
    target = jnp.zeros((count, 1), jnp.float32)
    for k in range(chunks):
        rows[k].wait()
        logits = matmul_nt(final, unembed[k])
        top = jnp.maximum(top, jnp.max(logits, axis=1, keepdims=True))
        place = target_ref[...] - info[4] * (chunks * size) - k * size
        target = target + jnp.sum(jnp.where(lane == place, logits, 0.0), axis=1, keepdims=True)
    column = iota(out_ref.shape, 1)
    out_ref[...] = jnp.where(column == 0, top, jnp.where(column == 1, target, 0.0))


def place_kernel(info, g_own, g_oth, u_own, u_oth, d_both, _, out_ref):
    left = info[2] == 0
    for k, (own, oth) in enumerate(((g_own[...], g_oth[...]), (u_own[...], u_oth[...]))):
        out_ref[k, :, :FF] = jnp.where(left, own, oth)
        out_ref[k, :, FF:] = jnp.where(left, oth, own)
    out_ref[2, :, :FF] = d_both[0]
    out_ref[2, :, FF:] = d_both[1]


def cast_kernel(first_row, blocks, x_ref, *refs):
    out_ref, held, turned, sems_in, sems_out = refs[-5:]
    groups, size = held.shape[:2]
    fetches, stores = [], []
    for g in range(groups):
        rows = pl.ds(first_row + g * size, size)
        fetches.append(pltpu.make_async_copy(x_ref.at[rows], held.at[g], sems_in.at[g]))
        target = out_ref.at[:, g * 16 : (g + 1) * 16]
        stores.append(pltpu.make_async_copy(turned.at[g], target, sems_out.at[g]))
    for fetch in fetches:
        fetch.start()
    target = iota((size, size), 0)
    source = (target & 15) * blocks + lax.shift_right_logical(target, 4)
    order = jnp.where(iota((size, size), 1) == source, 1.0, 0.0).astype(jnp.bfloat16)
    for g in range(groups):
        fetches[g].wait()
        rows = jnp.dot(order, held[g].astype(jnp.bfloat16), preferred_element_type=jnp.float32)
        turned[g] = rows.astype(jnp.bfloat16).reshape(turned.shape[1:])
        stores[g].start()
    for store in stores:
        store.wait()


def tie_kernel(*_):
    pass


def params():
    return pltpu.CompilerParams(vmem_limit_bytes=VMEM, dimension_semantics=("arbitrary",))


def whole(shape):
    return pl.BlockSpec(shape, lambda *_: tuple(0 for _ in shape))


def paired(
    hidden_in, lengths, routes, route_weights, norm_gain, master, unembed, final_gain, target_ids
):
    rows = hidden_in.shape[1]
    width = hidden_in.shape[2]
    blk_count = lax.axis_size("blk")
    blk = lax.axis_index("blk")
    rep = lax.axis_index("rep")
    first = blk_count * FIRST
    second = blk_count * SECOND
    resid = hidden_in[0]
    info = jnp.stack([2 * blk + rep, 2 * blk + 1 - rep, rep, lengths[blk], blk])
    info = info.astype(jnp.int32)

    shard_rows = master.shape[1]
    flat = master.reshape(3 * shard_rows * blk_count, FF)

    groups = shard_rows // 16

    def turned(k, *after):
        return pl.pallas_call(
            functools.partial(cast_kernel, k * shard_rows * blk_count, blk_count),
            in_specs=[pl.BlockSpec(memory_space=pl.ANY)] * (1 + len(after)),
            out_specs=pl.BlockSpec(memory_space=pl.ANY),
            out_shape=jax.ShapeDtypeStruct((blk_count, shard_rows, FF), jnp.bfloat16),
            scratch_shapes=[
                pltpu.VMEM((groups, 16 * blk_count, FF), jnp.float32),
                pltpu.VMEM((groups, blk_count, 16, FF), jnp.bfloat16),
                pltpu.SemaphoreType.DMA((groups,)),
                pltpu.SemaphoreType.DMA((groups,)),
            ],
            compiler_params=pltpu.CompilerParams(vmem_limit_bytes=VMEM),
            name="cast",
        )(flat, *after)

    def moved(x):
        own = lax.all_to_all(x, "blk", split_axis=0, concat_axis=0, tiled=True)
        return own.reshape(width, FF)

    def swapped(x):
        return lax.ppermute(x, "rep", [(0, 1), (1, 0)])

    def tied(x, *after):
        return pl.pallas_call(
            tie_kernel,
            in_specs=[pl.BlockSpec(memory_space=pl.ANY)] * (1 + len(after)),
            out_specs=pl.BlockSpec(memory_space=pl.ANY),
            out_shape=jax.ShapeDtypeStruct(x.shape, x.dtype),
            input_output_aliases={0: 0},
            name="tie",
        )(x, *after)

    row_ext, pieces = pl.pallas_call(
        prep_kernel,
        grid_spec=pltpu.PrefetchScalarGridSpec(
            num_scalar_prefetch=2,
            grid=(1,),
            in_specs=[
                whole((rows, width)),
                whole((routes.shape[2], rows)),
                whole((routes.shape[2], rows)),
                whole((width,)),
            ],
            out_specs=[whole((rows, width + LANES)), whole((3 * rows, LANES))],
        ),
        out_shape=[
            jax.ShapeDtypeStruct((rows, width + LANES), jnp.bfloat16),
            jax.ShapeDtypeStruct((3 * rows, LANES), jnp.bfloat16),
        ],
        compiler_params=params(),
        name="prep",
    )(lengths, blk[None].astype(jnp.int32), resid, routes[0].T, route_weights[0].T, norm_gain)
    g_own = moved(turned(0, row_ext))
    g_oth = swapped(g_own)
    u_own = moved(turned(1))
    u_oth = swapped(u_own)
    d_own = moved(tied(turned(2), g_oth))

    tokens = lax.all_gather(row_ext, "blk", axis_index_groups=[list(RING)], axis=0, tiled=True)

    ring = jnp.array(RING, jnp.int32)

    def hidden_of(kernel, outs, picked, operands, specs):
        return pl.pallas_call(
            kernel,
            grid_spec=pltpu.PrefetchScalarGridSpec(
                num_scalar_prefetch=3,
                grid=(GROUPS,),
                in_specs=[pl.BlockSpec((blk_count // GROUPS * rows, width + LANES), lambda i, *_: (i, 0))]
                + [whole((width, FF))] * 2
                + specs,
                out_specs=[whole(out.shape) for out in outs],
                scratch_shapes=[
                    pltpu.VMEM((picked, width), jnp.float32),
                    pltpu.VMEM((blk_count, width + LANES), jnp.float32),
                ],
            ),
            out_shape=outs,
            compiler_params=params(),
            name="gate_up",
        )(info, lengths, ring, tokens, *operands)

    step = 512
    quarter = width // 4
    anywhere = pl.BlockSpec(memory_space=pl.ANY)

    def returned(x):
        slots = x.shape[0]
        x = x.reshape(blk_count, slots // blk_count, width)
        x = lax.all_to_all(x, "blk", split_axis=0, concat_axis=0, tiled=True)
        return x.reshape(slots, width)

    def bf16(*shape):
        return jax.ShapeDtypeStruct(shape, jnp.bfloat16)

    def f32(*shape):
        return jax.ShapeDtypeStruct(shape, jnp.float32)

    extra = LANES
    own_hidden, spot, own_share = hidden_of(
        own_kernel,
        [bf16(first + extra, FF), bf16(second, extra), f32(blk_count, LANES)],
        first + extra,
        (g_own, u_own),
        [],
    )
    d_own = tied(d_own, own_hidden)
    d_both = lax.all_gather(d_own, "rep", axis=0)
    own_out, late_out, own_part = pl.pallas_call(
        own_down_kernel,
        in_specs=[anywhere] * 3,
        out_specs=[anywhere] * 3,
        out_shape=[bf16(first, width), bf16(extra, width), f32(blk_count, width)],
        scratch_shapes=[
            pltpu.VMEM((first + extra, FF), jnp.bfloat16),
            pltpu.VMEM((blk_count, LANES), jnp.float32),
            pltpu.VMEM((4, quarter, FF), jnp.bfloat16),
            pltpu.VMEM((4, first + extra, quarter), jnp.bfloat16),
            pltpu.VMEM((4, blk_count, quarter), jnp.float32),
            pltpu.SemaphoreType.DMA((5, 4)),
        ],
        compiler_params=pltpu.CompilerParams(vmem_limit_bytes=VMEM),
        name="own_down",
    )(own_hidden, own_share, d_own)
    own_out = tied(own_out, u_oth)
    own_back = returned(own_out)
    oth_hidden, oth_share, base_part = hidden_of(
        oth_kernel,
        [bf16(second + blk_count, FF), f32(blk_count, LANES), f32(blk_count, width)],
        second + blk_count,
        (g_oth, u_oth, resid, own_out),
        [whole((rows, width)), anywhere],
    )
    oth_out, last_part = pl.pallas_call(
        oth_down_kernel,
        grid_spec=pltpu.PrefetchScalarGridSpec(
            num_scalar_prefetch=1,
            grid=(1,),
            in_specs=[anywhere] * 7,
            out_specs=[anywhere] * 2,
            scratch_shapes=[
                pltpu.VMEM((second + blk_count, FF), jnp.bfloat16),
                pltpu.VMEM((blk_count, LANES), jnp.float32),
                pltpu.VMEM((second, extra), jnp.bfloat16),
                pltpu.VMEM((extra, width), jnp.bfloat16),
                pltpu.VMEM((blk_count, width), jnp.float32),
                pltpu.VMEM((blk_count, width), jnp.float32),
                pltpu.VMEM((4, quarter, FF), jnp.bfloat16),
                pltpu.VMEM((4, second, quarter), jnp.bfloat16),
                pltpu.VMEM((4, 2 * blk_count, quarter), jnp.bfloat16),
                pltpu.SemaphoreType.DMA((4, 6)),
            ],
        ),
        out_shape=[bf16(second, width), bf16(2 * blk_count, width)],
        compiler_params=params(),
        name="oth_down",
    )(info, oth_hidden, oth_share, spot, late_out, base_part, own_part, d_both)
    last_parts = lax.all_gather(
        last_part[: blk_count + 8], "blk", axis_index_groups=[list(RING)], axis=0, tiled=True
    )
    oth_back = returned(oth_out)

    server = pl.pallas_call(
        place_kernel,
        grid_spec=pltpu.PrefetchScalarGridSpec(
            num_scalar_prefetch=1,
            grid=(4,),
            in_specs=[pl.BlockSpec((quarter, FF), lambda i, *_: (i, 0))] * 4
            + [pl.BlockSpec((2, quarter, FF), lambda i, *_: (0, i, 0)), anywhere],
            out_specs=pl.BlockSpec((3, quarter, 2 * FF), lambda i, *_: (0, i, 0)),
        ),
        out_shape=jax.ShapeDtypeStruct((3, width, 2 * FF), jnp.bfloat16),
        compiler_params=params(),
        name="place",
    )(info, g_own, g_oth, u_own, u_oth, d_both, oth_out)

    first_mix, second_mix = pl.pallas_call(
        mix_kernel,
        grid_spec=pltpu.PrefetchScalarGridSpec(
            num_scalar_prefetch=1,
            grid=(1,),
            in_specs=[
                pl.BlockSpec((rows, LANES), lambda i, *_: (0, width // LANES)),
                whole((3 * rows, LANES)),
            ],
            out_specs=[whole((3 * rows, first)), whole((3 * rows, second))],
        ),
        out_shape=[
            jax.ShapeDtypeStruct((3 * rows, first), jnp.bfloat16),
            jax.ShapeDtypeStruct((3 * rows, second), jnp.bfloat16),
        ],
        compiler_params=params(),
        name="mix",
    )(info, row_ext, pieces)

    def weigh_specs(slots):
        return [whole((3 * rows, slots)), pl.BlockSpec((slots, step), lambda i, *_: (0, i))]

    column = pl.BlockSpec((rows, step), lambda i, *_: (0, i))
    base = pl.pallas_call(
        first_kernel,
        grid=(width // step,),
        in_specs=weigh_specs(first) + [column],
        out_specs=column,
        out_shape=f32(rows, width),
        compiler_params=params(),
        name="first",
    )(first_mix, own_back, resid)
    vocab = unembed.shape[0] // 8
    tops = pl.pallas_call(
        logits_kernel,
        grid_spec=pltpu.PrefetchScalarGridSpec(
            num_scalar_prefetch=1,
            grid=(1,),
            in_specs=[anywhere, whole((width,)), whole((blk_count, 1)), anywhere],
            out_specs=whole((blk_count, LANES)),
            scratch_shapes=[
                pltpu.VMEM((blk_count * (blk_count + 8), width), jnp.bfloat16),
                pltpu.VMEM((8, vocab, width), jnp.bfloat16),
                pltpu.SemaphoreType.DMA((9,)),
            ],
        ),
        out_shape=f32(blk_count, LANES),
        compiler_params=params(),
        name="logits",
    )(info, last_parts, final_gain, target_ids[:, None], unembed)

    out_rows, square = pl.pallas_call(
        combine_kernel,
        grid_spec=pltpu.PrefetchScalarGridSpec(
            num_scalar_prefetch=1,
            grid=(1,),
            in_specs=[anywhere] * 5,
            out_specs=[whole((rows, width)), whole((1, LANES))],
            scratch_shapes=[
                pltpu.VMEM((3 * rows, second), jnp.bfloat16),
                pltpu.VMEM((second // LANES, LANES, width), jnp.bfloat16),
                pltpu.VMEM((rows, width), jnp.float32),
                pltpu.SemaphoreType.DMA((second // LANES + 2,)),
            ],
        ),
        out_shape=[bf16(rows, width), f32(1, LANES)],
        compiler_params=params(),
        name="combine",
    )(info, second_mix, oth_back, base, server, tops)

    def everywhere(copies):
        return lax.all_to_all(copies, "blk", split_axis=0, concat_axis=0, tiled=True)

    stats = jnp.concatenate([tops[:, :2].T, square[:, :blk_count]], axis=0)
    parts = everywhere(jnp.broadcast_to(stats[None], (blk_count,) + stats.shape))
    sums = jnp.sum(parts[:, 1:], axis=0)
    norms = jnp.sqrt(sums[1] / (lengths.astype(jnp.float32) * width) + 1e-06)
    request_stats = jnp.stack([norms, jnp.max(parts[:, 0], axis=0), sums[0]])
    return (out_rows[None], server, request_stats)


def local(hidden_in, lengths, routes, route_weights, norm_gain, master, *rest):
    blk_count = lax.axis_size("blk")
    fits = (
        lax.axis_size("rep") == 2
        and master.shape[3] == FF
        and EXPERTS == 2 * blk_count
        and blk_count == len(RING)
        and hidden_in.shape[1] == LEN
        and lengths.shape[0] == blk_count
    )
    form = paired if fits else general
    return form(hidden_in, lengths, routes, route_weights, norm_gain, master, *rest)


def solution(mesh):
    return jax.shard_map(
        local,
        mesh=mesh,
        in_specs=(
            P("rep", "blk", None),
            P("rep"),
            P("rep", "blk", None),
            P("rep", "blk", None),
            P(),
            P(None, "blk", None, "rep"),
            P("blk", None),
            P(),
            P("rep"),
        ),
        out_specs=(P("rep", "blk", None), P(None, None, "blk"), P(None, "rep")),
        check_vma=False,
    )
```

```python
import functools

import jax
import jax.numpy as jnp
from jax import lax
from jax.experimental import pallas as pl
from jax.experimental.pallas import tpu as pltpu
from jax.sharding import PartitionSpec as P

FF = 512
EXPERTS = 32
LEN = 128
CAP = 36
FIRST = 32
SECOND = 40
GROUPS = 4
RING = (0, 1, 4, 5, 8, 9, 12, 13, 14, 15, 10, 11, 6, 7, 2, 3)
LANES = 128
VMEM = 63 * 1024 * 1024


def merged(x, axis, combine):
    everything = jax.tree.map(lambda part: lax.all_gather(part, axis), x)
    initial = jax.tree.map(lambda part: part[0], everything)

    def turn(k, so_far):
        return combine(so_far, jax.tree.map(lambda part: part[k], everything))

    return lax.fori_loop(1, lax.axis_size(axis), turn, initial)


def combine_stats(first, second):
    return (first[0] + second[0], jnp.maximum(first[1], second[1]))


def general(
    hidden_in, lengths, routes, route_weights, norm_gain, master, unembed, final_gain, target_ids
):
    rows_here = hidden_in.shape[1]
    width = hidden_in.shape[2]
    top_count = routes.shape[2]
    blk_count = lax.axis_size("blk")
    rep_count = lax.axis_size("rep")
    blk_index = lax.axis_index("blk")
    unit_count = master.shape[3] * rep_count
    split_ways = max(1, FF // unit_count)
    local_exp = max(1, unit_count // FF)
    group_width = min(unit_count, FF)
    capacity = CAP
    blocks = master.astype(jnp.bfloat16)
    arrived_blocks = lax.all_to_all(blocks, "blk", split_axis=2, concat_axis=1, tiled=True)
    server = lax.all_gather(arrived_blocks, "rep", axis=3, tiled=True)[:, :, 0, :]
    gate_w = server[0].reshape(width, local_exp, group_width)
    up_w = server[1].reshape(width, local_exp, group_width)
    down_w = server[2].reshape(width, local_exp, group_width)
    prompts_here = lengths.shape[0]
    slot_index = blk_index * rows_here + jnp.arange(rows_here, dtype=jnp.int32)
    prompt_of = slot_index // LEN
    position = slot_index % LEN
    prompt_match = prompt_of[:, None] == jnp.arange(prompts_here, dtype=jnp.int32)[None, :]
    row_len = jnp.sum(jnp.where(prompt_match, lengths[None, :], 0), axis=1)
    is_valid = position < row_len
    resid_f = hidden_in[0].astype(jnp.float32)
    normed = (
        resid_f * lax.rsqrt(jnp.mean(resid_f * resid_f, axis=-1, keepdims=True) + 1e-05) * norm_gain
    ).astype(jnp.bfloat16)
    expert_ids = routes[0].reshape(-1)
    pair_live = jnp.repeat(is_valid, top_count)
    pair_row = jnp.repeat(jnp.arange(rows_here, dtype=jnp.int32), top_count)
    expert_hits = (
        (expert_ids[:, None] == jnp.arange(EXPERTS, dtype=jnp.int32)[None, :]) & pair_live[:, None]
    ).astype(jnp.int32)
    slot_rank = jnp.sum((jnp.cumsum(expert_hits, axis=0) - 1) * expert_hits, axis=1)
    slot_id = jnp.where(pair_live, expert_ids * capacity + slot_rank, EXPERTS * capacity)
    source_row = jnp.zeros((EXPERTS * capacity + 1,), jnp.int32).at[slot_id].set(pair_row)[:-1]
    filled = jnp.zeros((EXPERTS * capacity + 1,), jnp.bfloat16).at[slot_id].set(1.0)[:-1]
    outgoing = (normed[source_row] * filled[:, None]).reshape(EXPERTS, capacity, width)
    sending = jnp.repeat(outgoing, split_ways, axis=0).reshape(
        blk_count, local_exp, capacity, width
    )
    arrived = lax.all_to_all(sending, "blk", split_axis=0, concat_axis=0, tiled=True)
    sources = arrived.shape[0]
    slot_count = arrived.shape[2]
    stride = sources
    while stride % 2 == 0 and stride * local_exp * slot_count > 1024:
        stride = stride // 2
    grouped = arrived.reshape(sources // stride, stride, local_exp, slot_count, width)

    def one_block(portion):
        gate_out = jnp.einsum("slnd,dlf->slnf", portion, gate_w, preferred_element_type=jnp.float32)
        up_out = jnp.einsum("slnd,dlf->slnf", portion, up_w, preferred_element_type=jnp.float32)
        hidden = (jax.nn.silu(gate_out) * up_out).astype(jnp.bfloat16)
        return jnp.einsum(
            "slnf,dlf->slnd", hidden, down_w, preferred_element_type=jnp.float32
        ).astype(jnp.bfloat16)

    returned = lax.all_to_all(
        lax.map(one_block, grouped).reshape(sources, local_exp, slot_count, width),
        "blk",
        split_axis=0,
        concat_axis=0,
        tiled=True,
    )
    summed_f = jnp.sum(
        returned.reshape(EXPERTS, split_ways, capacity, width).astype(jnp.float32), axis=1
    )
    expert_out = lax.optimization_barrier(summed_f.astype(jnp.bfloat16)).reshape(
        EXPERTS * capacity, width
    )
    gather_index = jnp.where(pair_live, expert_ids * capacity + slot_rank, 0)
    pair_weight = route_weights[0].reshape(-1) * pair_live.astype(jnp.float32)
    moe = jnp.sum(
        (expert_out[gather_index].astype(jnp.float32) * pair_weight[:, None]).reshape(
            rows_here, top_count, width
        ),
        axis=1,
    )
    out_rows = (resid_f + moe).astype(jnp.bfloat16)
    out_f = out_rows.astype(jnp.float32)
    row_squares = jnp.sum(out_f * out_f, axis=-1) * is_valid.astype(jnp.float32)
    square_local = jnp.sum(jnp.where(prompt_match, row_squares[:, None], 0.0), axis=0)
    is_last = is_valid & (position == row_len - 1)
    picker = (prompt_match & is_last[:, None]).astype(jnp.bfloat16)
    last_local = lax.dot_general(
        picker, out_rows, (((0,), (0,)), ((), ())), preferred_element_type=jnp.float32
    )
    last_rows, square_total = lax.psum((last_local, square_local), "blk")
    norms = jnp.sqrt(square_total / (lengths.astype(jnp.float32) * width) + 1e-06)
    final = (
        last_rows
        * lax.rsqrt(jnp.mean(last_rows * last_rows, axis=-1, keepdims=True) + 1e-05)
        * final_gain
    ).astype(jnp.bfloat16)
    logits = lax.dot_general(
        final, unembed, (((1,), (1,)), ((), ())), preferred_element_type=jnp.float32
    )
    vocab_base = blk_index * unembed.shape[0]
    target_hit = (
        target_ids[:, None] == vocab_base + jnp.arange(unembed.shape[0], dtype=jnp.int32)[None, :]
    )
    target_part = jnp.sum(jnp.where(target_hit, logits, 0.0), axis=1)
    top_part = jnp.max(logits, axis=1)
    target_logit, top_logit = merged((target_part, top_part), "blk", combine_stats)
    request_stats = jnp.stack([norms, top_logit, target_logit])
    return (out_rows[None], server, request_stats)


def iota(shape, dim):
    return lax.broadcasted_iota(jnp.int32, shape, dim)


def prep_kernel(lengths_ref, blk_ref, hidden_ref, routes_ref, weights_ref, gain_ref, rows_ref, pieces_ref):
    rows, width = hidden_ref.shape
    length = lengths_ref[blk_ref[0]]
    x = hidden_ref[...].astype(jnp.float32)
    scale = lax.rsqrt(jnp.mean(x * x, axis=-1, keepdims=True) + 1e-05)
    rows_ref[:, :width] = (x * scale * gain_ref[...][None]).astype(jnp.bfloat16)
    column = iota((rows, LANES), 1)
    lane = column & (EXPERTS - 1)
    row = iota((rows, LANES), 0)
    hit = jnp.zeros((rows, LANES), jnp.float32)
    weight = jnp.zeros((rows, LANES), jnp.float32)
    named_by = jnp.transpose(routes_ref[...].astype(jnp.float32)).astype(jnp.int32)
    weight_by = jnp.transpose(weights_ref[...])
    for k in range(routes_ref.shape[0]):
        named = named_by[:, k : k + 1] == lane
        hit = hit + jnp.where(named, 1.0, 0.0)
        weight = weight + jnp.where(named, weight_by[:, k : k + 1], 0.0)
    live = row < length
    hit = jnp.where(live, hit, 0.0)
    weight = jnp.where(live, weight, 0.0)
    before = jnp.where(iota((rows, rows), 1) < iota((rows, rows), 0), 1.0, 0.0)
    rank = jnp.dot(
        before.astype(jnp.bfloat16), hit.astype(jnp.bfloat16), preferred_element_type=jnp.float32
    )
    told = jnp.where(hit > 0.0, rank, -1.0)
    for k in range(3):
        piece = weight.astype(jnp.bfloat16)
        pieces_ref[k * rows : (k + 1) * rows, :] = piece
        value = piece.astype(jnp.float32)
        told = jnp.where(column >= (k + 1) * EXPERTS, value, told)
        weight = weight - value
    rows_ref[:, width:] = told.astype(jnp.bfloat16)


def pick(info, lengths_ref, ring_ref, which, x_ref, width, place, slots, lasts):
    step = pl.program_id(0)
    rows = x_ref.shape[0]
    sources = rows // LEN
    ranks = x_ref[:, width:].astype(jnp.float32)
    lane = iota((rows, LANES), 1)
    row = iota((rows, 1), 0)
    source = row // LEN
    rank = jnp.sum(jnp.where(lane == info[which], ranks, 0.0), axis=1, keepdims=True)
    slot = jnp.where(rank >= 0.0, place(source.astype(jnp.float32), rank), -1.0)
    slot_lane = iota((rows, slots), 1).astype(jnp.float32)
    one_hot = jnp.where(slot == slot_lane, 1.0, 0.0).astype(jnp.bfloat16)
    dims = (((0,), (0,)), ((), ()))
    chosen = lax.dot_general(
        one_hot, x_ref[:, :width], dims, preferred_element_type=jnp.float32
    )
    home = jnp.full_like(row, -1)
    for s in range(sources):
        owner = ring_ref[step * sources + s]
        home = jnp.where(row == s * LEN + lengths_ref[owner] - 1, owner, home)
    home = jnp.where(rank >= 0.0, home, -1)
    count = lasts.shape[0]
    one_hot = jnp.where(home == iota((rows, count), 1), 1.0, 0.0).astype(jnp.bfloat16)
    last = lax.dot_general(one_hot, x_ref[...], dims, preferred_element_type=jnp.float32)

    @pl.when(step == 0)
    def _():
        lasts[...] = last

    @pl.when(step != 0)
    def _():
        lasts[...] += last

    return chosen


def share_of(info, which, lasts, width):
    ext = lasts[:, width:]
    lane = iota(ext.shape, 1)
    is_own = (lane >= EXPERTS) & ((lane & (EXPERTS - 1)) == info[which])
    return jnp.broadcast_to(
        jnp.sum(jnp.where(is_own, ext, 0.0), axis=1, keepdims=True), ext.shape
    )


def activ(x, g_ref, u_ref):
    x = x.astype(jnp.bfloat16)
    gate = jnp.dot(x, g_ref[...], preferred_element_type=jnp.float32)
    up = jnp.dot(x, u_ref[...], preferred_element_type=jnp.float32)
    return (gate / (1.0 + jnp.exp(-gate)) * up).astype(jnp.bfloat16)


def own_kernel(
    info, lengths_ref, ring_ref, x_ref, g_ref, u_ref, out_ref, spot_ref, share_ref, picked, lasts
):
    step = pl.program_id(0)
    sources = x_ref.shape[0] // LEN
    width = g_ref.shape[0]
    more = CAP - FIRST
    early = sources * FIRST
    all_early = GROUPS * early
    all_rows = all_early + GROUPS * sources * more

    def place(source, rank):
        return jnp.where(
            rank < FIRST, source * FIRST + rank, early + source * more + (rank - FIRST)
        )

    chosen = pick(
        info, lengths_ref, ring_ref, 0, x_ref, width, place, early + sources * more, lasts
    )
    for s in range(sources):
        start = pl.multiple_of(ring_ref[step * sources + s] * FIRST, FIRST)
        picked[pl.ds(start, FIRST), :] = chosen[s * FIRST : (s + 1) * FIRST]
    start = pl.multiple_of(all_early + step * sources * more, sources * more)
    picked[pl.ds(start, sources * more), :] = chosen[early:]

    @pl.when(step == GROUPS - 1)
    def _():
        count = lasts.shape[0]
        picked[all_rows : all_rows + count, :] = lasts[:, :width]
        blank = picked.shape[0] - all_rows - count
        picked[all_rows + count :, :] = jnp.zeros((blank, width), jnp.float32)
        out_ref[...] = activ(picked[...], g_ref, u_ref)
        share_ref[...] = share_of(info, 0, lasts, width)
        column = iota(spot_ref.shape, 1)
        owner = lax.shift_right_logical(column, more.bit_length() - 1)
        source = jnp.full_like(column, -1)
        for k, b in enumerate(RING):
            source = jnp.where(owner == k, b, source)
        spot = jnp.where(source >= 0, source * SECOND + (column & (more - 1)), -1)
        spot_ref[...] = jnp.where(iota(spot_ref.shape, 0) == spot, 1.0, 0.0).astype(jnp.bfloat16)


def oth_kernel(
    info,
    lengths_ref,
    ring_ref,
    x_ref,
    g_ref,
    u_ref,
    resid_ref,
    _,
    out_ref,
    share_ref,
    base_ref,
    picked,
    lasts,
):
    step = pl.program_id(0)
    sources = x_ref.shape[0] // LEN
    width = g_ref.shape[0]
    all_rows = GROUPS * sources * SECOND

    def place(source, rank):
        return source * SECOND + (SECOND - CAP) + rank

    chosen = pick(info, lengths_ref, ring_ref, 1, x_ref, width, place, sources * SECOND, lasts)
    for s in range(sources):
        start = pl.multiple_of(ring_ref[step * sources + s] * SECOND, SECOND)
        picked[pl.ds(start, SECOND), :] = chosen[s * SECOND : (s + 1) * SECOND]

    @pl.when(step == GROUPS - 1)
    def _():
        picked[all_rows:, :] = lasts[:, :width]
        out_ref[...] = activ(picked[...], g_ref, u_ref)
        share_ref[...] = share_of(info, 1, lasts, width)
        resid = resid_ref[...].astype(jnp.float32)
        is_last = iota(resid.shape, 0) == info[3] - 1
        last = jnp.sum(jnp.where(is_last, resid, 0.0), axis=0, keepdims=True)
        base_ref[...] = jnp.where(iota(base_ref.shape, 0) == info[4], last, 0.0)


def matmul_nt(hidden_ref, d):
    return lax.dot_general(
        hidden_ref[...], d, (((1,), (1,)), ((), ())), preferred_element_type=jnp.float32
    )


def started(copies):
    for copy in copies:
        copy.start()
    return copies


def waited(copies):
    for copy in copies:
        copy.wait()


def own_down_kernel(
    hidden_any, share_any, d_any, out_any, late_any, part_any, hidden, share, d, out, part, sems
):
    chunks, size = d.shape[:2]
    rows, count = out_any.shape[0], part.shape[1]
    at = rows + count * (CAP - FIRST)
    copy = pltpu.make_async_copy
    first = started(
        [copy(hidden_any, hidden, sems.at[0, 0]), copy(share_any, share, sems.at[0, 1])]
    )
    downs = started(
        [
            copy(d_any.at[k * size : (k + 1) * size], d.at[k], sems.at[1, k])
            for k in range(chunks)
        ]
    )
    waited(first)
    stores = []
    for k in range(chunks):
        downs[k].wait()
        out[k] = matmul_nt(hidden, d[k]).astype(jnp.bfloat16)
        part[k] = share[:, :1] * out[k, at : at + count].astype(jnp.float32)
        columns = slice(k * size, (k + 1) * size)
        stores += started(
            [
                copy(out.at[k, :rows], out_any.at[:, columns], sems.at[2, k]),
                copy(out.at[k, rows:], late_any.at[:, columns], sems.at[3, k]),
                copy(part.at[k], part_any.at[:, columns], sems.at[4, k]),
            ]
        )
    waited(stores)


def oth_down_kernel(
    info,
    hidden_any,
    share_any,
    spot_any,
    late_any,
    base_any,
    part_any,
    d_any,
    out_any,
    sum_any,
    hidden,
    share,
    spot,
    late,
    base,
    part,
    d,
    out,
    total,
    sems,
):
    chunks, size = d.shape[:2]
    rows = out_any.shape[0]
    copy = pltpu.make_async_copy
    other = 1 - info[2]
    sources = (hidden_any, share_any, spot_any, late_any, base_any, part_any)
    targets = (hidden, share, spot, late, base, part)
    downs = started(
        [
            copy(d_any.at[other, k * size : (k + 1) * size], d.at[k], sems.at[1, k])
            for k in range(chunks)
        ]
    )
    first = started([copy(x, y, sems.at[0, k]) for k, (x, y) in enumerate(zip(sources, targets))])
    waited(first)
    stores = []
    for k in range(chunks):
        downs[k].wait()
        columns = slice(k * size, (k + 1) * size)
        placed = jnp.dot(spot[...], late[:, columns], preferred_element_type=jnp.float32)
        value = matmul_nt(hidden, d[k])
        out[k] = (placed + value[:rows]).astype(jnp.bfloat16)
        last = value[rows:].astype(jnp.bfloat16).astype(jnp.float32)
        total[k] = base[:, columns] + part[:, columns] + share[:, :1] * last
        stores += started(
            [
                copy(total.at[k], sum_any.at[:, columns], sems.at[3, k]),
                copy(out.at[k], out_any.at[:, columns], sems.at[2, k]),
            ]
        )
    waited(stores)


def mix_kernel(info, rank_ref, pieces_ref, first_ref, second_ref):
    rows = rank_ref.shape[0]
    late = SECOND - CAP
    own, oth = info[2], 1 - info[2]
    for mix_ref, stride, spans in (
        (first_ref, FIRST, ((own, 0, FIRST, 0),)),
        (second_ref, SECOND, ((own, 0, late, FIRST), (oth, late, CAP, 0))),
    ):
        slots = mix_ref.shape[1]
        expert = iota((LANES, slots), 0)
        lane = iota((LANES, slots), 1)
        within = jnp.zeros((1, slots), jnp.float32)
        spread = jnp.zeros((LANES, slots), jnp.float32)
        for parity, offset, count, lowest in spans:
            start = jnp.where((expert & 1) == parity, (expert >> 1) * stride + offset, slots)
            inside = (lane >= start) & (lane < start + count)
            spread = spread + jnp.where(inside, 1.0, 0.0)
            ranks = jnp.where(inside, lane - start + lowest, 0)
            within = within + jnp.sum(ranks, axis=0, keepdims=True).astype(jnp.float32)
        spread = spread.astype(jnp.bfloat16)
        rank = jnp.dot(rank_ref[...], spread, preferred_element_type=jnp.float32)
        match = rank == within
        for k in range(3):
            part = jnp.dot(
                pieces_ref[k * rows : (k + 1) * rows, :], spread, preferred_element_type=jnp.float32
            )
            mix_ref[k * rows : (k + 1) * rows, :] = jnp.where(match, part, 0.0).astype(jnp.bfloat16)


def weigh(mix_ref, back_ref):
    rows = mix_ref.shape[0] // 3
    parts = jnp.dot(mix_ref[...], back_ref[...], preferred_element_type=jnp.float32)
    return parts[2 * rows :] + parts[rows : 2 * rows] + parts[:rows]


def first_kernel(mix_ref, back_ref, resid_ref, base_ref):
    base_ref[...] = resid_ref[...].astype(jnp.float32) + weigh(mix_ref, back_ref)


def combine_kernel(
    info, mix_any, back_any, base_any, _, __, out_ref, square_ref, mix, back, base, sems
):
    chunks, size = back.shape[:2]
    rows = base.shape[0]
    copy = pltpu.make_async_copy
    first = started([copy(mix_any, mix, sems.at[chunks])])
    backs = started(
        [copy(back_any.at[k * size : (k + 1) * size], back.at[k], sems.at[k]) for k in range(chunks)]
    )
    late = started([copy(base_any, base, sems.at[chunks + 1])])
    waited(first)
    parts = jnp.zeros((mix.shape[0], base.shape[1]), jnp.float32)
    for k in range(chunks):
        backs[k].wait()
        parts = parts + jnp.dot(
            mix[:, k * size : (k + 1) * size], back[k], preferred_element_type=jnp.float32
        )
    waited(late)
    moe = parts[2 * rows :] + parts[rows : 2 * rows] + parts[:rows]
    out = (base[...] + moe).astype(jnp.bfloat16)
    out_ref[...] = out
    out_f = out.astype(jnp.float32)
    row = iota(out_f.shape, 0)
    total = jnp.sum(jnp.where(row < info[3], out_f * out_f, 0.0), axis=0, keepdims=True)
    square_ref[...] = jnp.broadcast_to(
        jnp.sum(total, axis=1, keepdims=True), square_ref.shape
    )


def place_kernel(info, g_own, g_oth, u_own, u_oth, d_both, _, out_ref):
    left = info[2] == 0
    for k, (own, oth) in enumerate(((g_own[...], g_oth[...]), (u_own[...], u_oth[...]))):
        out_ref[k, :, :FF] = jnp.where(left, own, oth)
        out_ref[k, :, FF:] = jnp.where(left, oth, own)
    out_ref[2, :, :FF] = d_both[0]
    out_ref[2, :, FF:] = d_both[1]


def cast_kernel(first_row, blocks, x_ref, *refs):
    out_ref, held, turned, sems_in, sems_out = refs[-5:]
    groups, size = held.shape[:2]
    fetches, stores = [], []
    for g in range(groups):
        rows = pl.ds(first_row + g * size, size)
        fetches.append(pltpu.make_async_copy(x_ref.at[rows], held.at[g], sems_in.at[g]))
        target = out_ref.at[:, g * 16 : (g + 1) * 16]
        stores.append(pltpu.make_async_copy(turned.at[g], target, sems_out.at[g]))
    for fetch in fetches:
        fetch.start()
    target = iota((size, size), 0)
    source = (target & 15) * blocks + lax.shift_right_logical(target, 4)
    order = jnp.where(iota((size, size), 1) == source, 1.0, 0.0).astype(jnp.bfloat16)
    for g in range(groups):
        fetches[g].wait()
        rows = jnp.dot(order, held[g].astype(jnp.bfloat16), preferred_element_type=jnp.float32)
        turned[g] = rows.astype(jnp.bfloat16).reshape(turned.shape[1:])
        stores[g].start()
    for store in stores:
        store.wait()


def tie_kernel(*_):
    pass


def params():
    return pltpu.CompilerParams(vmem_limit_bytes=VMEM, dimension_semantics=("arbitrary",))


def whole(shape):
    return pl.BlockSpec(shape, lambda *_: tuple(0 for _ in shape))


def paired(
    hidden_in, lengths, routes, route_weights, norm_gain, master, unembed, final_gain, target_ids
):
    rows = hidden_in.shape[1]
    width = hidden_in.shape[2]
    blk_count = lax.axis_size("blk")
    blk = lax.axis_index("blk")
    rep = lax.axis_index("rep")
    first = blk_count * FIRST
    second = blk_count * SECOND
    resid = hidden_in[0]
    info = jnp.stack([2 * blk + rep, 2 * blk + 1 - rep, rep, lengths[blk], blk])
    info = info.astype(jnp.int32)

    shard_rows = master.shape[1]
    flat = master.reshape(3 * shard_rows * blk_count, FF)

    groups = shard_rows // 16

    def turned(k, *after):
        return pl.pallas_call(
            functools.partial(cast_kernel, k * shard_rows * blk_count, blk_count),
            in_specs=[pl.BlockSpec(memory_space=pl.ANY)] * (1 + len(after)),
            out_specs=pl.BlockSpec(memory_space=pl.ANY),
            out_shape=jax.ShapeDtypeStruct((blk_count, shard_rows, FF), jnp.bfloat16),
            scratch_shapes=[
                pltpu.VMEM((groups, 16 * blk_count, FF), jnp.float32),
                pltpu.VMEM((groups, blk_count, 16, FF), jnp.bfloat16),
                pltpu.SemaphoreType.DMA((groups,)),
                pltpu.SemaphoreType.DMA((groups,)),
            ],
            compiler_params=pltpu.CompilerParams(vmem_limit_bytes=VMEM),
            name="cast",
        )(flat, *after)

    def moved(x):
        own = lax.all_to_all(x, "blk", split_axis=0, concat_axis=0, tiled=True)
        return own.reshape(width, FF)

    def swapped(x):
        return lax.ppermute(x, "rep", [(0, 1), (1, 0)])

    def tied(x, *after):
        return pl.pallas_call(
            tie_kernel,
            in_specs=[pl.BlockSpec(memory_space=pl.ANY)] * (1 + len(after)),
            out_specs=pl.BlockSpec(memory_space=pl.ANY),
            out_shape=jax.ShapeDtypeStruct(x.shape, x.dtype),
            input_output_aliases={0: 0},
            name="tie",
        )(x, *after)

    row_ext, pieces = pl.pallas_call(
        prep_kernel,
        grid_spec=pltpu.PrefetchScalarGridSpec(
            num_scalar_prefetch=2,
            grid=(1,),
            in_specs=[
                whole((rows, width)),
                whole((routes.shape[2], rows)),
                whole((routes.shape[2], rows)),
                whole((width,)),
            ],
            out_specs=[whole((rows, width + LANES)), whole((3 * rows, LANES))],
        ),
        out_shape=[
            jax.ShapeDtypeStruct((rows, width + LANES), jnp.bfloat16),
            jax.ShapeDtypeStruct((3 * rows, LANES), jnp.bfloat16),
        ],
        compiler_params=params(),
        name="prep",
    )(lengths, blk[None].astype(jnp.int32), resid, routes[0].T, route_weights[0].T, norm_gain)
    g_own = moved(turned(0, row_ext))
    g_oth = swapped(g_own)
    u_own = moved(turned(1))
    u_oth = swapped(u_own)
    d_own = moved(tied(turned(2), g_oth))

    tokens = lax.all_gather(row_ext, "blk", axis_index_groups=[list(RING)], axis=0, tiled=True)

    ring = jnp.array(RING, jnp.int32)

    def hidden_of(kernel, outs, picked, operands, specs):
        return pl.pallas_call(
            kernel,
            grid_spec=pltpu.PrefetchScalarGridSpec(
                num_scalar_prefetch=3,
                grid=(GROUPS,),
                in_specs=[pl.BlockSpec((blk_count // GROUPS * rows, width + LANES), lambda i, *_: (i, 0))]
                + [whole((width, FF))] * 2
                + specs,
                out_specs=[whole(out.shape) for out in outs],
                scratch_shapes=[
                    pltpu.VMEM((picked, width), jnp.float32),
                    pltpu.VMEM((blk_count, width + LANES), jnp.float32),
                ],
            ),
            out_shape=outs,
            compiler_params=params(),
            name="gate_up",
        )(info, lengths, ring, tokens, *operands)

    step = 512
    quarter = width // 4
    anywhere = pl.BlockSpec(memory_space=pl.ANY)

    def returned(x):
        slots = x.shape[0]
        x = x.reshape(blk_count, slots // blk_count, width)
        x = lax.all_to_all(x, "blk", split_axis=0, concat_axis=0, tiled=True)
        return x.reshape(slots, width)

    def bf16(*shape):
        return jax.ShapeDtypeStruct(shape, jnp.bfloat16)

    def f32(*shape):
        return jax.ShapeDtypeStruct(shape, jnp.float32)

    extra = LANES
    own_hidden, spot, own_share = hidden_of(
        own_kernel,
        [bf16(first + extra, FF), bf16(second, extra), f32(blk_count, LANES)],
        first + extra,
        (g_own, u_own),
        [],
    )
    d_own = tied(d_own, own_hidden)
    d_both = lax.all_gather(d_own, "rep", axis=0)
    own_out, late_out, own_part = pl.pallas_call(
        own_down_kernel,
        in_specs=[anywhere] * 3,
        out_specs=[anywhere] * 3,
        out_shape=[bf16(first, width), bf16(extra, width), f32(blk_count, width)],
        scratch_shapes=[
            pltpu.VMEM((first + extra, FF), jnp.bfloat16),
            pltpu.VMEM((blk_count, LANES), jnp.float32),
            pltpu.VMEM((4, quarter, FF), jnp.bfloat16),
            pltpu.VMEM((4, first + extra, quarter), jnp.bfloat16),
            pltpu.VMEM((4, blk_count, quarter), jnp.float32),
            pltpu.SemaphoreType.DMA((5, 4)),
        ],
        compiler_params=pltpu.CompilerParams(vmem_limit_bytes=VMEM),
        name="own_down",
    )(own_hidden, own_share, d_own)
    own_out = tied(own_out, u_oth)
    own_back = returned(own_out)
    oth_hidden, oth_share, base_part = hidden_of(
        oth_kernel,
        [bf16(second + blk_count, FF), f32(blk_count, LANES), f32(blk_count, width)],
        second + blk_count,
        (g_oth, u_oth, resid, own_out),
        [whole((rows, width)), anywhere],
    )
    oth_out, last_part = pl.pallas_call(
        oth_down_kernel,
        grid_spec=pltpu.PrefetchScalarGridSpec(
            num_scalar_prefetch=1,
            grid=(1,),
            in_specs=[anywhere] * 7,
            out_specs=[anywhere] * 2,
            scratch_shapes=[
                pltpu.VMEM((second + blk_count, FF), jnp.bfloat16),
                pltpu.VMEM((blk_count, LANES), jnp.float32),
                pltpu.VMEM((second, extra), jnp.bfloat16),
                pltpu.VMEM((extra, width), jnp.bfloat16),
                pltpu.VMEM((blk_count, width), jnp.float32),
                pltpu.VMEM((blk_count, width), jnp.float32),
                pltpu.VMEM((4, quarter, FF), jnp.bfloat16),
                pltpu.VMEM((4, second, quarter), jnp.bfloat16),
                pltpu.VMEM((4, blk_count, quarter), jnp.float32),
                pltpu.SemaphoreType.DMA((4, 6)),
            ],
        ),
        out_shape=[bf16(second, width), f32(blk_count, width)],
        compiler_params=params(),
        name="oth_down",
    )(info, oth_hidden, oth_share, spot, late_out, base_part, own_part, d_both)
    last_parts = lax.all_gather(last_part, "blk", axis_index_groups=[list(RING)], axis=0)
    oth_back = returned(oth_out)

    server = pl.pallas_call(
        place_kernel,
        grid_spec=pltpu.PrefetchScalarGridSpec(
            num_scalar_prefetch=1,
            grid=(4,),
            in_specs=[pl.BlockSpec((quarter, FF), lambda i, *_: (i, 0))] * 4
            + [pl.BlockSpec((2, quarter, FF), lambda i, *_: (0, i, 0)), anywhere],
            out_specs=pl.BlockSpec((3, quarter, 2 * FF), lambda i, *_: (0, i, 0)),
        ),
        out_shape=jax.ShapeDtypeStruct((3, width, 2 * FF), jnp.bfloat16),
        compiler_params=params(),
        name="place",
    )(info, g_own, g_oth, u_own, u_oth, d_both, oth_out)

    first_mix, second_mix = pl.pallas_call(
        mix_kernel,
        grid_spec=pltpu.PrefetchScalarGridSpec(
            num_scalar_prefetch=1,
            grid=(1,),
            in_specs=[
                pl.BlockSpec((rows, LANES), lambda i, *_: (0, width // LANES)),
                whole((3 * rows, LANES)),
            ],
            out_specs=[whole((3 * rows, first)), whole((3 * rows, second))],
        ),
        out_shape=[
            jax.ShapeDtypeStruct((3 * rows, first), jnp.bfloat16),
            jax.ShapeDtypeStruct((3 * rows, second), jnp.bfloat16),
        ],
        compiler_params=params(),
        name="mix",
    )(info, row_ext, pieces)

    def weigh_specs(slots):
        return [whole((3 * rows, slots)), pl.BlockSpec((slots, step), lambda i, *_: (0, i))]

    column = pl.BlockSpec((rows, step), lambda i, *_: (0, i))
    base = pl.pallas_call(
        first_kernel,
        grid=(width // step,),
        in_specs=weigh_specs(first) + [column],
        out_specs=column,
        out_shape=f32(rows, width),
        compiler_params=params(),
        name="first",
    )(first_mix, own_back, resid)
    last_rows = lax.reduce_precision(jnp.sum(last_parts, axis=0), 8, 7)
    final = (
        last_rows
        * lax.rsqrt(jnp.mean(last_rows * last_rows, axis=-1, keepdims=True) + 1e-05)
        * final_gain
    ).astype(jnp.bfloat16)
    logits = lax.dot_general(
        final, unembed, (((1,), (1,)), ((), ())), preferred_element_type=jnp.float32
    )
    vocab_base = blk * unembed.shape[0]
    target_hit = (
        target_ids[:, None] == vocab_base + jnp.arange(unembed.shape[0], dtype=jnp.int32)[None, :]
    )
    target_part = jnp.sum(jnp.where(target_hit, logits, 0.0), axis=1)
    top_part = jnp.max(logits, axis=1)

    out_rows, square = pl.pallas_call(
        combine_kernel,
        grid_spec=pltpu.PrefetchScalarGridSpec(
            num_scalar_prefetch=1,
            grid=(1,),
            in_specs=[anywhere] * 5,
            out_specs=[whole((rows, width)), whole((1, LANES))],
            scratch_shapes=[
                pltpu.VMEM((3 * rows, second), jnp.bfloat16),
                pltpu.VMEM((second // LANES, LANES, width), jnp.bfloat16),
                pltpu.VMEM((rows, width), jnp.float32),
                pltpu.SemaphoreType.DMA((second // LANES + 2,)),
            ],
        ),
        out_shape=[bf16(rows, width), f32(1, LANES)],
        compiler_params=params(),
        name="combine",
    )(info, second_mix, oth_back, base, server, top_part[None])

    def everywhere(copies):
        return lax.all_to_all(copies, "blk", split_axis=0, concat_axis=0, tiled=True)

    prompt = jnp.arange(blk_count, dtype=jnp.int32)
    square_part = jnp.where(prompt == blk, square[0, :blk_count], 0.0)
    stats = jnp.stack([top_part, target_part, square_part])
    parts = everywhere(jnp.broadcast_to(stats[None], (blk_count,) + stats.shape))
    sums = jnp.sum(parts[:, 1:], axis=0)
    norms = jnp.sqrt(sums[1] / (lengths.astype(jnp.float32) * width) + 1e-06)
    request_stats = jnp.stack([norms, jnp.max(parts[:, 0], axis=0), sums[0]])
    return (out_rows[None], server, request_stats)


def local(hidden_in, lengths, routes, route_weights, norm_gain, master, *rest):
    blk_count = lax.axis_size("blk")
    fits = (
        lax.axis_size("rep") == 2
        and master.shape[3] == FF
        and EXPERTS == 2 * blk_count
        and blk_count == len(RING)
        and hidden_in.shape[1] == LEN
        and lengths.shape[0] == blk_count
    )
    form = paired if fits else general
    return form(hidden_in, lengths, routes, route_weights, norm_gain, master, *rest)


def solution(mesh):
    return jax.shard_map(
        local,
        mesh=mesh,
        in_specs=(
            P("rep", "blk", None),
            P("rep"),
            P("rep", "blk", None),
            P("rep", "blk", None),
            P(),
            P(None, "blk", None, "rep"),
            P("blk", None),
            P(),
            P("rep"),
        ),
        out_specs=(P("rep", "blk", None), P(None, None, "blk"), P(None, "rep")),
        check_vma=False,
    )
```

```python
import functools

import jax
import jax.numpy as jnp
from jax import lax
from jax.experimental import pallas as pl
from jax.experimental.pallas import tpu as pltpu
from jax.sharding import PartitionSpec as P

FF = 512
EXPERTS = 32
LEN = 128
CAP = 36
FIRST = 32
SECOND = 40
GROUPS = 4
RING = (0, 1, 4, 5, 8, 9, 12, 13, 14, 15, 10, 11, 6, 7, 2, 3)
LANES = 128
VMEM = 63 * 1024 * 1024


def merged(x, axis, combine):
    everything = jax.tree.map(lambda part: lax.all_gather(part, axis), x)
    initial = jax.tree.map(lambda part: part[0], everything)

    def turn(k, so_far):
        return combine(so_far, jax.tree.map(lambda part: part[k], everything))

    return lax.fori_loop(1, lax.axis_size(axis), turn, initial)


def combine_stats(first, second):
    return (first[0] + second[0], jnp.maximum(first[1], second[1]))


def general(
    hidden_in, lengths, routes, route_weights, norm_gain, master, unembed, final_gain, target_ids
):
    rows_here = hidden_in.shape[1]
    width = hidden_in.shape[2]
    top_count = routes.shape[2]
    blk_count = lax.axis_size("blk")
    rep_count = lax.axis_size("rep")
    blk_index = lax.axis_index("blk")
    unit_count = master.shape[3] * rep_count
    split_ways = max(1, FF // unit_count)
    local_exp = max(1, unit_count // FF)
    group_width = min(unit_count, FF)
    capacity = CAP
    blocks = master.astype(jnp.bfloat16)
    arrived_blocks = lax.all_to_all(blocks, "blk", split_axis=2, concat_axis=1, tiled=True)
    server = lax.all_gather(arrived_blocks, "rep", axis=3, tiled=True)[:, :, 0, :]
    gate_w = server[0].reshape(width, local_exp, group_width)
    up_w = server[1].reshape(width, local_exp, group_width)
    down_w = server[2].reshape(width, local_exp, group_width)
    prompts_here = lengths.shape[0]
    slot_index = blk_index * rows_here + jnp.arange(rows_here, dtype=jnp.int32)
    prompt_of = slot_index // LEN
    position = slot_index % LEN
    prompt_match = prompt_of[:, None] == jnp.arange(prompts_here, dtype=jnp.int32)[None, :]
    row_len = jnp.sum(jnp.where(prompt_match, lengths[None, :], 0), axis=1)
    is_valid = position < row_len
    resid_f = hidden_in[0].astype(jnp.float32)
    normed = (
        resid_f * lax.rsqrt(jnp.mean(resid_f * resid_f, axis=-1, keepdims=True) + 1e-05) * norm_gain
    ).astype(jnp.bfloat16)
    expert_ids = routes[0].reshape(-1)
    pair_live = jnp.repeat(is_valid, top_count)
    pair_row = jnp.repeat(jnp.arange(rows_here, dtype=jnp.int32), top_count)
    expert_hits = (
        (expert_ids[:, None] == jnp.arange(EXPERTS, dtype=jnp.int32)[None, :]) & pair_live[:, None]
    ).astype(jnp.int32)
    slot_rank = jnp.sum((jnp.cumsum(expert_hits, axis=0) - 1) * expert_hits, axis=1)
    slot_id = jnp.where(pair_live, expert_ids * capacity + slot_rank, EXPERTS * capacity)
    source_row = jnp.zeros((EXPERTS * capacity + 1,), jnp.int32).at[slot_id].set(pair_row)[:-1]
    filled = jnp.zeros((EXPERTS * capacity + 1,), jnp.bfloat16).at[slot_id].set(1.0)[:-1]
    outgoing = (normed[source_row] * filled[:, None]).reshape(EXPERTS, capacity, width)
    sending = jnp.repeat(outgoing, split_ways, axis=0).reshape(
        blk_count, local_exp, capacity, width
    )
    arrived = lax.all_to_all(sending, "blk", split_axis=0, concat_axis=0, tiled=True)
    sources = arrived.shape[0]
    slot_count = arrived.shape[2]
    stride = sources
    while stride % 2 == 0 and stride * local_exp * slot_count > 1024:
        stride = stride // 2
    grouped = arrived.reshape(sources // stride, stride, local_exp, slot_count, width)

    def one_block(portion):
        gate_out = jnp.einsum("slnd,dlf->slnf", portion, gate_w, preferred_element_type=jnp.float32)
        up_out = jnp.einsum("slnd,dlf->slnf", portion, up_w, preferred_element_type=jnp.float32)
        hidden = (jax.nn.silu(gate_out) * up_out).astype(jnp.bfloat16)
        return jnp.einsum(
            "slnf,dlf->slnd", hidden, down_w, preferred_element_type=jnp.float32
        ).astype(jnp.bfloat16)

    returned = lax.all_to_all(
        lax.map(one_block, grouped).reshape(sources, local_exp, slot_count, width),
        "blk",
        split_axis=0,
        concat_axis=0,
        tiled=True,
    )
    summed_f = jnp.sum(
        returned.reshape(EXPERTS, split_ways, capacity, width).astype(jnp.float32), axis=1
    )
    expert_out = lax.optimization_barrier(summed_f.astype(jnp.bfloat16)).reshape(
        EXPERTS * capacity, width
    )
    gather_index = jnp.where(pair_live, expert_ids * capacity + slot_rank, 0)
    pair_weight = route_weights[0].reshape(-1) * pair_live.astype(jnp.float32)
    moe = jnp.sum(
        (expert_out[gather_index].astype(jnp.float32) * pair_weight[:, None]).reshape(
            rows_here, top_count, width
        ),
        axis=1,
    )
    out_rows = (resid_f + moe).astype(jnp.bfloat16)
    out_f = out_rows.astype(jnp.float32)
    row_squares = jnp.sum(out_f * out_f, axis=-1) * is_valid.astype(jnp.float32)
    square_local = jnp.sum(jnp.where(prompt_match, row_squares[:, None], 0.0), axis=0)
    is_last = is_valid & (position == row_len - 1)
    picker = (prompt_match & is_last[:, None]).astype(jnp.bfloat16)
    last_local = lax.dot_general(
        picker, out_rows, (((0,), (0,)), ((), ())), preferred_element_type=jnp.float32
    )
    last_rows, square_total = lax.psum((last_local, square_local), "blk")
    norms = jnp.sqrt(square_total / (lengths.astype(jnp.float32) * width) + 1e-06)
    final = (
        last_rows
        * lax.rsqrt(jnp.mean(last_rows * last_rows, axis=-1, keepdims=True) + 1e-05)
        * final_gain
    ).astype(jnp.bfloat16)
    logits = lax.dot_general(
        final, unembed, (((1,), (1,)), ((), ())), preferred_element_type=jnp.float32
    )
    vocab_base = blk_index * unembed.shape[0]
    target_hit = (
        target_ids[:, None] == vocab_base + jnp.arange(unembed.shape[0], dtype=jnp.int32)[None, :]
    )
    target_part = jnp.sum(jnp.where(target_hit, logits, 0.0), axis=1)
    top_part = jnp.max(logits, axis=1)
    target_logit, top_logit = merged((target_part, top_part), "blk", combine_stats)
    request_stats = jnp.stack([norms, top_logit, target_logit])
    return (out_rows[None], server, request_stats)


def iota(shape, dim):
    return lax.broadcasted_iota(jnp.int32, shape, dim)


def prep_kernel(lengths_ref, blk_ref, hidden_ref, routes_ref, weights_ref, gain_ref, rows_ref, pieces_ref):
    rows, width = hidden_ref.shape
    length = lengths_ref[blk_ref[0]]
    x = hidden_ref[...].astype(jnp.float32)
    scale = lax.rsqrt(jnp.mean(x * x, axis=-1, keepdims=True) + 1e-05)
    rows_ref[:, :width] = (x * scale * gain_ref[...][None]).astype(jnp.bfloat16)
    column = iota((rows, LANES), 1)
    lane = column & (EXPERTS - 1)
    row = iota((rows, LANES), 0)
    hit = jnp.zeros((rows, LANES), jnp.float32)
    weight = jnp.zeros((rows, LANES), jnp.float32)
    named_by = jnp.transpose(routes_ref[...].astype(jnp.float32)).astype(jnp.int32)
    weight_by = jnp.transpose(weights_ref[...])
    for k in range(routes_ref.shape[0]):
        named = named_by[:, k : k + 1] == lane
        hit = hit + jnp.where(named, 1.0, 0.0)
        weight = weight + jnp.where(named, weight_by[:, k : k + 1], 0.0)
    live = row < length
    hit = jnp.where(live, hit, 0.0)
    weight = jnp.where(live, weight, 0.0)
    before = jnp.where(iota((rows, rows), 1) < iota((rows, rows), 0), 1.0, 0.0)
    rank = jnp.dot(
        before.astype(jnp.bfloat16), hit.astype(jnp.bfloat16), preferred_element_type=jnp.float32
    )
    told = jnp.where(hit > 0.0, rank, -1.0)
    for k in range(3):
        piece = weight.astype(jnp.bfloat16)
        pieces_ref[k * rows : (k + 1) * rows, :] = piece
        value = piece.astype(jnp.float32)
        told = jnp.where(column >= (k + 1) * EXPERTS, value, told)
        weight = weight - value
    is_last = iota(x.shape, 0) == length - 1
    last = jnp.sum(jnp.where(is_last, x, 0.0), axis=0, keepdims=True)
    place = iota((EXPERTS, LANES), 0)
    packed = jnp.zeros((EXPERTS, LANES), jnp.float32)
    for k in range(width // LANES):
        packed = jnp.where(place == k, last[:, k * LANES : (k + 1) * LANES], packed)
    packed = jnp.concatenate([jnp.zeros((3 * EXPERTS, LANES), jnp.float32), packed], axis=0)
    told = jnp.where(column >= 3 * EXPERTS, jnp.transpose(packed), told)
    rows_ref[:, width:] = told.astype(jnp.bfloat16)


def pick(info, lengths_ref, ring_ref, which, x_ref, width, place, slots, lasts):
    step = pl.program_id(0)
    rows = x_ref.shape[0]
    sources = rows // LEN
    ranks = x_ref[:, width:].astype(jnp.float32)
    lane = iota((rows, LANES), 1)
    row = iota((rows, 1), 0)
    source = row // LEN
    rank = jnp.sum(jnp.where(lane == info[which], ranks, 0.0), axis=1, keepdims=True)
    slot = jnp.where(rank >= 0.0, place(source.astype(jnp.float32), rank), -1.0)
    slot_lane = iota((rows, slots), 1).astype(jnp.float32)
    one_hot = jnp.where(slot == slot_lane, 1.0, 0.0).astype(jnp.bfloat16)
    dims = (((0,), (0,)), ((), ()))
    chosen = lax.dot_general(
        one_hot, x_ref[:, :width], dims, preferred_element_type=jnp.float32
    )
    home = jnp.full_like(row, -1)
    for s in range(sources):
        owner = ring_ref[step * sources + s]
        home = jnp.where(row == s * LEN + lengths_ref[owner] - 1, owner, home)
    home = jnp.where(rank >= 0.0, home, -1)
    count = lasts.shape[0]
    one_hot = jnp.where(home == iota((rows, count), 1), 1.0, 0.0).astype(jnp.bfloat16)
    last = lax.dot_general(one_hot, x_ref[...], dims, preferred_element_type=jnp.float32)

    @pl.when(step == 0)
    def _():
        lasts[...] = last

    @pl.when(step != 0)
    def _():
        lasts[...] += last

    return chosen


def share_of(info, which, lasts, width):
    ext = lasts[:, width:]
    lane = iota(ext.shape, 1)
    is_own = (lane == EXPERTS + info[which]) | (lane == 2 * EXPERTS + info[which])
    return jnp.broadcast_to(
        jnp.sum(jnp.where(is_own, ext, 0.0), axis=1, keepdims=True), ext.shape
    )


def activ(x, g_ref, u_ref):
    x = x.astype(jnp.bfloat16)
    gate = jnp.dot(x, g_ref[...], preferred_element_type=jnp.float32)
    up = jnp.dot(x, u_ref[...], preferred_element_type=jnp.float32)
    return (gate / (1.0 + jnp.exp(-gate)) * up).astype(jnp.bfloat16)


def own_kernel(
    info, lengths_ref, ring_ref, x_ref, g_ref, u_ref, out_ref, spot_ref, share_ref, picked, lasts
):
    step = pl.program_id(0)
    sources = x_ref.shape[0] // LEN
    width = g_ref.shape[0]
    more = CAP - FIRST
    early = sources * FIRST
    all_early = GROUPS * early
    all_rows = all_early + GROUPS * sources * more

    def place(source, rank):
        return jnp.where(
            rank < FIRST, source * FIRST + rank, early + source * more + (rank - FIRST)
        )

    chosen = pick(
        info, lengths_ref, ring_ref, 0, x_ref, width, place, early + sources * more, lasts
    )
    for s in range(sources):
        start = pl.multiple_of(ring_ref[step * sources + s] * FIRST, FIRST)
        picked[pl.ds(start, FIRST), :] = chosen[s * FIRST : (s + 1) * FIRST]
    start = pl.multiple_of(all_early + step * sources * more, sources * more)
    picked[pl.ds(start, sources * more), :] = chosen[early:]

    @pl.when(step == GROUPS - 1)
    def _():
        count = lasts.shape[0]
        picked[all_rows : all_rows + count, :] = lasts[:, :width]
        blank = picked.shape[0] - all_rows - count
        picked[all_rows + count :, :] = jnp.zeros((blank, width), jnp.float32)
        out_ref[...] = activ(picked[...], g_ref, u_ref)
        share_ref[...] = share_of(info, 0, lasts, width)
        column = iota(spot_ref.shape, 1)
        owner = lax.shift_right_logical(column, more.bit_length() - 1)
        source = jnp.full_like(column, -1)
        for k, b in enumerate(RING):
            source = jnp.where(owner == k, b, source)
        spot = jnp.where(source >= 0, source * SECOND + (column & (more - 1)), -1)
        spot_ref[...] = jnp.where(iota(spot_ref.shape, 0) == spot, 1.0, 0.0).astype(jnp.bfloat16)


def oth_kernel(
    info,
    lengths_ref,
    ring_ref,
    x_ref,
    g_ref,
    u_ref,
    _,
    out_ref,
    share_ref,
    base_ref,
    picked,
    lasts,
):
    step = pl.program_id(0)
    sources = x_ref.shape[0] // LEN
    width = g_ref.shape[0]
    all_rows = GROUPS * sources * SECOND

    def place(source, rank):
        return source * SECOND + (SECOND - CAP) + rank

    @pl.when(step == 0)
    def _():
        base_ref[...] = jnp.zeros_like(base_ref)

    chosen = pick(info, lengths_ref, ring_ref, 1, x_ref, width, place, sources * SECOND, lasts)
    for s in range(sources):
        start = pl.multiple_of(ring_ref[step * sources + s] * SECOND, SECOND)
        picked[pl.ds(start, SECOND), :] = chosen[s * SECOND : (s + 1) * SECOND]
        ext = x_ref[s * LEN : (s + 1) * LEN, width:].astype(jnp.float32)
        packed = jnp.transpose(ext)[3 * EXPERTS :]
        mine = iota((base_ref.shape[0], LANES), 0) == ring_ref[step * sources + s]
        for k in range(width // LANES):
            lanes = slice(k * LANES, (k + 1) * LANES)
            base_ref[:, lanes] = jnp.where(mine, packed[k : k + 1], base_ref[:, lanes])

    @pl.when(step == GROUPS - 1)
    def _():
        picked[all_rows:, :] = lasts[:, :width]
        out_ref[...] = activ(picked[...], g_ref, u_ref)
        share_ref[...] = share_of(info, 1, lasts, width)


def matmul_nt(hidden_ref, d):
    return lax.dot_general(
        hidden_ref[...], d, (((1,), (1,)), ((), ())), preferred_element_type=jnp.float32
    )


def started(copies):
    for copy in copies:
        copy.start()
    return copies


def waited(copies):
    for copy in copies:
        copy.wait()


def own_down_kernel(
    hidden_any, share_any, d_any, out_any, late_any, part_any, hidden, share, d, out, part, sems
):
    chunks, size = d.shape[:2]
    rows, count = out_any.shape[0], part.shape[1]
    at = rows + count * (CAP - FIRST)
    copy = pltpu.make_async_copy
    first = started(
        [copy(hidden_any, hidden, sems.at[0, 0]), copy(share_any, share, sems.at[0, 1])]
    )
    downs = started(
        [
            copy(d_any.at[k * size : (k + 1) * size], d.at[k], sems.at[1, k])
            for k in range(chunks)
        ]
    )
    waited(first)
    stores = []
    for k in range(chunks):
        downs[k].wait()
        out[k] = matmul_nt(hidden, d[k]).astype(jnp.bfloat16)
        part[k] = share[:, :1] * out[k, at : at + count].astype(jnp.float32)
        columns = slice(k * size, (k + 1) * size)
        stores += started(
            [
                copy(out.at[k, :rows], out_any.at[:, columns], sems.at[2, k]),
                copy(out.at[k, rows:], late_any.at[:, columns], sems.at[3, k]),
                copy(part.at[k], part_any.at[:, columns], sems.at[4, k]),
            ]
        )
    waited(stores)


def oth_down_kernel(
    info,
    hidden_any,
    share_any,
    spot_any,
    late_any,
    part_any,
    d_any,
    out_any,
    sum_any,
    hidden,
    share,
    spot,
    late,
    part,
    d,
    out,
    total,
    sems,
):
    chunks, size = d.shape[:2]
    rows = out_any.shape[0]
    copy = pltpu.make_async_copy
    other = 1 - info[2]
    sources = (hidden_any, share_any, spot_any, late_any, part_any)
    targets = (hidden, share, spot, late, part)
    downs = started(
        [
            copy(d_any.at[other, k * size : (k + 1) * size], d.at[k], sems.at[1, k])
            for k in range(chunks)
        ]
    )
    first = started([copy(x, y, sems.at[0, k]) for k, (x, y) in enumerate(zip(sources, targets))])
    waited(first)
    stores = []
    for k in range(chunks):
        downs[k].wait()
        columns = slice(k * size, (k + 1) * size)
        placed = jnp.dot(spot[...], late[:, columns], preferred_element_type=jnp.float32)
        value = matmul_nt(hidden, d[k])
        out[k] = (placed + value[:rows]).astype(jnp.bfloat16)
        last = value[rows:].astype(jnp.bfloat16).astype(jnp.float32)
        total[k] = (part[:, columns] + share[:, :1] * last).astype(jnp.bfloat16)
        stores += started(
            [
                copy(total.at[k], sum_any.at[:, columns], sems.at[3, k]),
                copy(out.at[k], out_any.at[:, columns], sems.at[2, k]),
            ]
        )
    waited(stores)


def mix_kernel(info, rank_ref, pieces_ref, first_ref, second_ref):
    rows = rank_ref.shape[0]
    late = SECOND - CAP
    own, oth = info[2], 1 - info[2]
    for mix_ref, stride, spans in (
        (first_ref, FIRST, ((own, 0, FIRST, 0),)),
        (second_ref, SECOND, ((own, 0, late, FIRST), (oth, late, CAP, 0))),
    ):
        slots = mix_ref.shape[1]
        expert = iota((LANES, slots), 0)
        lane = iota((LANES, slots), 1)
        within = jnp.zeros((1, slots), jnp.float32)
        spread = jnp.zeros((LANES, slots), jnp.float32)
        for parity, offset, count, lowest in spans:
            start = jnp.where((expert & 1) == parity, (expert >> 1) * stride + offset, slots)
            inside = (lane >= start) & (lane < start + count)
            spread = spread + jnp.where(inside, 1.0, 0.0)
            ranks = jnp.where(inside, lane - start + lowest, 0)
            within = within + jnp.sum(ranks, axis=0, keepdims=True).astype(jnp.float32)
        spread = spread.astype(jnp.bfloat16)
        rank = jnp.dot(rank_ref[...], spread, preferred_element_type=jnp.float32)
        match = rank == within
        for k in range(3):
            part = jnp.dot(
                pieces_ref[k * rows : (k + 1) * rows, :], spread, preferred_element_type=jnp.float32
            )
            mix_ref[k * rows : (k + 1) * rows, :] = jnp.where(match, part, 0.0).astype(jnp.bfloat16)


def weigh(mix_ref, back_ref):
    rows = mix_ref.shape[0] // 3
    parts = jnp.dot(mix_ref[...], back_ref[...], preferred_element_type=jnp.float32)
    return parts[2 * rows :] + parts[rows : 2 * rows] + parts[:rows]


def first_kernel(mix_ref, back_ref, resid_ref, base_ref):
    base_ref[...] = resid_ref[...].astype(jnp.float32) + weigh(mix_ref, back_ref)


def combine_kernel(
    info, mix_any, back_any, base_any, _, __, out_ref, square_ref, mix, back, base, sems
):
    chunks, size = back.shape[:2]
    rows = base.shape[0]
    copy = pltpu.make_async_copy
    first = started([copy(mix_any, mix, sems.at[chunks])])
    backs = started(
        [copy(back_any.at[k * size : (k + 1) * size], back.at[k], sems.at[k]) for k in range(chunks)]
    )
    late = started([copy(base_any, base, sems.at[chunks + 1])])
    waited(first)
    parts = jnp.zeros((mix.shape[0], base.shape[1]), jnp.float32)
    for k in range(chunks):
        backs[k].wait()
        parts = parts + jnp.dot(
            mix[:, k * size : (k + 1) * size], back[k], preferred_element_type=jnp.float32
        )
    waited(late)
    moe = parts[2 * rows :] + parts[rows : 2 * rows] + parts[:rows]
    out = (base[...] + moe).astype(jnp.bfloat16)
    out_ref[...] = out
    out_f = out.astype(jnp.float32)
    row = iota(out_f.shape, 0)
    total = jnp.sum(jnp.where(row < info[3], out_f * out_f, 0.0), axis=0, keepdims=True)
    square_ref[...] = jnp.broadcast_to(
        jnp.sum(total, axis=1, keepdims=True), square_ref.shape
    )


def place_kernel(info, g_own, g_oth, u_own, u_oth, d_both, _, out_ref):
    left = info[2] == 0
    for k, (own, oth) in enumerate(((g_own[...], g_oth[...]), (u_own[...], u_oth[...]))):
        out_ref[k, :, :FF] = jnp.where(left, own, oth)
        out_ref[k, :, FF:] = jnp.where(left, oth, own)
    out_ref[2, :, :FF] = d_both[0]
    out_ref[2, :, FF:] = d_both[1]


def cast_kernel(first_row, blocks, x_ref, *refs):
    out_ref, held, turned, sems_in, sems_out = refs[-5:]
    groups, size = held.shape[:2]
    fetches, stores = [], []
    for g in range(groups):
        rows = pl.ds(first_row + g * size, size)
        fetches.append(pltpu.make_async_copy(x_ref.at[rows], held.at[g], sems_in.at[g]))
        target = out_ref.at[:, g * 16 : (g + 1) * 16]
        stores.append(pltpu.make_async_copy(turned.at[g], target, sems_out.at[g]))
    for fetch in fetches:
        fetch.start()
    target = iota((size, size), 0)
    source = (target & 15) * blocks + lax.shift_right_logical(target, 4)
    order = jnp.where(iota((size, size), 1) == source, 1.0, 0.0).astype(jnp.bfloat16)
    for g in range(groups):
        fetches[g].wait()
        rows = jnp.dot(order, held[g].astype(jnp.bfloat16), preferred_element_type=jnp.float32)
        turned[g] = rows.astype(jnp.bfloat16).reshape(turned.shape[1:])
        stores[g].start()
    for store in stores:
        store.wait()


def tie_kernel(*_):
    pass


def params():
    return pltpu.CompilerParams(vmem_limit_bytes=VMEM, dimension_semantics=("arbitrary",))


def whole(shape):
    return pl.BlockSpec(shape, lambda *_: tuple(0 for _ in shape))


def paired(
    hidden_in, lengths, routes, route_weights, norm_gain, master, unembed, final_gain, target_ids
):
    rows = hidden_in.shape[1]
    width = hidden_in.shape[2]
    blk_count = lax.axis_size("blk")
    blk = lax.axis_index("blk")
    rep = lax.axis_index("rep")
    first = blk_count * FIRST
    second = blk_count * SECOND
    resid = hidden_in[0]
    info = jnp.stack([2 * blk + rep, 2 * blk + 1 - rep, rep, lengths[blk], blk])
    info = info.astype(jnp.int32)

    shard_rows = master.shape[1]
    flat = master.reshape(3 * shard_rows * blk_count, FF)

    groups = shard_rows // 16

    def turned(k, *after):
        return pl.pallas_call(
            functools.partial(cast_kernel, k * shard_rows * blk_count, blk_count),
            in_specs=[pl.BlockSpec(memory_space=pl.ANY)] * (1 + len(after)),
            out_specs=pl.BlockSpec(memory_space=pl.ANY),
            out_shape=jax.ShapeDtypeStruct((blk_count, shard_rows, FF), jnp.bfloat16),
            scratch_shapes=[
                pltpu.VMEM((groups, 16 * blk_count, FF), jnp.float32),
                pltpu.VMEM((groups, blk_count, 16, FF), jnp.bfloat16),
                pltpu.SemaphoreType.DMA((groups,)),
                pltpu.SemaphoreType.DMA((groups,)),
            ],
            compiler_params=pltpu.CompilerParams(vmem_limit_bytes=VMEM),
            name="cast",
        )(flat, *after)

    def moved(x):
        own = lax.all_to_all(x, "blk", split_axis=0, concat_axis=0, tiled=True)
        return own.reshape(width, FF)

    def swapped(x):
        return lax.ppermute(x, "rep", [(0, 1), (1, 0)])

    def tied(x, *after):
        return pl.pallas_call(
            tie_kernel,
            in_specs=[pl.BlockSpec(memory_space=pl.ANY)] * (1 + len(after)),
            out_specs=pl.BlockSpec(memory_space=pl.ANY),
            out_shape=jax.ShapeDtypeStruct(x.shape, x.dtype),
            input_output_aliases={0: 0},
            name="tie",
        )(x, *after)

    row_ext, pieces = pl.pallas_call(
        prep_kernel,
        grid_spec=pltpu.PrefetchScalarGridSpec(
            num_scalar_prefetch=2,
            grid=(1,),
            in_specs=[
                whole((rows, width)),
                whole((routes.shape[2], rows)),
                whole((routes.shape[2], rows)),
                whole((width,)),
            ],
            out_specs=[whole((rows, width + LANES)), whole((3 * rows, LANES))],
        ),
        out_shape=[
            jax.ShapeDtypeStruct((rows, width + LANES), jnp.bfloat16),
            jax.ShapeDtypeStruct((3 * rows, LANES), jnp.bfloat16),
        ],
        compiler_params=params(),
        name="prep",
    )(lengths, blk[None].astype(jnp.int32), resid, routes[0].T, route_weights[0].T, norm_gain)
    g_own = moved(turned(0, row_ext))
    g_oth = swapped(g_own)
    u_own = moved(turned(1))
    u_oth = swapped(u_own)
    d_own = moved(tied(turned(2), g_oth))

    tokens = lax.all_gather(row_ext, "blk", axis_index_groups=[list(RING)], axis=0, tiled=True)

    ring = jnp.array(RING, jnp.int32)

    def hidden_of(kernel, outs, picked, operands, specs):
        return pl.pallas_call(
            kernel,
            grid_spec=pltpu.PrefetchScalarGridSpec(
                num_scalar_prefetch=3,
                grid=(GROUPS,),
                in_specs=[pl.BlockSpec((blk_count // GROUPS * rows, width + LANES), lambda i, *_: (i, 0))]
                + [whole((width, FF))] * 2
                + specs,
                out_specs=[whole(out.shape) for out in outs],
                scratch_shapes=[
                    pltpu.VMEM((picked, width), jnp.float32),
                    pltpu.VMEM((blk_count, width + LANES), jnp.float32),
                ],
            ),
            out_shape=outs,
            compiler_params=params(),
            name="gate_up",
        )(info, lengths, ring, tokens, *operands)

    step = 512
    quarter = width // 4
    anywhere = pl.BlockSpec(memory_space=pl.ANY)

    def returned(x):
        slots = x.shape[0]
        x = x.reshape(blk_count, slots // blk_count, width)
        x = lax.all_to_all(x, "blk", split_axis=0, concat_axis=0, tiled=True)
        return x.reshape(slots, width)

    def bf16(*shape):
        return jax.ShapeDtypeStruct(shape, jnp.bfloat16)

    def f32(*shape):
        return jax.ShapeDtypeStruct(shape, jnp.float32)

    extra = LANES
    own_hidden, spot, own_share = hidden_of(
        own_kernel,
        [bf16(first + extra, FF), bf16(second, extra), f32(blk_count, LANES)],
        first + extra,
        (g_own, u_own),
        [],
    )
    d_own = tied(d_own, own_hidden)
    d_both = lax.all_gather(d_own, "rep", axis=0)
    own_out, late_out, own_part = pl.pallas_call(
        own_down_kernel,
        in_specs=[anywhere] * 3,
        out_specs=[anywhere] * 3,
        out_shape=[bf16(first, width), bf16(extra, width), f32(blk_count, width)],
        scratch_shapes=[
            pltpu.VMEM((first + extra, FF), jnp.bfloat16),
            pltpu.VMEM((blk_count, LANES), jnp.float32),
            pltpu.VMEM((4, quarter, FF), jnp.bfloat16),
            pltpu.VMEM((4, first + extra, quarter), jnp.bfloat16),
            pltpu.VMEM((4, blk_count, quarter), jnp.float32),
            pltpu.SemaphoreType.DMA((5, 4)),
        ],
        compiler_params=pltpu.CompilerParams(vmem_limit_bytes=VMEM),
        name="own_down",
    )(own_hidden, own_share, d_own)
    own_out = tied(own_out, u_oth)
    own_back = returned(own_out)
    oth_hidden, oth_share, resid_last = hidden_of(
        oth_kernel,
        [bf16(second + blk_count, FF), f32(blk_count, LANES), f32(blk_count, width)],
        second + blk_count,
        (g_oth, u_oth, own_out),
        [anywhere],
    )
    oth_out, last_part = pl.pallas_call(
        oth_down_kernel,
        grid_spec=pltpu.PrefetchScalarGridSpec(
            num_scalar_prefetch=1,
            grid=(1,),
            in_specs=[anywhere] * 6,
            out_specs=[anywhere] * 2,
            scratch_shapes=[
                pltpu.VMEM((second + blk_count, FF), jnp.bfloat16),
                pltpu.VMEM((blk_count, LANES), jnp.float32),
                pltpu.VMEM((second, extra), jnp.bfloat16),
                pltpu.VMEM((extra, width), jnp.bfloat16),
                pltpu.VMEM((blk_count, width), jnp.float32),
                pltpu.VMEM((4, quarter, FF), jnp.bfloat16),
                pltpu.VMEM((4, second, quarter), jnp.bfloat16),
                pltpu.VMEM((4, blk_count, quarter), jnp.bfloat16),
                pltpu.SemaphoreType.DMA((4, 6)),
            ],
        ),
        out_shape=[bf16(second, width), bf16(blk_count, width)],
        compiler_params=params(),
        name="oth_down",
    )(info, oth_hidden, oth_share, spot, late_out, own_part, d_both)
    last_parts = lax.all_gather(last_part, "blk", axis_index_groups=[list(RING)], axis=0)
    oth_back = returned(oth_out)

    server = pl.pallas_call(
        place_kernel,
        grid_spec=pltpu.PrefetchScalarGridSpec(
            num_scalar_prefetch=1,
            grid=(4,),
            in_specs=[pl.BlockSpec((quarter, FF), lambda i, *_: (i, 0))] * 4
            + [pl.BlockSpec((2, quarter, FF), lambda i, *_: (0, i, 0)), anywhere],
            out_specs=pl.BlockSpec((3, quarter, 2 * FF), lambda i, *_: (0, i, 0)),
        ),
        out_shape=jax.ShapeDtypeStruct((3, width, 2 * FF), jnp.bfloat16),
        compiler_params=params(),
        name="place",
    )(info, g_own, g_oth, u_own, u_oth, d_both, oth_out)

    first_mix, second_mix = pl.pallas_call(
        mix_kernel,
        grid_spec=pltpu.PrefetchScalarGridSpec(
            num_scalar_prefetch=1,
            grid=(1,),
            in_specs=[
                pl.BlockSpec((rows, LANES), lambda i, *_: (0, width // LANES)),
                whole((3 * rows, LANES)),
            ],
            out_specs=[whole((3 * rows, first)), whole((3 * rows, second))],
        ),
        out_shape=[
            jax.ShapeDtypeStruct((3 * rows, first), jnp.bfloat16),
            jax.ShapeDtypeStruct((3 * rows, second), jnp.bfloat16),
        ],
        compiler_params=params(),
        name="mix",
    )(info, row_ext, pieces)

    def weigh_specs(slots):
        return [whole((3 * rows, slots)), pl.BlockSpec((slots, step), lambda i, *_: (0, i))]

    column = pl.BlockSpec((rows, step), lambda i, *_: (0, i))
    base = pl.pallas_call(
        first_kernel,
        grid=(width // step,),
        in_specs=weigh_specs(first) + [column],
        out_specs=column,
        out_shape=f32(rows, width),
        compiler_params=params(),
        name="first",
    )(first_mix, own_back, resid)
    last_rows = lax.reduce_precision(
        resid_last + jnp.sum(last_parts.astype(jnp.float32), axis=0), 8, 7
    )
    final = (
        last_rows
        * lax.rsqrt(jnp.mean(last_rows * last_rows, axis=-1, keepdims=True) + 1e-05)
        * final_gain
    ).astype(jnp.bfloat16)
    logits = lax.dot_general(
        final, unembed, (((1,), (1,)), ((), ())), preferred_element_type=jnp.float32
    )
    vocab_base = blk * unembed.shape[0]
    target_hit = (
        target_ids[:, None] == vocab_base + jnp.arange(unembed.shape[0], dtype=jnp.int32)[None, :]
    )
    target_part = jnp.sum(jnp.where(target_hit, logits, 0.0), axis=1)
    top_part = jnp.max(logits, axis=1)

    out_rows, square = pl.pallas_call(
        combine_kernel,
        grid_spec=pltpu.PrefetchScalarGridSpec(
            num_scalar_prefetch=1,
            grid=(1,),
            in_specs=[anywhere] * 5,
            out_specs=[whole((rows, width)), whole((1, LANES))],
            scratch_shapes=[
                pltpu.VMEM((3 * rows, second), jnp.bfloat16),
                pltpu.VMEM((second // LANES, LANES, width), jnp.bfloat16),
                pltpu.VMEM((rows, width), jnp.float32),
                pltpu.SemaphoreType.DMA((second // LANES + 2,)),
            ],
        ),
        out_shape=[bf16(rows, width), f32(1, LANES)],
        compiler_params=params(),
        name="combine",
    )(info, second_mix, oth_back, base, server, top_part[None])

    def everywhere(copies):
        return lax.all_to_all(copies, "blk", split_axis=0, concat_axis=0, tiled=True)

    prompt = jnp.arange(blk_count, dtype=jnp.int32)
    square_part = jnp.where(prompt == blk, square[0, :blk_count], 0.0)
    stats = jnp.stack([top_part, target_part, square_part])
    parts = everywhere(jnp.broadcast_to(stats[None], (blk_count,) + stats.shape))
    sums = jnp.sum(parts[:, 1:], axis=0)
    norms = jnp.sqrt(sums[1] / (lengths.astype(jnp.float32) * width) + 1e-06)
    request_stats = jnp.stack([norms, jnp.max(parts[:, 0], axis=0), sums[0]])
    return (out_rows[None], server, request_stats)


def local(hidden_in, lengths, routes, route_weights, norm_gain, master, *rest):
    blk_count = lax.axis_size("blk")
    fits = (
        lax.axis_size("rep") == 2
        and master.shape[3] == FF
        and EXPERTS == 2 * blk_count
        and blk_count == len(RING)
        and hidden_in.shape[1] == LEN
        and lengths.shape[0] == blk_count
    )
    form = paired if fits else general
    return form(hidden_in, lengths, routes, route_weights, norm_gain, master, *rest)


def solution(mesh):
    return jax.shard_map(
        local,
        mesh=mesh,
        in_specs=(
            P("rep", "blk", None),
            P("rep"),
            P("rep", "blk", None),
            P("rep", "blk", None),
            P(),
            P(None, "blk", None, "rep"),
            P("blk", None),
            P(),
            P("rep"),
        ),
        out_specs=(P("rep", "blk", None), P(None, None, "blk"), P(None, "rep")),
        check_vma=False,
    )
```

```python
import functools

import jax
import jax.numpy as jnp
from jax import lax
from jax.experimental import pallas as pl
from jax.experimental.pallas import tpu as pltpu
from jax.sharding import PartitionSpec as P

FF = 512
EXPERTS = 32
LEN = 128
CAP = 36
FIRST = 32
SECOND = 40
GROUPS = 4
RING = (0, 1, 4, 5, 8, 9, 12, 13, 14, 15, 10, 11, 6, 7, 2, 3)
LANES = 128
VMEM = 63 * 1024 * 1024


def merged(x, axis, combine):
    everything = jax.tree.map(lambda part: lax.all_gather(part, axis), x)
    initial = jax.tree.map(lambda part: part[0], everything)

    def turn(k, so_far):
        return combine(so_far, jax.tree.map(lambda part: part[k], everything))

    return lax.fori_loop(1, lax.axis_size(axis), turn, initial)


def combine_stats(first, second):
    return (first[0] + second[0], jnp.maximum(first[1], second[1]))


def general(
    hidden_in, lengths, routes, route_weights, norm_gain, master, unembed, final_gain, target_ids
):
    rows_here = hidden_in.shape[1]
    width = hidden_in.shape[2]
    top_count = routes.shape[2]
    blk_count = lax.axis_size("blk")
    rep_count = lax.axis_size("rep")
    blk_index = lax.axis_index("blk")
    unit_count = master.shape[3] * rep_count
    split_ways = max(1, FF // unit_count)
    local_exp = max(1, unit_count // FF)
    group_width = min(unit_count, FF)
    capacity = CAP
    blocks = master.astype(jnp.bfloat16)
    arrived_blocks = lax.all_to_all(blocks, "blk", split_axis=2, concat_axis=1, tiled=True)
    server = lax.all_gather(arrived_blocks, "rep", axis=3, tiled=True)[:, :, 0, :]
    gate_w = server[0].reshape(width, local_exp, group_width)
    up_w = server[1].reshape(width, local_exp, group_width)
    down_w = server[2].reshape(width, local_exp, group_width)
    prompts_here = lengths.shape[0]
    slot_index = blk_index * rows_here + jnp.arange(rows_here, dtype=jnp.int32)
    prompt_of = slot_index // LEN
    position = slot_index % LEN
    prompt_match = prompt_of[:, None] == jnp.arange(prompts_here, dtype=jnp.int32)[None, :]
    row_len = jnp.sum(jnp.where(prompt_match, lengths[None, :], 0), axis=1)
    is_valid = position < row_len
    resid_f = hidden_in[0].astype(jnp.float32)
    normed = (
        resid_f * lax.rsqrt(jnp.mean(resid_f * resid_f, axis=-1, keepdims=True) + 1e-05) * norm_gain
    ).astype(jnp.bfloat16)
    expert_ids = routes[0].reshape(-1)
    pair_live = jnp.repeat(is_valid, top_count)
    pair_row = jnp.repeat(jnp.arange(rows_here, dtype=jnp.int32), top_count)
    expert_hits = (
        (expert_ids[:, None] == jnp.arange(EXPERTS, dtype=jnp.int32)[None, :]) & pair_live[:, None]
    ).astype(jnp.int32)
    slot_rank = jnp.sum((jnp.cumsum(expert_hits, axis=0) - 1) * expert_hits, axis=1)
    slot_id = jnp.where(pair_live, expert_ids * capacity + slot_rank, EXPERTS * capacity)
    source_row = jnp.zeros((EXPERTS * capacity + 1,), jnp.int32).at[slot_id].set(pair_row)[:-1]
    filled = jnp.zeros((EXPERTS * capacity + 1,), jnp.bfloat16).at[slot_id].set(1.0)[:-1]
    outgoing = (normed[source_row] * filled[:, None]).reshape(EXPERTS, capacity, width)
    sending = jnp.repeat(outgoing, split_ways, axis=0).reshape(
        blk_count, local_exp, capacity, width
    )
    arrived = lax.all_to_all(sending, "blk", split_axis=0, concat_axis=0, tiled=True)
    sources = arrived.shape[0]
    slot_count = arrived.shape[2]
    stride = sources
    while stride % 2 == 0 and stride * local_exp * slot_count > 1024:
        stride = stride // 2
    grouped = arrived.reshape(sources // stride, stride, local_exp, slot_count, width)

    def one_block(portion):
        gate_out = jnp.einsum("slnd,dlf->slnf", portion, gate_w, preferred_element_type=jnp.float32)
        up_out = jnp.einsum("slnd,dlf->slnf", portion, up_w, preferred_element_type=jnp.float32)
        hidden = (jax.nn.silu(gate_out) * up_out).astype(jnp.bfloat16)
        return jnp.einsum(
            "slnf,dlf->slnd", hidden, down_w, preferred_element_type=jnp.float32
        ).astype(jnp.bfloat16)

    returned = lax.all_to_all(
        lax.map(one_block, grouped).reshape(sources, local_exp, slot_count, width),
        "blk",
        split_axis=0,
        concat_axis=0,
        tiled=True,
    )
    summed_f = jnp.sum(
        returned.reshape(EXPERTS, split_ways, capacity, width).astype(jnp.float32), axis=1
    )
    expert_out = lax.optimization_barrier(summed_f.astype(jnp.bfloat16)).reshape(
        EXPERTS * capacity, width
    )
    gather_index = jnp.where(pair_live, expert_ids * capacity + slot_rank, 0)
    pair_weight = route_weights[0].reshape(-1) * pair_live.astype(jnp.float32)
    moe = jnp.sum(
        (expert_out[gather_index].astype(jnp.float32) * pair_weight[:, None]).reshape(
            rows_here, top_count, width
        ),
        axis=1,
    )
    out_rows = (resid_f + moe).astype(jnp.bfloat16)
    out_f = out_rows.astype(jnp.float32)
    row_squares = jnp.sum(out_f * out_f, axis=-1) * is_valid.astype(jnp.float32)
    square_local = jnp.sum(jnp.where(prompt_match, row_squares[:, None], 0.0), axis=0)
    is_last = is_valid & (position == row_len - 1)
    picker = (prompt_match & is_last[:, None]).astype(jnp.bfloat16)
    last_local = lax.dot_general(
        picker, out_rows, (((0,), (0,)), ((), ())), preferred_element_type=jnp.float32
    )
    last_rows, square_total = lax.psum((last_local, square_local), "blk")
    norms = jnp.sqrt(square_total / (lengths.astype(jnp.float32) * width) + 1e-06)
    final = (
        last_rows
        * lax.rsqrt(jnp.mean(last_rows * last_rows, axis=-1, keepdims=True) + 1e-05)
        * final_gain
    ).astype(jnp.bfloat16)
    logits = lax.dot_general(
        final, unembed, (((1,), (1,)), ((), ())), preferred_element_type=jnp.float32
    )
    vocab_base = blk_index * unembed.shape[0]
    target_hit = (
        target_ids[:, None] == vocab_base + jnp.arange(unembed.shape[0], dtype=jnp.int32)[None, :]
    )
    target_part = jnp.sum(jnp.where(target_hit, logits, 0.0), axis=1)
    top_part = jnp.max(logits, axis=1)
    target_logit, top_logit = merged((target_part, top_part), "blk", combine_stats)
    request_stats = jnp.stack([norms, top_logit, target_logit])
    return (out_rows[None], server, request_stats)


def iota(shape, dim):
    return lax.broadcasted_iota(jnp.int32, shape, dim)


def prep_kernel(lengths_ref, blk_ref, hidden_ref, routes_ref, weights_ref, gain_ref, rows_ref, pieces_ref):
    rows, width = hidden_ref.shape
    length = lengths_ref[blk_ref[0]]
    x = hidden_ref[...].astype(jnp.float32)
    scale = lax.rsqrt(jnp.mean(x * x, axis=-1, keepdims=True) + 1e-05)
    rows_ref[:, :width] = (x * scale * gain_ref[...][None]).astype(jnp.bfloat16)
    column = iota((rows, LANES), 1)
    lane = column & (EXPERTS - 1)
    row = iota((rows, LANES), 0)
    hit = jnp.zeros((rows, LANES), jnp.float32)
    weight = jnp.zeros((rows, LANES), jnp.float32)
    named_by = jnp.transpose(routes_ref[...].astype(jnp.float32)).astype(jnp.int32)
    weight_by = jnp.transpose(weights_ref[...])
    for k in range(routes_ref.shape[0]):
        named = named_by[:, k : k + 1] == lane
        hit = hit + jnp.where(named, 1.0, 0.0)
        weight = weight + jnp.where(named, weight_by[:, k : k + 1], 0.0)
    live = row < length
    hit = jnp.where(live, hit, 0.0)
    weight = jnp.where(live, weight, 0.0)
    before = jnp.where(iota((rows, rows), 1) < iota((rows, rows), 0), 1.0, 0.0)
    rank = jnp.dot(
        before.astype(jnp.bfloat16), hit.astype(jnp.bfloat16), preferred_element_type=jnp.float32
    )
    told = jnp.where(hit > 0.0, rank, -1.0)
    for k in range(3):
        piece = weight.astype(jnp.bfloat16)
        pieces_ref[k * rows : (k + 1) * rows, :] = piece
        value = piece.astype(jnp.float32)
        told = jnp.where(column >= (k + 1) * EXPERTS, value, told)
        weight = weight - value
    is_last = iota(x.shape, 0) == length - 1
    last = jnp.sum(jnp.where(is_last, x, 0.0), axis=0, keepdims=True)
    place = iota((EXPERTS, LANES), 0)
    packed = jnp.zeros((EXPERTS, LANES), jnp.float32)
    for k in range(width // LANES):
        packed = jnp.where(place == k, last[:, k * LANES : (k + 1) * LANES], packed)
    packed = jnp.concatenate([jnp.zeros((3 * EXPERTS, LANES), jnp.float32), packed], axis=0)
    told = jnp.where(column >= 3 * EXPERTS, jnp.transpose(packed), told)
    rows_ref[:, width:] = told.astype(jnp.bfloat16)


def pick(info, lengths_ref, ring_ref, which, x_ref, width, place, slots, lasts):
    step = pl.program_id(0)
    rows = x_ref.shape[0]
    sources = rows // LEN
    ranks = x_ref[:, width:].astype(jnp.float32)
    lane = iota((rows, LANES), 1)
    row = iota((rows, 1), 0)
    source = row // LEN
    rank = jnp.sum(jnp.where(lane == info[which], ranks, 0.0), axis=1, keepdims=True)
    slot = jnp.where(rank >= 0.0, place(source.astype(jnp.float32), rank), -1.0)
    slot_lane = iota((rows, slots), 1).astype(jnp.float32)
    one_hot = jnp.where(slot == slot_lane, 1.0, 0.0).astype(jnp.bfloat16)
    dims = (((0,), (0,)), ((), ()))
    chosen = lax.dot_general(
        one_hot, x_ref[:, :width], dims, preferred_element_type=jnp.float32
    )
    home = jnp.full_like(row, -1)
    for s in range(sources):
        owner = ring_ref[step * sources + s]
        home = jnp.where(row == s * LEN + lengths_ref[owner] - 1, owner, home)
    home = jnp.where(rank >= 0.0, home, -1)
    count = lasts.shape[0]
    one_hot = jnp.where(home == iota((rows, count), 1), 1.0, 0.0).astype(jnp.bfloat16)
    last = lax.dot_general(one_hot, x_ref[...], dims, preferred_element_type=jnp.float32)

    @pl.when(step == 0)
    def _():
        lasts[...] = last

    @pl.when(step != 0)
    def _():
        lasts[...] += last

    return chosen


def share_of(info, which, lasts, width):
    ext = lasts[:, width:]
    lane = iota(ext.shape, 1)
    is_own = (lane == EXPERTS + info[which]) | (lane == 2 * EXPERTS + info[which])
    return jnp.broadcast_to(
        jnp.sum(jnp.where(is_own, ext, 0.0), axis=1, keepdims=True), ext.shape
    )


def activ(x, g_ref, u_ref):
    x = x.astype(jnp.bfloat16)
    gate = jnp.dot(x, g_ref[...], preferred_element_type=jnp.float32)
    up = jnp.dot(x, u_ref[...], preferred_element_type=jnp.float32)
    return (gate / (1.0 + jnp.exp(-gate)) * up).astype(jnp.bfloat16)


def own_kernel(
    info, lengths_ref, ring_ref, x_ref, g_ref, u_ref, out_ref, spot_ref, share_ref, picked, lasts
):
    step = pl.program_id(0)
    sources = x_ref.shape[0] // LEN
    width = g_ref.shape[0]
    more = CAP - FIRST
    early = sources * FIRST
    all_early = GROUPS * early
    all_rows = all_early + GROUPS * sources * more

    def place(source, rank):
        return jnp.where(
            rank < FIRST, source * FIRST + rank, early + source * more + (rank - FIRST)
        )

    chosen = pick(
        info, lengths_ref, ring_ref, 0, x_ref, width, place, early + sources * more, lasts
    )
    for s in range(sources):
        start = pl.multiple_of(ring_ref[step * sources + s] * FIRST, FIRST)
        picked[pl.ds(start, FIRST), :] = chosen[s * FIRST : (s + 1) * FIRST]
    start = pl.multiple_of(all_early + step * sources * more, sources * more)
    picked[pl.ds(start, sources * more), :] = chosen[early:]

    @pl.when(step == GROUPS - 1)
    def _():
        count = lasts.shape[0]
        picked[all_rows : all_rows + count, :] = lasts[:, :width]
        blank = picked.shape[0] - all_rows - count
        picked[all_rows + count :, :] = jnp.zeros((blank, width), jnp.float32)
        out_ref[...] = activ(picked[...], g_ref, u_ref)
        share_ref[...] = share_of(info, 0, lasts, width)
        column = iota(spot_ref.shape, 1)
        owner = lax.shift_right_logical(column, more.bit_length() - 1)
        source = jnp.full_like(column, -1)
        for k, b in enumerate(RING):
            source = jnp.where(owner == k, b, source)
        spot = jnp.where(source >= 0, source * SECOND + (column & (more - 1)), -1)
        spot_ref[...] = jnp.where(iota(spot_ref.shape, 0) == spot, 1.0, 0.0).astype(jnp.bfloat16)


def oth_kernel(
    info,
    lengths_ref,
    ring_ref,
    x_ref,
    g_ref,
    u_ref,
    _,
    out_ref,
    share_ref,
    base_ref,
    picked,
    lasts,
):
    step = pl.program_id(0)
    sources = x_ref.shape[0] // LEN
    width = g_ref.shape[0]
    all_rows = GROUPS * sources * SECOND

    def place(source, rank):
        return source * SECOND + (SECOND - CAP) + rank

    @pl.when(step == 0)
    def _():
        base_ref[...] = jnp.zeros_like(base_ref)

    chosen = pick(info, lengths_ref, ring_ref, 1, x_ref, width, place, sources * SECOND, lasts)
    for s in range(sources):
        start = pl.multiple_of(ring_ref[step * sources + s] * SECOND, SECOND)
        picked[pl.ds(start, SECOND), :] = chosen[s * SECOND : (s + 1) * SECOND]
        ext = x_ref[s * LEN : (s + 1) * LEN, width:].astype(jnp.float32)
        packed = jnp.transpose(ext)[3 * EXPERTS :]
        mine = iota((base_ref.shape[0], LANES), 0) == ring_ref[step * sources + s]
        for k in range(width // LANES):
            lanes = slice(k * LANES, (k + 1) * LANES)
            base_ref[:, lanes] = jnp.where(mine, packed[k : k + 1], base_ref[:, lanes])

    @pl.when(step == GROUPS - 1)
    def _():
        picked[all_rows:, :] = lasts[:, :width]
        out_ref[...] = activ(picked[...], g_ref, u_ref)
        share_ref[...] = share_of(info, 1, lasts, width)


def matmul_nt(hidden_ref, d):
    return lax.dot_general(
        hidden_ref[...], d, (((1,), (1,)), ((), ())), preferred_element_type=jnp.float32
    )


def started(copies):
    for copy in copies:
        copy.start()
    return copies


def waited(copies):
    for copy in copies:
        copy.wait()


def own_down_kernel(
    hidden_any, share_any, d_any, out_any, late_any, part_any, hidden, share, d, out, part, sems
):
    chunks, size = d.shape[:2]
    rows, count = out_any.shape[0], part.shape[1]
    at = rows + count * (CAP - FIRST)
    copy = pltpu.make_async_copy
    first = started(
        [copy(hidden_any, hidden, sems.at[0, 0]), copy(share_any, share, sems.at[0, 1])]
    )
    downs = started(
        [
            copy(d_any.at[k * size : (k + 1) * size], d.at[k], sems.at[1, k])
            for k in range(chunks)
        ]
    )
    waited(first)
    stores = []
    for k in range(chunks):
        downs[k].wait()
        out[k] = matmul_nt(hidden, d[k]).astype(jnp.bfloat16)
        part[k] = share[:, :1] * out[k, at : at + count].astype(jnp.float32)
        columns = slice(k * size, (k + 1) * size)
        stores += started(
            [
                copy(out.at[k, :rows], out_any.at[:, columns], sems.at[2, k]),
                copy(out.at[k, rows:], late_any.at[:, columns], sems.at[3, k]),
                copy(part.at[k], part_any.at[:, columns], sems.at[4, k]),
            ]
        )
    waited(stores)


def oth_down_kernel(
    info,
    hidden_any,
    share_any,
    spot_any,
    late_any,
    part_any,
    d_any,
    out_any,
    sum_any,
    hidden,
    share,
    spot,
    late,
    part,
    d,
    out,
    total,
    blank,
    sems,
):
    chunks, size = d.shape[:2]
    rows = out_any.shape[0]
    copy = pltpu.make_async_copy
    other = 1 - info[2]
    sources = (hidden_any, share_any, spot_any, late_any, part_any)
    targets = (hidden, share, spot, late, part)
    downs = started(
        [
            copy(d_any.at[other, k * size : (k + 1) * size], d.at[k], sems.at[1, k])
            for k in range(chunks)
        ]
    )
    first = started([copy(x, y, sems.at[0, k]) for k, (x, y) in enumerate(zip(sources, targets))])
    waited(first)
    blank[...] = jnp.zeros_like(blank)
    stores = started([copy(blank, sum_any.at[:, chunks * size :], sems.at[2, chunks])])
    for k in range(chunks):
        downs[k].wait()
        columns = slice(k * size, (k + 1) * size)
        placed = jnp.dot(spot[...], late[:, columns], preferred_element_type=jnp.float32)
        value = matmul_nt(hidden, d[k])
        out[k] = (placed + value[:rows]).astype(jnp.bfloat16)
        last = value[rows:].astype(jnp.bfloat16).astype(jnp.float32)
        total[k] = (part[:, columns] + share[:, :1] * last).astype(jnp.bfloat16)
        stores += started(
            [
                copy(total.at[k], sum_any.at[:, columns], sems.at[3, k]),
                copy(out.at[k], out_any.at[:, columns], sems.at[2, k]),
            ]
        )
    waited(stores)


def mix_kernel(info, rank_ref, pieces_ref, first_ref, second_ref):
    rows = rank_ref.shape[0]
    late = SECOND - CAP
    own, oth = info[2], 1 - info[2]
    for mix_ref, stride, spans in (
        (first_ref, FIRST, ((own, 0, FIRST, 0),)),
        (second_ref, SECOND, ((own, 0, late, FIRST), (oth, late, CAP, 0))),
    ):
        slots = mix_ref.shape[1]
        expert = iota((LANES, slots), 0)
        lane = iota((LANES, slots), 1)
        within = jnp.zeros((1, slots), jnp.float32)
        spread = jnp.zeros((LANES, slots), jnp.float32)
        for parity, offset, count, lowest in spans:
            start = jnp.where((expert & 1) == parity, (expert >> 1) * stride + offset, slots)
            inside = (lane >= start) & (lane < start + count)
            spread = spread + jnp.where(inside, 1.0, 0.0)
            ranks = jnp.where(inside, lane - start + lowest, 0)
            within = within + jnp.sum(ranks, axis=0, keepdims=True).astype(jnp.float32)
        spread = spread.astype(jnp.bfloat16)
        rank = jnp.dot(rank_ref[...], spread, preferred_element_type=jnp.float32)
        match = rank == within
        for k in range(3):
            part = jnp.dot(
                pieces_ref[k * rows : (k + 1) * rows, :], spread, preferred_element_type=jnp.float32
            )
            mix_ref[k * rows : (k + 1) * rows, :] = jnp.where(match, part, 0.0).astype(jnp.bfloat16)


def weigh(mix_ref, back_ref):
    rows = mix_ref.shape[0] // 3
    parts = jnp.dot(mix_ref[...], back_ref[...], preferred_element_type=jnp.float32)
    return parts[2 * rows :] + parts[rows : 2 * rows] + parts[:rows]


def first_kernel(mix_ref, back_ref, resid_ref, base_ref):
    base_ref[...] = resid_ref[...].astype(jnp.float32) + weigh(mix_ref, back_ref)


def combine_kernel(
    info, mix_any, back_any, base_any, _, __, out_ref, square_ref, mix, back, base, sems
):
    chunks, size = back.shape[:2]
    rows = base.shape[0]
    copy = pltpu.make_async_copy
    first = started([copy(mix_any, mix, sems.at[chunks])])
    backs = started(
        [copy(back_any.at[k * size : (k + 1) * size], back.at[k], sems.at[k]) for k in range(chunks)]
    )
    late = started([copy(base_any, base, sems.at[chunks + 1])])
    waited(first)
    parts = jnp.zeros((mix.shape[0], base.shape[1]), jnp.float32)
    for k in range(chunks):
        backs[k].wait()
        parts = parts + jnp.dot(
            mix[:, k * size : (k + 1) * size], back[k], preferred_element_type=jnp.float32
        )
    waited(late)
    moe = parts[2 * rows :] + parts[rows : 2 * rows] + parts[:rows]
    out = (base[...] + moe).astype(jnp.bfloat16)
    out_ref[...] = out
    out_f = out.astype(jnp.float32)
    row = iota(out_f.shape, 0)
    total = jnp.sum(jnp.where(row < info[3], out_f * out_f, 0.0), axis=0, keepdims=True)
    square_ref[...] = jnp.broadcast_to(
        jnp.sum(total, axis=1, keepdims=True), square_ref.shape
    )


def place_kernel(info, g_own, g_oth, u_own, u_oth, d_both, _, out_ref):
    left = info[2] == 0
    for k, (own, oth) in enumerate(((g_own[...], g_oth[...]), (u_own[...], u_oth[...]))):
        out_ref[k, :, :FF] = jnp.where(left, own, oth)
        out_ref[k, :, FF:] = jnp.where(left, oth, own)
    out_ref[2, :, :FF] = d_both[0]
    out_ref[2, :, FF:] = d_both[1]


def cast_kernel(first_row, blocks, x_ref, *refs):
    out_ref, held, turned, sems_in, sems_out = refs[-5:]
    groups, size = held.shape[:2]
    fetches, stores = [], []
    for g in range(groups):
        rows = pl.ds(first_row + g * size, size)
        fetches.append(pltpu.make_async_copy(x_ref.at[rows], held.at[g], sems_in.at[g]))
        target = out_ref.at[:, g * 16 : (g + 1) * 16]
        stores.append(pltpu.make_async_copy(turned.at[g], target, sems_out.at[g]))
    for fetch in fetches:
        fetch.start()
    target = iota((size, size), 0)
    source = (target & 15) * blocks + lax.shift_right_logical(target, 4)
    order = jnp.where(iota((size, size), 1) == source, 1.0, 0.0).astype(jnp.bfloat16)
    for g in range(groups):
        fetches[g].wait()
        rows = jnp.dot(order, held[g].astype(jnp.bfloat16), preferred_element_type=jnp.float32)
        turned[g] = rows.astype(jnp.bfloat16).reshape(turned.shape[1:])
        stores[g].start()
    for store in stores:
        store.wait()


def tie_kernel(*_):
    pass


def params():
    return pltpu.CompilerParams(vmem_limit_bytes=VMEM, dimension_semantics=("arbitrary",))


def whole(shape):
    return pl.BlockSpec(shape, lambda *_: tuple(0 for _ in shape))


def paired(
    hidden_in, lengths, routes, route_weights, norm_gain, master, unembed, final_gain, target_ids
):
    rows = hidden_in.shape[1]
    width = hidden_in.shape[2]
    blk_count = lax.axis_size("blk")
    blk = lax.axis_index("blk")
    rep = lax.axis_index("rep")
    first = blk_count * FIRST
    second = blk_count * SECOND
    resid = hidden_in[0]
    info = jnp.stack([2 * blk + rep, 2 * blk + 1 - rep, rep, lengths[blk], blk])
    info = info.astype(jnp.int32)

    shard_rows = master.shape[1]
    flat = master.reshape(3 * shard_rows * blk_count, FF)

    groups = shard_rows // 16

    def turned(k, *after):
        return pl.pallas_call(
            functools.partial(cast_kernel, k * shard_rows * blk_count, blk_count),
            in_specs=[pl.BlockSpec(memory_space=pl.ANY)] * (1 + len(after)),
            out_specs=pl.BlockSpec(memory_space=pl.ANY),
            out_shape=jax.ShapeDtypeStruct((blk_count, shard_rows, FF), jnp.bfloat16),
            scratch_shapes=[
                pltpu.VMEM((groups, 16 * blk_count, FF), jnp.float32),
                pltpu.VMEM((groups, blk_count, 16, FF), jnp.bfloat16),
                pltpu.SemaphoreType.DMA((groups,)),
                pltpu.SemaphoreType.DMA((groups,)),
            ],
            compiler_params=pltpu.CompilerParams(vmem_limit_bytes=VMEM),
            name="cast",
        )(flat, *after)

    def moved(x):
        own = lax.all_to_all(x, "blk", split_axis=0, concat_axis=0, tiled=True)
        return own.reshape(width, FF)

    def swapped(x):
        return lax.ppermute(x, "rep", [(0, 1), (1, 0)])

    def tied(x, *after):
        return pl.pallas_call(
            tie_kernel,
            in_specs=[pl.BlockSpec(memory_space=pl.ANY)] * (1 + len(after)),
            out_specs=pl.BlockSpec(memory_space=pl.ANY),
            out_shape=jax.ShapeDtypeStruct(x.shape, x.dtype),
            input_output_aliases={0: 0},
            name="tie",
        )(x, *after)

    row_ext, pieces = pl.pallas_call(
        prep_kernel,
        grid_spec=pltpu.PrefetchScalarGridSpec(
            num_scalar_prefetch=2,
            grid=(1,),
            in_specs=[
                whole((rows, width)),
                whole((routes.shape[2], rows)),
                whole((routes.shape[2], rows)),
                whole((width,)),
            ],
            out_specs=[whole((rows, width + LANES)), whole((3 * rows, LANES))],
        ),
        out_shape=[
            jax.ShapeDtypeStruct((rows, width + LANES), jnp.bfloat16),
            jax.ShapeDtypeStruct((3 * rows, LANES), jnp.bfloat16),
        ],
        compiler_params=params(),
        name="prep",
    )(lengths, blk[None].astype(jnp.int32), resid, routes[0].T, route_weights[0].T, norm_gain)
    g_own = moved(turned(0, row_ext))
    g_oth = swapped(g_own)
    u_own = moved(turned(1))
    u_oth = swapped(u_own)
    d_own = moved(tied(turned(2), g_oth))

    tokens = lax.all_gather(row_ext, "blk", axis_index_groups=[list(RING)], axis=0, tiled=True)

    ring = jnp.array(RING, jnp.int32)

    def hidden_of(kernel, outs, picked, operands, specs):
        return pl.pallas_call(
            kernel,
            grid_spec=pltpu.PrefetchScalarGridSpec(
                num_scalar_prefetch=3,
                grid=(GROUPS,),
                in_specs=[pl.BlockSpec((blk_count // GROUPS * rows, width + LANES), lambda i, *_: (i, 0))]
                + [whole((width, FF))] * 2
                + specs,
                out_specs=[whole(out.shape) for out in outs],
                scratch_shapes=[
                    pltpu.VMEM((picked, width), jnp.float32),
                    pltpu.VMEM((blk_count, width + LANES), jnp.float32),
                ],
            ),
            out_shape=outs,
            compiler_params=params(),
            name="gate_up",
        )(info, lengths, ring, tokens, *operands)

    step = 512
    quarter = width // 4
    anywhere = pl.BlockSpec(memory_space=pl.ANY)

    def returned(x):
        slots = x.shape[0]
        x = x.reshape(blk_count, slots // blk_count, width)
        x = lax.all_to_all(x, "blk", split_axis=0, concat_axis=0, tiled=True)
        return x.reshape(slots, width)

    def bf16(*shape):
        return jax.ShapeDtypeStruct(shape, jnp.bfloat16)

    def f32(*shape):
        return jax.ShapeDtypeStruct(shape, jnp.float32)

    extra = LANES
    own_hidden, spot, own_share = hidden_of(
        own_kernel,
        [bf16(first + extra, FF), bf16(second, extra), f32(blk_count, LANES)],
        first + extra,
        (g_own, u_own),
        [],
    )
    d_own = tied(d_own, own_hidden)
    d_both = lax.all_gather(d_own, "rep", axis=0)
    own_out, late_out, own_part = pl.pallas_call(
        own_down_kernel,
        in_specs=[anywhere] * 3,
        out_specs=[anywhere] * 3,
        out_shape=[bf16(first, width), bf16(extra, width), f32(blk_count, width)],
        scratch_shapes=[
            pltpu.VMEM((first + extra, FF), jnp.bfloat16),
            pltpu.VMEM((blk_count, LANES), jnp.float32),
            pltpu.VMEM((4, quarter, FF), jnp.bfloat16),
            pltpu.VMEM((4, first + extra, quarter), jnp.bfloat16),
            pltpu.VMEM((4, blk_count, quarter), jnp.float32),
            pltpu.SemaphoreType.DMA((5, 4)),
        ],
        compiler_params=pltpu.CompilerParams(vmem_limit_bytes=VMEM),
        name="own_down",
    )(own_hidden, own_share, d_own)
    own_out = tied(own_out, u_oth)
    own_back = returned(own_out)
    oth_hidden, oth_share, resid_last = hidden_of(
        oth_kernel,
        [bf16(second + blk_count, FF), f32(blk_count, LANES), f32(blk_count, width)],
        second + blk_count,
        (g_oth, u_oth, own_out),
        [anywhere],
    )
    oth_out, last_part = pl.pallas_call(
        oth_down_kernel,
        grid_spec=pltpu.PrefetchScalarGridSpec(
            num_scalar_prefetch=1,
            grid=(1,),
            in_specs=[anywhere] * 6,
            out_specs=[anywhere] * 2,
            scratch_shapes=[
                pltpu.VMEM((second + blk_count, FF), jnp.bfloat16),
                pltpu.VMEM((blk_count, LANES), jnp.float32),
                pltpu.VMEM((second, extra), jnp.bfloat16),
                pltpu.VMEM((extra, width), jnp.bfloat16),
                pltpu.VMEM((blk_count, width), jnp.float32),
                pltpu.VMEM((4, quarter, FF), jnp.bfloat16),
                pltpu.VMEM((4, second, quarter), jnp.bfloat16),
                pltpu.VMEM((4, blk_count, quarter), jnp.bfloat16),
                pltpu.VMEM((blk_count, width // 2), jnp.bfloat16),
                pltpu.SemaphoreType.DMA((4, 6)),
            ],
        ),
        out_shape=[bf16(second, width), bf16(blk_count, width + width // 2)],
        compiler_params=params(),
        name="oth_down",
    )(info, oth_hidden, oth_share, spot, late_out, own_part, d_both)
    last_parts = lax.all_gather(last_part, "blk", axis_index_groups=[list(RING)], axis=0)
    oth_back = returned(oth_out)

    server = pl.pallas_call(
        place_kernel,
        grid_spec=pltpu.PrefetchScalarGridSpec(
            num_scalar_prefetch=1,
            grid=(4,),
            in_specs=[pl.BlockSpec((quarter, FF), lambda i, *_: (i, 0))] * 4
            + [pl.BlockSpec((2, quarter, FF), lambda i, *_: (0, i, 0)), anywhere],
            out_specs=pl.BlockSpec((3, quarter, 2 * FF), lambda i, *_: (0, i, 0)),
        ),
        out_shape=jax.ShapeDtypeStruct((3, width, 2 * FF), jnp.bfloat16),
        compiler_params=params(),
        name="place",
    )(info, g_own, g_oth, u_own, u_oth, d_both, oth_out)

    first_mix, second_mix = pl.pallas_call(
        mix_kernel,
        grid_spec=pltpu.PrefetchScalarGridSpec(
            num_scalar_prefetch=1,
            grid=(1,),
            in_specs=[
                pl.BlockSpec((rows, LANES), lambda i, *_: (0, width // LANES)),
                whole((3 * rows, LANES)),
            ],
            out_specs=[whole((3 * rows, first)), whole((3 * rows, second))],
        ),
        out_shape=[
            jax.ShapeDtypeStruct((3 * rows, first), jnp.bfloat16),
            jax.ShapeDtypeStruct((3 * rows, second), jnp.bfloat16),
        ],
        compiler_params=params(),
        name="mix",
    )(info, row_ext, pieces)

    def weigh_specs(slots):
        return [whole((3 * rows, slots)), pl.BlockSpec((slots, step), lambda i, *_: (0, i))]

    column = pl.BlockSpec((rows, step), lambda i, *_: (0, i))
    base = pl.pallas_call(
        first_kernel,
        grid=(width // step,),
        in_specs=weigh_specs(first) + [column],
        out_specs=column,
        out_shape=f32(rows, width),
        compiler_params=params(),
        name="first",
    )(first_mix, own_back, resid)
    last_rows = lax.reduce_precision(
        resid_last + jnp.sum(last_parts[:, :, :width].astype(jnp.float32), axis=0), 8, 7
    )
    final = (
        last_rows
        * lax.rsqrt(jnp.mean(last_rows * last_rows, axis=-1, keepdims=True) + 1e-05)
        * final_gain
    ).astype(jnp.bfloat16)
    logits = lax.dot_general(
        final, unembed, (((1,), (1,)), ((), ())), preferred_element_type=jnp.float32
    )
    vocab_base = blk * unembed.shape[0]
    target_hit = (
        target_ids[:, None] == vocab_base + jnp.arange(unembed.shape[0], dtype=jnp.int32)[None, :]
    )
    target_part = jnp.sum(jnp.where(target_hit, logits, 0.0), axis=1)
    top_part = jnp.max(logits, axis=1)

    out_rows, square = pl.pallas_call(
        combine_kernel,
        grid_spec=pltpu.PrefetchScalarGridSpec(
            num_scalar_prefetch=1,
            grid=(1,),
            in_specs=[anywhere] * 5,
            out_specs=[whole((rows, width)), whole((1, LANES))],
            scratch_shapes=[
                pltpu.VMEM((3 * rows, second), jnp.bfloat16),
                pltpu.VMEM((second // LANES, LANES, width), jnp.bfloat16),
                pltpu.VMEM((rows, width), jnp.float32),
                pltpu.SemaphoreType.DMA((second // LANES + 2,)),
            ],
        ),
        out_shape=[bf16(rows, width), f32(1, LANES)],
        compiler_params=params(),
        name="combine",
    )(info, second_mix, oth_back, base, server, top_part[None])

    def everywhere(copies):
        return lax.all_to_all(copies, "blk", split_axis=0, concat_axis=0, tiled=True)

    prompt = jnp.arange(blk_count, dtype=jnp.int32)
    square_part = jnp.where(prompt == blk, square[0, :blk_count], 0.0)
    stats = jnp.stack([top_part, target_part, square_part])
    parts = everywhere(jnp.broadcast_to(stats[None], (blk_count,) + stats.shape))
    sums = jnp.sum(parts[:, 1:], axis=0)
    norms = jnp.sqrt(sums[1] / (lengths.astype(jnp.float32) * width) + 1e-06)
    request_stats = jnp.stack([norms, jnp.max(parts[:, 0], axis=0), sums[0]])
    return (out_rows[None], server, request_stats)


def local(hidden_in, lengths, routes, route_weights, norm_gain, master, *rest):
    blk_count = lax.axis_size("blk")
    fits = (
        lax.axis_size("rep") == 2
        and master.shape[3] == FF
        and EXPERTS == 2 * blk_count
        and blk_count == len(RING)
        and hidden_in.shape[1] == LEN
        and lengths.shape[0] == blk_count
    )
    form = paired if fits else general
    return form(hidden_in, lengths, routes, route_weights, norm_gain, master, *rest)


def solution(mesh):
    return jax.shard_map(
        local,
        mesh=mesh,
        in_specs=(
            P("rep", "blk", None),
            P("rep"),
            P("rep", "blk", None),
            P("rep", "blk", None),
            P(),
            P(None, "blk", None, "rep"),
            P("blk", None),
            P(),
            P("rep"),
        ),
        out_specs=(P("rep", "blk", None), P(None, None, "blk"), P(None, "rep")),
        check_vma=False,
    )
```

```python
import functools

import jax
import jax.numpy as jnp
from jax import lax
from jax.experimental import pallas as pl
from jax.experimental.pallas import tpu as pltpu
from jax.sharding import PartitionSpec as P

FF = 512
EXPERTS = 32
LEN = 128
CAP = 36
FIRST = 32
SECOND = 40
GROUPS = 4
RING = (0, 1, 4, 5, 8, 9, 12, 13, 14, 15, 10, 11, 6, 7, 2, 3)
LANES = 128
VMEM = 63 * 1024 * 1024


def merged(x, axis, combine):
    everything = jax.tree.map(lambda part: lax.all_gather(part, axis), x)
    initial = jax.tree.map(lambda part: part[0], everything)

    def turn(k, so_far):
        return combine(so_far, jax.tree.map(lambda part: part[k], everything))

    return lax.fori_loop(1, lax.axis_size(axis), turn, initial)


def combine_stats(first, second):
    return (first[0] + second[0], jnp.maximum(first[1], second[1]))


def general(
    hidden_in, lengths, routes, route_weights, norm_gain, master, unembed, final_gain, target_ids
):
    rows_here = hidden_in.shape[1]
    width = hidden_in.shape[2]
    top_count = routes.shape[2]
    blk_count = lax.axis_size("blk")
    rep_count = lax.axis_size("rep")
    blk_index = lax.axis_index("blk")
    unit_count = master.shape[3] * rep_count
    split_ways = max(1, FF // unit_count)
    local_exp = max(1, unit_count // FF)
    group_width = min(unit_count, FF)
    capacity = CAP
    blocks = master.astype(jnp.bfloat16)
    arrived_blocks = lax.all_to_all(blocks, "blk", split_axis=2, concat_axis=1, tiled=True)
    server = lax.all_gather(arrived_blocks, "rep", axis=3, tiled=True)[:, :, 0, :]
    gate_w = server[0].reshape(width, local_exp, group_width)
    up_w = server[1].reshape(width, local_exp, group_width)
    down_w = server[2].reshape(width, local_exp, group_width)
    prompts_here = lengths.shape[0]
    slot_index = blk_index * rows_here + jnp.arange(rows_here, dtype=jnp.int32)
    prompt_of = slot_index // LEN
    position = slot_index % LEN
    prompt_match = prompt_of[:, None] == jnp.arange(prompts_here, dtype=jnp.int32)[None, :]
    row_len = jnp.sum(jnp.where(prompt_match, lengths[None, :], 0), axis=1)
    is_valid = position < row_len
    resid_f = hidden_in[0].astype(jnp.float32)
    normed = (
        resid_f * lax.rsqrt(jnp.mean(resid_f * resid_f, axis=-1, keepdims=True) + 1e-05) * norm_gain
    ).astype(jnp.bfloat16)
    expert_ids = routes[0].reshape(-1)
    pair_live = jnp.repeat(is_valid, top_count)
    pair_row = jnp.repeat(jnp.arange(rows_here, dtype=jnp.int32), top_count)
    expert_hits = (
        (expert_ids[:, None] == jnp.arange(EXPERTS, dtype=jnp.int32)[None, :]) & pair_live[:, None]
    ).astype(jnp.int32)
    slot_rank = jnp.sum((jnp.cumsum(expert_hits, axis=0) - 1) * expert_hits, axis=1)
    slot_id = jnp.where(pair_live, expert_ids * capacity + slot_rank, EXPERTS * capacity)
    source_row = jnp.zeros((EXPERTS * capacity + 1,), jnp.int32).at[slot_id].set(pair_row)[:-1]
    filled = jnp.zeros((EXPERTS * capacity + 1,), jnp.bfloat16).at[slot_id].set(1.0)[:-1]
    outgoing = (normed[source_row] * filled[:, None]).reshape(EXPERTS, capacity, width)
    sending = jnp.repeat(outgoing, split_ways, axis=0).reshape(
        blk_count, local_exp, capacity, width
    )
    arrived = lax.all_to_all(sending, "blk", split_axis=0, concat_axis=0, tiled=True)
    sources = arrived.shape[0]
    slot_count = arrived.shape[2]
    stride = sources
    while stride % 2 == 0 and stride * local_exp * slot_count > 1024:
        stride = stride // 2
    grouped = arrived.reshape(sources // stride, stride, local_exp, slot_count, width)

    def one_block(portion):
        gate_out = jnp.einsum("slnd,dlf->slnf", portion, gate_w, preferred_element_type=jnp.float32)
        up_out = jnp.einsum("slnd,dlf->slnf", portion, up_w, preferred_element_type=jnp.float32)
        hidden = (jax.nn.silu(gate_out) * up_out).astype(jnp.bfloat16)
        return jnp.einsum(
            "slnf,dlf->slnd", hidden, down_w, preferred_element_type=jnp.float32
        ).astype(jnp.bfloat16)

    returned = lax.all_to_all(
        lax.map(one_block, grouped).reshape(sources, local_exp, slot_count, width),
        "blk",
        split_axis=0,
        concat_axis=0,
        tiled=True,
    )
    summed_f = jnp.sum(
        returned.reshape(EXPERTS, split_ways, capacity, width).astype(jnp.float32), axis=1
    )
    expert_out = lax.optimization_barrier(summed_f.astype(jnp.bfloat16)).reshape(
        EXPERTS * capacity, width
    )
    gather_index = jnp.where(pair_live, expert_ids * capacity + slot_rank, 0)
    pair_weight = route_weights[0].reshape(-1) * pair_live.astype(jnp.float32)
    moe = jnp.sum(
        (expert_out[gather_index].astype(jnp.float32) * pair_weight[:, None]).reshape(
            rows_here, top_count, width
        ),
        axis=1,
    )
    out_rows = (resid_f + moe).astype(jnp.bfloat16)
    out_f = out_rows.astype(jnp.float32)
    row_squares = jnp.sum(out_f * out_f, axis=-1) * is_valid.astype(jnp.float32)
    square_local = jnp.sum(jnp.where(prompt_match, row_squares[:, None], 0.0), axis=0)
    is_last = is_valid & (position == row_len - 1)
    picker = (prompt_match & is_last[:, None]).astype(jnp.bfloat16)
    last_local = lax.dot_general(
        picker, out_rows, (((0,), (0,)), ((), ())), preferred_element_type=jnp.float32
    )
    last_rows, square_total = lax.psum((last_local, square_local), "blk")
    norms = jnp.sqrt(square_total / (lengths.astype(jnp.float32) * width) + 1e-06)
    final = (
        last_rows
        * lax.rsqrt(jnp.mean(last_rows * last_rows, axis=-1, keepdims=True) + 1e-05)
        * final_gain
    ).astype(jnp.bfloat16)
    logits = lax.dot_general(
        final, unembed, (((1,), (1,)), ((), ())), preferred_element_type=jnp.float32
    )
    vocab_base = blk_index * unembed.shape[0]
    target_hit = (
        target_ids[:, None] == vocab_base + jnp.arange(unembed.shape[0], dtype=jnp.int32)[None, :]
    )
    target_part = jnp.sum(jnp.where(target_hit, logits, 0.0), axis=1)
    top_part = jnp.max(logits, axis=1)
    target_logit, top_logit = merged((target_part, top_part), "blk", combine_stats)
    request_stats = jnp.stack([norms, top_logit, target_logit])
    return (out_rows[None], server, request_stats)


def iota(shape, dim):
    return lax.broadcasted_iota(jnp.int32, shape, dim)


def prep_kernel(lengths_ref, blk_ref, hidden_ref, routes_ref, weights_ref, gain_ref, rows_ref, pieces_ref):
    rows, width = hidden_ref.shape
    length = lengths_ref[blk_ref[0]]
    x = hidden_ref[...].astype(jnp.float32)
    scale = lax.rsqrt(jnp.mean(x * x, axis=-1, keepdims=True) + 1e-05)
    rows_ref[:, :width] = (x * scale * gain_ref[...][None]).astype(jnp.bfloat16)
    column = iota((rows, LANES), 1)
    lane = column & (EXPERTS - 1)
    row = iota((rows, LANES), 0)
    hit = jnp.zeros((rows, LANES), jnp.float32)
    weight = jnp.zeros((rows, LANES), jnp.float32)
    named_by = jnp.transpose(routes_ref[...].astype(jnp.float32)).astype(jnp.int32)
    weight_by = jnp.transpose(weights_ref[...])
    for k in range(routes_ref.shape[0]):
        named = named_by[:, k : k + 1] == lane
        hit = hit + jnp.where(named, 1.0, 0.0)
        weight = weight + jnp.where(named, weight_by[:, k : k + 1], 0.0)
    live = row < length
    hit = jnp.where(live, hit, 0.0)
    weight = jnp.where(live, weight, 0.0)
    before = jnp.where(iota((rows, rows), 1) < iota((rows, rows), 0), 1.0, 0.0)
    rank = jnp.dot(
        before.astype(jnp.bfloat16), hit.astype(jnp.bfloat16), preferred_element_type=jnp.float32
    )
    told = jnp.where(hit > 0.0, rank, -1.0)
    for k in range(3):
        piece = weight.astype(jnp.bfloat16)
        pieces_ref[k * rows : (k + 1) * rows, :] = piece
        value = piece.astype(jnp.float32)
        told = jnp.where(column >= (k + 1) * EXPERTS, value, told)
        weight = weight - value
    rows_ref[:, width:] = told.astype(jnp.bfloat16)


def pick(info, lengths_ref, ring_ref, which, x_ref, width, place, slots, lasts):
    step = pl.program_id(0)
    rows = x_ref.shape[0]
    sources = rows // LEN
    ranks = x_ref[:, width:].astype(jnp.float32)
    lane = iota((rows, LANES), 1)
    row = iota((rows, 1), 0)
    source = row // LEN
    rank = jnp.sum(jnp.where(lane == info[which], ranks, 0.0), axis=1, keepdims=True)
    slot = jnp.where(rank >= 0.0, place(source.astype(jnp.float32), rank), -1.0)
    slot_lane = iota((rows, slots), 1).astype(jnp.float32)
    one_hot = jnp.where(slot == slot_lane, 1.0, 0.0).astype(jnp.bfloat16)
    dims = (((0,), (0,)), ((), ()))
    chosen = lax.dot_general(
        one_hot, x_ref[:, :width], dims, preferred_element_type=jnp.float32
    )
    home = jnp.full_like(row, -1)
    for s in range(sources):
        owner = ring_ref[step * sources + s]
        home = jnp.where(row == s * LEN + lengths_ref[owner] - 1, owner, home)
    home = jnp.where(rank >= 0.0, home, -1)
    count = lasts.shape[0]
    one_hot = jnp.where(home == iota((rows, count), 1), 1.0, 0.0).astype(jnp.bfloat16)
    last = lax.dot_general(one_hot, x_ref[...], dims, preferred_element_type=jnp.float32)

    @pl.when(step == 0)
    def _():
        lasts[...] = last

    @pl.when(step != 0)
    def _():
        lasts[...] += last

    return chosen


def share_of(info, which, lasts, width):
    ext = lasts[:, width:]
    lane = iota(ext.shape, 1)
    is_own = (lane >= EXPERTS) & ((lane & (EXPERTS - 1)) == info[which])
    return jnp.broadcast_to(
        jnp.sum(jnp.where(is_own, ext, 0.0), axis=1, keepdims=True), ext.shape
    )


def activ(x, g_ref, u_ref):
    x = x.astype(jnp.bfloat16)
    gate = jnp.dot(x, g_ref[...], preferred_element_type=jnp.float32)
    up = jnp.dot(x, u_ref[...], preferred_element_type=jnp.float32)
    return (gate / (1.0 + jnp.exp(-gate)) * up).astype(jnp.bfloat16)


def own_kernel(
    info, lengths_ref, ring_ref, x_ref, g_ref, u_ref, out_ref, spot_ref, share_ref, picked, lasts
):
    step = pl.program_id(0)
    sources = x_ref.shape[0] // LEN
    width = g_ref.shape[0]
    more = CAP - FIRST
    early = sources * FIRST
    all_early = GROUPS * early
    all_rows = all_early + GROUPS * sources * more

    def place(source, rank):
        return jnp.where(
            rank < FIRST, source * FIRST + rank, early + source * more + (rank - FIRST)
        )

    chosen = pick(
        info, lengths_ref, ring_ref, 0, x_ref, width, place, early + sources * more, lasts
    )
    for s in range(sources):
        start = pl.multiple_of(ring_ref[step * sources + s] * FIRST, FIRST)
        picked[pl.ds(start, FIRST), :] = chosen[s * FIRST : (s + 1) * FIRST]
    start = pl.multiple_of(all_early + step * sources * more, sources * more)
    picked[pl.ds(start, sources * more), :] = chosen[early:]

    @pl.when(step == GROUPS - 1)
    def _():
        count = lasts.shape[0]
        picked[all_rows : all_rows + count, :] = lasts[:, :width]
        blank = picked.shape[0] - all_rows - count
        picked[all_rows + count :, :] = jnp.zeros((blank, width), jnp.float32)
        out_ref[...] = activ(picked[...], g_ref, u_ref)
        share_ref[...] = share_of(info, 0, lasts, width)
        column = iota(spot_ref.shape, 1)
        owner = lax.shift_right_logical(column, more.bit_length() - 1)
        source = jnp.full_like(column, -1)
        for k, b in enumerate(RING):
            source = jnp.where(owner == k, b, source)
        spot = jnp.where(source >= 0, source * SECOND + (column & (more - 1)), -1)
        spot_ref[...] = jnp.where(iota(spot_ref.shape, 0) == spot, 1.0, 0.0).astype(jnp.bfloat16)


def oth_kernel(
    info,
    lengths_ref,
    ring_ref,
    x_ref,
    g_ref,
    u_ref,
    resid_ref,
    _,
    out_ref,
    share_ref,
    base_ref,
    picked,
    lasts,
):
    step = pl.program_id(0)
    sources = x_ref.shape[0] // LEN
    width = g_ref.shape[0]
    all_rows = GROUPS * sources * SECOND

    def place(source, rank):
        return source * SECOND + (SECOND - CAP) + rank

    chosen = pick(info, lengths_ref, ring_ref, 1, x_ref, width, place, sources * SECOND, lasts)
    for s in range(sources):
        start = pl.multiple_of(ring_ref[step * sources + s] * SECOND, SECOND)
        picked[pl.ds(start, SECOND), :] = chosen[s * SECOND : (s + 1) * SECOND]

    @pl.when(step == GROUPS - 1)
    def _():
        picked[all_rows:, :] = lasts[:, :width]
        out_ref[...] = activ(picked[...], g_ref, u_ref)
        share_ref[...] = share_of(info, 1, lasts, width)
        resid = resid_ref[...].astype(jnp.float32)
        is_last = iota(resid.shape, 0) == info[3] - 1
        last = jnp.sum(jnp.where(is_last, resid, 0.0), axis=0, keepdims=True)
        base_ref[...] = jnp.where(iota(base_ref.shape, 0) == info[4], last, 0.0)


def matmul_nt(hidden_ref, d):
    return lax.dot_general(
        hidden_ref[...], d, (((1,), (1,)), ((), ())), preferred_element_type=jnp.float32
    )


def started(copies):
    for copy in copies:
        copy.start()
    return copies


def waited(copies):
    for copy in copies:
        copy.wait()


def own_down_kernel(
    hidden_any, share_any, d_any, out_any, late_any, part_any, hidden, share, d, out, part, sems
):
    chunks, size = d.shape[:2]
    rows, count = out_any.shape[0], part.shape[1]
    at = rows + count * (CAP - FIRST)
    copy = pltpu.make_async_copy
    first = started(
        [copy(hidden_any, hidden, sems.at[0, 0]), copy(share_any, share, sems.at[0, 1])]
    )
    downs = started(
        [
            copy(d_any.at[k * size : (k + 1) * size], d.at[k], sems.at[1, k])
            for k in range(chunks)
        ]
    )
    waited(first)
    stores = []
    for k in range(chunks):
        downs[k].wait()
        out[k] = matmul_nt(hidden, d[k]).astype(jnp.bfloat16)
        part[k] = share[:, :1] * out[k, at : at + count].astype(jnp.float32)
        columns = slice(k * size, (k + 1) * size)
        stores += started(
            [
                copy(out.at[k, :rows], out_any.at[:, columns], sems.at[2, k]),
                copy(out.at[k, rows:], late_any.at[:, columns], sems.at[3, k]),
                copy(part.at[k], part_any.at[:, columns], sems.at[4, k]),
            ]
        )
    waited(stores)


def oth_down_kernel(
    _,
    hidden_any,
    share_any,
    spot_any,
    late_any,
    base_any,
    part_any,
    d_any,
    out_any,
    sum_any,
    hidden,
    share,
    spot,
    late,
    base,
    part,
    d,
    out,
    total,
    sems,
):
    chunks, size = d.shape[:2]
    rows = out_any.shape[0]
    copy = pltpu.make_async_copy
    sources = (hidden_any, share_any, spot_any, late_any, base_any, part_any)
    targets = (hidden, share, spot, late, base, part)
    downs = started(
        [
            copy(d_any.at[k * size : (k + 1) * size], d.at[k], sems.at[1, k])
            for k in range(chunks)
        ]
    )
    first = started([copy(x, y, sems.at[0, k]) for k, (x, y) in enumerate(zip(sources, targets))])
    waited(first)
    stores = []
    for k in range(chunks):
        downs[k].wait()
        columns = slice(k * size, (k + 1) * size)
        placed = jnp.dot(spot[...], late[:, columns], preferred_element_type=jnp.float32)
        value = matmul_nt(hidden, d[k])
        out[k] = (placed + value[:rows]).astype(jnp.bfloat16)
        last = value[rows:].astype(jnp.bfloat16).astype(jnp.float32)
        total[k] = base[:, columns] + part[:, columns] + share[:, :1] * last
        stores += started(
            [
                copy(total.at[k], sum_any.at[:, columns], sems.at[3, k]),
                copy(out.at[k], out_any.at[:, columns], sems.at[2, k]),
            ]
        )
    waited(stores)


def mix_kernel(info, rank_ref, pieces_ref, first_ref, second_ref):
    rows = rank_ref.shape[0]
    late = SECOND - CAP
    own, oth = info[2], 1 - info[2]
    for mix_ref, stride, spans in (
        (first_ref, FIRST, ((own, 0, FIRST, 0),)),
        (second_ref, SECOND, ((own, 0, late, FIRST), (oth, late, CAP, 0))),
    ):
        slots = mix_ref.shape[1]
        expert = iota((LANES, slots), 0)
        lane = iota((LANES, slots), 1)
        within = jnp.zeros((1, slots), jnp.float32)
        spread = jnp.zeros((LANES, slots), jnp.float32)
        for parity, offset, count, lowest in spans:
            start = jnp.where((expert & 1) == parity, (expert >> 1) * stride + offset, slots)
            inside = (lane >= start) & (lane < start + count)
            spread = spread + jnp.where(inside, 1.0, 0.0)
            ranks = jnp.where(inside, lane - start + lowest, 0)
            within = within + jnp.sum(ranks, axis=0, keepdims=True).astype(jnp.float32)
        spread = spread.astype(jnp.bfloat16)
        rank = jnp.dot(rank_ref[...], spread, preferred_element_type=jnp.float32)
        match = rank == within
        for k in range(3):
            part = jnp.dot(
                pieces_ref[k * rows : (k + 1) * rows, :], spread, preferred_element_type=jnp.float32
            )
            mix_ref[k * rows : (k + 1) * rows, :] = jnp.where(match, part, 0.0).astype(jnp.bfloat16)


def weigh(mix_ref, back_ref):
    rows = mix_ref.shape[0] // 3
    parts = jnp.dot(mix_ref[...], back_ref[...], preferred_element_type=jnp.float32)
    return parts[2 * rows :] + parts[rows : 2 * rows] + parts[:rows]


def first_kernel(mix_ref, back_ref, resid_ref, base_ref):
    base_ref[...] = resid_ref[...].astype(jnp.float32) + weigh(mix_ref, back_ref)


def combine_kernel(
    info, mix_any, back_any, base_any, _, __, out_ref, square_ref, mix, back, base, sems
):
    chunks, size = back.shape[:2]
    rows = base.shape[0]
    copy = pltpu.make_async_copy
    first = started([copy(mix_any, mix, sems.at[chunks])])
    backs = started(
        [copy(back_any.at[k * size : (k + 1) * size], back.at[k], sems.at[k]) for k in range(chunks)]
    )
    late = started([copy(base_any, base, sems.at[chunks + 1])])
    waited(first)
    parts = jnp.zeros((mix.shape[0], base.shape[1]), jnp.float32)
    for k in range(chunks):
        backs[k].wait()
        parts = parts + jnp.dot(
            mix[:, k * size : (k + 1) * size], back[k], preferred_element_type=jnp.float32
        )
    waited(late)
    moe = parts[2 * rows :] + parts[rows : 2 * rows] + parts[:rows]
    out = (base[...] + moe).astype(jnp.bfloat16)
    out_ref[...] = out
    out_f = out.astype(jnp.float32)
    row = iota(out_f.shape, 0)
    total = jnp.sum(jnp.where(row < info[3], out_f * out_f, 0.0), axis=0, keepdims=True)
    square_ref[...] = jnp.broadcast_to(
        jnp.sum(total, axis=1, keepdims=True), square_ref.shape
    )


def place_kernel(info, g_own, g_oth, u_both, d_own, d_oth, _, out_ref):
    left = info[2] == 0
    for k, (own, oth) in ((0, (g_own[...], g_oth[...])), (2, (d_own[...], d_oth[...]))):
        out_ref[k, :, :FF] = jnp.where(left, own, oth)
        out_ref[k, :, FF:] = jnp.where(left, oth, own)
    out_ref[1, :, :FF] = u_both[0]
    out_ref[1, :, FF:] = u_both[1]


def cast_kernel(first_row, blocks, x_ref, *refs):
    out_ref, held, turned, sems_in, sems_out = refs[-5:]
    groups, size = held.shape[:2]
    fetches, stores = [], []
    for g in range(groups):
        rows = pl.ds(first_row + g * size, size)
        fetches.append(pltpu.make_async_copy(x_ref.at[rows], held.at[g], sems_in.at[g]))
        target = out_ref.at[:, g * 16 : (g + 1) * 16]
        stores.append(pltpu.make_async_copy(turned.at[g], target, sems_out.at[g]))
    for fetch in fetches:
        fetch.start()
    target = iota((size, size), 0)
    source = (target & 15) * blocks + lax.shift_right_logical(target, 4)
    order = jnp.where(iota((size, size), 1) == source, 1.0, 0.0).astype(jnp.bfloat16)
    for g in range(groups):
        fetches[g].wait()
        rows = jnp.dot(order, held[g].astype(jnp.bfloat16), preferred_element_type=jnp.float32)
        turned[g] = rows.astype(jnp.bfloat16).reshape(turned.shape[1:])
        stores[g].start()
    for store in stores:
        store.wait()


def tie_kernel(*_):
    pass


def params():
    return pltpu.CompilerParams(vmem_limit_bytes=VMEM, dimension_semantics=("arbitrary",))


def whole(shape):
    return pl.BlockSpec(shape, lambda *_: tuple(0 for _ in shape))


def paired(
    hidden_in, lengths, routes, route_weights, norm_gain, master, unembed, final_gain, target_ids
):
    rows = hidden_in.shape[1]
    width = hidden_in.shape[2]
    blk_count = lax.axis_size("blk")
    blk = lax.axis_index("blk")
    rep = lax.axis_index("rep")
    first = blk_count * FIRST
    second = blk_count * SECOND
    resid = hidden_in[0]
    info = jnp.stack([2 * blk + rep, 2 * blk + 1 - rep, rep, lengths[blk], blk])
    info = info.astype(jnp.int32)

    shard_rows = master.shape[1]
    flat = master.reshape(3 * shard_rows * blk_count, FF)

    groups = shard_rows // 16

    def turned(k, *after):
        return pl.pallas_call(
            functools.partial(cast_kernel, k * shard_rows * blk_count, blk_count),
            in_specs=[pl.BlockSpec(memory_space=pl.ANY)] * (1 + len(after)),
            out_specs=pl.BlockSpec(memory_space=pl.ANY),
            out_shape=jax.ShapeDtypeStruct((blk_count, shard_rows, FF), jnp.bfloat16),
            scratch_shapes=[
                pltpu.VMEM((groups, 16 * blk_count, FF), jnp.float32),
                pltpu.VMEM((groups, blk_count, 16, FF), jnp.bfloat16),
                pltpu.SemaphoreType.DMA((groups,)),
                pltpu.SemaphoreType.DMA((groups,)),
            ],
            compiler_params=pltpu.CompilerParams(vmem_limit_bytes=VMEM),
            name="cast",
        )(flat, *after)

    def moved(x):
        own = lax.all_to_all(x, "blk", split_axis=0, concat_axis=0, tiled=True)
        return own.reshape(width, FF)

    def swapped(x):
        return lax.ppermute(x, "rep", [(0, 1), (1, 0)])

    def tied(x, *after):
        return pl.pallas_call(
            tie_kernel,
            in_specs=[pl.BlockSpec(memory_space=pl.ANY)] * (1 + len(after)),
            out_specs=pl.BlockSpec(memory_space=pl.ANY),
            out_shape=jax.ShapeDtypeStruct(x.shape, x.dtype),
            input_output_aliases={0: 0},
            name="tie",
        )(x, *after)

    row_ext, pieces = pl.pallas_call(
        prep_kernel,
        grid_spec=pltpu.PrefetchScalarGridSpec(
            num_scalar_prefetch=2,
            grid=(1,),
            in_specs=[
                whole((rows, width)),
                whole((routes.shape[2], rows)),
                whole((routes.shape[2], rows)),
                whole((width,)),
            ],
            out_specs=[whole((rows, width + LANES)), whole((3 * rows, LANES))],
        ),
        out_shape=[
            jax.ShapeDtypeStruct((rows, width + LANES), jnp.bfloat16),
            jax.ShapeDtypeStruct((3 * rows, LANES), jnp.bfloat16),
        ],
        compiler_params=params(),
        name="prep",
    )(lengths, blk[None].astype(jnp.int32), resid, routes[0].T, route_weights[0].T, norm_gain)
    g_own = moved(turned(0, row_ext))
    g_oth = swapped(g_own)
    u_own = moved(turned(1))
    u_both = lax.all_gather(u_own, "rep", axis=0)
    d_own = moved(tied(turned(2), g_oth))

    tokens = lax.all_gather(row_ext, "blk", axis_index_groups=[list(RING)], axis=0, tiled=True)

    ring = jnp.array(RING, jnp.int32)

    other = pl.BlockSpec((None, width, FF), lambda i, info, *_: (1 - info[2], 0, 0))

    def hidden_of(kernel, outs, picked, operands, up, specs):
        return pl.pallas_call(
            kernel,
            grid_spec=pltpu.PrefetchScalarGridSpec(
                num_scalar_prefetch=3,
                grid=(GROUPS,),
                in_specs=[pl.BlockSpec((blk_count // GROUPS * rows, width + LANES), lambda i, *_: (i, 0))]
                + [whole((width, FF)), up]
                + specs,
                out_specs=[whole(out.shape) for out in outs],
                scratch_shapes=[
                    pltpu.VMEM((picked, width), jnp.float32),
                    pltpu.VMEM((blk_count, width + LANES), jnp.float32),
                ],
            ),
            out_shape=outs,
            compiler_params=params(),
            name="gate_up",
        )(info, lengths, ring, tokens, *operands)

    step = 512
    quarter = width // 4
    anywhere = pl.BlockSpec(memory_space=pl.ANY)

    def returned(x):
        slots = x.shape[0]
        x = x.reshape(blk_count, slots // blk_count, width)
        x = lax.all_to_all(x, "blk", split_axis=0, concat_axis=0, tiled=True)
        return x.reshape(slots, width)

    def bf16(*shape):
        return jax.ShapeDtypeStruct(shape, jnp.bfloat16)

    def f32(*shape):
        return jax.ShapeDtypeStruct(shape, jnp.float32)

    extra = LANES
    own_hidden, spot, own_share = hidden_of(
        own_kernel,
        [bf16(first + extra, FF), bf16(second, extra), f32(blk_count, LANES)],
        first + extra,
        (g_own, u_own),
        whole((width, FF)),
        [],
    )
    d_own = tied(d_own, own_hidden)
    d_oth = swapped(d_own)
    own_out, late_out, own_part = pl.pallas_call(
        own_down_kernel,
        in_specs=[anywhere] * 3,
        out_specs=[anywhere] * 3,
        out_shape=[bf16(first, width), bf16(extra, width), f32(blk_count, width)],
        scratch_shapes=[
            pltpu.VMEM((first + extra, FF), jnp.bfloat16),
            pltpu.VMEM((blk_count, LANES), jnp.float32),
            pltpu.VMEM((4, quarter, FF), jnp.bfloat16),
            pltpu.VMEM((4, first + extra, quarter), jnp.bfloat16),
            pltpu.VMEM((4, blk_count, quarter), jnp.float32),
            pltpu.SemaphoreType.DMA((5, 4)),
        ],
        compiler_params=pltpu.CompilerParams(vmem_limit_bytes=VMEM),
        name="own_down",
    )(own_hidden, own_share, d_own)
    own_back = returned(own_out)
    oth_hidden, oth_share, base_part = hidden_of(
        oth_kernel,
        [bf16(second + blk_count, FF), f32(blk_count, LANES), f32(blk_count, width)],
        second + blk_count,
        (g_oth, u_both, resid, own_out),
        other,
        [whole((rows, width)), anywhere],
    )
    oth_out, last_part = pl.pallas_call(
        oth_down_kernel,
        grid_spec=pltpu.PrefetchScalarGridSpec(
            num_scalar_prefetch=1,
            grid=(1,),
            in_specs=[anywhere] * 7,
            out_specs=[anywhere] * 2,
            scratch_shapes=[
                pltpu.VMEM((second + blk_count, FF), jnp.bfloat16),
                pltpu.VMEM((blk_count, LANES), jnp.float32),
                pltpu.VMEM((second, extra), jnp.bfloat16),
                pltpu.VMEM((extra, width), jnp.bfloat16),
                pltpu.VMEM((blk_count, width), jnp.float32),
                pltpu.VMEM((blk_count, width), jnp.float32),
                pltpu.VMEM((4, quarter, FF), jnp.bfloat16),
                pltpu.VMEM((4, second, quarter), jnp.bfloat16),
                pltpu.VMEM((4, blk_count, quarter), jnp.float32),
                pltpu.SemaphoreType.DMA((4, 6)),
            ],
        ),
        out_shape=[bf16(second, width), f32(blk_count, width)],
        compiler_params=params(),
        name="oth_down",
    )(info, oth_hidden, oth_share, spot, late_out, base_part, own_part, d_oth)
    last_parts = lax.all_gather(last_part, "blk", axis_index_groups=[list(RING)], axis=0)
    oth_back = returned(oth_out)

    server = pl.pallas_call(
        place_kernel,
        grid_spec=pltpu.PrefetchScalarGridSpec(
            num_scalar_prefetch=1,
            grid=(4,),
            in_specs=[pl.BlockSpec((quarter, FF), lambda i, *_: (i, 0))] * 2
            + [pl.BlockSpec((2, quarter, FF), lambda i, *_: (0, i, 0))]
            + [pl.BlockSpec((quarter, FF), lambda i, *_: (i, 0))] * 2
            + [anywhere],
            out_specs=pl.BlockSpec((3, quarter, 2 * FF), lambda i, *_: (0, i, 0)),
        ),
        out_shape=jax.ShapeDtypeStruct((3, width, 2 * FF), jnp.bfloat16),
        compiler_params=params(),
        name="place",
    )(info, g_own, g_oth, u_both, d_own, d_oth, oth_out)

    first_mix, second_mix = pl.pallas_call(
        mix_kernel,
        grid_spec=pltpu.PrefetchScalarGridSpec(
            num_scalar_prefetch=1,
            grid=(1,),
            in_specs=[
                pl.BlockSpec((rows, LANES), lambda i, *_: (0, width // LANES)),
                whole((3 * rows, LANES)),
            ],
            out_specs=[whole((3 * rows, first)), whole((3 * rows, second))],
        ),
        out_shape=[
            jax.ShapeDtypeStruct((3 * rows, first), jnp.bfloat16),
            jax.ShapeDtypeStruct((3 * rows, second), jnp.bfloat16),
        ],
        compiler_params=params(),
        name="mix",
    )(info, row_ext, pieces)

    def weigh_specs(slots):
        return [whole((3 * rows, slots)), pl.BlockSpec((slots, step), lambda i, *_: (0, i))]

    column = pl.BlockSpec((rows, step), lambda i, *_: (0, i))
    base = pl.pallas_call(
        first_kernel,
        grid=(width // step,),
        in_specs=weigh_specs(first) + [column],
        out_specs=column,
        out_shape=f32(rows, width),
        compiler_params=params(),
        name="first",
    )(first_mix, own_back, resid)
    last_rows = lax.reduce_precision(jnp.sum(last_parts, axis=0), 8, 7)
    final = (
        last_rows
        * lax.rsqrt(jnp.mean(last_rows * last_rows, axis=-1, keepdims=True) + 1e-05)
        * final_gain
    ).astype(jnp.bfloat16)
    logits = lax.dot_general(
        final, unembed, (((1,), (1,)), ((), ())), preferred_element_type=jnp.float32
    )
    vocab_base = blk * unembed.shape[0]
    target_hit = (
        target_ids[:, None] == vocab_base + jnp.arange(unembed.shape[0], dtype=jnp.int32)[None, :]
    )
    target_part = jnp.sum(jnp.where(target_hit, logits, 0.0), axis=1)
    top_part = jnp.max(logits, axis=1)

    out_rows, square = pl.pallas_call(
        combine_kernel,
        grid_spec=pltpu.PrefetchScalarGridSpec(
            num_scalar_prefetch=1,
            grid=(1,),
            in_specs=[anywhere] * 5,
            out_specs=[whole((rows, width)), whole((1, LANES))],
            scratch_shapes=[
                pltpu.VMEM((3 * rows, second), jnp.bfloat16),
                pltpu.VMEM((second // LANES, LANES, width), jnp.bfloat16),
                pltpu.VMEM((rows, width), jnp.float32),
                pltpu.SemaphoreType.DMA((second // LANES + 2,)),
            ],
        ),
        out_shape=[bf16(rows, width), f32(1, LANES)],
        compiler_params=params(),
        name="combine",
    )(info, second_mix, oth_back, base, server, top_part[None])

    def everywhere(copies):
        return lax.all_to_all(copies, "blk", split_axis=0, concat_axis=0, tiled=True)

    prompt = jnp.arange(blk_count, dtype=jnp.int32)
    square_part = jnp.where(prompt == blk, square[0, :blk_count], 0.0)
    stats = jnp.stack([top_part, target_part, square_part])
    parts = everywhere(jnp.broadcast_to(stats[None], (blk_count,) + stats.shape))
    sums = jnp.sum(parts[:, 1:], axis=0)
    norms = jnp.sqrt(sums[1] / (lengths.astype(jnp.float32) * width) + 1e-06)
    request_stats = jnp.stack([norms, jnp.max(parts[:, 0], axis=0), sums[0]])
    return (out_rows[None], server, request_stats)


def local(hidden_in, lengths, routes, route_weights, norm_gain, master, *rest):
    blk_count = lax.axis_size("blk")
    fits = (
        lax.axis_size("rep") == 2
        and master.shape[3] == FF
        and EXPERTS == 2 * blk_count
        and blk_count == len(RING)
        and hidden_in.shape[1] == LEN
        and lengths.shape[0] == blk_count
    )
    form = paired if fits else general
    return form(hidden_in, lengths, routes, route_weights, norm_gain, master, *rest)


def solution(mesh):
    return jax.shard_map(
        local,
        mesh=mesh,
        in_specs=(
            P("rep", "blk", None),
            P("rep"),
            P("rep", "blk", None),
            P("rep", "blk", None),
            P(),
            P(None, "blk", None, "rep"),
            P("blk", None),
            P(),
            P("rep"),
        ),
        out_specs=(P("rep", "blk", None), P(None, None, "blk"), P(None, "rep")),
        check_vma=False,
    )
```

```python
import functools

import jax
import jax.numpy as jnp
from jax import lax
from jax.experimental import pallas as pl
from jax.experimental.pallas import tpu as pltpu
from jax.sharding import PartitionSpec as P

FF = 512
EXPERTS = 32
LEN = 128
CAP = 36
FIRST = 32
SECOND = 40
GROUPS = 4
RING = (0, 1, 4, 5, 8, 9, 12, 13, 14, 15, 10, 11, 6, 7, 2, 3)
LANES = 128
VMEM = 63 * 1024 * 1024


def merged(x, axis, combine):
    everything = jax.tree.map(lambda part: lax.all_gather(part, axis), x)
    initial = jax.tree.map(lambda part: part[0], everything)

    def turn(k, so_far):
        return combine(so_far, jax.tree.map(lambda part: part[k], everything))

    return lax.fori_loop(1, lax.axis_size(axis), turn, initial)


def combine_stats(first, second):
    return (first[0] + second[0], jnp.maximum(first[1], second[1]))


def general(
    hidden_in, lengths, routes, route_weights, norm_gain, master, unembed, final_gain, target_ids
):
    rows_here = hidden_in.shape[1]
    width = hidden_in.shape[2]
    top_count = routes.shape[2]
    blk_count = lax.axis_size("blk")
    rep_count = lax.axis_size("rep")
    blk_index = lax.axis_index("blk")
    unit_count = master.shape[3] * rep_count
    split_ways = max(1, FF // unit_count)
    local_exp = max(1, unit_count // FF)
    group_width = min(unit_count, FF)
    capacity = CAP
    blocks = master.astype(jnp.bfloat16)
    arrived_blocks = lax.all_to_all(blocks, "blk", split_axis=2, concat_axis=1, tiled=True)
    server = lax.all_gather(arrived_blocks, "rep", axis=3, tiled=True)[:, :, 0, :]
    gate_w = server[0].reshape(width, local_exp, group_width)
    up_w = server[1].reshape(width, local_exp, group_width)
    down_w = server[2].reshape(width, local_exp, group_width)
    prompts_here = lengths.shape[0]
    slot_index = blk_index * rows_here + jnp.arange(rows_here, dtype=jnp.int32)
    prompt_of = slot_index // LEN
    position = slot_index % LEN
    prompt_match = prompt_of[:, None] == jnp.arange(prompts_here, dtype=jnp.int32)[None, :]
    row_len = jnp.sum(jnp.where(prompt_match, lengths[None, :], 0), axis=1)
    is_valid = position < row_len
    resid_f = hidden_in[0].astype(jnp.float32)
    normed = (
        resid_f * lax.rsqrt(jnp.mean(resid_f * resid_f, axis=-1, keepdims=True) + 1e-05) * norm_gain
    ).astype(jnp.bfloat16)
    expert_ids = routes[0].reshape(-1)
    pair_live = jnp.repeat(is_valid, top_count)
    pair_row = jnp.repeat(jnp.arange(rows_here, dtype=jnp.int32), top_count)
    expert_hits = (
        (expert_ids[:, None] == jnp.arange(EXPERTS, dtype=jnp.int32)[None, :]) & pair_live[:, None]
    ).astype(jnp.int32)
    slot_rank = jnp.sum((jnp.cumsum(expert_hits, axis=0) - 1) * expert_hits, axis=1)
    slot_id = jnp.where(pair_live, expert_ids * capacity + slot_rank, EXPERTS * capacity)
    source_row = jnp.zeros((EXPERTS * capacity + 1,), jnp.int32).at[slot_id].set(pair_row)[:-1]
    filled = jnp.zeros((EXPERTS * capacity + 1,), jnp.bfloat16).at[slot_id].set(1.0)[:-1]
    outgoing = (normed[source_row] * filled[:, None]).reshape(EXPERTS, capacity, width)
    sending = jnp.repeat(outgoing, split_ways, axis=0).reshape(
        blk_count, local_exp, capacity, width
    )
    arrived = lax.all_to_all(sending, "blk", split_axis=0, concat_axis=0, tiled=True)
    sources = arrived.shape[0]
    slot_count = arrived.shape[2]
    stride = sources
    while stride % 2 == 0 and stride * local_exp * slot_count > 1024:
        stride = stride // 2
    grouped = arrived.reshape(sources // stride, stride, local_exp, slot_count, width)

    def one_block(portion):
        gate_out = jnp.einsum("slnd,dlf->slnf", portion, gate_w, preferred_element_type=jnp.float32)
        up_out = jnp.einsum("slnd,dlf->slnf", portion, up_w, preferred_element_type=jnp.float32)
        hidden = (jax.nn.silu(gate_out) * up_out).astype(jnp.bfloat16)
        return jnp.einsum(
            "slnf,dlf->slnd", hidden, down_w, preferred_element_type=jnp.float32
        ).astype(jnp.bfloat16)

    returned = lax.all_to_all(
        lax.map(one_block, grouped).reshape(sources, local_exp, slot_count, width),
        "blk",
        split_axis=0,
        concat_axis=0,
        tiled=True,
    )
    summed_f = jnp.sum(
        returned.reshape(EXPERTS, split_ways, capacity, width).astype(jnp.float32), axis=1
    )
    expert_out = lax.optimization_barrier(summed_f.astype(jnp.bfloat16)).reshape(
        EXPERTS * capacity, width
    )
    gather_index = jnp.where(pair_live, expert_ids * capacity + slot_rank, 0)
    pair_weight = route_weights[0].reshape(-1) * pair_live.astype(jnp.float32)
    moe = jnp.sum(
        (expert_out[gather_index].astype(jnp.float32) * pair_weight[:, None]).reshape(
            rows_here, top_count, width
        ),
        axis=1,
    )
    out_rows = (resid_f + moe).astype(jnp.bfloat16)
    out_f = out_rows.astype(jnp.float32)
    row_squares = jnp.sum(out_f * out_f, axis=-1) * is_valid.astype(jnp.float32)
    square_local = jnp.sum(jnp.where(prompt_match, row_squares[:, None], 0.0), axis=0)
    is_last = is_valid & (position == row_len - 1)
    picker = (prompt_match & is_last[:, None]).astype(jnp.bfloat16)
    last_local = lax.dot_general(
        picker, out_rows, (((0,), (0,)), ((), ())), preferred_element_type=jnp.float32
    )
    last_rows, square_total = lax.psum((last_local, square_local), "blk")
    norms = jnp.sqrt(square_total / (lengths.astype(jnp.float32) * width) + 1e-06)
    final = (
        last_rows
        * lax.rsqrt(jnp.mean(last_rows * last_rows, axis=-1, keepdims=True) + 1e-05)
        * final_gain
    ).astype(jnp.bfloat16)
    logits = lax.dot_general(
        final, unembed, (((1,), (1,)), ((), ())), preferred_element_type=jnp.float32
    )
    vocab_base = blk_index * unembed.shape[0]
    target_hit = (
        target_ids[:, None] == vocab_base + jnp.arange(unembed.shape[0], dtype=jnp.int32)[None, :]
    )
    target_part = jnp.sum(jnp.where(target_hit, logits, 0.0), axis=1)
    top_part = jnp.max(logits, axis=1)
    target_logit, top_logit = merged((target_part, top_part), "blk", combine_stats)
    request_stats = jnp.stack([norms, top_logit, target_logit])
    return (out_rows[None], server, request_stats)


def iota(shape, dim):
    return lax.broadcasted_iota(jnp.int32, shape, dim)


def prep_kernel(lengths_ref, blk_ref, hidden_ref, routes_ref, weights_ref, gain_ref, rows_ref, pieces_ref):
    rows, width = hidden_ref.shape
    length = lengths_ref[blk_ref[0]]
    x = hidden_ref[...].astype(jnp.float32)
    scale = lax.rsqrt(jnp.mean(x * x, axis=-1, keepdims=True) + 1e-05)
    rows_ref[:, :width] = (x * scale * gain_ref[...][None]).astype(jnp.bfloat16)
    column = iota((rows, LANES), 1)
    lane = column & (EXPERTS - 1)
    row = iota((rows, LANES), 0)
    hit = jnp.zeros((rows, LANES), jnp.float32)
    weight = jnp.zeros((rows, LANES), jnp.float32)
    named_by = jnp.transpose(routes_ref[...].astype(jnp.float32)).astype(jnp.int32)
    weight_by = jnp.transpose(weights_ref[...])
    for k in range(routes_ref.shape[0]):
        named = named_by[:, k : k + 1] == lane
        hit = hit + jnp.where(named, 1.0, 0.0)
        weight = weight + jnp.where(named, weight_by[:, k : k + 1], 0.0)
    live = row < length
    hit = jnp.where(live, hit, 0.0)
    weight = jnp.where(live, weight, 0.0)
    before = jnp.where(iota((rows, rows), 1) < iota((rows, rows), 0), 1.0, 0.0)
    rank = jnp.dot(
        before.astype(jnp.bfloat16), hit.astype(jnp.bfloat16), preferred_element_type=jnp.float32
    )
    told = jnp.where(hit > 0.0, rank, -1.0)
    for k in range(3):
        piece = weight.astype(jnp.bfloat16)
        pieces_ref[k * rows : (k + 1) * rows, :] = piece
        value = piece.astype(jnp.float32)
        told = jnp.where(column >= (k + 1) * EXPERTS, value, told)
        weight = weight - value
    rows_ref[:, width:] = told.astype(jnp.bfloat16)


def pick(info, lengths_ref, ring_ref, which, x_ref, width, place, slots, lasts):
    step = pl.program_id(0)
    rows = x_ref.shape[0]
    sources = rows // LEN
    ranks = x_ref[:, width:].astype(jnp.float32)
    lane = iota((rows, LANES), 1)
    row = iota((rows, 1), 0)
    source = row // LEN
    rank = jnp.sum(jnp.where(lane == info[which], ranks, 0.0), axis=1, keepdims=True)
    slot = jnp.where(rank >= 0.0, place(source.astype(jnp.float32), rank), -1.0)
    slot_lane = iota((rows, slots), 1).astype(jnp.float32)
    one_hot = jnp.where(slot == slot_lane, 1.0, 0.0).astype(jnp.bfloat16)
    dims = (((0,), (0,)), ((), ()))
    chosen = lax.dot_general(
        one_hot, x_ref[:, :width], dims, preferred_element_type=jnp.float32
    )
    home = jnp.full_like(row, -1)
    for s in range(sources):
        owner = ring_ref[step * sources + s]
        home = jnp.where(row == s * LEN + lengths_ref[owner] - 1, owner, home)
    home = jnp.where(rank >= 0.0, home, -1)
    count = lasts.shape[0]
    one_hot = jnp.where(home == iota((rows, count), 1), 1.0, 0.0).astype(jnp.bfloat16)
    last = lax.dot_general(one_hot, x_ref[...], dims, preferred_element_type=jnp.float32)

    @pl.when(step == 0)
    def _():
        lasts[...] = last

    @pl.when(step != 0)
    def _():
        lasts[...] += last

    return chosen


def share_of(info, which, lasts, width):
    ext = lasts[:, width:]
    lane = iota(ext.shape, 1)
    is_own = (lane >= EXPERTS) & ((lane & (EXPERTS - 1)) == info[which])
    return jnp.broadcast_to(
        jnp.sum(jnp.where(is_own, ext, 0.0), axis=1, keepdims=True), ext.shape
    )


def activ(x, g_ref, u_ref):
    x = x.astype(jnp.bfloat16)
    gate = jnp.dot(x, g_ref[...], preferred_element_type=jnp.float32)
    up = jnp.dot(x, u_ref[...], preferred_element_type=jnp.float32)
    return (gate / (1.0 + jnp.exp(-gate)) * up).astype(jnp.bfloat16)


def own_kernel(
    info, lengths_ref, ring_ref, x_ref, g_ref, u_ref, out_ref, spot_ref, share_ref, picked, lasts
):
    step = pl.program_id(0)
    sources = x_ref.shape[0] // LEN
    width = g_ref.shape[0]
    more = CAP - FIRST
    early = sources * FIRST
    all_early = GROUPS * early
    all_rows = all_early + GROUPS * sources * more

    def place(source, rank):
        return jnp.where(
            rank < FIRST, source * FIRST + rank, early + source * more + (rank - FIRST)
        )

    chosen = pick(
        info, lengths_ref, ring_ref, 0, x_ref, width, place, early + sources * more, lasts
    )
    for s in range(sources):
        start = pl.multiple_of(ring_ref[step * sources + s] * FIRST, FIRST)
        picked[pl.ds(start, FIRST), :] = chosen[s * FIRST : (s + 1) * FIRST]
    start = pl.multiple_of(all_early + step * sources * more, sources * more)
    picked[pl.ds(start, sources * more), :] = chosen[early:]

    @pl.when(step == GROUPS - 1)
    def _():
        count = lasts.shape[0]
        picked[all_rows : all_rows + count, :] = lasts[:, :width]
        blank = picked.shape[0] - all_rows - count
        picked[all_rows + count :, :] = jnp.zeros((blank, width), jnp.float32)
        out_ref[...] = activ(picked[...], g_ref, u_ref)
        share_ref[...] = share_of(info, 0, lasts, width)
        column = iota(spot_ref.shape, 1)
        owner = lax.shift_right_logical(column, more.bit_length() - 1)
        source = jnp.full_like(column, -1)
        for k, b in enumerate(RING):
            source = jnp.where(owner == k, b, source)
        spot = jnp.where(source >= 0, source * SECOND + (column & (more - 1)), -1)
        spot_ref[...] = jnp.where(iota(spot_ref.shape, 0) == spot, 1.0, 0.0).astype(jnp.bfloat16)


def oth_kernel(
    info,
    lengths_ref,
    ring_ref,
    x_ref,
    g_ref,
    u_ref,
    resid_ref,
    _,
    out_ref,
    share_ref,
    base_ref,
    picked,
    lasts,
):
    step = pl.program_id(0)
    sources = x_ref.shape[0] // LEN
    width = g_ref.shape[0]
    all_rows = GROUPS * sources * SECOND

    def place(source, rank):
        return source * SECOND + (SECOND - CAP) + rank

    chosen = pick(info, lengths_ref, ring_ref, 1, x_ref, width, place, sources * SECOND, lasts)
    for s in range(sources):
        start = pl.multiple_of(ring_ref[step * sources + s] * SECOND, SECOND)
        picked[pl.ds(start, SECOND), :] = chosen[s * SECOND : (s + 1) * SECOND]

    @pl.when(step == GROUPS - 1)
    def _():
        picked[all_rows:, :] = lasts[:, :width]
        out_ref[...] = activ(picked[...], g_ref, u_ref)
        share_ref[...] = share_of(info, 1, lasts, width)
        resid = resid_ref[...].astype(jnp.float32)
        is_last = iota(resid.shape, 0) == info[3] - 1
        last = jnp.sum(jnp.where(is_last, resid, 0.0), axis=0, keepdims=True)
        base_ref[...] = jnp.where(iota(base_ref.shape, 0) == info[4], last, 0.0)


def matmul_nt(hidden_ref, d):
    return lax.dot_general(
        hidden_ref[...], d, (((1,), (1,)), ((), ())), preferred_element_type=jnp.float32
    )


def started(copies):
    for copy in copies:
        copy.start()
    return copies


def waited(copies):
    for copy in copies:
        copy.wait()


def own_down_kernel(
    hidden_any, share_any, d_any, out_any, late_any, part_any, hidden, share, d, out, part, sems
):
    chunks, size = d.shape[:2]
    rows, count = out_any.shape[0], part.shape[1]
    at = rows + count * (CAP - FIRST)
    copy = pltpu.make_async_copy
    first = started(
        [copy(hidden_any, hidden, sems.at[0, 0]), copy(share_any, share, sems.at[0, 1])]
    )
    downs = started(
        [
            copy(d_any.at[k * size : (k + 1) * size], d.at[k], sems.at[1, k])
            for k in range(chunks)
        ]
    )
    waited(first)
    stores = []
    for k in range(chunks):
        downs[k].wait()
        out[k] = matmul_nt(hidden, d[k]).astype(jnp.bfloat16)
        part[k] = share[:, :1] * out[k, at : at + count].astype(jnp.float32)
        columns = slice(k * size, (k + 1) * size)
        stores += started(
            [
                copy(out.at[k, :rows], out_any.at[:, columns], sems.at[2, k]),
                copy(out.at[k, rows:], late_any.at[:, columns], sems.at[3, k]),
                copy(part.at[k], part_any.at[:, columns], sems.at[4, k]),
            ]
        )
    waited(stores)


def oth_down_kernel(
    info,
    hidden_any,
    share_any,
    spot_any,
    late_any,
    base_any,
    part_any,
    d_any,
    out_any,
    sum_any,
    hidden,
    share,
    spot,
    late,
    base,
    part,
    d,
    out,
    total,
    sems,
):
    chunks, size = d.shape[:2]
    rows = out_any.shape[0]
    copy = pltpu.make_async_copy
    other = 1 - info[2]
    sources = (hidden_any, share_any, spot_any, late_any, base_any, part_any)
    targets = (hidden, share, spot, late, base, part)
    downs = started(
        [
            copy(d_any.at[other, k * size : (k + 1) * size], d.at[k], sems.at[1, k])
            for k in range(chunks)
        ]
    )
    first = started([copy(x, y, sems.at[0, k]) for k, (x, y) in enumerate(zip(sources, targets))])
    waited(first)
    stores = []
    for k in range(chunks):
        downs[k].wait()
        columns = slice(k * size, (k + 1) * size)
        placed = jnp.dot(spot[...], late[:, columns], preferred_element_type=jnp.float32)
        value = matmul_nt(hidden, d[k])
        out[k] = (placed + value[:rows]).astype(jnp.bfloat16)
        last = value[rows:].astype(jnp.bfloat16).astype(jnp.float32)
        total[k] = base[:, columns] + part[:, columns] + share[:, :1] * last
        stores += started(
            [
                copy(total.at[k], sum_any.at[:, columns], sems.at[3, k]),
                copy(out.at[k], out_any.at[:, columns], sems.at[2, k]),
            ]
        )
    waited(stores)


def mix_kernel(info, rank_ref, pieces_ref, first_ref, second_ref):
    rows = rank_ref.shape[0]
    late = SECOND - CAP
    own, oth = info[2], 1 - info[2]
    for mix_ref, stride, spans in (
        (first_ref, FIRST, ((own, 0, FIRST, 0),)),
        (second_ref, SECOND, ((own, 0, late, FIRST), (oth, late, CAP, 0))),
    ):
        slots = mix_ref.shape[1]
        expert = iota((LANES, slots), 0)
        lane = iota((LANES, slots), 1)
        within = jnp.zeros((1, slots), jnp.float32)
        spread = jnp.zeros((LANES, slots), jnp.float32)
        for parity, offset, count, lowest in spans:
            start = jnp.where((expert & 1) == parity, (expert >> 1) * stride + offset, slots)
            inside = (lane >= start) & (lane < start + count)
            spread = spread + jnp.where(inside, 1.0, 0.0)
            ranks = jnp.where(inside, lane - start + lowest, 0)
            within = within + jnp.sum(ranks, axis=0, keepdims=True).astype(jnp.float32)
        spread = spread.astype(jnp.bfloat16)
        rank = jnp.dot(rank_ref[...], spread, preferred_element_type=jnp.float32)
        match = rank == within
        for k in range(3):
            part = jnp.dot(
                pieces_ref[k * rows : (k + 1) * rows, :], spread, preferred_element_type=jnp.float32
            )
            mix_ref[k * rows : (k + 1) * rows, :] = jnp.where(match, part, 0.0).astype(jnp.bfloat16)


def weigh(mix_ref, back_ref):
    rows = mix_ref.shape[0] // 3
    parts = jnp.dot(mix_ref[...], back_ref[...], preferred_element_type=jnp.float32)
    return parts[2 * rows :] + parts[rows : 2 * rows] + parts[:rows]


def first_kernel(mix_ref, back_ref, resid_ref, base_ref):
    base_ref[...] = resid_ref[...].astype(jnp.float32) + weigh(mix_ref, back_ref)


def combine_kernel(
    info, mix_any, back_any, base_any, _, __, out_ref, square_ref, mix, back, base, sems
):
    chunks, size = back.shape[:2]
    rows = base.shape[0]
    copy = pltpu.make_async_copy
    first = started([copy(mix_any, mix, sems.at[chunks])])
    backs = started(
        [copy(back_any.at[k * size : (k + 1) * size], back.at[k], sems.at[k]) for k in range(chunks)]
    )
    late = started([copy(base_any, base, sems.at[chunks + 1])])
    waited(first)
    parts = jnp.zeros((mix.shape[0], base.shape[1]), jnp.float32)
    for k in range(chunks):
        backs[k].wait()
        parts = parts + jnp.dot(
            mix[:, k * size : (k + 1) * size], back[k], preferred_element_type=jnp.float32
        )
    waited(late)
    moe = parts[2 * rows :] + parts[rows : 2 * rows] + parts[:rows]
    out = (base[...] + moe).astype(jnp.bfloat16)
    out_ref[...] = out
    out_f = out.astype(jnp.float32)
    row = iota(out_f.shape, 0)
    total = jnp.sum(jnp.where(row < info[3], out_f * out_f, 0.0), axis=0, keepdims=True)
    square_ref[...] = jnp.broadcast_to(
        jnp.sum(total, axis=1, keepdims=True), square_ref.shape
    )


def place_kernel(info, g_own, g_oth, u_own, u_oth, d_both, _, out_ref):
    left = info[2] == 0
    for k, (own, oth) in enumerate(((g_own[...], g_oth[...]), (u_own[...], u_oth[...]))):
        out_ref[k, :, :FF] = jnp.where(left, own, oth)
        out_ref[k, :, FF:] = jnp.where(left, oth, own)
    out_ref[2, :, :FF] = d_both[0]
    out_ref[2, :, FF:] = d_both[1]


def cast_kernel(first_row, blocks, x_ref, *refs):
    out_ref, held, turned, sems_in, sems_out = refs[-5:]
    groups, size = held.shape[:2]
    fetches, stores = [], []
    for g in range(groups):
        rows = pl.ds(first_row + g * size, size)
        fetches.append(pltpu.make_async_copy(x_ref.at[rows], held.at[g], sems_in.at[g]))
        target = out_ref.at[:, g * 16 : (g + 1) * 16]
        stores.append(pltpu.make_async_copy(turned.at[g], target, sems_out.at[g]))
    for fetch in fetches:
        fetch.start()
    target = iota((size, size), 0)
    source = (target & 15) * blocks + lax.shift_right_logical(target, 4)
    order = jnp.where(iota((size, size), 1) == source, 1.0, 0.0).astype(jnp.bfloat16)
    for g in range(groups):
        fetches[g].wait()
        rows = jnp.dot(order, held[g].astype(jnp.bfloat16), preferred_element_type=jnp.float32)
        turned[g] = rows.astype(jnp.bfloat16).reshape(turned.shape[1:])
        stores[g].start()
    for store in stores:
        store.wait()


def tie_kernel(*_):
    pass


def params():
    return pltpu.CompilerParams(vmem_limit_bytes=VMEM, dimension_semantics=("arbitrary",))


def whole(shape):
    return pl.BlockSpec(shape, lambda *_: tuple(0 for _ in shape))


def paired(
    hidden_in, lengths, routes, route_weights, norm_gain, master, unembed, final_gain, target_ids
):
    rows = hidden_in.shape[1]
    width = hidden_in.shape[2]
    blk_count = lax.axis_size("blk")
    blk = lax.axis_index("blk")
    rep = lax.axis_index("rep")
    first = blk_count * FIRST
    second = blk_count * SECOND
    resid = hidden_in[0]
    info = jnp.stack([2 * blk + rep, 2 * blk + 1 - rep, rep, lengths[blk], blk])
    info = info.astype(jnp.int32)

    shard_rows = master.shape[1]
    flat = master.reshape(3 * shard_rows * blk_count, FF)

    groups = shard_rows // 16

    def turned(k, *after):
        return pl.pallas_call(
            functools.partial(cast_kernel, k * shard_rows * blk_count, blk_count),
            in_specs=[pl.BlockSpec(memory_space=pl.ANY)] * (1 + len(after)),
            out_specs=pl.BlockSpec(memory_space=pl.ANY),
            out_shape=jax.ShapeDtypeStruct((blk_count, shard_rows, FF), jnp.bfloat16),
            scratch_shapes=[
                pltpu.VMEM((groups, 16 * blk_count, FF), jnp.float32),
                pltpu.VMEM((groups, blk_count, 16, FF), jnp.bfloat16),
                pltpu.SemaphoreType.DMA((groups,)),
                pltpu.SemaphoreType.DMA((groups,)),
            ],
            compiler_params=pltpu.CompilerParams(vmem_limit_bytes=VMEM),
            name="cast",
        )(flat, *after)

    def moved(x):
        own = lax.all_to_all(x, "blk", split_axis=0, concat_axis=0, tiled=True)
        return own.reshape(width, FF)

    def swapped(x):
        return lax.ppermute(x, "rep", [(0, 1), (1, 0)])

    def tied(x, *after):
        return pl.pallas_call(
            tie_kernel,
            in_specs=[pl.BlockSpec(memory_space=pl.ANY)] * (1 + len(after)),
            out_specs=pl.BlockSpec(memory_space=pl.ANY),
            out_shape=jax.ShapeDtypeStruct(x.shape, x.dtype),
            input_output_aliases={0: 0},
            name="tie",
        )(x, *after)

    row_ext, pieces = pl.pallas_call(
        prep_kernel,
        grid_spec=pltpu.PrefetchScalarGridSpec(
            num_scalar_prefetch=2,
            grid=(1,),
            in_specs=[
                whole((rows, width)),
                whole((routes.shape[2], rows)),
                whole((routes.shape[2], rows)),
                whole((width,)),
            ],
            out_specs=[whole((rows, width + LANES)), whole((3 * rows, LANES))],
        ),
        out_shape=[
            jax.ShapeDtypeStruct((rows, width + LANES), jnp.bfloat16),
            jax.ShapeDtypeStruct((3 * rows, LANES), jnp.bfloat16),
        ],
        compiler_params=params(),
        name="prep",
    )(lengths, blk[None].astype(jnp.int32), resid, routes[0].T, route_weights[0].T, norm_gain)
    g_own = moved(turned(0, row_ext))
    g_oth = swapped(g_own)
    u_own = moved(turned(1))
    u_oth = swapped(u_own)
    d_own = moved(tied(turned(2), g_oth))

    tokens = lax.all_gather(row_ext, "blk", axis_index_groups=[list(RING)], axis=0, tiled=True)

    ring = jnp.array(RING, jnp.int32)

    def hidden_of(kernel, outs, picked, operands, specs):
        return pl.pallas_call(
            kernel,
            grid_spec=pltpu.PrefetchScalarGridSpec(
                num_scalar_prefetch=3,
                grid=(GROUPS,),
                in_specs=[pl.BlockSpec((blk_count // GROUPS * rows, width + LANES), lambda i, *_: (i, 0))]
                + [whole((width, FF))] * 2
                + specs,
                out_specs=[whole(out.shape) for out in outs],
                scratch_shapes=[
                    pltpu.VMEM((picked, width), jnp.float32),
                    pltpu.VMEM((blk_count, width + LANES), jnp.float32),
                ],
            ),
            out_shape=outs,
            compiler_params=params(),
            name="gate_up",
        )(info, lengths, ring, tokens, *operands)

    step = 512
    quarter = width // 4
    anywhere = pl.BlockSpec(memory_space=pl.ANY)

    def returned(x):
        slots = x.shape[0]
        x = x.reshape(blk_count, slots // blk_count, width)
        x = lax.all_to_all(x, "blk", split_axis=0, concat_axis=0, tiled=True)
        return x.reshape(slots, width)

    def bf16(*shape):
        return jax.ShapeDtypeStruct(shape, jnp.bfloat16)

    def f32(*shape):
        return jax.ShapeDtypeStruct(shape, jnp.float32)

    extra = LANES
    own_hidden, spot, own_share = hidden_of(
        own_kernel,
        [bf16(first + extra, FF), bf16(second, extra), f32(blk_count, LANES)],
        first + extra,
        (g_own, u_own),
        [],
    )
    d_own = tied(d_own, own_hidden)
    d_both = lax.all_gather(d_own, "rep", axis=0)
    own_out, late_out, own_part = pl.pallas_call(
        own_down_kernel,
        in_specs=[anywhere] * 3,
        out_specs=[anywhere] * 3,
        out_shape=[bf16(first, width), bf16(extra, width), f32(blk_count, width)],
        scratch_shapes=[
            pltpu.VMEM((first + extra, FF), jnp.bfloat16),
            pltpu.VMEM((blk_count, LANES), jnp.float32),
            pltpu.VMEM((4, quarter, FF), jnp.bfloat16),
            pltpu.VMEM((4, first + extra, quarter), jnp.bfloat16),
            pltpu.VMEM((4, blk_count, quarter), jnp.float32),
            pltpu.SemaphoreType.DMA((5, 4)),
        ],
        compiler_params=pltpu.CompilerParams(vmem_limit_bytes=VMEM),
        name="own_down",
    )(own_hidden, own_share, d_own)
    own_out = tied(own_out, u_oth)
    own_back = returned(own_out)
    oth_hidden, oth_share, base_part = hidden_of(
        oth_kernel,
        [bf16(second + blk_count, FF), f32(blk_count, LANES), f32(blk_count, width)],
        second + blk_count,
        (g_oth, u_oth, resid, own_out),
        [whole((rows, width)), anywhere],
    )
    oth_out, last_part = pl.pallas_call(
        oth_down_kernel,
        grid_spec=pltpu.PrefetchScalarGridSpec(
            num_scalar_prefetch=1,
            grid=(1,),
            in_specs=[anywhere] * 7,
            out_specs=[anywhere] * 2,
            scratch_shapes=[
                pltpu.VMEM((second + blk_count, FF), jnp.bfloat16),
                pltpu.VMEM((blk_count, LANES), jnp.float32),
                pltpu.VMEM((second, extra), jnp.bfloat16),
                pltpu.VMEM((extra, width), jnp.bfloat16),
                pltpu.VMEM((blk_count, width), jnp.float32),
                pltpu.VMEM((blk_count, width), jnp.float32),
                pltpu.VMEM((4, quarter, FF), jnp.bfloat16),
                pltpu.VMEM((4, second, quarter), jnp.bfloat16),
                pltpu.VMEM((4, blk_count, quarter), jnp.float32),
                pltpu.SemaphoreType.DMA((4, 6)),
            ],
        ),
        out_shape=[bf16(second, width), f32(blk_count, width)],
        compiler_params=params(),
        name="oth_down",
    )(info, oth_hidden, oth_share, spot, late_out, base_part, own_part, d_both)
    last_parts = lax.all_gather(last_part, "blk", axis_index_groups=[list(RING)], axis=0)
    oth_back = returned(oth_out)

    server = pl.pallas_call(
        place_kernel,
        grid_spec=pltpu.PrefetchScalarGridSpec(
            num_scalar_prefetch=1,
            grid=(4,),
            in_specs=[pl.BlockSpec((quarter, FF), lambda i, *_: (i, 0))] * 4
            + [pl.BlockSpec((2, quarter, FF), lambda i, *_: (0, i, 0)), anywhere],
            out_specs=pl.BlockSpec((3, quarter, 2 * FF), lambda i, *_: (0, i, 0)),
        ),
        out_shape=jax.ShapeDtypeStruct((3, width, 2 * FF), jnp.bfloat16),
        compiler_params=params(),
        name="place",
    )(info, g_own, g_oth, u_own, u_oth, d_both, oth_out)

    first_mix, second_mix = pl.pallas_call(
        mix_kernel,
        grid_spec=pltpu.PrefetchScalarGridSpec(
            num_scalar_prefetch=1,
            grid=(1,),
            in_specs=[
                pl.BlockSpec((rows, LANES), lambda i, *_: (0, width // LANES)),
                whole((3 * rows, LANES)),
            ],
            out_specs=[whole((3 * rows, first)), whole((3 * rows, second))],
        ),
        out_shape=[
            jax.ShapeDtypeStruct((3 * rows, first), jnp.bfloat16),
            jax.ShapeDtypeStruct((3 * rows, second), jnp.bfloat16),
        ],
        compiler_params=params(),
        name="mix",
    )(info, row_ext, pieces)

    def weigh_specs(slots):
        return [whole((3 * rows, slots)), pl.BlockSpec((slots, step), lambda i, *_: (0, i))]

    column = pl.BlockSpec((rows, step), lambda i, *_: (0, i))
    base = pl.pallas_call(
        first_kernel,
        grid=(width // step,),
        in_specs=weigh_specs(first) + [column],
        out_specs=column,
        out_shape=f32(rows, width),
        compiler_params=params(),
        name="first",
    )(first_mix, own_back, resid)
    last_rows = lax.reduce_precision(jnp.sum(last_parts, axis=0), 8, 7)
    final = (
        last_rows
        * lax.rsqrt(jnp.mean(last_rows * last_rows, axis=-1, keepdims=True) + 1e-05)
        * final_gain
    ).astype(jnp.bfloat16)
    logits = lax.dot_general(
        unembed, final, (((1,), (1,)), ((), ())), preferred_element_type=jnp.float32
    )
    vocab_base = blk * unembed.shape[0]
    target_hit = (
        target_ids[None, :] == vocab_base + jnp.arange(unembed.shape[0], dtype=jnp.int32)[:, None]
    )
    target_part = jnp.sum(jnp.where(target_hit, logits, 0.0), axis=0)
    top_part = jnp.max(logits, axis=0)

    out_rows, square = pl.pallas_call(
        combine_kernel,
        grid_spec=pltpu.PrefetchScalarGridSpec(
            num_scalar_prefetch=1,
            grid=(1,),
            in_specs=[anywhere] * 5,
            out_specs=[whole((rows, width)), whole((1, LANES))],
            scratch_shapes=[
                pltpu.VMEM((3 * rows, second), jnp.bfloat16),
                pltpu.VMEM((second // LANES, LANES, width), jnp.bfloat16),
                pltpu.VMEM((rows, width), jnp.float32),
                pltpu.SemaphoreType.DMA((second // LANES + 2,)),
            ],
        ),
        out_shape=[bf16(rows, width), f32(1, LANES)],
        compiler_params=params(),
        name="combine",
    )(info, second_mix, oth_back, base, server, top_part[None])

    def everywhere(copies):
        return lax.all_to_all(copies, "blk", split_axis=0, concat_axis=0, tiled=True)

    prompt = jnp.arange(blk_count, dtype=jnp.int32)
    square_part = jnp.where(prompt == blk, square[0, :blk_count], 0.0)
    stats = jnp.stack([top_part, target_part, square_part])
    parts = everywhere(jnp.broadcast_to(stats[None], (blk_count,) + stats.shape))
    sums = jnp.sum(parts[:, 1:], axis=0)
    norms = jnp.sqrt(sums[1] / (lengths.astype(jnp.float32) * width) + 1e-06)
    request_stats = jnp.stack([norms, jnp.max(parts[:, 0], axis=0), sums[0]])
    return (out_rows[None], server, request_stats)


def local(hidden_in, lengths, routes, route_weights, norm_gain, master, *rest):
    blk_count = lax.axis_size("blk")
    fits = (
        lax.axis_size("rep") == 2
        and master.shape[3] == FF
        and EXPERTS == 2 * blk_count
        and blk_count == len(RING)
        and hidden_in.shape[1] == LEN
        and lengths.shape[0] == blk_count
    )
    form = paired if fits else general
    return form(hidden_in, lengths, routes, route_weights, norm_gain, master, *rest)


def solution(mesh):
    return jax.shard_map(
        local,
        mesh=mesh,
        in_specs=(
            P("rep", "blk", None),
            P("rep"),
            P("rep", "blk", None),
            P("rep", "blk", None),
            P(),
            P(None, "blk", None, "rep"),
            P("blk", None),
            P(),
            P("rep"),
        ),
        out_specs=(P("rep", "blk", None), P(None, None, "blk"), P(None, "rep")),
        check_vma=False,
    )
```

```python
import functools

import jax
import jax.numpy as jnp
from jax import lax
from jax.experimental import pallas as pl
from jax.experimental.pallas import tpu as pltpu
from jax.sharding import PartitionSpec as P

FF = 512
EXPERTS = 32
LEN = 128
CAP = 36
FIRST = 32
SECOND = 40
GROUPS = 4
RING = (0, 1, 4, 5, 8, 9, 12, 13, 14, 15, 10, 11, 6, 7, 2, 3)
LANES = 128
VMEM = 63 * 1024 * 1024


def merged(x, axis, combine):
    everything = jax.tree.map(lambda part: lax.all_gather(part, axis), x)
    initial = jax.tree.map(lambda part: part[0], everything)

    def turn(k, so_far):
        return combine(so_far, jax.tree.map(lambda part: part[k], everything))

    return lax.fori_loop(1, lax.axis_size(axis), turn, initial)


def combine_stats(first, second):
    return (first[0] + second[0], jnp.maximum(first[1], second[1]))


def general(
    hidden_in, lengths, routes, route_weights, norm_gain, master, unembed, final_gain, target_ids
):
    rows_here = hidden_in.shape[1]
    width = hidden_in.shape[2]
    top_count = routes.shape[2]
    blk_count = lax.axis_size("blk")
    rep_count = lax.axis_size("rep")
    blk_index = lax.axis_index("blk")
    unit_count = master.shape[3] * rep_count
    split_ways = max(1, FF // unit_count)
    local_exp = max(1, unit_count // FF)
    group_width = min(unit_count, FF)
    capacity = CAP
    blocks = master.astype(jnp.bfloat16)
    arrived_blocks = lax.all_to_all(blocks, "blk", split_axis=2, concat_axis=1, tiled=True)
    server = lax.all_gather(arrived_blocks, "rep", axis=3, tiled=True)[:, :, 0, :]
    gate_w = server[0].reshape(width, local_exp, group_width)
    up_w = server[1].reshape(width, local_exp, group_width)
    down_w = server[2].reshape(width, local_exp, group_width)
    prompts_here = lengths.shape[0]
    slot_index = blk_index * rows_here + jnp.arange(rows_here, dtype=jnp.int32)
    prompt_of = slot_index // LEN
    position = slot_index % LEN
    prompt_match = prompt_of[:, None] == jnp.arange(prompts_here, dtype=jnp.int32)[None, :]
    row_len = jnp.sum(jnp.where(prompt_match, lengths[None, :], 0), axis=1)
    is_valid = position < row_len
    resid_f = hidden_in[0].astype(jnp.float32)
    normed = (
        resid_f * lax.rsqrt(jnp.mean(resid_f * resid_f, axis=-1, keepdims=True) + 1e-05) * norm_gain
    ).astype(jnp.bfloat16)
    expert_ids = routes[0].reshape(-1)
    pair_live = jnp.repeat(is_valid, top_count)
    pair_row = jnp.repeat(jnp.arange(rows_here, dtype=jnp.int32), top_count)
    expert_hits = (
        (expert_ids[:, None] == jnp.arange(EXPERTS, dtype=jnp.int32)[None, :]) & pair_live[:, None]
    ).astype(jnp.int32)
    slot_rank = jnp.sum((jnp.cumsum(expert_hits, axis=0) - 1) * expert_hits, axis=1)
    slot_id = jnp.where(pair_live, expert_ids * capacity + slot_rank, EXPERTS * capacity)
    source_row = jnp.zeros((EXPERTS * capacity + 1,), jnp.int32).at[slot_id].set(pair_row)[:-1]
    filled = jnp.zeros((EXPERTS * capacity + 1,), jnp.bfloat16).at[slot_id].set(1.0)[:-1]
    outgoing = (normed[source_row] * filled[:, None]).reshape(EXPERTS, capacity, width)
    sending = jnp.repeat(outgoing, split_ways, axis=0).reshape(
        blk_count, local_exp, capacity, width
    )
    arrived = lax.all_to_all(sending, "blk", split_axis=0, concat_axis=0, tiled=True)
    sources = arrived.shape[0]
    slot_count = arrived.shape[2]
    stride = sources
    while stride % 2 == 0 and stride * local_exp * slot_count > 1024:
        stride = stride // 2
    grouped = arrived.reshape(sources // stride, stride, local_exp, slot_count, width)

    def one_block(portion):
        gate_out = jnp.einsum("slnd,dlf->slnf", portion, gate_w, preferred_element_type=jnp.float32)
        up_out = jnp.einsum("slnd,dlf->slnf", portion, up_w, preferred_element_type=jnp.float32)
        hidden = (jax.nn.silu(gate_out) * up_out).astype(jnp.bfloat16)
        return jnp.einsum(
            "slnf,dlf->slnd", hidden, down_w, preferred_element_type=jnp.float32
        ).astype(jnp.bfloat16)

    returned = lax.all_to_all(
        lax.map(one_block, grouped).reshape(sources, local_exp, slot_count, width),
        "blk",
        split_axis=0,
        concat_axis=0,
        tiled=True,
    )
    summed_f = jnp.sum(
        returned.reshape(EXPERTS, split_ways, capacity, width).astype(jnp.float32), axis=1
    )
    expert_out = lax.optimization_barrier(summed_f.astype(jnp.bfloat16)).reshape(
        EXPERTS * capacity, width
    )
    gather_index = jnp.where(pair_live, expert_ids * capacity + slot_rank, 0)
    pair_weight = route_weights[0].reshape(-1) * pair_live.astype(jnp.float32)
    moe = jnp.sum(
        (expert_out[gather_index].astype(jnp.float32) * pair_weight[:, None]).reshape(
            rows_here, top_count, width
        ),
        axis=1,
    )
    out_rows = (resid_f + moe).astype(jnp.bfloat16)
    out_f = out_rows.astype(jnp.float32)
    row_squares = jnp.sum(out_f * out_f, axis=-1) * is_valid.astype(jnp.float32)
    square_local = jnp.sum(jnp.where(prompt_match, row_squares[:, None], 0.0), axis=0)
    is_last = is_valid & (position == row_len - 1)
    picker = (prompt_match & is_last[:, None]).astype(jnp.bfloat16)
    last_local = lax.dot_general(
        picker, out_rows, (((0,), (0,)), ((), ())), preferred_element_type=jnp.float32
    )
    last_rows, square_total = lax.psum((last_local, square_local), "blk")
    norms = jnp.sqrt(square_total / (lengths.astype(jnp.float32) * width) + 1e-06)
    final = (
        last_rows
        * lax.rsqrt(jnp.mean(last_rows * last_rows, axis=-1, keepdims=True) + 1e-05)
        * final_gain
    ).astype(jnp.bfloat16)
    logits = lax.dot_general(
        final, unembed, (((1,), (1,)), ((), ())), preferred_element_type=jnp.float32
    )
    vocab_base = blk_index * unembed.shape[0]
    target_hit = (
        target_ids[:, None] == vocab_base + jnp.arange(unembed.shape[0], dtype=jnp.int32)[None, :]
    )
    target_part = jnp.sum(jnp.where(target_hit, logits, 0.0), axis=1)
    top_part = jnp.max(logits, axis=1)
    target_logit, top_logit = merged((target_part, top_part), "blk", combine_stats)
    request_stats = jnp.stack([norms, top_logit, target_logit])
    return (out_rows[None], server, request_stats)


def iota(shape, dim):
    return lax.broadcasted_iota(jnp.int32, shape, dim)


def prep_kernel(lengths_ref, blk_ref, hidden_ref, routes_ref, weights_ref, gain_ref, rows_ref, pieces_ref):
    rows, width = hidden_ref.shape
    length = lengths_ref[blk_ref[0]]
    x = hidden_ref[...].astype(jnp.float32)
    scale = lax.rsqrt(jnp.mean(x * x, axis=-1, keepdims=True) + 1e-05)
    rows_ref[:, :width] = (x * scale * gain_ref[...][None]).astype(jnp.bfloat16)
    column = iota((rows, LANES), 1)
    lane = column & (EXPERTS - 1)
    row = iota((rows, LANES), 0)
    hit = jnp.zeros((rows, LANES), jnp.float32)
    weight = jnp.zeros((rows, LANES), jnp.float32)
    named_by = jnp.transpose(routes_ref[...].astype(jnp.float32)).astype(jnp.int32)
    weight_by = jnp.transpose(weights_ref[...])
    for k in range(routes_ref.shape[0]):
        named = named_by[:, k : k + 1] == lane
        hit = hit + jnp.where(named, 1.0, 0.0)
        weight = weight + jnp.where(named, weight_by[:, k : k + 1], 0.0)
    live = row < length
    hit = jnp.where(live, hit, 0.0)
    weight = jnp.where(live, weight, 0.0)
    before = jnp.where(iota((rows, rows), 1) < iota((rows, rows), 0), 1.0, 0.0)
    rank = jnp.dot(
        before.astype(jnp.bfloat16), hit.astype(jnp.bfloat16), preferred_element_type=jnp.float32
    )
    told = jnp.where(hit > 0.0, rank, -1.0)
    for k in range(3):
        piece = weight.astype(jnp.bfloat16)
        pieces_ref[k * rows : (k + 1) * rows, :] = piece
        value = piece.astype(jnp.float32)
        told = jnp.where(column >= (k + 1) * EXPERTS, value, told)
        weight = weight - value
    rows_ref[:, width:] = told.astype(jnp.bfloat16)


def pick(info, lengths_ref, ring_ref, which, x_ref, width, place, slots, lasts):
    step = pl.program_id(0)
    rows = x_ref.shape[0]
    sources = rows // LEN
    ranks = x_ref[:, width:].astype(jnp.float32)
    lane = iota((rows, LANES), 1)
    row = iota((rows, 1), 0)
    source = row // LEN
    rank = jnp.sum(jnp.where(lane == info[which], ranks, 0.0), axis=1, keepdims=True)
    slot = jnp.where(rank >= 0.0, place(source.astype(jnp.float32), rank), -1.0)
    slot_lane = iota((rows, slots), 1).astype(jnp.float32)
    one_hot = jnp.where(slot == slot_lane, 1.0, 0.0).astype(jnp.bfloat16)
    dims = (((0,), (0,)), ((), ()))
    chosen = lax.dot_general(
        one_hot, x_ref[:, :width], dims, preferred_element_type=jnp.float32
    )
    home = jnp.full_like(row, -1)
    for s in range(sources):
        owner = ring_ref[step * sources + s]
        home = jnp.where(row == s * LEN + lengths_ref[owner] - 1, owner, home)
    home = jnp.where(rank >= 0.0, home, -1)
    count = lasts.shape[0]
    one_hot = jnp.where(home == iota((rows, count), 1), 1.0, 0.0).astype(jnp.bfloat16)
    last = lax.dot_general(one_hot, x_ref[...], dims, preferred_element_type=jnp.float32)

    @pl.when(step == 0)
    def _():
        lasts[...] = last

    @pl.when(step != 0)
    def _():
        lasts[...] += last

    return chosen


def share_of(info, which, lasts, width):
    ext = lasts[:, width:]
    lane = iota(ext.shape, 1)
    is_own = (lane >= EXPERTS) & ((lane & (EXPERTS - 1)) == info[which])
    return jnp.broadcast_to(
        jnp.sum(jnp.where(is_own, ext, 0.0), axis=1, keepdims=True), ext.shape
    )


def activ(x, g_ref, u_ref):
    x = x.astype(jnp.bfloat16)
    gate = jnp.dot(x, g_ref[...], preferred_element_type=jnp.float32)
    up = jnp.dot(x, u_ref[...], preferred_element_type=jnp.float32)
    return (gate / (1.0 + jnp.exp(-gate)) * up).astype(jnp.bfloat16)


def own_kernel(
    info, lengths_ref, ring_ref, x_ref, g_ref, u_ref, out_ref, spot_ref, share_ref, picked, lasts
):
    step = pl.program_id(0)
    sources = x_ref.shape[0] // LEN
    width = g_ref.shape[0]
    more = CAP - FIRST
    early = sources * FIRST
    all_early = GROUPS * early
    all_rows = all_early + GROUPS * sources * more

    def place(source, rank):
        return jnp.where(
            rank < FIRST, source * FIRST + rank, early + source * more + (rank - FIRST)
        )

    chosen = pick(
        info, lengths_ref, ring_ref, 0, x_ref, width, place, early + sources * more, lasts
    )
    for s in range(sources):
        start = pl.multiple_of(ring_ref[step * sources + s] * FIRST, FIRST)
        picked[pl.ds(start, FIRST), :] = chosen[s * FIRST : (s + 1) * FIRST]
    start = pl.multiple_of(all_early + step * sources * more, sources * more)
    picked[pl.ds(start, sources * more), :] = chosen[early:]

    @pl.when(step == GROUPS - 1)
    def _():
        count = lasts.shape[0]
        picked[all_rows : all_rows + count, :] = lasts[:, :width]
        blank = picked.shape[0] - all_rows - count
        picked[all_rows + count :, :] = jnp.zeros((blank, width), jnp.float32)
        out_ref[...] = activ(picked[...], g_ref, u_ref)
        share_ref[...] = share_of(info, 0, lasts, width)
        column = iota(spot_ref.shape, 1)
        owner = lax.shift_right_logical(column, more.bit_length() - 1)
        source = jnp.full_like(column, -1)
        for k, b in enumerate(RING):
            source = jnp.where(owner == k, b, source)
        spot = jnp.where(source >= 0, source * SECOND + (column & (more - 1)), -1)
        spot_ref[...] = jnp.where(iota(spot_ref.shape, 0) == spot, 1.0, 0.0).astype(jnp.bfloat16)


def oth_kernel(
    info,
    lengths_ref,
    ring_ref,
    x_ref,
    g_ref,
    u_ref,
    resid_ref,
    _,
    out_ref,
    share_ref,
    base_ref,
    picked,
    lasts,
):
    step = pl.program_id(0)
    sources = x_ref.shape[0] // LEN
    width = g_ref.shape[0]
    all_rows = GROUPS * sources * SECOND

    def place(source, rank):
        return source * SECOND + (SECOND - CAP) + rank

    chosen = pick(info, lengths_ref, ring_ref, 1, x_ref, width, place, sources * SECOND, lasts)
    for s in range(sources):
        start = pl.multiple_of(ring_ref[step * sources + s] * SECOND, SECOND)
        picked[pl.ds(start, SECOND), :] = chosen[s * SECOND : (s + 1) * SECOND]

    @pl.when(step == GROUPS - 1)
    def _():
        picked[all_rows:, :] = lasts[:, :width]
        out_ref[...] = activ(picked[...], g_ref, u_ref)
        share_ref[...] = share_of(info, 1, lasts, width)
        resid = resid_ref[...].astype(jnp.float32)
        is_last = iota(resid.shape, 0) == info[3] - 1
        last = jnp.sum(jnp.where(is_last, resid, 0.0), axis=0, keepdims=True)
        base_ref[...] = jnp.where(iota(base_ref.shape, 0) == info[4], last, 0.0)


def matmul_nt(hidden_ref, d):
    return lax.dot_general(
        hidden_ref[...], d, (((1,), (1,)), ((), ())), preferred_element_type=jnp.float32
    )


def started(copies):
    for copy in copies:
        copy.start()
    return copies


def waited(copies):
    for copy in copies:
        copy.wait()


def own_down_kernel(
    hidden_any, share_any, d_any, out_any, late_any, part_any, hidden, share, d, out, part, sems
):
    chunks, size = d.shape[:2]
    rows, count = out_any.shape[0], part.shape[1]
    at = rows + count * (CAP - FIRST)
    copy = pltpu.make_async_copy
    first = started(
        [copy(hidden_any, hidden, sems.at[0, 0]), copy(share_any, share, sems.at[0, 1])]
    )
    downs = started(
        [
            copy(d_any.at[k * size : (k + 1) * size], d.at[k], sems.at[1, k])
            for k in range(chunks)
        ]
    )
    waited(first)
    stores = []
    for k in range(chunks):
        downs[k].wait()
        out[k] = matmul_nt(hidden, d[k]).astype(jnp.bfloat16)
        part[k] = share[:, :1] * out[k, at : at + count].astype(jnp.float32)
        columns = slice(k * size, (k + 1) * size)
        stores += started(
            [
                copy(out.at[k, :rows], out_any.at[:, columns], sems.at[2, k]),
                copy(out.at[k, rows:], late_any.at[:, columns], sems.at[3, k]),
                copy(part.at[k], part_any.at[:, columns], sems.at[4, k]),
            ]
        )
    waited(stores)


def oth_down_kernel(
    info,
    hidden_any,
    share_any,
    spot_any,
    late_any,
    base_any,
    part_any,
    d_any,
    out_any,
    sum_any,
    hidden,
    share,
    spot,
    late,
    base,
    part,
    d,
    out,
    total,
    sems,
):
    chunks, size = d.shape[:2]
    rows = out_any.shape[0]
    copy = pltpu.make_async_copy
    other = 1 - info[2]
    sources = (hidden_any, share_any, spot_any, late_any, base_any, part_any)
    targets = (hidden, share, spot, late, base, part)
    downs = started(
        [
            copy(d_any.at[other, k * size : (k + 1) * size], d.at[k], sems.at[1, k])
            for k in range(chunks)
        ]
    )
    first = started([copy(x, y, sems.at[0, k]) for k, (x, y) in enumerate(zip(sources, targets))])
    waited(first)
    stores = []
    for k in range(chunks):
        downs[k].wait()
        columns = slice(k * size, (k + 1) * size)
        placed = jnp.dot(spot[...], late[:, columns], preferred_element_type=jnp.float32)
        value = matmul_nt(hidden, d[k])
        out[k] = (placed + value[:rows]).astype(jnp.bfloat16)
        last = value[rows:].astype(jnp.bfloat16).astype(jnp.float32)
        total[k] = base[:, columns] + part[:, columns] + share[:, :1] * last
        stores += started(
            [
                copy(total.at[k], sum_any.at[:, columns], sems.at[3, k]),
                copy(out.at[k], out_any.at[:, columns], sems.at[2, k]),
            ]
        )
    waited(stores)


def mix_kernel(info, rank_ref, pieces_ref, first_ref, second_ref):
    rows = rank_ref.shape[0]
    late = SECOND - CAP
    own, oth = info[2], 1 - info[2]
    for mix_ref, stride, spans in (
        (first_ref, FIRST, ((own, 0, FIRST, 0),)),
        (second_ref, SECOND, ((own, 0, late, FIRST), (oth, late, CAP, 0))),
    ):
        slots = mix_ref.shape[1]
        expert = iota((LANES, slots), 0)
        lane = iota((LANES, slots), 1)
        within = jnp.zeros((1, slots), jnp.float32)
        spread = jnp.zeros((LANES, slots), jnp.float32)
        for parity, offset, count, lowest in spans:
            start = jnp.where((expert & 1) == parity, (expert >> 1) * stride + offset, slots)
            inside = (lane >= start) & (lane < start + count)
            spread = spread + jnp.where(inside, 1.0, 0.0)
            ranks = jnp.where(inside, lane - start + lowest, 0)
            within = within + jnp.sum(ranks, axis=0, keepdims=True).astype(jnp.float32)
        spread = spread.astype(jnp.bfloat16)
        rank = jnp.dot(rank_ref[...], spread, preferred_element_type=jnp.float32)
        match = rank == within
        for k in range(3):
            part = jnp.dot(
                pieces_ref[k * rows : (k + 1) * rows, :], spread, preferred_element_type=jnp.float32
            )
            mix_ref[k * rows : (k + 1) * rows, :] = jnp.where(match, part, 0.0).astype(jnp.bfloat16)


def weigh(mix_ref, back_ref):
    rows = mix_ref.shape[0] // 3
    parts = jnp.dot(mix_ref[...], back_ref[...], preferred_element_type=jnp.float32)
    return parts[2 * rows :] + parts[rows : 2 * rows] + parts[:rows]


def first_kernel(mix_ref, back_ref, resid_ref, base_ref):
    base_ref[...] = resid_ref[...].astype(jnp.float32) + weigh(mix_ref, back_ref)


def combine_kernel(
    info, mix_any, back_any, base_any, _, out_ref, square_ref, mix, back, base, sems
):
    chunks, size = back.shape[:2]
    rows = base.shape[0]
    copy = pltpu.make_async_copy
    first = started([copy(mix_any, mix, sems.at[chunks])])
    backs = started(
        [copy(back_any.at[k * size : (k + 1) * size], back.at[k], sems.at[k]) for k in range(chunks)]
    )
    late = started([copy(base_any, base, sems.at[chunks + 1])])
    waited(first)
    parts = jnp.zeros((mix.shape[0], base.shape[1]), jnp.float32)
    for k in range(chunks):
        backs[k].wait()
        parts = parts + jnp.dot(
            mix[:, k * size : (k + 1) * size], back[k], preferred_element_type=jnp.float32
        )
    waited(late)
    moe = parts[2 * rows :] + parts[rows : 2 * rows] + parts[:rows]
    out = (base[...] + moe).astype(jnp.bfloat16)
    out_ref[...] = out
    out_f = out.astype(jnp.float32)
    row = iota(out_f.shape, 0)
    total = jnp.sum(jnp.where(row < info[3], out_f * out_f, 0.0), axis=0, keepdims=True)
    square_ref[...] = jnp.broadcast_to(
        jnp.sum(total, axis=1, keepdims=True), square_ref.shape
    )


def place_kernel(info, g_own, g_oth, u_own, u_oth, d_both, _, out_ref):
    left = info[2] == 0
    for k, (own, oth) in enumerate(((g_own[...], g_oth[...]), (u_own[...], u_oth[...]))):
        out_ref[k, :, :FF] = jnp.where(left, own, oth)
        out_ref[k, :, FF:] = jnp.where(left, oth, own)
    out_ref[2, :, :FF] = d_both[0]
    out_ref[2, :, FF:] = d_both[1]


def cast_kernel(first_row, blocks, x_ref, *refs):
    out_ref, held, turned, sems_in, sems_out = refs[-5:]
    groups, size = held.shape[:2]
    fetches, stores = [], []
    for g in range(groups):
        rows = pl.ds(first_row + g * size, size)
        fetches.append(pltpu.make_async_copy(x_ref.at[rows], held.at[g], sems_in.at[g]))
        target = out_ref.at[:, g * 16 : (g + 1) * 16]
        stores.append(pltpu.make_async_copy(turned.at[g], target, sems_out.at[g]))
    for fetch in fetches:
        fetch.start()
    target = iota((size, size), 0)
    source = (target & 15) * blocks + lax.shift_right_logical(target, 4)
    order = jnp.where(iota((size, size), 1) == source, 1.0, 0.0).astype(jnp.bfloat16)
    for g in range(groups):
        fetches[g].wait()
        rows = jnp.dot(order, held[g].astype(jnp.bfloat16), preferred_element_type=jnp.float32)
        turned[g] = rows.astype(jnp.bfloat16).reshape(turned.shape[1:])
        stores[g].start()
    for store in stores:
        store.wait()


def tie_kernel(*_):
    pass


def params():
    return pltpu.CompilerParams(vmem_limit_bytes=VMEM, dimension_semantics=("arbitrary",))


def whole(shape):
    return pl.BlockSpec(shape, lambda *_: tuple(0 for _ in shape))


def paired(
    hidden_in, lengths, routes, route_weights, norm_gain, master, unembed, final_gain, target_ids
):
    rows = hidden_in.shape[1]
    width = hidden_in.shape[2]
    blk_count = lax.axis_size("blk")
    blk = lax.axis_index("blk")
    rep = lax.axis_index("rep")
    first = blk_count * FIRST
    second = blk_count * SECOND
    resid = hidden_in[0]
    info = jnp.stack([2 * blk + rep, 2 * blk + 1 - rep, rep, lengths[blk], blk])
    info = info.astype(jnp.int32)

    shard_rows = master.shape[1]
    flat = master.reshape(3 * shard_rows * blk_count, FF)

    groups = shard_rows // 16

    def turned(k, *after):
        return pl.pallas_call(
            functools.partial(cast_kernel, k * shard_rows * blk_count, blk_count),
            in_specs=[pl.BlockSpec(memory_space=pl.ANY)] * (1 + len(after)),
            out_specs=pl.BlockSpec(memory_space=pl.ANY),
            out_shape=jax.ShapeDtypeStruct((blk_count, shard_rows, FF), jnp.bfloat16),
            scratch_shapes=[
                pltpu.VMEM((groups, 16 * blk_count, FF), jnp.float32),
                pltpu.VMEM((groups, blk_count, 16, FF), jnp.bfloat16),
                pltpu.SemaphoreType.DMA((groups,)),
                pltpu.SemaphoreType.DMA((groups,)),
            ],
            compiler_params=pltpu.CompilerParams(vmem_limit_bytes=VMEM),
            name="cast",
        )(flat, *after)

    def moved(x):
        own = lax.all_to_all(x, "blk", split_axis=0, concat_axis=0, tiled=True)
        return own.reshape(width, FF)

    def swapped(x):
        return lax.ppermute(x, "rep", [(0, 1), (1, 0)])

    def tied(x, *after):
        return pl.pallas_call(
            tie_kernel,
            in_specs=[pl.BlockSpec(memory_space=pl.ANY)] * (1 + len(after)),
            out_specs=pl.BlockSpec(memory_space=pl.ANY),
            out_shape=jax.ShapeDtypeStruct(x.shape, x.dtype),
            input_output_aliases={0: 0},
            name="tie",
        )(x, *after)

    row_ext, pieces = pl.pallas_call(
        prep_kernel,
        grid_spec=pltpu.PrefetchScalarGridSpec(
            num_scalar_prefetch=2,
            grid=(1,),
            in_specs=[
                whole((rows, width)),
                whole((routes.shape[2], rows)),
                whole((routes.shape[2], rows)),
                whole((width,)),
            ],
            out_specs=[whole((rows, width + LANES)), whole((3 * rows, LANES))],
        ),
        out_shape=[
            jax.ShapeDtypeStruct((rows, width + LANES), jnp.bfloat16),
            jax.ShapeDtypeStruct((3 * rows, LANES), jnp.bfloat16),
        ],
        compiler_params=params(),
        name="prep",
    )(lengths, blk[None].astype(jnp.int32), resid, routes[0].T, route_weights[0].T, norm_gain)
    g_own = moved(turned(0, row_ext))
    g_oth = swapped(g_own)
    u_own = moved(turned(1))
    u_oth = swapped(u_own)
    d_own = moved(tied(turned(2), g_oth))

    tokens = lax.all_gather(row_ext, "blk", axis_index_groups=[list(RING)], axis=0, tiled=True)

    ring = jnp.array(RING, jnp.int32)

    def hidden_of(kernel, outs, picked, operands, specs):
        return pl.pallas_call(
            kernel,
            grid_spec=pltpu.PrefetchScalarGridSpec(
                num_scalar_prefetch=3,
                grid=(GROUPS,),
                in_specs=[pl.BlockSpec((blk_count // GROUPS * rows, width + LANES), lambda i, *_: (i, 0))]
                + [whole((width, FF))] * 2
                + specs,
                out_specs=[whole(out.shape) for out in outs],
                scratch_shapes=[
                    pltpu.VMEM((picked, width), jnp.float32),
                    pltpu.VMEM((blk_count, width + LANES), jnp.float32),
                ],
            ),
            out_shape=outs,
            compiler_params=params(),
            name="gate_up",
        )(info, lengths, ring, tokens, *operands)

    step = 512
    quarter = width // 4
    anywhere = pl.BlockSpec(memory_space=pl.ANY)

    def returned(x):
        slots = x.shape[0]
        x = x.reshape(blk_count, slots // blk_count, width)
        x = lax.all_to_all(x, "blk", split_axis=0, concat_axis=0, tiled=True)
        return x.reshape(slots, width)

    def bf16(*shape):
        return jax.ShapeDtypeStruct(shape, jnp.bfloat16)

    def f32(*shape):
        return jax.ShapeDtypeStruct(shape, jnp.float32)

    extra = LANES
    own_hidden, spot, own_share = hidden_of(
        own_kernel,
        [bf16(first + extra, FF), bf16(second, extra), f32(blk_count, LANES)],
        first + extra,
        (g_own, u_own),
        [],
    )
    d_own = tied(d_own, own_hidden)
    d_both = lax.all_gather(d_own, "rep", axis=0)
    own_out, late_out, own_part = pl.pallas_call(
        own_down_kernel,
        in_specs=[anywhere] * 3,
        out_specs=[anywhere] * 3,
        out_shape=[bf16(first, width), bf16(extra, width), f32(blk_count, width)],
        scratch_shapes=[
            pltpu.VMEM((first + extra, FF), jnp.bfloat16),
            pltpu.VMEM((blk_count, LANES), jnp.float32),
            pltpu.VMEM((4, quarter, FF), jnp.bfloat16),
            pltpu.VMEM((4, first + extra, quarter), jnp.bfloat16),
            pltpu.VMEM((4, blk_count, quarter), jnp.float32),
            pltpu.SemaphoreType.DMA((5, 4)),
        ],
        compiler_params=pltpu.CompilerParams(vmem_limit_bytes=VMEM),
        name="own_down",
    )(own_hidden, own_share, d_own)
    own_out = tied(own_out, u_oth)
    own_back = returned(own_out)
    oth_hidden, oth_share, base_part = hidden_of(
        oth_kernel,
        [bf16(second + blk_count, FF), f32(blk_count, LANES), f32(blk_count, width)],
        second + blk_count,
        (g_oth, u_oth, resid, own_out),
        [whole((rows, width)), anywhere],
    )
    oth_out, last_part = pl.pallas_call(
        oth_down_kernel,
        grid_spec=pltpu.PrefetchScalarGridSpec(
            num_scalar_prefetch=1,
            grid=(1,),
            in_specs=[anywhere] * 7,
            out_specs=[anywhere] * 2,
            scratch_shapes=[
                pltpu.VMEM((second + blk_count, FF), jnp.bfloat16),
                pltpu.VMEM((blk_count, LANES), jnp.float32),
                pltpu.VMEM((second, extra), jnp.bfloat16),
                pltpu.VMEM((extra, width), jnp.bfloat16),
                pltpu.VMEM((blk_count, width), jnp.float32),
                pltpu.VMEM((blk_count, width), jnp.float32),
                pltpu.VMEM((4, quarter, FF), jnp.bfloat16),
                pltpu.VMEM((4, second, quarter), jnp.bfloat16),
                pltpu.VMEM((4, blk_count, quarter), jnp.float32),
                pltpu.SemaphoreType.DMA((4, 6)),
            ],
        ),
        out_shape=[bf16(second, width), f32(blk_count, width)],
        compiler_params=params(),
        name="oth_down",
    )(info, oth_hidden, oth_share, spot, late_out, base_part, own_part, d_both)
    last_parts = lax.all_gather(last_part, "blk", axis_index_groups=[list(RING)], axis=0)
    oth_back = returned(oth_out)

    server = pl.pallas_call(
        place_kernel,
        grid_spec=pltpu.PrefetchScalarGridSpec(
            num_scalar_prefetch=1,
            grid=(4,),
            in_specs=[pl.BlockSpec((quarter, FF), lambda i, *_: (i, 0))] * 4
            + [pl.BlockSpec((2, quarter, FF), lambda i, *_: (0, i, 0)), anywhere],
            out_specs=pl.BlockSpec((3, quarter, 2 * FF), lambda i, *_: (0, i, 0)),
        ),
        out_shape=jax.ShapeDtypeStruct((3, width, 2 * FF), jnp.bfloat16),
        compiler_params=params(),
        name="place",
    )(info, g_own, g_oth, u_own, u_oth, d_both, oth_out)

    first_mix, second_mix = pl.pallas_call(
        mix_kernel,
        grid_spec=pltpu.PrefetchScalarGridSpec(
            num_scalar_prefetch=1,
            grid=(1,),
            in_specs=[
                pl.BlockSpec((rows, LANES), lambda i, *_: (0, width // LANES)),
                whole((3 * rows, LANES)),
            ],
            out_specs=[whole((3 * rows, first)), whole((3 * rows, second))],
        ),
        out_shape=[
            jax.ShapeDtypeStruct((3 * rows, first), jnp.bfloat16),
            jax.ShapeDtypeStruct((3 * rows, second), jnp.bfloat16),
        ],
        compiler_params=params(),
        name="mix",
    )(info, row_ext, pieces)

    def weigh_specs(slots):
        return [whole((3 * rows, slots)), pl.BlockSpec((slots, step), lambda i, *_: (0, i))]

    column = pl.BlockSpec((rows, step), lambda i, *_: (0, i))
    base = pl.pallas_call(
        first_kernel,
        grid=(width // step,),
        in_specs=weigh_specs(first) + [column],
        out_specs=column,
        out_shape=f32(rows, width),
        compiler_params=params(),
        name="first",
    )(first_mix, own_back, resid)
    last_rows = lax.reduce_precision(jnp.sum(last_parts, axis=0), 8, 7)
    final = (
        last_rows
        * lax.rsqrt(jnp.mean(last_rows * last_rows, axis=-1, keepdims=True) + 1e-05)
        * final_gain
    ).astype(jnp.bfloat16)
    logits = lax.dot_general(
        final, unembed, (((1,), (1,)), ((), ())), preferred_element_type=jnp.float32
    )
    vocab_base = blk * unembed.shape[0]
    target_hit = (
        target_ids[:, None] == vocab_base + jnp.arange(unembed.shape[0], dtype=jnp.int32)[None, :]
    )
    target_part = jnp.sum(jnp.where(target_hit, logits, 0.0), axis=1)
    top_part = jnp.max(logits, axis=1)

    out_rows, square = pl.pallas_call(
        combine_kernel,
        grid_spec=pltpu.PrefetchScalarGridSpec(
            num_scalar_prefetch=1,
            grid=(1,),
            in_specs=[anywhere] * 4,
            out_specs=[whole((rows, width)), whole((1, LANES))],
            scratch_shapes=[
                pltpu.VMEM((3 * rows, second), jnp.bfloat16),
                pltpu.VMEM((second // LANES, LANES, width), jnp.bfloat16),
                pltpu.VMEM((rows, width), jnp.float32),
                pltpu.SemaphoreType.DMA((second // LANES + 2,)),
            ],
        ),
        out_shape=[bf16(rows, width), f32(1, LANES)],
        compiler_params=params(),
        name="combine",
    )(info, second_mix, oth_back, base, server)

    def everywhere(copies):
        return lax.all_to_all(copies, "blk", split_axis=0, concat_axis=0, tiled=True)

    prompt = jnp.arange(blk_count, dtype=jnp.int32)
    square_part = jnp.where(prompt == blk, square[0, :blk_count], 0.0)
    stats = jnp.stack([top_part, target_part, square_part])
    parts = everywhere(jnp.broadcast_to(stats[None], (blk_count,) + stats.shape))
    sums = jnp.sum(parts[:, 1:], axis=0)
    norms = jnp.sqrt(sums[1] / (lengths.astype(jnp.float32) * width) + 1e-06)
    request_stats = jnp.stack([norms, jnp.max(parts[:, 0], axis=0), sums[0]])
    return (out_rows[None], server, request_stats)


def local(hidden_in, lengths, routes, route_weights, norm_gain, master, *rest):
    blk_count = lax.axis_size("blk")
    fits = (
        lax.axis_size("rep") == 2
        and master.shape[3] == FF
        and EXPERTS == 2 * blk_count
        and blk_count == len(RING)
        and hidden_in.shape[1] == LEN
        and lengths.shape[0] == blk_count
    )
    form = paired if fits else general
    return form(hidden_in, lengths, routes, route_weights, norm_gain, master, *rest)


def solution(mesh):
    return jax.shard_map(
        local,
        mesh=mesh,
        in_specs=(
            P("rep", "blk", None),
            P("rep"),
            P("rep", "blk", None),
            P("rep", "blk", None),
            P(),
            P(None, "blk", None, "rep"),
            P("blk", None),
            P(),
            P("rep"),
        ),
        out_specs=(P("rep", "blk", None), P(None, None, "blk"), P(None, "rep")),
        check_vma=False,
    )
```
